32 devices in a mesh: wide: 16 (over z, x, core), narrow: 2 (over y).
Axes of the slice: x: 2, y: 2, z: 4, core: 2. Of those that a mesh axis runs over, the one named last changes fastest.
Arguments:
- stream: bfloat16 [2, 16, 576, 768], P('narrow', 'wide'), may hold values from -6 to 6
- lengths: int32 [2, 16], P(None, 'wide'), may hold values from 256 to 576, as said below
- layout_boxes: int32 [16, 4, 512], P('wide'), may hold values from 0 to 999, as said below
- self_attn_in: bfloat16 [2, 768, 2304], P('narrow'), may hold values from -0.21875 to 0.21875
- self_attn_out: bfloat16 [2, 768, 768], P('narrow'), may hold values from -1.25 to 1.25
- self_ff_up: bfloat16 [2, 768, 3072], P('narrow'), may hold values from -0.21875 to 0.21875
- self_ff_down: bfloat16 [2, 3072, 768], P('narrow'), may hold values from -0.109375 to 0.109375
- self_vectors: float32 [2, 6, 768], P('narrow'), may hold values from -3 to 3
- self_gains: float32 [2, 2, 768], P('narrow'), may hold values from 0.25 to 1.75
- self_up_bias: float32 [2, 3072], P('narrow'), may hold values from -3 to 3
- cross_attn_in: bfloat16 [2, 768, 2304], P('narrow'), may hold values from -0.21875 to 0.21875
- cross_attn_out: bfloat16 [2, 768, 768], P('narrow'), may hold values from -1.25 to 1.25
- cross_ff_up: bfloat16 [2, 768, 3072], P('narrow'), may hold values from -0.21875 to 0.21875
- cross_ff_down: bfloat16 [2, 3072, 768], P('narrow'), may hold values from -0.109375 to 0.109375
- cross_vectors: float32 [2, 6, 768], P('narrow'), may hold values from -3 to 3
- cross_gains: float32 [2, 2, 768], P('narrow'), may hold values from 0.25 to 1.75
- cross_up_bias: float32 [2, 3072], P('narrow'), may hold values from -3 to 3
- box_table: float32 [2, 768], P('narrow'), may hold values from -5 to 5
- cotangent: bfloat16 [2, 16, 576, 768], P('narrow', 'wide'), may hold values from -6 to 6
Outputs:
- out_stream: float32 [2, 16, 576, 768], P('narrow', 'wide')
- grad_stream: float32 [2, 16, 576, 768], P('narrow', 'wide')
- grad_self_attn_in: float32 [2, 768, 2304], P('narrow', 'wide')
- grad_self_attn_out: float32 [2, 768, 768], P('narrow', 'wide')
- grad_self_ff_up: float32 [2, 768, 3072], P('narrow', 'wide')
- grad_self_ff_down: float32 [2, 3072, 768], P('narrow', 'wide')
- grad_self_vectors: float32 [2, 6, 768], P('narrow', None, 'wide')
- grad_self_gains: float32 [2, 2, 768], P('narrow', None, 'wide')
- grad_self_up_bias: float32 [2, 3072], P('narrow', 'wide')
- grad_cross_attn_in: float32 [2, 768, 2304], P('narrow', 'wide')
- grad_cross_attn_out: float32 [2, 768, 768], P('narrow', 'wide')
- grad_cross_ff_up: float32 [2, 768, 3072], P('narrow', 'wide')
- grad_cross_ff_down: float32 [2, 3072, 768], P('narrow', 'wide')
- grad_cross_vectors: float32 [2, 6, 768], P('narrow', None, 'wide')
- grad_cross_gains: float32 [2, 2, 768], P('narrow', None, 'wide')
- grad_cross_up_bias: float32 [2, 3072], P('narrow', 'wide')
- grad_box_table: float32 [2, 768], P('narrow', 'wide')
The draws below stay inside these ranges and needn't reach their ends.
Inputs may be any that keep to these rules, and one draw needn't show every extreme that they name: `lengths`: row 0 holds each page's text tokens, 256 to 512, with 512 on some page; row 1 holds each page's image patches, 256 or 576, with 576 on some page. `layout_boxes`: each box has x0 < x1 and y0 < y1.
All inputs are finite; a program needn't handle non-finite values.
Results may differ from the reference program's by a relative error of at most 0.033.
Values may be sent and summed in bfloat16 or wider, within the bound.
A program may use at most 320 MiB of HBM per device.

```python
import jax
import jax.numpy as jnp
from jax import lax

D = 768
FF = 3072
H = 12
HD = 64
NB = 32
TEXT = 512
GRID_LO = 16
GRID_HI = 24
PAGES = 16
SLOTS = 576


def draw_lengths(key, part):
    key = jax.random.fold_in(key, 11)
    key_text, key_image, key_chosen = jax.random.split(key, 3)
    text_count = jax.random.randint(key_text, (PAGES,), TEXT // 2, TEXT + 1)
    larger = jax.random.randint(key_image, (PAGES,), 0, 2)
    image_count = GRID_LO * GRID_LO + larger * (GRID_HI * GRID_HI - GRID_LO * GRID_LO)
    chosen = jax.random.randint(key_chosen, (2,), 0, PAGES)
    places = jnp.arange(PAGES)
    text_count = jnp.where(places == chosen[0], TEXT, text_count)
    image_count = jnp.where(places == chosen[1], GRID_HI * GRID_HI, image_count)
    return jnp.stack([text_count, image_count]).astype(jnp.int32)


def draw_layout_boxes(key, part):
    key = jax.random.fold_in(key, 23)
    key_left, key_top, key_wide, key_tall = jax.random.split(key, 4)
    left_edge = jax.random.randint(key_left, (PAGES, TEXT), 0, 900)
    top_edge = jax.random.randint(key_top, (PAGES, TEXT), 0, 950)
    box_width = jax.random.randint(key_wide, (PAGES, TEXT), 10, 100)
    box_height = jax.random.randint(key_tall, (PAGES, TEXT), 8, 50)
    return jnp.stack([left_edge, top_edge, left_edge + box_width, top_edge + box_height], axis=1).astype(jnp.int32)


def levels(key, shape, cuts, low, largest):
    loudness = 1.0
    for position, blocks in cuts:
        heights = jax.random.uniform(jax.random.fold_in(jax.random.fold_in(key, 6), position), (blocks,), jnp.float32, low / len(cuts), largest / len(cuts))
        loudness = loudness * jnp.repeat(jnp.exp(heights), shape[position] // blocks).reshape((-1,) + (1,) * (len(shape) - 1 - position))
    return loudness


def noise(stream_key, shape, scale, reach, cuts=(), held_as=jnp.bfloat16):
    entries = scale * jax.random.normal(stream_key, shape, jnp.float32)
    if cuts:
        entries = entries * levels(stream_key, shape, cuts, -0.22, 0.18)
    return jnp.clip(entries, -reach, reach).astype(held_as)


def setup_inputs(seed: int = 0) -> dict:
    streams_of = jax.random.split(jax.random.key(seed), 20)
    stream = noise(streams_of[0], (2, PAGES, SLOTS, D), 1.0, 6.0, ((0, 2), (1, 16)))
    lengths = draw_lengths(jax.random.fold_in(streams_of[19], 71), 0)
    layout_boxes = draw_layout_boxes(jax.random.fold_in(streams_of[19], 71), 0)
    self_attn_in = noise(streams_of[3], (2, D, 3 * D), D ** -0.5, 0.21875, ((0, 2),))
    self_attn_out = noise(streams_of[4], (2, D, D), (D // 32) ** -0.5, 1.25, ((0, 2),))
    self_ff_up = noise(streams_of[5], (2, D, FF), D ** -0.5, 0.21875, ((0, 2),))
    self_ff_down = noise(streams_of[6], (2, FF, D), FF ** -0.5, 0.109375, ((0, 2),))
    self_vectors = noise(streams_of[7], (2, 6, D), 0.5, 3.0, ((0, 2),), jnp.float32)
    self_gains = jnp.clip(1.0 + 0.15 * jax.random.normal(streams_of[8], (2, 2, D), jnp.float32), 0.25, 1.75)
    self_up_bias = noise(streams_of[9], (2, FF), 0.5, 3.0, ((0, 2),), jnp.float32)
    cross_attn_in = noise(streams_of[10], (2, D, 3 * D), D ** -0.5, 0.21875, ((0, 2),))
    cross_attn_out = noise(streams_of[11], (2, D, D), (D // 32) ** -0.5, 1.25, ((0, 2),))
    cross_ff_up = noise(streams_of[12], (2, D, FF), D ** -0.5, 0.21875, ((0, 2),))
    cross_ff_down = noise(streams_of[13], (2, FF, D), FF ** -0.5, 0.109375, ((0, 2),))
    cross_vectors = noise(streams_of[14], (2, 6, D), 0.5, 3.0, ((0, 2),), jnp.float32)
    cross_gains = jnp.clip(1.0 + 0.15 * jax.random.normal(streams_of[15], (2, 2, D), jnp.float32), 0.25, 1.75)
    cross_up_bias = noise(streams_of[16], (2, FF), 0.5, 3.0, ((0, 2),), jnp.float32)
    box_table = noise(streams_of[17], (2, 2 * NB * H), 1.0, 5.0, ((0, 2),), jnp.float32)
    cotangent = noise(streams_of[18], (2, PAGES, SLOTS, D), 1.0, 6.0, ((0, 2), (1, 16)))
    return {"stream": stream, "lengths": lengths, "layout_boxes": layout_boxes, "self_attn_in": self_attn_in, "self_attn_out": self_attn_out, "self_ff_up": self_ff_up, "self_ff_down": self_ff_down, "self_vectors": self_vectors, "self_gains": self_gains, "self_up_bias": self_up_bias, "cross_attn_in": cross_attn_in, "cross_attn_out": cross_attn_out, "cross_ff_up": cross_ff_up, "cross_ff_down": cross_ff_down, "cross_vectors": cross_vectors, "cross_gains": cross_gains, "cross_up_bias": cross_up_bias, "box_table": box_table, "cotangent": cotangent}


@jax.custom_vjp
def low(v):
    return lax.optimization_barrier(v.astype(jnp.bfloat16)).astype(jnp.float32)

@jax.custom_vjp
def low_back(v):
    return v

def low_keep(v):
    return (low(v), None)

def low_pass(kept, grad):
    return (grad,)

def back_keep(v):
    return (v, None)

def back_low(kept, grad):
    return (low(grad),)
low.defvjp(low_keep, low_pass)
low_back.defvjp(back_keep, back_low)
norm_eps = 1e-05
spacing = 64
masked_score = -1e+30

def norm_rows(values, scales, shifts):
    average = lax.optimization_barrier(jnp.mean(values, axis=-1, keepdims=True))
    centred = values - average
    variance = lax.optimization_barrier(jnp.mean(centred * centred, axis=-1, keepdims=True))
    return centred * lax.rsqrt(variance + norm_eps) * scales + shifts

def matmul(left_side, right_side):
    return jnp.dot(left_side, right_side, precision=lax.Precision.HIGHEST)

def page_centres(boxes_page, patch_count):
    slot_count = GRID_HI * GRID_HI
    padding = jnp.zeros((slot_count - TEXT,), jnp.int32)
    text_x = jnp.concatenate([(boxes_page[0] + boxes_page[2]) // 2, padding]).astype(jnp.int32)
    text_y = jnp.concatenate([(boxes_page[1] + boxes_page[3]) // 2, padding]).astype(jnp.int32)
    grid_side = jnp.where(patch_count > GRID_LO * GRID_LO, GRID_HI, GRID_LO).astype(jnp.int32)
    places = jnp.arange(slot_count, dtype=jnp.int32)
    patch_x = (places % grid_side * 1000 + 500) // grid_side
    patch_y = (places // grid_side * 1000 + 500) // grid_side
    return ((text_x, text_y), (patch_x, patch_y))

def box_bias(centres, tables):
    summed = 0.0
    for direction in range(2):
        coords = centres[direction]
        bucket = jnp.clip((coords[:, None] - coords[None, :]) // spacing + NB // 2, 0, NB - 1).astype(jnp.int32)
        summed = summed + jnp.take(tables[direction], bucket, axis=0)
    return jnp.transpose(summed, (2, 0, 1))

def attend(queries, keys_all, values_all, bias, key_live):
    slot_count = queries.shape[0]
    heads_q = queries.reshape(slot_count, H, HD)
    heads_k = keys_all.reshape(slot_count, H, HD)
    heads_v = values_all.reshape(slot_count, H, HD)
    scores = jnp.einsum('ihd,jhd->hij', heads_q, heads_k, precision=lax.Precision.HIGHEST)
    scores = low_back(scores) * HD ** (-0.5) + bias
    scores = jnp.where(key_live[None, None, :], scores, masked_score)
    peaks = lax.optimization_barrier(jnp.max(scores, axis=-1, keepdims=True))
    raised = jnp.exp(scores - peaks)
    soft_probs = raised / lax.optimization_barrier(jnp.sum(raised, axis=-1, keepdims=True))
    blended = jnp.einsum('hij,jhd->ihd', low(soft_probs), heads_v, precision=lax.Precision.HIGHEST)
    return blended.reshape(slot_count, H * HD)

def block(states, source, weights, key_live, bias):
    attn_in, attn_out, ff_up, ff_down, vectors, gains, up_bias = weights
    own_rows = low(states)
    source_rows = own_rows if source is None else source
    queries = low(low_back(matmul(own_rows, attn_in[:, :D]) + vectors[0]))
    keys_all = low(low_back(matmul(source_rows, attn_in[:, D:2 * D])))
    values_all = low(low_back(matmul(source_rows, attn_in[:, 2 * D:]) + vectors[1]))
    blended = low(low_back(attend(queries, keys_all, values_all, bias, key_live)))
    branch = low_back(matmul(blended, attn_out) + vectors[2])
    normed = norm_rows(states + branch, gains[0], vectors[3])
    hidden = low_back(matmul(low(normed), ff_up) + up_bias)
    active = low(jax.nn.gelu(hidden, approximate=False))
    out_branch = low_back(matmul(active, ff_down) + vectors[4])
    return norm_rows(normed + out_branch, gains[1], vectors[5])

def stream_of(weights, stream_index):
    return tuple((member[stream_index] for member in weights))

def page_pair(pair, counts_page, boxes_page, first_layer, second, tables):
    slot_count = pair.shape[1]
    places = jnp.arange(slot_count, dtype=jnp.int32)
    text_live = places < counts_page[0]
    image_live = places < counts_page[1]
    text_centres, image_centres = page_centres(boxes_page, counts_page[1])
    first_text = block(pair[0], None, stream_of(first_layer, 0), text_live, box_bias(text_centres, tables[0]))
    first_image = block(pair[1], None, stream_of(first_layer, 1), image_live, box_bias(image_centres, tables[1]))
    second_text = block(first_text, low_back(low(first_image)), stream_of(second, 0), image_live, 0.0)
    second_image = block(first_image, low_back(low(first_text)), stream_of(second, 1), text_live, 0.0)
    return jnp.stack([second_text * text_live[:, None], second_image * image_live[:, None]])

def reference(stream, lengths, layout_boxes, self_attn_in, self_attn_out, self_ff_up, self_ff_down, self_vectors, self_gains, self_up_bias, cross_attn_in, cross_attn_out, cross_ff_up, cross_ff_down, cross_vectors, cross_gains, cross_up_bias, box_table, cotangent):
    first_layer = tuple((member.astype(jnp.float32) for member in (self_attn_in, self_attn_out, self_ff_up, self_ff_down, self_vectors, self_gains, self_up_bias)))
    second = tuple((member.astype(jnp.float32) for member in (cross_attn_in, cross_attn_out, cross_ff_up, cross_ff_down, cross_vectors, cross_gains, cross_up_bias)))
    tables = box_table.astype(jnp.float32).reshape(2, 2, NB, H)
    inputs = jnp.transpose(stream.astype(jnp.float32), (1, 0, 2, 3))
    counts = jnp.transpose(lengths)

    def forward(rows_in, first_set, second_set, table_set):

        def one_page(page_data):
            return page_pair(page_data[0], page_data[1], page_data[2], first_set, second_set, table_set)
        return lax.map(jax.checkpoint(one_page), (rows_in, counts, layout_boxes))
    outputs, pullback = jax.vjp(forward, inputs, first_layer, second, tables)
    grad_inputs, grad_first, grad_second, grad_tables = pullback(jnp.transpose(cotangent.astype(jnp.float32), (1, 0, 2, 3)))
    return (jnp.transpose(outputs, (1, 0, 2, 3)), jnp.transpose(grad_inputs, (1, 0, 2, 3)), grad_first[0], grad_first[1], grad_first[2], grad_first[3], grad_first[4], grad_first[5], grad_first[6], grad_second[0], grad_second[1], grad_second[2], grad_second[3], grad_second[4], grad_second[5], grad_second[6], grad_tables.reshape(2, 2 * NB * H))
```

```python
import functools

import jax
import jax.numpy as jnp
from jax import lax
from jax.experimental import pallas as pl
from jax.experimental.pallas import tpu as pltpu
from jax.sharding import PartitionSpec as P

H = 12
HD = 64
NB = 32
TEXT = 512
GRID_LO = 16
GRID_HI = 24
PAIRS = H // 2
STRIP = 192
MIB = 1 << 20

norm_eps = 1e-05
spacing = 64
masked_score = -1e30

f32 = jnp.float32
bf16 = jnp.bfloat16
SMEM = pltpu.MemorySpace.SMEM


def nn(left, right):
    return lax.dot_general(left, right, (((1,), (0,)), ((), ())), preferred_element_type=f32)


def nt(left, right):
    return lax.dot_general(left, right, (((1,), (1,)), ((), ())), preferred_element_type=f32)


def tn(left, right):
    return lax.dot_general(left, right, (((0,), (0,)), ((), ())), preferred_element_type=f32)


def whole(shape):
    return pl.BlockSpec(shape, lambda i: (0,) * len(shape))


def scalar_spec():
    return pl.BlockSpec(memory_space=SMEM)


def call(kernel, grid, in_specs, out_specs, out_shape, scratch, flops, moved, vmem=48):
    return pl.pallas_call(
        kernel,
        grid=grid,
        in_specs=in_specs,
        out_specs=out_specs,
        out_shape=out_shape,
        scratch_shapes=scratch,
        compiler_params=pltpu.CompilerParams(
            dimension_semantics=("arbitrary",),
            vmem_limit_bytes=vmem * MIB,
            fuse_transposed_lhs_in_matmul=True,
        ),
        cost_estimate=pl.CostEstimate(
            flops=int(flops), bytes_accessed=int(moved), transcendentals=0
        ),
    )


def shape_of(shape, dtype):
    return jax.ShapeDtypeStruct(shape, dtype)


def normalise(values):
    average = jnp.mean(values, axis=-1, keepdims=True)
    centred = values - average
    variance = jnp.mean(centred * centred, axis=-1, keepdims=True)
    scale = lax.rsqrt(variance + norm_eps)
    return centred * scale, scale


def normalise_back(grad, unit, scale, gains):
    inner = grad * gains
    mean_one = jnp.mean(inner, axis=-1, keepdims=True)
    mean_two = jnp.mean(inner * unit, axis=-1, keepdims=True)
    return scale * (inner - mean_one - unit * mean_two)


def gelu_both(u):
    size = jnp.abs(u)
    t = 1.0 / (1.0 + (0.3275911 * 0.7071067811865476) * size)
    bell = jnp.exp(-0.5 * (u * u))
    poly = t * (
        0.127414796
        + t * (-0.142248368 + t * (0.7107068705 + t * (-0.7265760135 + t * 0.5307027145)))
    )
    tail = poly * bell
    share = jnp.where(u < 0, tail, 1.0 - tail)
    return u * share, share + u * bell * 0.3989422804014327


def project(rows, weight, vectors, first, count):
    n, d = rows.shape

    def kernel(x_ref, w_ref, v_ref, o_ref):
        part = pl.program_id(0) + first
        shift = jnp.where(part == 0, v_ref[0:1], jnp.where(part == 2, v_ref[1:2], 0.0))
        o_ref[...] = (nn(x_ref[...], w_ref[...]) + shift).astype(bf16)

    return call(
        kernel,
        (count,),
        [
            whole((n, d)),
            pl.BlockSpec((None, d, d), lambda i: (0, 0, i + first)),
            pl.BlockSpec((None, 6, d), lambda i: (0, 0, 0)),
        ],
        pl.BlockSpec((n, d), lambda i: (0, i)),
        shape_of((n, count * d), bf16),
        [],
        2 * n * d * d * count,
        2 * d * d * count,
    )(rows, weight, vectors)


def head_masks():
    lane = lax.broadcasted_iota(jnp.int32, (1, 2 * HD), 1)
    return [
        jnp.where(lane < HD, HD**-0.5, 0.0).astype(bf16),
        jnp.where(lane < HD, 0.0, HD**-0.5).astype(bf16),
    ]


def low_lanes(rows):
    return lax.broadcasted_iota(jnp.int32, (rows, 2 * HD), 1) < HD


def hot_columns(coord_x, coord_y, rows, reverse=False):
    lane = lax.broadcasted_iota(jnp.int32, (rows, 128), 1)
    cell = jnp.where((lane & 16) == 0, coord_x >> 6, coord_y >> 6)
    place = lane & 15
    if reverse:
        place = 15 - place
    return jnp.where((cell == place) & (lane < 64), 1.0, 0.0)


def slanted(row, first):
    wide = jnp.broadcast_to(row, (16, 128))
    return pltpu.roll(wide, (128 - first) % 128, 1, stride=1, stride_axis=0)


def spread_tables(table_x, table_y):
    lane = lax.broadcasted_iota(jnp.int32, (16, 128), 1)
    keep = lane < 16
    outs = []
    rows = []
    for row in (table_x, table_y):
        base = jnp.where(keep, slanted(row, 16), 0.0)
        before = jnp.where(keep, slanted(row, 15), 0.0)
        rows.append((base, before - base))

    def split(value, offset):
        upper = value.astype(bf16).astype(f32)
        lower = value - upper
        joined = upper + pltpu.roll(lower, 32, 1)
        return pltpu.roll(joined, offset, 1) if offset else joined

    zero = jnp.zeros((16, 128), f32)
    outs.append(jnp.concatenate([split(rows[0][0], 0), split(rows[1][0], 16)], axis=0))
    outs.append(jnp.concatenate([split(rows[0][1], 0), zero], axis=0))
    outs.append(jnp.concatenate([zero, split(rows[1][1], 16)], axis=0))
    return [value.astype(bf16) for value in outs]


def attend_forward(arrays, offsets, count, places, tables):
    n = arrays[0].shape[0]
    boxed = places is not None

    def kernel(*refs):
        if boxed:
            cnt, q_ref, k_ref, v_ref, col_ref, row_ref, t_ref, o_ref, p_ref = refs[:9]
            hot_i, hot_j, step_x, step_y = refs[9:]
        else:
            cnt, q_ref, k_ref, v_ref, o_ref, p_ref = refs
        live_count = cnt[0]
        if boxed:

            @pl.when(pl.program_id(0) == 0)
            def _():
                cx, cy = col_ref[:, 0:1], col_ref[:, 1:2]
                hots = hot_columns(cx, cy, n)
                lane = lax.broadcasted_iota(jnp.int32, (n, 128), 1)
                hot_i[...] = jnp.where(lane == 64, 1.0, hots).astype(bf16)
                hot_j[...] = jnp.where(lane < 32, hots, 0.0).astype(bf16)
                rx, ry = row_ref[0:1], row_ref[1:2]
                step_x[...] = jnp.where((cx & 63) < (rx & 63), 1.0, 0.0)
                step_y[...] = jnp.where((cy & 63) < (ry & 63), 1.0, 0.0)

        masks = head_masks()
        k = k_ref[...]
        v = v_ref[...]
        if boxed:
            lane = lax.broadcasted_iota(jnp.int32, (n, 128), 1)
            place = lax.broadcasted_iota(jnp.int32, (n, 128), 0)
            dead = jnp.where((lane == 64) & (place >= live_count), masked_score, 0.0)
            dead = dead.astype(bf16)
            pair = pl.program_id(0)
            sides = []
            hj = hot_j[...][:, :32]
            for h in range(2):
                base, dx, dy = spread_tables(
                    t_ref[pl.ds(4 * pair + 2 * h, 1)], t_ref[pl.ds(4 * pair + 2 * h + 1, 1)]
                )
                sides.append(
                    (
                        jnp.concatenate([k, nn(hj, base).astype(bf16) + dead], axis=1),
                        nn(hj, dx).astype(bf16),
                        nn(hj, dy).astype(bf16),
                    )
                )
        else:
            live = lax.broadcasted_iota(jnp.int32, (1, n), 1) < live_count
        low = low_lanes(STRIP)
        for r in range(0, n, STRIP):
            q = q_ref[r : r + STRIP]
            found = []
            for h in range(2):
                part = q * masks[h]
                if boxed:
                    hi = hot_i[r : r + STRIP]
                    s = nt(jnp.concatenate([part, hi], axis=1), sides[h][0])
                    s = s + step_x[r : r + STRIP] * nt(hi, sides[h][1])
                    s = s + step_y[r : r + STRIP] * nt(hi, sides[h][2])
                else:
                    s = jnp.where(live, nt(part, k), masked_score)
                peak = jnp.max(s, axis=-1, keepdims=True)
                e = jnp.exp(s - peak)
                total = jnp.sum(e, axis=-1, keepdims=True)
                soft = (e * (1.0 / total)).astype(bf16)
                p_ref[h, r : r + STRIP] = soft
                found.append(nn(soft, v))
            o_ref[r : r + STRIP] = jnp.where(low, found[0], found[1]).astype(bf16)

    def pair_block(offset):
        return pl.BlockSpec((n, 128), lambda i: (0, i + offset))

    in_specs = [scalar_spec()] + [pair_block(offset) for offset in offsets]
    args = [count, *arrays]
    scratch = []
    if boxed:
        in_specs += [whole((n, 2)), whole((2, n)), whole((2 * H, 128))]
        args += [*places, tables]
        scratch = [
            pltpu.VMEM((n, 128), bf16),
            pltpu.VMEM((n, 128), bf16),
            pltpu.VMEM((n, n), f32),
            pltpu.VMEM((n, n), f32),
        ]
    return call(
        kernel,
        (PAIRS,),
        in_specs,
        [pair_block(0), pl.BlockSpec((2, n, n), lambda i: (i, 0, 0))],
        [shape_of((n, H * HD), bf16), shape_of((H, n, n), bf16)],
        scratch,
        16 * n * n * H * HD,
        2 * H * n * n,
    )(*args)


def feed_forward(blended, states, weights, count, last):
    _, attn_out, ff_up, ff_down, vectors, gains, up_bias = weights
    n, d = blended.shape
    steps = ff_up.shape[2] // d

    def kernel(cnt, o_ref, x_ref, wo_ref, wu_ref, wd_ref, v_ref, g_ref, e_ref, *rest):
        if last:
            unit1, scale1, rb, act, der, unit2, scale2, out, r_s, acc = rest
        else:
            unit1, scale1, rb, act, der, unit2, scale2, out, out_b, r_s, acc = rest
        step = pl.program_id(0)

        @pl.when(step == 0)
        def _():
            branch = nn(o_ref[...], wo_ref[...]) + v_ref[2:3]
            unit, scale = normalise(x_ref[...].astype(f32) + branch)
            unit1[...] = unit
            scale1[...] = scale
            r = unit * g_ref[0:1] + v_ref[3:4]
            r_s[...] = r
            rb[...] = r.astype(bf16)
            acc[...] = r + v_ref[4:5]

        hidden = nn(rb[...], wu_ref[...]) + e_ref[...]
        active, slope = gelu_both(hidden)
        active = active.astype(bf16)
        act[...] = active
        der[...] = slope.astype(bf16)
        acc[...] += nn(active, wd_ref[...])

        @pl.when(step == steps - 1)
        def _():
            unit, scale = normalise(acc[...])
            unit2[...] = unit
            scale2[...] = scale
            z = unit * g_ref[1:2] + v_ref[5:6]
            if last:
                row = lax.broadcasted_iota(jnp.int32, (n, 1), 0)
                out[...] = jnp.where(row < cnt[0], z, 0.0)
            else:
                out[...] = z
                out_b[...] = z.astype(bf16)

    columns = pl.BlockSpec((n, d), lambda i: (0, i))
    outs = [
        (whole((n, d)), shape_of((n, d), f32)),
        (whole((n, 1)), shape_of((n, 1), f32)),
        (whole((n, d)), shape_of((n, d), bf16)),
        (columns, shape_of((n, steps * d), bf16)),
        (columns, shape_of((n, steps * d), bf16)),
        (whole((n, d)), shape_of((n, d), f32)),
        (whole((n, 1)), shape_of((n, 1), f32)),
        (whole((n, d)), shape_of((n, d), f32)),
    ]
    if not last:
        outs.append((whole((n, d)), shape_of((n, d), bf16)))
    return call(
        kernel,
        (steps,),
        [
            scalar_spec(),
            whole((n, d)),
            whole((n, d)),
            pl.BlockSpec((None, d, d), lambda i: (0, 0, 0)),
            pl.BlockSpec((None, d, d), lambda i: (0, 0, i)),
            pl.BlockSpec((None, d, d), lambda i: (0, i, 0)),
            pl.BlockSpec((None, 6, d), lambda i: (0, 0, 0)),
            pl.BlockSpec((None, 2, d), lambda i: (0, 0, 0)),
            pl.BlockSpec((1, d), lambda i: (0, i)),
        ],
        [spec for spec, _ in outs],
        [shape for _, shape in outs],
        [pltpu.VMEM((n, d), f32), pltpu.VMEM((n, d), f32)],
        2 * n * d * d * (1 + 2 * steps),
        2 * d * d * (1 + 2 * steps),
    )(count, blended, states, attn_out, ff_up, ff_down, vectors, gains, up_bias)


def store_rows(rows):
    d = rows[0].shape[1]
    blank = jnp.zeros((8 - len(rows), d), f32)
    return jnp.concatenate(rows + [blank], axis=0)


def slot_place(index, bits):
    place = 0
    for b in range(bits):
        place = place | (((index >> b) & 1) << (bits - 1 - b))
    return place


class Slots:
    def __init__(self, devices, rows):
        self.devices = devices
        self.rows = rows // devices
        self.bits = (devices // 2).bit_length() - 1
        self.split = self.rows % 16 == 0 and devices & (devices - 1) == 0 and devices > 1

    def put(self, me, held, shards, first_shard, write):
        core = me & 1
        for k in range(shards // 2):
            place = slot_place((first_shard // 2 + k) ^ (me >> 1), self.bits)
            for which in range(2):
                start = (2 * k + (core if which == 0 else 1 - core)) * self.rows
                rows = held[pl.ds(pl.multiple_of(start, 16), self.rows)]
                write(which, place, rows)


def down_gradient(me, count, grads, unit, scale, gains, active, devices, top):
    n, d = unit.shape
    ff = active.shape[1]
    steps = ff // d
    slots = Slots(devices, ff)
    shards = devices // steps

    def kernel(me_ref, cnt, *refs):
        ups = refs[: len(grads)]
        unit_ref, scale_ref, g_ref, act_ref = refs[len(grads) : len(grads) + 4]
        dz, gb, sums, *outs, held = refs[len(grads) + 4 :]
        step = pl.program_id(0)

        @pl.when(step == 0)
        def _():
            if top:
                row = lax.broadcasted_iota(jnp.int32, (n, 1), 0)
                g = jnp.where(row < cnt[0], ups[0][...].astype(f32), 0.0)
            else:
                g = ups[0][...] + ups[1][...].astype(f32)
            unit = unit_ref[...]
            back = normalise_back(g, unit, scale_ref[...], g_ref[1:2])
            dz[...] = back
            low = back.astype(bf16)
            gb[...] = low
            sums[...] = store_rows(
                [
                    jnp.sum(g * unit, axis=0, keepdims=True),
                    jnp.sum(g, axis=0, keepdims=True),
                    jnp.sum(low.astype(f32), axis=0, keepdims=True),
                ]
            )

        value = tn(act_ref[...], gb[...]).astype(bf16)
        if slots.split:
            held[...] = value

            def write(which, place, rows):
                outs[which][place] = rows

            slots.put(me_ref[0], held, shards, shards * step, write)
        else:
            outs[0][...] = value

    if slots.split:
        block = (devices // 2, slots.rows, d)
        out_list = [(whole(block), shape_of(block, bf16))] * 2
    else:
        out_list = [(pl.BlockSpec((d, d), lambda i: (i, 0)), shape_of((ff, d), bf16))]
    out_list = [
        (whole((n, d)), shape_of((n, d), f32)),
        (whole((n, d)), shape_of((n, d), bf16)),
        (whole((8, d)), shape_of((8, d), f32)),
    ] + out_list
    results = call(
        kernel,
        (steps,),
        [scalar_spec(), scalar_spec()]
        + [whole((n, d))] * len(grads)
        + [
            whole((n, d)),
            whole((n, 1)),
            pl.BlockSpec((None, 2, d), lambda i: (0, 0, 0)),
            pl.BlockSpec((n, d), lambda i: (0, i)),
        ],
        [spec for spec, _ in out_list],
        [shape for _, shape in out_list],
        [pltpu.VMEM((d, d), bf16)],
        2 * n * d * ff,
        4 * d * ff,
    )(me, count, *grads, unit, scale, gains, active)
    return results[0], results[1], results[2], results[3:]


def feed_backward(grad_sum, grad_branch, slope, unit, scale, weights):
    _, attn_out, ff_up, ff_down, _, gains, _ = weights
    n, d = grad_sum.shape
    steps = ff_up.shape[2] // d

    def kernel(
        dz, gb, der, wd, wu, wo, g_ref, unit_ref, scale_ref, du, ups, ga, gr, do, sums, acc
    ):
        step = pl.program_id(0)

        @pl.when(step == 0)
        def _():
            acc[...] = dz[...]

        grad = (nt(gb[...], wd[...]) * der[...].astype(f32)).astype(bf16)
        du[...] = grad
        ups[...] = jnp.sum(grad.astype(f32), axis=0, keepdims=True)
        acc[...] += nt(grad, wu[...])

        @pl.when(step == steps - 1)
        def _():
            g = acc[...]
            unit = unit_ref[...]
            back = normalise_back(g, unit, scale_ref[...], g_ref[0:1])
            gr[...] = back
            low = back.astype(bf16)
            ga[...] = low
            sums[...] = store_rows(
                [
                    jnp.sum(g * unit, axis=0, keepdims=True),
                    jnp.sum(g, axis=0, keepdims=True),
                    jnp.sum(low.astype(f32), axis=0, keepdims=True),
                ]
            )
            do[...] = nt(low, wo[...]).astype(bf16)

    columns = pl.BlockSpec((n, d), lambda i: (0, i))
    return call(
        kernel,
        (steps,),
        [
            whole((n, d)),
            whole((n, d)),
            columns,
            pl.BlockSpec((None, d, d), lambda i: (0, i, 0)),
            pl.BlockSpec((None, d, d), lambda i: (0, 0, i)),
            pl.BlockSpec((None, d, d), lambda i: (0, 0, 0)),
            pl.BlockSpec((None, 2, d), lambda i: (0, 0, 0)),
            whole((n, d)),
            whole((n, 1)),
        ],
        [
            columns,
            pl.BlockSpec((1, d), lambda i: (0, i)),
            whole((n, d)),
            whole((n, d)),
            whole((n, d)),
            whole((8, d)),
        ],
        [
            shape_of((n, steps * d), bf16),
            shape_of((1, steps * d), f32),
            shape_of((n, d), bf16),
            shape_of((n, d), f32),
            shape_of((n, d), bf16),
            shape_of((8, d), f32),
        ],
        [pltpu.VMEM((n, d), f32)],
        2 * n * d * d * (1 + 2 * steps),
        2 * d * d * (1 + 2 * steps),
    )(grad_sum, grad_branch, slope, ff_down, ff_up, attn_out, gains, unit, scale)


def weight_gradients(me, jobs, lefts, rights, devices):
    n, d = lefts[0].shape
    slots = Slots(devices, d)
    steps = len(jobs)

    def kernel(me_ref, *refs):
        left_refs = refs[: len(lefts)]
        right_refs = refs[len(lefts) : len(lefts) + len(rights)]
        *outs, turned, held = refs[len(lefts) + len(rights) :]
        step = pl.program_id(0)
        for index in range(len(lefts)):
            mine = [j for j, job in enumerate(jobs) if job[0] == index]

            @pl.when(step == mine[0])
            def _(index=index):
                turned[...] = left_refs[index][...].T

        for index in range(len(rights)):
            mine = [j for j, job in enumerate(jobs) if job[1] == index]

            @pl.when((step >= mine[0]) & (step <= mine[-1]))
            def _(index=index):
                value = nn(turned[...], right_refs[index][...]).astype(bf16)
                if slots.split:
                    held[...] = value
                else:
                    outs[0][...] = value

        if slots.split:

            def write(which, place, rows):
                outs[which][place, step] = rows

            slots.put(me_ref[0], held, devices, 0, write)

    def right_spec(index):
        mine = [(j, job[2]) for j, job in enumerate(jobs) if job[1] == index]
        first, block = mine[0]

        def place(i):
            return (0, jnp.clip(i - first, 0, len(mine) - 1) + block)

        return pl.BlockSpec((n, d), place)

    if slots.split:
        block = (devices // 2, steps, slots.rows, d)
        out_list = [(whole(block), shape_of(block, bf16))] * 2
    else:
        out_list = [(pl.BlockSpec((d, d), lambda i: (0, i)), shape_of((d, steps * d), bf16))]
    return call(
        kernel,
        (steps,),
        [scalar_spec()]
        + [whole((n, d))] * len(lefts)
        + [right_spec(index) for index in range(len(rights))],
        [spec for spec, _ in out_list],
        [shape for _, shape in out_list],
        [pltpu.VMEM((d, n), bf16), pltpu.VMEM((d, d), bf16)],
        2 * n * d * d * steps,
        4 * d * d * steps,
    )(me, *lefts, *rights)


def attend_backward(arrays, offsets, grad_blended, soft, places):
    n = grad_blended.shape[0]
    boxed = places is not None

    def kernel(*refs):
        q_ref, k_ref, v_ref, g_ref, p_ref = refs[:5]
        if boxed:
            col_ref, row_ref = refs[5:7]
            dq_ref, dk_ref, dv_ref, sums, tab = refs[7:12]
            hot_i, hot_j, step_x, step_y, ds_s, far = refs[12:]

            @pl.when(pl.program_id(0) == 0)
            def _():
                cx, cy = col_ref[:, 0:1], col_ref[:, 1:2]
                rx, ry = row_ref[0:1], row_ref[1:2]
                lane = lax.broadcasted_iota(jnp.int32, (n, 128), 1)
                hots = hot_columns(cx, cy, n, reverse=True)
                hot_j[...] = jnp.where(lane < 32, hots, 0.0).astype(bf16)
                row = lax.broadcasted_iota(jnp.int32, (32, n), 0)
                cell = jnp.where(row < 16, rx >> 6, ry >> 6)
                hot_i[...] = jnp.where(cell == (row & 15), 1.0, 0.0).astype(bf16)
                step_x[...] = jnp.where((cx & 63) < (rx & 63), 1.0, 0.0).astype(bf16)
                step_y[...] = jnp.where((cy & 63) < (ry & 63), 1.0, 0.0).astype(bf16)
        else:
            dq_ref, dk_ref, dv_ref, sums, ds_s = refs[5:]
        masks = head_masks()
        q = q_ref[...]
        k = k_ref[...]
        v = v_ref[...]
        g = g_ref[...]
        grads = []
        for h in range(2):
            queries = []
            for r in range(0, n, STRIP):
                gh = g[r : r + STRIP] * masks[h]
                p = p_ref[h, r : r + STRIP].astype(f32)
                dp = nt(gh, v)
                mean = jnp.sum(p * dp, axis=-1, keepdims=True)
                ds = (p * (dp - mean)).astype(bf16)
                ds_s[r : r + STRIP] = ds
                if boxed:
                    hj = hot_j[...]
                    wide = nn(ds, jnp.concatenate([k, hj], axis=1))
                    queries.append(wide[:, :128])
                    far[r : r + STRIP, 0:128] = wide[:, 128:]
                    far[r : r + STRIP, 128:256] = nn(ds * step_x[r : r + STRIP], hj)
                    far[r : r + STRIP, 256:384] = nn(ds * step_y[r : r + STRIP], hj)
                else:
                    queries.append(nn(ds, k))
            grads.append(
                (jnp.concatenate(queries, axis=0), tn(ds_s[...], q), tn(p_ref[h], g))
            )
            if boxed:
                value = far[...]
                upper = value.astype(bf16)
                lower = (value - upper.astype(f32)).astype(bf16)
                cells = nn(hot_i[...], upper) + nn(hot_i[...], lower)
                lane = lax.broadcasted_iota(jnp.int32, (16, 128), 1)
                for direction in range(2):
                    rows = slice(16 * direction, 16 * direction + 16)
                    level = cells[rows, 0:128]
                    above = cells[rows, 128 * (direction + 1) : 128 * (direction + 2)]
                    inside = (lane >= 16 * direction) & (lane < 16 * direction + 16)
                    level = jnp.where(inside, level - above, 0.0)
                    above = jnp.where(inside, above, 0.0)
                    turn = (128 + 1 - 16 * direction) % 128
                    line = pltpu.roll(level, turn, 1, stride=1, stride_axis=0)
                    line = line + pltpu.roll(above, (turn + 127) % 128, 1, stride=1, stride_axis=0)
                    line = jnp.sum(line, axis=0, keepdims=True) * HD**0.5
                    tab[2 * h + direction : 2 * h + direction + 1] = line
        low = low_lanes(n)
        outs = []
        for index, ref in enumerate((dq_ref, dk_ref, dv_ref)):
            value = jnp.where(low, grads[0][index], grads[1][index]).astype(bf16)
            ref[...] = value
            outs.append(jnp.sum(value.astype(f32), axis=0, keepdims=True))
        sums[...] = store_rows([outs[0], outs[2]])

    def pair_block(offset):
        return pl.BlockSpec((n, 128), lambda i: (0, i + offset))

    in_specs = [pair_block(offset) for offset in offsets] + [
        pair_block(0),
        pl.BlockSpec((2, n, n), lambda i: (i, 0, 0)),
    ]
    args = [*arrays, grad_blended, soft]
    outs = [(pair_block(0), shape_of((n, H * HD), bf16))] * 3
    outs.append((pl.BlockSpec((8, 128), lambda i: (0, i)), shape_of((8, H * HD), f32)))
    scratch = [pltpu.VMEM((n, n), bf16)]
    if boxed:
        in_specs += [whole((n, 2)), whole((2, n))]
        args += [*places]
        outs.append(
            (pl.BlockSpec((None, 4, 128), lambda i: (i, 0, 0)), shape_of((PAIRS, 4, 128), f32))
        )
        scratch = [
            pltpu.VMEM((32, n), bf16),
            pltpu.VMEM((n, 128), bf16),
            pltpu.VMEM((n, n), bf16),
            pltpu.VMEM((n, n), bf16),
            pltpu.VMEM((n, n), bf16),
            pltpu.VMEM((n, 384), f32),
        ]
    return call(
        kernel,
        (PAIRS,),
        in_specs,
        [spec for spec, _ in outs],
        [shape for _, shape in outs],
        scratch,
        16 * n * n * H * HD,
        2 * H * n * n,
    )(*args)


def project_back(grads, weight, first, residual, out_type):
    n, d = grads[0].shape
    steps = len(grads)

    def kernel(*refs):
        g_refs = refs[:steps]
        w_ref = refs[steps]
        out, acc = refs[-2:]
        step = pl.program_id(0)
        for index in range(steps):

            @pl.when(step == index)
            def _(index=index):
                value = nt(g_refs[index][...], w_ref[...])
                if index > 0:
                    value = value + acc[...]
                elif residual is not None:
                    value = value + refs[steps + 1][...]
                if index == steps - 1:
                    out[...] = value.astype(out_type)
                else:
                    acc[...] = value

    extra = [] if residual is None else [residual]
    return call(
        kernel,
        (steps,),
        [whole((n, d))] * steps
        + [pl.BlockSpec((None, d, d), lambda i: (0, 0, i + first))]
        + [whole((n, d))] * len(extra),
        whole((n, d)),
        shape_of((n, d), out_type),
        [pltpu.VMEM((n, d), f32)],
        2 * n * d * d * steps,
        2 * d * d * steps,
    )(*grads, weight, *extra)


MESH = pl.DeviceIdType.MESH


class Parts:
    def __init__(self):
        self.inputs, self.outputs, self.scratch = [], [], []

    def inp(self, name, array, spec):
        self.inputs.append((name, array, spec))

    def out(self, name, shape, dtype, spec):
        self.outputs.append((name, shape_of(shape, dtype), spec))

    def tmp(self, name, kind):
        self.scratch.append((name, kind))

    def run(self, body, steps, flops, moved, collective):
        names = [x[0] for x in self.inputs + self.outputs + self.scratch]

        def kernel(*refs):
            body(dict(zip(names, refs)))

        results = pl.pallas_call(
            kernel,
            grid=(steps,),
            in_specs=[x[2] for x in self.inputs],
            out_specs=[x[2] for x in self.outputs],
            out_shape=[x[1] for x in self.outputs],
            scratch_shapes=[x[1] for x in self.scratch],
            compiler_params=pltpu.CompilerParams(
                dimension_semantics=("arbitrary",),
                vmem_limit_bytes=63 * MIB,
                fuse_transposed_lhs_in_matmul=True,
                collective_id=collective,
                has_side_effects=True,
            ),
            cost_estimate=pl.CostEstimate(
                flops=int(flops), bytes_accessed=int(moved), transcendentals=0
            ),
        )(*[x[1] for x in self.inputs])
        return dict(zip([x[0] for x in self.outputs], results))


def fixed(shape):
    return pl.BlockSpec(shape, lambda i: (0,) * len(shape), pipeline_mode=pl.Buffered(1))


def anywhere():
    return pl.BlockSpec(memory_space=pl.ANY)


def bit_of(me, bit):
    return lax.rem(lax.div(me, bit), 2)


class Chunk:
    def __init__(self, name, blocks, rows, bits, d):
        self.name, self.blocks, self.rows, self.bits, self.d = name, blocks, rows, bits, d

    def shape(self, slots):
        return (slots, self.blocks, self.rows, self.d)

    def place(self, me, shard_bits):
        place = 0
        for position, bit in enumerate(self.bits[1:]):
            mine = bit_of(me, bit)
            static = shard_bits[bit]
            place = place + (1 - mine if static else mine) * (4 >> position)
        return place

    def put(self, me, held, shards, base, keep, send, block, height):
        core = bit_of(me, 1)
        for k in range(shards // 2):
            shard_bits = {}
            for bit in self.bits[1:]:
                if bit < shards:
                    shard_bits[bit] = (2 * k // bit) % 2
            place = 0
            for position, bit in enumerate(self.bits[1:]):
                mine = bit_of(me, bit)
                if bit in shard_bits:
                    different = 1 - mine if shard_bits[bit] else mine
                else:
                    theirs = bit_of(base, bit)
                    different = mine + theirs - 2 * mine * theirs
                place = place + different * (4 >> position)
            for which, ref in ((core, keep), (1 - core, send)):
                start = pl.multiple_of((2 * k + which) * height, 16)
                for b in range(height // self.rows):
                    rows = held[pl.ds(pl.multiple_of(start + b * self.rows, 16), self.rows)]
                    ref[place, block + b] = rows


class Leg:
    def __init__(self, chunk, blocks, first, times):
        self.chunk, self.blocks, self.first, self.times = chunk, blocks, first, times
        self.last = first + len(times)


class Traffic:
    def __init__(self, parts, legs, carried, fresh, small=None, cross=None):
        self.legs, self.carried, self.fresh = legs, carried, fresh
        self.small, self.cross = small, cross
        self.hops = []
        self.loads = []
        bits = set()
        chunks = {}
        for leg in legs:
            info = chunks.setdefault(leg.chunk, [leg.first, leg.last])
            info[0], info[1] = min(info[0], leg.first), max(info[1], leg.last)
        for chunk in fresh:
            chunks.setdefault(chunk, [0, 0])
        for chunk, (first, last) in chunks.items():
            name = chunk.name
            slots = 8 if first == 0 else 16 >> first
            if last == 4:
                parts.tmp(name + ".keep", pltpu.VMEM(chunk.shape(slots), bf16))
                shape = (chunk.blocks, chunk.rows, chunk.d)
                parts.out(name + ".done", shape, f32, fixed(shape))
            else:
                shape = chunk.shape(slots)
                parts.out(name + ".keep", shape, bf16, fixed(shape))
            if chunk in fresh:
                if last == 0:
                    shape = chunk.shape(8)
                    parts.out(name + ".send", shape, bf16, fixed(shape))
                else:
                    parts.tmp(name + ".send", pltpu.VMEM(chunk.shape(8), bf16))
            else:
                kept, sent = carried[chunk]
                parts.inp(name + ".hbm", kept, anywhere())
                self.loads.append((chunk, slots))
                if first == 0:
                    parts.inp(name + ".send", sent, anywhere())
            for hop in range(first, last):
                parts.tmp(f"{name}.got{hop}", pltpu.VMEM(chunk.shape(8 >> hop), bf16))
                bits.add(chunk.bits[hop])
        for leg in legs:
            for hop, (start, end) in zip(range(leg.first, leg.last), leg.times):
                self.hops.append((leg, hop, start, end))
        count = len(self.hops)
        if small is not None:
            shape, times = small
            self.small_times = times
            parts.tmp("small.sum", pltpu.VMEM(shape, f32))
            parts.tmp("small.got", pltpu.VMEM((4,) + shape, f32))
            parts.out("small.done", shape, f32, fixed(shape))
            bits |= {1, 2, 4, 8}
            self.small_base = count
            count += 4
        if cross is not None:
            shape, times = cross
            self.cross_times = times
            parts.tmp("cross.out", pltpu.VMEM(shape, bf16))
            parts.tmp("cross.got", pltpu.VMEM(shape, bf16))
            parts.out("cross.in", shape, bf16, fixed(shape))
            self.cross_base = count
            count += 1
        parts.tmp("sent", pltpu.SemaphoreType.DMA((count,)))
        parts.tmp("arrived", pltpu.SemaphoreType.DMA((count,)))
        if self.loads:
            parts.tmp("loaded", pltpu.SemaphoreType.DMA((len(self.loads),)))
        self.bits = sorted(bits)

    def device(self, me, bit):
        return {"wide": me + bit - 2 * bit * bit_of(me, bit)}

    def open(self, refs, me, side):
        loads = []
        for index, (chunk, slots) in enumerate(self.loads):
            copy = pltpu.make_async_copy(
                refs[chunk.name + ".hbm"].at[pl.ds(0, slots)],
                refs[chunk.name + ".keep"],
                refs["loaded"].at[index],
            )
            copy.start()
            loads.append(copy)
        barrier = pltpu.get_barrier_semaphore()
        peers = [self.device(me, bit) for bit in self.bits]
        if self.cross is not None:
            peers.append({"narrow": 1 - side})
        for peer in peers:
            pl.semaphore_signal(barrier, inc=1, device_id=peer, device_id_type=MESH)
        pl.semaphore_wait(barrier, len(peers))
        for copy in loads:
            copy.wait()

    def hop_copy(self, refs, me, index):
        leg, hop, _, _ = self.hops[index]
        chunk = leg.chunk
        low, high = leg.blocks
        blocks = pl.ds(low, high - low)
        slots = 8 >> hop
        if hop == 0:
            source = refs[chunk.name + ".send"].at[pl.ds(0, 8), blocks]
        else:
            source = refs[chunk.name + ".keep"].at[pl.ds(slots, slots), blocks]
        return pltpu.make_async_remote_copy(
            src_ref=source,
            dst_ref=refs[f"{chunk.name}.got{hop}"].at[pl.ds(0, slots), blocks],
            send_sem=refs["sent"].at[index],
            recv_sem=refs["arrived"].at[index],
            device_id=self.device(me, chunk.bits[hop]),
            device_id_type=MESH,
        )

    def finish(self, refs, me, index):
        self.hop_copy(refs, me, index).wait()
        leg, hop, _, _ = self.hops[index]
        name = leg.chunk.name
        keep, got = refs[name + ".keep"], refs[f"{name}.got{hop}"]
        low, high = leg.blocks
        if hop == 3:
            for b in range(low, high):
                refs[name + ".done"][b] = keep[0, b].astype(f32) + got[0, b].astype(f32)
        else:

            @pl.loop(0, 8 >> hop)
            def _(slot):
                for b in range(low, high):
                    total = keep[slot, b].astype(f32) + got[slot, b].astype(f32)
                    keep[slot, b] = total.astype(bf16)

    def small_copy(self, refs, me, hop):
        return pltpu.make_async_remote_copy(
            src_ref=refs["small.sum"],
            dst_ref=refs["small.got"].at[hop],
            send_sem=refs["sent"].at[self.small_base + hop],
            recv_sem=refs["arrived"].at[self.small_base + hop],
            device_id=self.device(me, 1 << hop),
            device_id_type=MESH,
        )

    def cross_copy(self, refs, side):
        return pltpu.make_async_remote_copy(
            src_ref=refs["cross.out"],
            dst_ref=refs["cross.got"],
            send_sem=refs["sent"].at[self.cross_base],
            recv_sem=refs["arrived"].at[self.cross_base],
            device_id={"narrow": 1 - side},
            device_id_type=MESH,
        )

    def events(self):
        found = []
        for index, (_, _, start, end) in enumerate(self.hops):
            found.append((*end, 0, "finish", index))
            found.append((*start, 1, "start", index))
        if self.small is not None:
            for hop, (start, end) in enumerate(self.small_times):
                found.append((*end, 0, "small finish", hop))
                found.append((*start, 1, "small start", hop))
        if self.cross is not None:
            start, end = self.cross_times
            found.append((*end, 0, "cross finish", 0))
            found.append((*start, 1, "cross start", 0))
        return sorted(found, key=lambda e: e[:3])

    def fire(self, refs, me, side, step, low, high):
        found = [e for e in self.events() if low <= e[1] < high]
        for at in sorted({e[0] for e in found}):

            @pl.when(step == at)
            def _(at=at):
                for _, _, _, action, index in [e for e in found if e[0] == at]:
                    if action == "start":
                        self.hop_copy(refs, me, index).start()
                    elif action == "finish":
                        self.finish(refs, me, index)
                    elif action == "small start":
                        self.small_copy(refs, me, index).start()
                    elif action == "small finish":
                        self.small_copy(refs, me, index).wait()
                        total = refs["small.sum"][...] + refs["small.got"][index]
                        refs["small.sum"][...] = total
                        if index == 3:
                            refs["small.done"][...] = total
                    elif action == "cross start":
                        self.cross_copy(refs, side).start()
                    else:
                        self.cross_copy(refs, side).wait()
                        refs["cross.in"][...] = refs["cross.got"][...]


PRE, MID, POST = 0, 1, 2


def ff_back(grads, count, saved, weights, down, up, legs, carried, collective):
    _, attn_out, ff_up, ff_down, _, gains, _ = weights
    unit1, scale1, rb, act, slope, unit2, scale2, blended = saved
    n, d = unit1.shape
    tiles = act.shape[1] // d
    steps = 2 * tiles + 1
    top = len(grads) == 1
    parts = Parts()
    parts.inp("count", count, scalar_spec())
    for index, grad in enumerate(grads):
        parts.inp(f"grad{index}", grad, fixed((n, d)))
    first = lambda i: jnp.minimum(i, tiles - 1)
    later = lambda i: jnp.clip(i - tiles, 0, tiles - 1)
    parts.inp("act", act, pl.BlockSpec((n, d), lambda i: (0, first(i))))
    parts.inp("slope", slope, pl.BlockSpec((n, d), lambda i: (0, later(i))))
    parts.inp("wd", ff_down, pl.BlockSpec((None, d, d), lambda i: (0, later(i), 0)))
    parts.inp("wu", ff_up, pl.BlockSpec((None, d, d), lambda i: (0, 0, later(i))))
    parts.inp("wo", attn_out, fixed((None, d, d)))
    parts.inp("gains", gains, fixed((None, 2, d)))
    parts.inp("unit1", unit1, fixed((n, d)))
    parts.inp("scale1", scale1, fixed((n, 1)))
    parts.inp("unit2", unit2, fixed((n, d)))
    parts.inp("scale2", scale2, fixed((n, 1)))
    parts.inp("rb", rb, fixed((n, d)))
    parts.inp("blended", blended, fixed((n, d)))
    parts.out("gr", (n, d), f32, fixed((n, d)))
    parts.out("do", (n, d), bf16, fixed((n, d)))
    parts.out("sums", (16, d), f32, fixed((16, d)))
    parts.tmp("acc", pltpu.VMEM((n, d), f32))
    parts.tmp("gb", pltpu.VMEM((n, d), bf16))
    parts.tmp("turned", pltpu.VMEM((d, n), bf16))
    parts.tmp("held", pltpu.VMEM((d, d), bf16))
    traffic = Traffic(parts, legs, carried, [down, up])

    def body(refs):
        step = pl.program_id(0)
        me, side = lax.axis_index("wide"), lax.axis_index("narrow")
        sums = refs["sums"]

        @pl.when(step == 0)
        def _():
            traffic.open(refs, me, side)
            if top:
                row = lax.broadcasted_iota(jnp.int32, (n, 1), 0)
                g = jnp.where(row < refs["count"][0], refs["grad0"][...].astype(f32), 0.0)
            else:
                g = refs["grad0"][...] + refs["grad1"][...].astype(f32)
            unit = refs["unit2"][...]
            back = normalise_back(g, unit, refs["scale2"][...], refs["gains"][1:2])
            refs["acc"][...] = back
            low = back.astype(bf16)
            refs["gb"][...] = low
            sums[0:8] = jnp.zeros((8, d), f32)
            sums[8:16] = jnp.zeros((8, d), f32)
            sums[4:5] = jnp.sum(low.astype(f32), axis=0, keepdims=True)
            sums[5:6] = jnp.sum(g, axis=0, keepdims=True)
            sums[7:8] = jnp.sum(g * unit, axis=0, keepdims=True)

        traffic.fire(refs, me, side, step, PRE, MID)

        @pl.when(step < tiles)
        def _():
            refs["held"][...] = tn(refs["act"][...], refs["gb"][...]).astype(bf16)
            down.put(
                me, refs["held"], 16 // tiles, step * (16 // tiles),
                refs["down.keep"], refs["down.send"], 0, d * tiles // 16,
            )

        @pl.when(step == tiles)
        def _():
            refs["turned"][...] = refs["rb"][...].T

        @pl.when((step >= tiles) & (step < 2 * tiles))
        def _():
            grad = nt(refs["gb"][...], refs["wd"][...]) * refs["slope"][...].astype(f32)
            grad = grad.astype(bf16)
            sums[pl.ds(8 + step - tiles, 1)] = jnp.sum(grad.astype(f32), axis=0, keepdims=True)
            refs["acc"][...] += nt(grad, refs["wu"][...])
            refs["held"][...] = nn(refs["turned"][...], grad).astype(bf16)

        @pl.when(step == 2 * tiles)
        def _():
            refs["turned"][...] = refs["blended"][...].T
            g = refs["acc"][...]
            unit = refs["unit1"][...]
            back = normalise_back(g, unit, refs["scale1"][...], refs["gains"][0:1])
            refs["gr"][...] = back
            low = back.astype(bf16)
            sums[2:3] = jnp.sum(low.astype(f32), axis=0, keepdims=True)
            sums[3:4] = jnp.sum(g, axis=0, keepdims=True)
            sums[6:7] = jnp.sum(g * unit, axis=0, keepdims=True)
            refs["do"][...] = nt(low, refs["wo"][...]).astype(bf16)
            refs["held"][...] = nn(refs["turned"][...], low).astype(bf16)

        @pl.when(step >= tiles)
        def _():
            up.put(
                me, refs["held"], 16, 0, refs["up.keep"], refs["up.send"], step - tiles, up.rows
            )

        traffic.fire(refs, me, side, step, MID, 10)

    return parts.run(body, steps, 2 * n * d * d * (4 * tiles), 4 * d * d * tiles, collective)


def attn_back(
    arrays, offsets, grad_blended, soft, places, weight, left_rows, residual, inner,
    legs, carried, small, cross, collective,
):
    n, d = grad_blended.shape
    groups = 3
    wide = d // groups
    heads = H // groups
    steps = 2 * groups
    boxed = places is not None
    parts = Parts()
    early = lambda i: jnp.minimum(i, groups - 1)
    later = lambda i: jnp.clip(i - groups, 0, groups - 1)
    for name, array, offset in zip("qkv", arrays, offsets):
        parts.inp(
            name, array, pl.BlockSpec((n, wide), lambda i, o=offset: (0, early(i) + o // 2))
        )
    parts.inp("g", grad_blended, pl.BlockSpec((n, wide), lambda i: (0, early(i))))
    parts.inp("p", soft, pl.BlockSpec((heads, n, n), lambda i: (early(i), 0, 0)))
    for index, name in enumerate(("wq", "wk", "wv")):
        when = early if (not boxed and index > 0) else later
        parts.inp(
            name,
            weight,
            pl.BlockSpec((None, d, wide), lambda i, w=when, k=index: (0, 0, w(i) + groups * k)),
        )
    for index, rows in enumerate(left_rows):
        parts.inp(f"left{index}", rows, fixed((n, d)))
        parts.tmp(f"turned{index}", pltpu.VMEM((d, n), bf16))
    parts.inp("gr", residual, fixed((n, d)))
    parts.out("own", (n, d), f32, fixed((n, d)))
    parts.out("sums", (8, d), f32, pl.BlockSpec((8, wide), lambda i: (0, early(i))))
    for name in ("dq", "dk", "dv"):
        parts.tmp(name, pltpu.VMEM((groups, n, wide), bf16))
    parts.tmp("ds", pltpu.VMEM((n, n), bf16))
    parts.tmp("held", pltpu.VMEM((d, d), bf16))
    if boxed:
        col, row = places
        parts.inp("col", col, fixed((n, 2)))
        parts.inp("row", row, fixed((2, n)))
        parts.inp("small1", small[0], fixed((16, d)))
        parts.inp("small2", small[1], fixed((16, d)))
        parts.inp("sums2", small[2], fixed((8, d)))
        parts.tmp("hot_i", pltpu.VMEM((32, n), bf16))
        parts.tmp("hot_j", pltpu.VMEM((n, 128), bf16))
        parts.tmp("step_x", pltpu.VMEM((n, n), bf16))
        parts.tmp("step_y", pltpu.VMEM((n, n), bf16))
        parts.tmp("far", pltpu.VMEM((n, 384), f32))
        parts.tmp("tab", pltpu.VMEM((2 * H, 128), f32))
        parts.tmp("sums1", pltpu.VMEM((8, d), f32))
        traffic = Traffic(parts, legs, carried, [inner], small=((32, d), small[3]))
    else:
        parts.tmp("acc", pltpu.VMEM((n, d), f32))
        traffic = Traffic(parts, legs, carried, [inner], cross=((n, d), cross))

    def body(refs):
        step = pl.program_id(0)
        me, side = lax.axis_index("wide"), lax.axis_index("narrow")

        @pl.when(step == 0)
        def _():
            traffic.open(refs, me, side)

        traffic.fire(refs, me, side, step, PRE, MID)

        @pl.when(step == 0)
        def _():
            for index in range(len(left_rows)):
                refs[f"turned{index}"][...] = refs[f"left{index}"][...].T
            if boxed:
                cx, cy = refs["col"][:, 0:1], refs["col"][:, 1:2]
                rx, ry = refs["row"][0:1], refs["row"][1:2]
                lane = lax.broadcasted_iota(jnp.int32, (n, 128), 1)
                hots = hot_columns(cx, cy, n, reverse=True)
                refs["hot_j"][...] = jnp.where(lane < 32, hots, 0.0).astype(bf16)
                row = lax.broadcasted_iota(jnp.int32, (32, n), 0)
                cell = jnp.where(row < 16, rx >> 6, ry >> 6)
                refs["hot_i"][...] = jnp.where(cell == (row & 15), 1.0, 0.0).astype(bf16)
                refs["step_x"][...] = jnp.where((cx & 63) < (rx & 63), 1.0, 0.0).astype(bf16)
                refs["step_y"][...] = jnp.where((cy & 63) < (ry & 63), 1.0, 0.0).astype(bf16)

        def pair_back(pair):
            masks = head_masks()
            lanes = slice(128 * pair, 128 * pair + 128)
            q, k, v, g = (refs[x][:, lanes] for x in "qkvg")
            ds_s = refs["ds"]
            grads = []
            for h in range(2):
                queries = []
                for r in range(0, n, STRIP):
                    gh = g[r : r + STRIP] * masks[h]
                    p = refs["p"][2 * pair + h, r : r + STRIP].astype(f32)
                    dp = nt(gh, v)
                    mean = jnp.sum(p * dp, axis=-1, keepdims=True)
                    ds = (p * (dp - mean)).astype(bf16)
                    ds_s[r : r + STRIP] = ds
                    if boxed:
                        hj = refs["hot_j"][...]
                        far = refs["far"]
                        both = nn(ds, jnp.concatenate([k, hj], axis=1))
                        queries.append(both[:, :128])
                        far[r : r + STRIP, 0:128] = both[:, 128:]
                        far[r : r + STRIP, 128:256] = nn(ds * refs["step_x"][r : r + STRIP], hj)
                        far[r : r + STRIP, 256:384] = nn(ds * refs["step_y"][r : r + STRIP], hj)
                    else:
                        queries.append(nn(ds, k))
                grads.append(
                    (
                        jnp.concatenate(queries, axis=0),
                        tn(ds_s[...], q),
                        tn(refs["p"][2 * pair + h], g),
                    )
                )
                if boxed:
                    value = refs["far"][...]
                    upper = value.astype(bf16)
                    lower = (value - upper.astype(f32)).astype(bf16)
                    hi = refs["hot_i"][...]
                    cells = nn(hi, upper) + nn(hi, lower)
                    lane = lax.broadcasted_iota(jnp.int32, (16, 128), 1)
                    for direction in range(2):
                        rows = slice(16 * direction, 16 * direction + 16)
                        level = cells[rows, 0:128]
                        above = cells[rows, 128 * (direction + 1) : 128 * (direction + 2)]
                        inside = (lane >= 16 * direction) & (lane < 16 * direction + 16)
                        level = jnp.where(inside, level - above, 0.0)
                        above = jnp.where(inside, above, 0.0)
                        turn = (128 + 1 - 16 * direction) % 128
                        line = pltpu.roll(level, turn, 1, stride=1, stride_axis=0)
                        turn = (turn + 127) % 128
                        line = line + pltpu.roll(above, turn, 1, stride=1, stride_axis=0)
                        line = jnp.sum(line, axis=0, keepdims=True) * HD**0.5
                        index = 2 * heads * step + 4 * pair + 2 * h + direction
                        refs["tab"][pl.ds(index, 1)] = line
            low = low_lanes(n)
            outs = []
            for index, name in enumerate(("dq", "dk", "dv")):
                value = jnp.where(low, grads[0][index], grads[1][index]).astype(bf16)
                refs[name][step, :, lanes] = value
                outs.append(jnp.sum(value.astype(f32), axis=0, keepdims=True))
            sums = store_rows([outs[0], outs[2]])
            refs["sums"][:, lanes] = sums
            if boxed:
                start = pl.multiple_of(step * wide + 128 * pair, 128)
                refs["sums1"][:, pl.ds(start, 128)] = sums

        @pl.when(step < groups)
        def _():
            pair_back(0)

        traffic.fire(refs, me, side, step, MID, POST)

        @pl.when(step < groups)
        def _():
            pair_back(1)

        def gradient(group):
            turned = [refs[f"turned{index}"] for index in range(len(left_rows))]
            for index, name in enumerate(("dq", "dk", "dv")):
                left = turned[min(index, 1) if len(turned) == 2 else 0]
                refs["held"][:, index * wide : (index + 1) * wide] = nn(
                    left[...], refs[name][group]
                ).astype(bf16)
            inner.put(
                me, refs["held"], 16, 0, refs["in.keep"], refs["in.send"], group, inner.rows
            )

        if boxed:

            @pl.when(step < groups)
            def _():
                gradient(step)

            @pl.when(step == groups - 1)
            def _():
                total = refs["small.sum"]
                total[0:16] = refs["small1"][...]
                total[0:2] = refs["sums1"][0:2]
                total[16:32] = refs["small2"][...]
                total[16:18] = refs["sums2"][0:2]
                each = d // 128
                for index in range(2 * H):
                    at = 128 * (index % each)
                    row = 12 + index // each
                    total[row : row + 1, at : at + 128] = refs["tab"][index : index + 1]

            @pl.when(step >= groups)
            def _():
                group = step - groups
                value = nt(refs["dq"][group], refs["wq"][...])
                value = value + nt(refs["dk"][group], refs["wk"][...])
                value = value + nt(refs["dv"][group], refs["wv"][...])

                @pl.when(step == groups)
                def _():
                    refs["own"][...] = refs["gr"][...] + value

                @pl.when(step > groups)
                def _():
                    refs["own"][...] += value

        else:

            @pl.when(step < groups)
            def _():
                value = nt(refs["dk"][step], refs["wk"][...])
                value = value + nt(refs["dv"][step], refs["wv"][...])

                @pl.when(step == 0)
                def _():
                    refs["acc"][...] = value

                @pl.when((step > 0) & (step < groups - 1))
                def _():
                    refs["acc"][...] += value

                @pl.when(step == groups - 1)
                def _():
                    refs["cross.out"][...] = (refs["acc"][...] + value).astype(bf16)

            @pl.when(step >= groups)
            def _():
                group = step - groups
                value = nt(refs["dq"][group], refs["wq"][...])

                @pl.when(step == groups)
                def _():
                    refs["own"][...] = refs["gr"][...] + value

                @pl.when(step > groups)
                def _():
                    refs["own"][...] += value

        if not boxed:
            traffic.fire(refs, me, side, step, POST, POST + 0.1)

            @pl.when(step >= groups)
            def _():
                gradient(step - groups)

            traffic.fire(refs, me, side, step, POST + 0.1, 10)
        else:
            traffic.fire(refs, me, side, step, POST, 10)

    return parts.run(body, steps, 16 * n * n * d + 12 * n * d * d, 2 * H * n * n, collective)


def backward_with_hops(first, second, saved_one, saved_two, one, two, extra):
    top, own_count, places, own_b, mid_b, partner_b, soft_one, soft_two = extra
    d = own_b.shape[1]

    def chunks():
        return (
            Chunk("down", 4, 48, (1, 2, 4, 8), d),
            Chunk("up", 5, 48, (1, 2, 4, 8), d),
            Chunk("in", 3, 48, (1, 4, 2, 8), d),
        )

    down2, up2, in2 = chunks()
    down1, up1, in1 = (Chunk(c.name, c.blocks, c.rows, c.bits, d) for c in chunks())
    for chunk in (up2, in2):
        chunk.name += ".early"
    early_down2 = Chunk("down.early", 4, 48, down2.bits, d)

    up_fresh = Chunk("up", 5, 48, up2.bits, d)
    a = ff_back(
        [top], own_count, saved_two, second, down2, up_fresh,
        [Leg(down2, (0, 4), 0, [((3, 2), (4, 2)), ((4, 2), (8, 3))])],
        {}, 0,
    )
    in_fresh = Chunk("in", 3, 48, in2.bits, d)
    b = attn_back(
        *two, a["do"], soft_two, None, second[0], [mid_b, partner_b], a["gr"], in_fresh,
        [
            Leg(up2, (0, 5), 0, [((0, 0), (0, 1)), ((0, 1), (5, 4))]),
            Leg(early_down2, (0, 4), 2, [((0, 0), (1, 0)), ((1, 0), (2, 1))]),
        ],
        {up2: (a["up.keep"], a["up.send"]), early_down2: (a["down.keep"], None)},
        None, ((2, 2), (5, 3)), 1,
    )
    up_fresh = Chunk("up", 5, 48, up1.bits, d)
    c = ff_back(
        [b["own"], b["cross.in"]], own_count, saved_one, first, down1, up_fresh,
        [
            Leg(in2, (0, 3), 0, [((0, 0), (1, 2)), ((1, 2), (7, 2))]),
            Leg(up2, (0, 5), 2, [((0, 0), (4, 1.5)), ((4, 1.5), (8, 2))]),
            Leg(down1, (0, 4), 0, [((3, 2), (4, 2)), ((4, 2), (8, 3))]),
        ],
        {
            in2: (b["in.keep"], b["in.send"]),
            up2: (b["up.early.keep"], None),
        },
        2,
    )
    early_down1 = Chunk("down.early", 4, 48, down1.bits, d)
    early_up1 = Chunk("up.early", 5, 48, up1.bits, d)
    e = attn_back(
        *one, c["do"], soft_one, places, first[0], [own_b], c["gr"], in1,
        [
            Leg(early_down1, (0, 4), 2, [((0, 0), (0, 2)), ((0, 2), (1, 2))]),
            Leg(in2, (0, 3), 2, [((0, 0), (1, 1)), ((1, 2), (2, 1))]),
            Leg(
                early_up1, (0, 3), 0,
                [((0, 0), (0, 1)), ((0, 1), (2, 1)), ((2, 1), (3, 2)), ((3, 2), (5, 3))],
            ),
            Leg(
                early_up1, (3, 5), 0,
                [((0, 0), (0, 1)), ((0, 1.5), (2, 2)), ((2, 2), (5, 2.5)), ((5, 2.5), (5, 4))],
            ),
            Leg(in1, (0, 1), 0, [((0, 2), (1, 1)), ((1, 1), (2, 1)), ((2, 1), (2, 2)), ((2, 2), (3, 2))]),
            Leg(in1, (1, 2), 0, [((1, 2), (2, 1)), ((2, 1), (3, 2)), ((3, 2), (4, 2)), ((4, 2), (5, 2))]),
            Leg(in1, (2, 3), 0, [((2, 2), (3, 2)), ((3, 2), (5, 2.7)), ((5, 2.7), (5, 3.5)), ((5, 3.5), (5, 5))]),
        ],
        {
            early_down1: (c["down.keep"], None),
            in2: (c["in.early.keep"], None),
            early_up1: (c["up.keep"], c["up.send"]),
        },
        (
            c["sums"], a["sums"], b["sums"],
            [((2, 2), (3, 2)), ((3, 2), (4, 2)), ((4, 2), (5, 2)), ((5, 2), (5, 3))],
        ),
        None, 3,
    )
    small = e["small.done"]
    return (
        e["own"],
        (e["in.done"], e["up.early.done"], e["down.early.done"]),
        (e["in.early.done"], c["up.early.done"], b["down.early.done"]),
        small,
    )


def swap(value, axis, bit):
    size = lax.axis_size(axis)
    return lax.ppermute(value, axis, [(i, i ^ bit) for i in range(size)])


def reduce_slots(parts, axis):
    keep, send = parts
    bit = 1
    while True:
        got = swap(send, axis, bit)
        count = keep.shape[0]
        if count == 1:
            return keep[0].astype(f32) + got[0].astype(f32)
        half = count // 2
        send = (keep[half:].astype(f32) + got[half:].astype(f32)).astype(keep.dtype)
        keep = (keep[:half].astype(f32) + got[:half].astype(f32)).astype(keep.dtype)
        bit *= 2


def reduce_small(rows, me, axis):
    size = lax.axis_size(axis)
    count = rows.shape[0]
    cut = jnp.transpose(rows.reshape(count, size, -1), (1, 0, 2))
    cut = jnp.take(cut, jnp.arange(size, dtype=jnp.int32) ^ me, axis=0)
    bit = 1
    while bit < size:
        pairs = cut.reshape(cut.shape[0] // 2, 2, *cut.shape[1:])
        cut = pairs[:, 0] + swap(pairs[:, 1], axis, bit)
        bit *= 2
    return cut[0]


def body(
    stream,
    lengths,
    layout_boxes,
    self_attn_in,
    self_attn_out,
    self_ff_up,
    self_ff_down,
    self_vectors,
    self_gains,
    self_up_bias,
    cross_attn_in,
    cross_attn_out,
    cross_ff_up,
    cross_ff_down,
    cross_vectors,
    cross_gains,
    cross_up_bias,
    box_table,
    cotangent,
):
    side = lax.axis_index("narrow")
    place = lax.axis_index("wide")
    devices = lax.axis_size("wide")
    me = place.astype(jnp.int32).reshape(1)
    n, d = stream.shape[2:]
    ff = self_ff_up.shape[2]
    first = (
        self_attn_in,
        self_attn_out,
        self_ff_up,
        self_ff_down,
        self_vectors,
        self_gains,
        self_up_bias,
    )
    second = (
        cross_attn_in,
        cross_attn_out,
        cross_ff_up,
        cross_ff_down,
        cross_vectors,
        cross_gains,
        cross_up_bias,
    )
    own_b = stream.reshape(n, d)
    top = cotangent.reshape(n, d)
    own_count = jnp.where(side == 0, lengths[0], lengths[1])
    other_count = jnp.where(side == 0, lengths[1], lengths[0])
    slot = jnp.arange(n, dtype=jnp.int32)
    padding = ((0, 0), (0, n - TEXT))
    boxes = layout_boxes[0]
    text = jnp.pad((boxes[:2] + boxes[2:]) >> 1, padding)
    grid_side = jnp.where(own_count > GRID_LO * GRID_LO, GRID_HI, GRID_LO).astype(jnp.int32)
    patch = jnp.stack([slot % grid_side, slot // grid_side])
    patch = (patch * 1000 + 500) // grid_side
    centres = jnp.where(side == 0, text, patch)
    places = (centres.T, centres)
    tables = jnp.pad(
        jnp.transpose(box_table.reshape(2, NB, H), (2, 0, 1)).reshape(2 * H, NB),
        ((0, 0), (0, 128 - NB)),
    )

    qkv_one = project(own_b, self_attn_in, self_vectors, 0, 3)
    one = ([qkv_one] * 3, (0, PAIRS, 2 * PAIRS))
    blend_one, soft_one = attend_forward(*one, own_count, places, tables)
    saved_one = feed_forward(blend_one, own_b, first, own_count, False)
    unit_one, scale_one, rb_one, act_one, slope_one, unit_two, scale_two, mid, mid_b = saved_one
    partner_b = swap(mid_b, "narrow", 1)
    q_two = project(mid_b, cross_attn_in, cross_vectors, 0, 1)
    kv_two = project(partner_b, cross_attn_in, cross_vectors, 1, 2)
    two = ([q_two, kv_two, kv_two], (0, 0, PAIRS))
    blend_two, soft_two = attend_forward(*two, other_count, None, None)
    saved_two = feed_forward(blend_two, mid, second, own_count, True)
    unit_three, scale_three, rb_two, act_two, slope_two, unit_four, scale_four, final = saved_two

    if devices == 16:
        saved = (unit_one, scale_one, rb_one, act_one, slope_one, unit_two, scale_two, blend_one)
        later = (
            unit_three, scale_three, rb_two, act_two, slope_two, unit_four, scale_four, blend_two
        )
        extra = (top, own_count, places, own_b, mid_b, partner_b, soft_one, soft_two)
        grad_stream, sums_one, sums_two, small = backward_with_hops(
            first, second, saved, later, one, two, extra
        )
        share = d // devices
        cut = lax.dynamic_slice(small, (0, place * share), (small.shape[0], share))
        steps = ff // d

        def layer(done, base):
            inside, up, down = done
            groups = inside.shape[0]
            inside = inside.reshape(groups, share, 3, d // groups)
            ups = small[base + 8 : base + 8 + steps].reshape(1, ff)
            return (
                jnp.transpose(inside, (1, 2, 0, 3)).reshape(1, share, 3 * d),
                up[steps][None],
                jnp.transpose(up[:steps], (1, 0, 2)).reshape(1, share, ff),
                down.reshape(1, ff // devices, d),
                cut[base : base + 6][None],
                cut[base + 6 : base + 8][None],
                lax.dynamic_slice(ups, (0, place * (ff // devices)), (1, ff // devices)),
            )

        lines = small[12:16].reshape(H, 2, 128)[:, :, :NB]
        lines = jnp.transpose(lines, (1, 2, 0)).reshape(1, 2 * NB * H)
        tables_out = lax.dynamic_slice(lines, (0, place * share), (1, share))
        return (
            (final[None, None], grad_stream[None, None])
            + layer(sums_one, 0)
            + layer(sums_two, 16)
            + (tables_out,)
        )

    def large(parts):
        if len(parts) == 2:
            return reduce_slots(parts, "wide")
        return lax.psum_scatter(parts[0].astype(f32), "wide", scatter_dimension=0, tiled=True)

    def columns(value, lead):
        if value.ndim == 2:
            return value[:, lead[0] * d : lead[1] * d][None]
        picked = value[lead[0] : lead[1]]
        return jnp.transpose(picked, (1, 0, 2)).reshape(1, picked.shape[1], -1)

    dz, gb, sums_four, down_two = down_gradient(
        me, own_count, [top], unit_four, scale_four, cross_gains, act_two, devices, True
    )
    down_two = large(down_two)
    du, ups_two, ga, gr, do, sums_three = feed_backward(
        dz, gb, slope_two, unit_three, scale_three, second
    )
    steps = ff // d
    jobs = [(0, 0, 0)] * steps + [(1, 1, 0)]
    up_two = large(weight_gradients(me, jobs, [rb_two, blend_two], [du, ga], devices))
    dq, dk, dv, sums_two_attn = attend_backward(*two, do, soft_two, None)
    grad_partner = project_back([dk, dv], cross_attn_in, 1, None, bf16)
    returned = swap(grad_partner, "narrow", 1)
    grad_own = project_back([dq], cross_attn_in, 0, gr, f32)
    in_two = large(
        weight_gradients(
            me, [(0, 0, 0), (1, 1, 0), (1, 2, 0)], [mid_b, partner_b], [dq, dk, dv], devices
        )
    )

    dz, gb, sums_two, down_one = down_gradient(
        me, own_count, [grad_own, returned], unit_two, scale_two, self_gains, act_one, devices, False
    )
    down_one = large(down_one)
    du, ups_one, ga, gr, do, sums_one = feed_backward(
        dz, gb, slope_one, unit_one, scale_one, first
    )
    up_one = large(weight_gradients(me, jobs, [rb_one, blend_one], [du, ga], devices))
    dq, dk, dv, sums_one_attn, grad_tables = attend_backward(*one, do, soft_one, places)
    in_one = large(
        weight_gradients(
            me, [(0, 0, 0), (0, 1, 0), (0, 2, 0)], [own_b], [dq, dk, dv], devices
        )
    )
    grad_stream = project_back([dq, dk, dv], self_attn_in, 0, gr, f32)

    def ups_rows(ups):
        return jnp.transpose(
            ups.reshape(devices, steps, d // devices), (1, 0, 2)
        ).reshape(steps, d)

    table_row = jnp.transpose(
        grad_tables.reshape(H, 2, 128)[:, :, :NB], (1, 2, 0)
    ).reshape(1, 2 * NB * H)
    small = jnp.concatenate(
        [
            sums_one_attn[:2],
            sums_one[2:3],
            sums_one[1:2],
            sums_two[2:3],
            sums_two[1:2],
            sums_one[0:1],
            sums_two[0:1],
            ups_rows(ups_one),
            sums_two_attn[:2],
            sums_three[2:3],
            sums_three[1:2],
            sums_four[2:3],
            sums_four[1:2],
            sums_three[0:1],
            sums_four[0:1],
            ups_rows(ups_two),
            table_row,
        ]
    )
    small = reduce_small(small, me, "wide")
    half = 8 + steps

    def layer(values, base, inside, up, down):
        return (
            columns(inside, (0, 3)),
            columns(up, (steps, steps + 1)),
            columns(up, (0, steps)),
            down[None],
            values[base : base + 6][None],
            values[base + 6 : base + 8][None],
            values[base + 8 : base + half].reshape(1, -1),
        )

    return (
        (final[None, None], grad_stream[None, None])
        + layer(small, 0, in_one, up_one, down_one)
        + layer(small, half, in_two, up_two, down_two)
        + (small[2 * half :],)
    )


def solution(mesh):
    matrix = P("narrow", None, None)
    layer_in = (matrix,) * 6 + (P("narrow", None),)
    rows = P("narrow", "wide", None, None)
    in_specs = (
        (rows, P(None, "wide"), P("wide", None, None))
        + layer_in * 2
        + (P("narrow", None), rows)
    )
    layer_out = (P("narrow", "wide", None),) * 4 + (
        P("narrow", None, "wide"),
        P("narrow", None, "wide"),
        P("narrow", "wide"),
    )
    out_specs = (rows, rows) + layer_out * 2 + (P("narrow", "wide"),)
    return jax.shard_map(body, mesh=mesh, in_specs=in_specs, out_specs=out_specs, check_vma=False)
```

```python
import functools

import jax
import jax.numpy as jnp
from jax import lax
from jax.experimental import pallas as pl
from jax.experimental.pallas import tpu as pltpu
from jax.sharding import PartitionSpec as P

H = 12
HD = 64
NB = 32
TEXT = 512
GRID_LO = 16
GRID_HI = 24
PAIRS = H // 2
STRIP = 192
SUB = 32
MIB = 1 << 20

norm_eps = 1e-05
spacing = 64
masked_score = -1e30

f32 = jnp.float32
bf16 = jnp.bfloat16
SMEM = pltpu.MemorySpace.SMEM


def nn(left, right):
    return lax.dot_general(left, right, (((1,), (0,)), ((), ())), preferred_element_type=f32)


def nt(left, right):
    return lax.dot_general(left, right, (((1,), (1,)), ((), ())), preferred_element_type=f32)


def tn(left, right):
    return lax.dot_general(left, right, (((0,), (0,)), ((), ())), preferred_element_type=f32)


def whole(shape):
    return pl.BlockSpec(shape, lambda i: (0,) * len(shape))


def scalar_spec():
    return pl.BlockSpec(memory_space=SMEM)


def call(kernel, grid, in_specs, out_specs, out_shape, scratch, flops, moved, vmem=48):
    return pl.pallas_call(
        kernel,
        grid=grid,
        in_specs=in_specs,
        out_specs=out_specs,
        out_shape=out_shape,
        scratch_shapes=scratch,
        compiler_params=pltpu.CompilerParams(
            dimension_semantics=("arbitrary",),
            vmem_limit_bytes=vmem * MIB,
            fuse_transposed_lhs_in_matmul=True,
        ),
        cost_estimate=pl.CostEstimate(
            flops=int(flops), bytes_accessed=int(moved), transcendentals=0
        ),
    )


def shape_of(shape, dtype):
    return jax.ShapeDtypeStruct(shape, dtype)


def normalise(values):
    average = jnp.mean(values, axis=-1, keepdims=True)
    centred = values - average
    variance = jnp.mean(centred * centred, axis=-1, keepdims=True)
    scale = lax.rsqrt(variance + norm_eps)
    return centred * scale, scale


def normalise_back(grad, unit, scale, gains):
    inner = grad * gains
    mean_one = jnp.mean(inner, axis=-1, keepdims=True)
    mean_two = jnp.mean(inner * unit, axis=-1, keepdims=True)
    return scale * (inner - mean_one - unit * mean_two)


def gelu_both(u):
    t = pltpu.reciprocal(1.0 + (0.3275911 * 0.7071067811865476) * jnp.abs(u), approx=True)
    bell = jnp.exp(-0.5 * (u * u))
    poly = t * (
        0.127414796
        + t * (-0.142248368 + t * (0.7107068705 + t * (-0.7265760135 + t * 0.5307027145)))
    )
    tail = poly * bell
    share = jnp.where(u < 0, tail, 1.0 - tail)
    return u * share, share + (u * 0.3989422804014327) * bell


def each_strip(n, size, body, start=None, unroll=4):
    def step(index, carry):
        return body(pl.ds(pl.multiple_of(index * size, size), size), carry)

    return lax.fori_loop(0, n // size, step, start, unroll=unroll)


def fold(values):
    total = values[0:8]
    for r in range(8, values.shape[0], 8):
        total = total + values[r : r + 8]
    return total


def project(rows, weight, vectors, first, count):
    n, d = rows.shape

    def kernel(x_ref, w_ref, v_ref, o_ref):
        part = pl.program_id(0) + first
        shift = jnp.where(part == 0, v_ref[0:1], jnp.where(part == 2, v_ref[1:2], 0.0))
        o_ref[...] = (nn(x_ref[...], w_ref[...]) + shift).astype(bf16)

    return call(
        kernel,
        (count,),
        [
            whole((n, d)),
            pl.BlockSpec((None, d, d), lambda i: (0, 0, i + first)),
            pl.BlockSpec((None, 6, d), lambda i: (0, 0, 0)),
        ],
        pl.BlockSpec((n, d), lambda i: (0, i)),
        shape_of((n, count * d), bf16),
        [],
        2 * n * d * d * count,
        2 * d * d * count,
    )(rows, weight, vectors)


def head_masks():
    lane = lax.broadcasted_iota(jnp.int32, (1, 2 * HD), 1)
    return [
        jnp.where(lane < HD, HD**-0.5, 0.0).astype(bf16),
        jnp.where(lane < HD, 0.0, HD**-0.5).astype(bf16),
    ]


def low_lanes(rows):
    return lax.broadcasted_iota(jnp.int32, (rows, 2 * HD), 1) < HD


def hot_columns(coord_x, coord_y, rows, reverse=False):
    lane = lax.broadcasted_iota(jnp.int32, (rows, 128), 1)
    cell = jnp.where((lane & 16) == 0, coord_x >> 6, coord_y >> 6)
    place = lane & 15
    if reverse:
        place = 15 - place
    return jnp.where((cell == place) & (lane < 64), 1.0, 0.0)


def slanted(row, first):
    wide = jnp.broadcast_to(row, (16, 128))
    return pltpu.roll(wide, (128 - first) % 128, 1, stride=1, stride_axis=0)


def spread_tables(table_x, table_y):
    lane = lax.broadcasted_iota(jnp.int32, (16, 128), 1)
    keep = lane < 16
    outs = []
    rows = []
    for row in (table_x, table_y):
        base = jnp.where(keep, slanted(row, 16), 0.0)
        before = jnp.where(keep, slanted(row, 15), 0.0)
        rows.append((base, before - base))

    def split(value, offset):
        upper = value.astype(bf16).astype(f32)
        lower = value - upper
        joined = upper + pltpu.roll(lower, 32, 1)
        return pltpu.roll(joined, offset, 1) if offset else joined

    zero = jnp.zeros((16, 128), f32)
    outs.append(jnp.concatenate([split(rows[0][0], 0), split(rows[1][0], 16)], axis=0))
    outs.append(jnp.concatenate([split(rows[0][1], 0), zero], axis=0))
    outs.append(jnp.concatenate([zero, split(rows[1][1], 16)], axis=0))
    return [value.astype(bf16) for value in outs]


def attend_forward(arrays, offsets, count, places, tables):
    n = arrays[0].shape[0]
    keys = -(-n // 128) * 128
    heads = 4
    boxed = places is not None

    def kernel(*refs):
        if boxed:
            cnt, q_ref, k_ref, v_ref, col_ref, row_ref, t_ref, o_ref, p_ref, f_ref = refs[:10]
            k_s, v_s, s_s, step_x, step_y, hot_i, hot_j = refs[10:]
        else:
            cnt, q_ref, k_ref, v_ref, o_ref, p_ref, f_ref, k_s, v_s, s_s = refs
            s_s = [[s_s.at[0]], [s_s.at[1]]]
        live_count = cnt[0]
        group = pl.program_id(0)

        @pl.when(group == 0)
        def _():
            k_s[n:keys] = jnp.zeros((keys - n, 64 * heads), bf16)
            v_s[n:keys] = jnp.zeros((keys - n, 64 * heads), bf16)
            if boxed:
                cx, cy = col_ref[:, 0:1], col_ref[:, 1:2]
                hots = hot_columns(cx, cy, n)
                lane = lax.broadcasted_iota(jnp.int32, (n, 128), 1)
                hot_i[...] = jnp.where(lane == 64, 1.0, hots).astype(bf16)
                hot_j[0:n] = jnp.where(lane < 32, hots, 0.0).astype(bf16)
                hot_j[n:keys] = jnp.zeros((keys - n, 128), bf16)
                rx, ry = row_ref[0:1], row_ref[1:2]
                step_x[...] = jnp.where((cx & 63) < (rx & 63), 1.0, 0.0)
                step_y[...] = jnp.where((cy & 63) < (ry & 63), 1.0, 0.0)

        if boxed:
            s_s = [[s_s.at[3 * h + k] for k in range(3)] for h in range(2)]
            lane = lax.broadcasted_iota(jnp.int32, (keys, 128), 1)
            place = lax.broadcasted_iota(jnp.int32, (keys, 128), 0)
            dead = jnp.where((lane == 64) & (place >= live_count), masked_score, 0.0)
            dead = dead.astype(bf16)
        k_s[0:n] = k_ref[...]
        v_s[0:n] = v_ref[...]
        masks = head_masks()
        low = low_lanes(n)
        tiles = [slice(128 * t, 128 * t + 128) for t in range(keys // 128)]

        def scores(head):
            lanes = slice(128 * (head // 2), 128 * (head // 2) + 128)
            part = q_ref[:, lanes] * masks[head % 2]
            to = s_s[head % 2]
            if boxed:
                row = 2 * (heads * group + head)
                base, dx, dy = spread_tables(t_ref[pl.ds(row, 1)], t_ref[pl.ds(row + 1, 1)])
                hi, hj = hot_i[...], hot_j[:, :32]
                side = nn(hj, base).astype(bf16) + dead
                side = jnp.concatenate([k_s[:, lanes], side], axis=1)
                to[0][...] = nt(jnp.concatenate([part, hi], axis=1), side)
                to[1][...] = nt(hi, nn(hj, dx).astype(bf16))
                to[2][...] = nt(hi, nn(hj, dy).astype(bf16))
            else:
                to[0][...] = nt(part, k_s[:, lanes])

        def soften(head):
            at = s_s[head % 2]
            for r in range(0, n, SUB):
                rows = slice(r, r + SUB)
                parts = []
                for t, lanes in enumerate(tiles):
                    s = at[0][rows, lanes]
                    if boxed:
                        s = s + step_x[rows, lanes] * at[1][rows, lanes]
                        s = s + step_y[rows, lanes] * at[2][rows, lanes]
                    elif 128 * t + 128 > GRID_LO * GRID_LO:
                        lane = lax.broadcasted_iota(jnp.int32, (1, 128), 1) + 128 * t
                        s = jnp.where(lane < live_count, s, masked_score)
                    parts.append(s)
                peak = functools.reduce(jnp.maximum, parts)
                peak = jnp.max(peak, axis=-1, keepdims=True)
                parts = [jnp.exp(s - peak) for s in parts]
                total = functools.reduce(jnp.add, parts)
                total = 1.0 / jnp.sum(total, axis=-1, keepdims=True)
                for s, lanes in zip(parts, tiles):
                    p_ref[head, rows, lanes] = (s * total).astype(bf16)

        scores(0)
        blends = []
        for head in range(heads):
            if head + 1 < heads:
                scores(head + 1)
            soften(head)
            lanes = slice(128 * (head // 2), 128 * (head // 2) + 128)
            blends.append(nn(p_ref[head], v_s[:, lanes]))
            if head % 2 == 1:
                blend = jnp.where(low, blends[head - 1], blends[head])
                f_ref[:, lanes] = blend
                o_ref[:, lanes] = blend.astype(bf16)

    def wide_block(offset):
        return pl.BlockSpec((n, 64 * heads), lambda i: (0, i + offset * 128 // (64 * heads)))

    in_specs = [scalar_spec()] + [wide_block(offset) for offset in offsets]
    args = [count, *arrays]
    scratch = [
        pltpu.VMEM((keys, 64 * heads), bf16),
        pltpu.VMEM((keys, 64 * heads), bf16),
        pltpu.VMEM((6 if boxed else 2, n, keys), f32),
    ]
    if boxed:
        in_specs += [whole((n, 2)), whole((2, keys)), whole((2 * H, 128))]
        args += [places[0], jnp.pad(places[1], ((0, 0), (0, keys - n))), tables]
        scratch += [pltpu.VMEM((n, keys), f32)] * 2
        scratch += [pltpu.VMEM((n, 128), bf16), pltpu.VMEM((keys, 128), bf16)]
    return call(
        kernel,
        (H // heads,),
        in_specs,
        [wide_block(0), pl.BlockSpec((heads, n, keys), lambda i: (i, 0, 0)), wide_block(0)],
        [
            shape_of((n, H * HD), bf16),
            shape_of((H, n, keys), bf16),
            shape_of((n, H * HD), f32),
        ],
        scratch,
        16 * n * n * H * HD,
        2 * H * n * n,
        vmem=60,
    )(*args)


def feed_forward(blended, states, weights, count, last):
    _, attn_out, ff_up, ff_down, vectors, gains, up_bias = weights
    n, d = blended.shape
    steps = ff_up.shape[2] // d

    def kernel(cnt, o_ref, x_ref, wo_ref, wu_ref, wd_ref, v_ref, g_ref, e_ref, *rest):
        if last:
            unit1, scale1, rb, act, der, unit2, scale2, out, r_s, acc = rest
        else:
            unit1, scale1, rb, act, der, unit2, scale2, out, out_b, r_s, acc = rest
        step = pl.program_id(0)

        @pl.when(step == 0)
        def _():
            branch = nn(o_ref[...], wo_ref[...]) + v_ref[2:3]
            unit, scale = normalise(x_ref[...].astype(f32) + branch)
            unit1[...] = unit
            scale1[...] = scale
            r = unit * g_ref[0:1] + v_ref[3:4]
            r_s[...] = r
            rb[...] = r.astype(bf16)
            acc[...] = r + v_ref[4:5]

        hidden = nn(rb[...], wu_ref[...]) + e_ref[...]
        active, slope = gelu_both(hidden)
        active = active.astype(bf16)
        act[...] = active
        der[...] = slope.astype(bf16)
        acc[...] += nn(active, wd_ref[...])

        @pl.when(step == steps - 1)
        def _():
            unit, scale = normalise(acc[...])
            unit2[...] = unit
            scale2[...] = scale
            z = unit * g_ref[1:2] + v_ref[5:6]
            if last:
                row = lax.broadcasted_iota(jnp.int32, (n, 1), 0)
                out[...] = jnp.where(row < cnt[0], z, 0.0)
            else:
                out[...] = z
                out_b[...] = z.astype(bf16)

    columns = pl.BlockSpec((n, d), lambda i: (0, i))
    outs = [
        (whole((n, d)), shape_of((n, d), f32)),
        (whole((n, 1)), shape_of((n, 1), f32)),
        (whole((n, d)), shape_of((n, d), bf16)),
        (columns, shape_of((n, steps * d), bf16)),
        (columns, shape_of((n, steps * d), bf16)),
        (whole((n, d)), shape_of((n, d), f32)),
        (whole((n, 1)), shape_of((n, 1), f32)),
        (whole((n, d)), shape_of((n, d), f32)),
    ]
    if not last:
        outs.append((whole((n, d)), shape_of((n, d), bf16)))
    return call(
        kernel,
        (steps,),
        [
            scalar_spec(),
            whole((n, d)),
            whole((n, d)),
            pl.BlockSpec((None, d, d), lambda i: (0, 0, 0)),
            pl.BlockSpec((None, d, d), lambda i: (0, 0, i)),
            pl.BlockSpec((None, d, d), lambda i: (0, i, 0)),
            pl.BlockSpec((None, 6, d), lambda i: (0, 0, 0)),
            pl.BlockSpec((None, 2, d), lambda i: (0, 0, 0)),
            pl.BlockSpec((1, d), lambda i: (0, i)),
        ],
        [spec for spec, _ in outs],
        [shape for _, shape in outs],
        [pltpu.VMEM((n, d), f32), pltpu.VMEM((n, d), f32)],
        2 * n * d * d * (1 + 2 * steps),
        2 * d * d * (1 + 2 * steps),
    )(count, blended, states, attn_out, ff_up, ff_down, vectors, gains, up_bias)


def store_rows(rows):
    d = rows[0].shape[1]
    blank = jnp.zeros((8 - len(rows), d), f32)
    return jnp.concatenate(rows + [blank], axis=0)


def slot_place(index, bits):
    place = 0
    for b in range(bits):
        place = place | (((index >> b) & 1) << (bits - 1 - b))
    return place


class Slots:
    def __init__(self, devices, rows):
        self.devices = devices
        self.rows = rows // devices
        self.bits = (devices // 2).bit_length() - 1
        self.split = self.rows % 16 == 0 and devices & (devices - 1) == 0 and devices > 1

    def put(self, me, held, shards, first_shard, write):
        core = me & 1
        for k in range(shards // 2):
            place = slot_place((first_shard // 2 + k) ^ (me >> 1), self.bits)
            for which in range(2):
                start = (2 * k + (core if which == 0 else 1 - core)) * self.rows
                rows = held[pl.ds(pl.multiple_of(start, 16), self.rows)]
                write(which, place, rows)


def down_gradient(me, count, grads, unit, scale, gains, active, devices, top):
    n, d = unit.shape
    ff = active.shape[1]
    steps = ff // d
    slots = Slots(devices, ff)
    shards = devices // steps

    def kernel(me_ref, cnt, *refs):
        ups = refs[: len(grads)]
        unit_ref, scale_ref, g_ref, act_ref = refs[len(grads) : len(grads) + 4]
        dz, gb, sums, *outs, held = refs[len(grads) + 4 :]
        step = pl.program_id(0)

        @pl.when(step == 0)
        def _():
            if top:
                row = lax.broadcasted_iota(jnp.int32, (n, 1), 0)
                g = jnp.where(row < cnt[0], ups[0][...].astype(f32), 0.0)
            else:
                g = ups[0][...] + ups[1][...].astype(f32)
            unit = unit_ref[...]
            back = normalise_back(g, unit, scale_ref[...], g_ref[1:2])
            dz[...] = back
            low = back.astype(bf16)
            gb[...] = low
            sums[...] = store_rows(
                [
                    jnp.sum(g * unit, axis=0, keepdims=True),
                    jnp.sum(g, axis=0, keepdims=True),
                    jnp.sum(low.astype(f32), axis=0, keepdims=True),
                ]
            )

        value = tn(act_ref[...], gb[...]).astype(bf16)
        if slots.split:
            held[...] = value

            def write(which, place, rows):
                outs[which][place] = rows

            slots.put(me_ref[0], held, shards, shards * step, write)
        else:
            outs[0][...] = value

    if slots.split:
        block = (devices // 2, slots.rows, d)
        out_list = [(whole(block), shape_of(block, bf16))] * 2
    else:
        out_list = [(pl.BlockSpec((d, d), lambda i: (i, 0)), shape_of((ff, d), bf16))]
    out_list = [
        (whole((n, d)), shape_of((n, d), f32)),
        (whole((n, d)), shape_of((n, d), bf16)),
        (whole((8, d)), shape_of((8, d), f32)),
    ] + out_list
    results = call(
        kernel,
        (steps,),
        [scalar_spec(), scalar_spec()]
        + [whole((n, d))] * len(grads)
        + [
            whole((n, d)),
            whole((n, 1)),
            pl.BlockSpec((None, 2, d), lambda i: (0, 0, 0)),
            pl.BlockSpec((n, d), lambda i: (0, i)),
        ],
        [spec for spec, _ in out_list],
        [shape for _, shape in out_list],
        [pltpu.VMEM((d, d), bf16)],
        2 * n * d * ff,
        4 * d * ff,
    )(me, count, *grads, unit, scale, gains, active)
    return results[0], results[1], results[2], results[3:]


def feed_backward(grad_sum, grad_branch, slope, unit, scale, weights):
    _, attn_out, ff_up, ff_down, _, gains, _ = weights
    n, d = grad_sum.shape
    steps = ff_up.shape[2] // d

    def kernel(
        dz, gb, der, wd, wu, wo, g_ref, unit_ref, scale_ref, du, ups, ga, gr, do, sums, acc
    ):
        step = pl.program_id(0)

        @pl.when(step == 0)
        def _():
            acc[...] = dz[...]

        grad = (nt(gb[...], wd[...]) * der[...].astype(f32)).astype(bf16)
        du[...] = grad
        ups[...] = jnp.sum(grad.astype(f32), axis=0, keepdims=True)
        acc[...] += nt(grad, wu[...])

        @pl.when(step == steps - 1)
        def _():
            g = acc[...]
            unit = unit_ref[...]
            back = normalise_back(g, unit, scale_ref[...], g_ref[0:1])
            gr[...] = back
            low = back.astype(bf16)
            ga[...] = low
            sums[...] = store_rows(
                [
                    jnp.sum(g * unit, axis=0, keepdims=True),
                    jnp.sum(g, axis=0, keepdims=True),
                    jnp.sum(low.astype(f32), axis=0, keepdims=True),
                ]
            )
            do[...] = nt(low, wo[...]).astype(bf16)

    columns = pl.BlockSpec((n, d), lambda i: (0, i))
    return call(
        kernel,
        (steps,),
        [
            whole((n, d)),
            whole((n, d)),
            columns,
            pl.BlockSpec((None, d, d), lambda i: (0, i, 0)),
            pl.BlockSpec((None, d, d), lambda i: (0, 0, i)),
            pl.BlockSpec((None, d, d), lambda i: (0, 0, 0)),
            pl.BlockSpec((None, 2, d), lambda i: (0, 0, 0)),
            whole((n, d)),
            whole((n, 1)),
        ],
        [
            columns,
            pl.BlockSpec((1, d), lambda i: (0, i)),
            whole((n, d)),
            whole((n, d)),
            whole((n, d)),
            whole((8, d)),
        ],
        [
            shape_of((n, steps * d), bf16),
            shape_of((1, steps * d), f32),
            shape_of((n, d), bf16),
            shape_of((n, d), f32),
            shape_of((n, d), bf16),
            shape_of((8, d), f32),
        ],
        [pltpu.VMEM((n, d), f32)],
        2 * n * d * d * (1 + 2 * steps),
        2 * d * d * (1 + 2 * steps),
    )(grad_sum, grad_branch, slope, ff_down, ff_up, attn_out, gains, unit, scale)


def weight_gradients(me, jobs, lefts, rights, devices):
    n, d = lefts[0].shape
    slots = Slots(devices, d)
    steps = len(jobs)

    def kernel(me_ref, *refs):
        left_refs = refs[: len(lefts)]
        right_refs = refs[len(lefts) : len(lefts) + len(rights)]
        *outs, turned, held = refs[len(lefts) + len(rights) :]
        step = pl.program_id(0)
        for index in range(len(lefts)):
            mine = [j for j, job in enumerate(jobs) if job[0] == index]

            @pl.when(step == mine[0])
            def _(index=index):
                turned[...] = left_refs[index][...].T

        for index in range(len(rights)):
            mine = [j for j, job in enumerate(jobs) if job[1] == index]

            @pl.when((step >= mine[0]) & (step <= mine[-1]))
            def _(index=index):
                value = nn(turned[...], right_refs[index][...]).astype(bf16)
                if slots.split:
                    held[...] = value
                else:
                    outs[0][...] = value

        if slots.split:

            def write(which, place, rows):
                outs[which][place, step] = rows

            slots.put(me_ref[0], held, devices, 0, write)

    def right_spec(index):
        mine = [(j, job[2]) for j, job in enumerate(jobs) if job[1] == index]
        first, block = mine[0]

        def place(i):
            return (0, jnp.clip(i - first, 0, len(mine) - 1) + block)

        return pl.BlockSpec((n, d), place)

    if slots.split:
        block = (devices // 2, steps, slots.rows, d)
        out_list = [(whole(block), shape_of(block, bf16))] * 2
    else:
        out_list = [(pl.BlockSpec((d, d), lambda i: (0, i)), shape_of((d, steps * d), bf16))]
    return call(
        kernel,
        (steps,),
        [scalar_spec()]
        + [whole((n, d))] * len(lefts)
        + [right_spec(index) for index in range(len(rights))],
        [spec for spec, _ in out_list],
        [shape for _, shape in out_list],
        [pltpu.VMEM((d, n), bf16), pltpu.VMEM((d, d), bf16)],
        2 * n * d * d * steps,
        4 * d * d * steps,
    )(me, *lefts, *rights)


def attend_backward(arrays, offsets, grad_blended, soft, places):
    n = grad_blended.shape[0]
    boxed = places is not None
    keys = soft.shape[2]

    def kernel(*refs):
        q_ref, k_ref, v_ref, g_ref, p_ref = refs[:5]
        if boxed:
            col_ref, row_ref = refs[5:7]
            dq_ref, dk_ref, dv_ref, sums, tab = refs[7:12]
            hot_i, hot_j, step_x, step_y, ds_s, far = refs[12:]

            @pl.when(pl.program_id(0) == 0)
            def _():
                cx, cy = col_ref[:, 0:1], col_ref[:, 1:2]
                rx, ry = row_ref[0:1], row_ref[1:2]
                hots = hot_columns(cx, cy, n, reverse=True)
                lane = lax.broadcasted_iota(jnp.int32, (n, 128), 1)
                hot_j[...] = jnp.where(lane < 32, hots, 0.0).astype(bf16)
                row = lax.broadcasted_iota(jnp.int32, (32, n), 0)
                cell = jnp.where(row < 16, rx >> 6, ry >> 6)
                hot_i[...] = jnp.where(cell == (row & 15), 1.0, 0.0).astype(bf16)
                step_x[...] = jnp.where((cx & 63) < (rx & 63), 1.0, 0.0).astype(bf16)
                step_y[...] = jnp.where((cy & 63) < (ry & 63), 1.0, 0.0).astype(bf16)
        else:
            dq_ref, dk_ref, dv_ref, sums, ds_s = refs[5:]
        masks = head_masks()
        q = q_ref[...]
        k = k_ref[...]
        v = v_ref[...]
        g = g_ref[...]
        grads = []
        for h in range(2):
            queries = []
            for r in range(0, n, STRIP):
                gh = g[r : r + STRIP] * masks[h]
                p = p_ref[h, r : r + STRIP, :n].astype(f32)
                dp = nt(gh, v)
                mean = jnp.sum(p * dp, axis=-1, keepdims=True)
                ds = (p * (dp - mean)).astype(bf16)
                ds_s[r : r + STRIP] = ds
                if boxed:
                    hj = hot_j[...]
                    wide = nn(ds, jnp.concatenate([k, hj], axis=1))
                    queries.append(wide[:, :128])
                    far[r : r + STRIP, 0:128] = wide[:, 128:]
                    far[r : r + STRIP, 128:256] = nn(ds * step_x[r : r + STRIP], hj)
                    far[r : r + STRIP, 256:384] = nn(ds * step_y[r : r + STRIP], hj)
                else:
                    queries.append(nn(ds, k))
            grads.append(
                (jnp.concatenate(queries, axis=0), tn(ds_s[...], q), tn(p_ref[h, :, :n], g))
            )
            if boxed:
                value = far[...]
                upper = value.astype(bf16)
                lower = (value - upper.astype(f32)).astype(bf16)
                cells = nn(hot_i[...], upper) + nn(hot_i[...], lower)
                lane = lax.broadcasted_iota(jnp.int32, (16, 128), 1)
                for direction in range(2):
                    rows = slice(16 * direction, 16 * direction + 16)
                    level = cells[rows, 0:128]
                    above = cells[rows, 128 * (direction + 1) : 128 * (direction + 2)]
                    inside = (lane >= 16 * direction) & (lane < 16 * direction + 16)
                    level = jnp.where(inside, level - above, 0.0)
                    above = jnp.where(inside, above, 0.0)
                    turn = (128 + 1 - 16 * direction) % 128
                    line = pltpu.roll(level, turn, 1, stride=1, stride_axis=0)
                    line = line + pltpu.roll(above, (turn + 127) % 128, 1, stride=1, stride_axis=0)
                    line = jnp.sum(line, axis=0, keepdims=True) * HD**0.5
                    tab[2 * h + direction : 2 * h + direction + 1] = line
        low = low_lanes(n)
        outs = []
        for index, ref in enumerate((dq_ref, dk_ref, dv_ref)):
            value = jnp.where(low, grads[0][index], grads[1][index]).astype(bf16)
            ref[...] = value
            outs.append(jnp.sum(value.astype(f32), axis=0, keepdims=True))
        sums[...] = store_rows([outs[0], outs[2]])

    def pair_block(offset):
        return pl.BlockSpec((n, 128), lambda i: (0, i + offset))

    in_specs = [pair_block(offset) for offset in offsets] + [
        pair_block(0),
        pl.BlockSpec((2, n, keys), lambda i: (i, 0, 0)),
    ]
    args = [*arrays, grad_blended, soft]
    outs = [(pair_block(0), shape_of((n, H * HD), bf16))] * 3
    outs.append((pl.BlockSpec((8, 128), lambda i: (0, i)), shape_of((8, H * HD), f32)))
    scratch = [pltpu.VMEM((n, n), bf16)]
    if boxed:
        in_specs += [whole((n, 2)), whole((2, n))]
        args += [*places]
        outs.append(
            (pl.BlockSpec((None, 4, 128), lambda i: (i, 0, 0)), shape_of((PAIRS, 4, 128), f32))
        )
        scratch = [
            pltpu.VMEM((32, n), bf16),
            pltpu.VMEM((n, 128), bf16),
            pltpu.VMEM((n, n), bf16),
            pltpu.VMEM((n, n), bf16),
            pltpu.VMEM((n, n), bf16),
            pltpu.VMEM((n, 384), f32),
        ]
    return call(
        kernel,
        (PAIRS,),
        in_specs,
        [spec for spec, _ in outs],
        [shape for _, shape in outs],
        scratch,
        16 * n * n * H * HD,
        2 * H * n * n,
    )(*args)


def project_back(grads, weight, first, residual, out_type):
    n, d = grads[0].shape
    steps = len(grads)

    def kernel(*refs):
        g_refs = refs[:steps]
        w_ref = refs[steps]
        out, acc = refs[-2:]
        step = pl.program_id(0)
        for index in range(steps):

            @pl.when(step == index)
            def _(index=index):
                value = nt(g_refs[index][...], w_ref[...])
                if index > 0:
                    value = value + acc[...]
                elif residual is not None:
                    value = value + refs[steps + 1][...]
                if index == steps - 1:
                    out[...] = value.astype(out_type)
                else:
                    acc[...] = value

    extra = [] if residual is None else [residual]
    return call(
        kernel,
        (steps,),
        [whole((n, d))] * steps
        + [pl.BlockSpec((None, d, d), lambda i: (0, 0, i + first))]
        + [whole((n, d))] * len(extra),
        whole((n, d)),
        shape_of((n, d), out_type),
        [pltpu.VMEM((n, d), f32)],
        2 * n * d * d * steps,
        2 * d * d * steps,
    )(*grads, weight, *extra)


def feed_forward_sending(blended, states, weights, next_in, next_vectors):
    _, attn_out, ff_up, ff_down, vectors, gains, up_bias = weights
    n, d = blended.shape
    tiles = ff_up.shape[2] // d
    strips = 3
    size = n // strips
    last = strips * tiles
    parts = Parts()
    strip = lambda i: jnp.minimum(i // tiles, strips - 1)
    tile = lambda i: jnp.where(i < last, i % tiles, tiles - 1)
    h_o = parts.inp(blended, fixed((n, d)))
    h_x = parts.inp(states, fixed((n, d)))
    h_wo = parts.inp(attn_out, fixed((None, d, d)))
    h_wu = parts.inp(ff_up, pl.BlockSpec((None, d, d), lambda i: (0, 0, tile(i))))
    h_wd = parts.inp(ff_down, pl.BlockSpec((None, d, d), lambda i: (0, tile(i), 0)))
    h_v, h_g = parts.inp(vectors, fixed((None, 6, d))), parts.inp(gains, fixed((None, 2, d)))
    h_e = parts.inp(up_bias, pl.BlockSpec((1, d), lambda i: (0, tile(i))))
    h_wq = parts.inp(next_in, pl.BlockSpec((None, d, d), lambda i: (0, 0, 0)))
    h_nv = parts.inp(next_vectors, fixed((None, 6, d)))
    h_unit1, h_scale1 = parts.out((n, d), f32), parts.out((n, 1), f32)
    h_rb = parts.out((n, d), bf16)
    block = pl.BlockSpec((size, d), lambda i: (strip(i), tile(i)))
    h_act = parts.out((n, tiles * d), bf16, block)
    h_der = parts.out((n, tiles * d), bf16, block)
    h_unit2, h_scale2 = parts.out((n, d), f32), parts.out((n, 1), f32)
    h_out, h_out_b = parts.out((n, d), f32), parts.out((n, d), bf16)
    h_partner, h_q = parts.out((n, d), bf16), parts.out((n, d), bf16)
    h_acc = parts.vmem((size, d), f32)
    h_got = parts.vmem((n, d), bf16)
    h_sent = parts.tmp(pltpu.SemaphoreType.DMA((strips,)))
    h_arrived = parts.tmp(pltpu.SemaphoreType.DMA((strips,)))

    def body(refs):
        i = pl.program_id(0)
        partner = {"narrow": 1 - lax.axis_index("narrow")}
        v_ref, g_ref, acc = refs[h_v], refs[h_g], refs[h_acc]

        def send(index):
            rows = pl.ds(size * index, size)
            return pltpu.make_async_remote_copy(
                src_ref=refs[h_out_b].at[rows],
                dst_ref=refs[h_got].at[rows],
                send_sem=refs[h_sent].at[index],
                recv_sem=refs[h_arrived].at[index],
                device_id=partner,
                device_id_type=MESH,
            )

        @pl.when(i == 0)
        def _():
            barrier = pltpu.get_barrier_semaphore()
            pl.semaphore_signal(barrier, inc=1, device_id=partner, device_id_type=MESH)
            pl.semaphore_wait(barrier, 1)

        for index in range(strips):
            rows = slice(size * index, size * index + size)

            @pl.when(i == index * tiles)
            def _(rows=rows):
                branch = nn(refs[h_o][rows], refs[h_wo][...]) + v_ref[2:3]
                unit, scale = normalise(refs[h_x][rows].astype(f32) + branch)
                refs[h_unit1][rows] = unit
                refs[h_scale1][rows] = scale
                r = unit * g_ref[0:1] + v_ref[3:4]
                refs[h_rb][rows] = r.astype(bf16)
                acc[...] = r + v_ref[4:5]

        @pl.when(i < last)
        def _():
            rows = pl.ds(pl.multiple_of(lax.div(i, tiles) * size, size), size)
            hidden = nn(refs[h_rb][rows], refs[h_wu][...]) + refs[h_e][...]
            active, slope = gelu_both(hidden)
            active = active.astype(bf16)
            refs[h_act][...] = active
            refs[h_der][...] = slope.astype(bf16)
            acc[...] += nn(active, refs[h_wd][...])

        for index in range(strips):
            rows = slice(size * index, size * index + size)

            @pl.when(i == index * tiles + tiles - 1)
            def _(rows=rows, index=index):
                unit, scale = normalise(acc[...])
                refs[h_unit2][rows] = unit
                refs[h_scale2][rows] = scale
                z = unit * g_ref[1:2] + v_ref[5:6]
                refs[h_out][rows] = z
                refs[h_out_b][rows] = z.astype(bf16)
                send(index).start()

        @pl.when(i == last)
        def _():
            q = nn(refs[h_out_b][...], refs[h_wq][...]) + refs[h_nv][0:1]
            refs[h_q][...] = q.astype(bf16)
            for index in range(strips):
                send(index).wait()
            refs[h_partner][...] = refs[h_got][...]

    results = parts.run(
        body, last + 1, 2 * n * d * d * (2 + 2 * tiles), 2 * d * d * (2 + 2 * tiles * strips), 4
    )
    order = (
        h_unit1, h_scale1, h_rb, h_act, h_der, h_unit2, h_scale2, h_out, h_out_b, h_partner, h_q
    )
    return [results[h] for h in order]


MESH = pl.DeviceIdType.MESH
DOWN, UP, IN = 0, 1, 2
SIZES = (4, 5, 3)

Z_FIRST = (
    (2, 0, 1),
    (2, 1, 0),
    (2, 1, 4),
    (2, 2, 2),
    (1, 0, 1),
    (1, 1, 0),
    (1, 1, 1),
)
HOPS = (
    (
        (2, 0, 0, 0, ((29, 37), (37, 53), (53, 61), (64, 69))),
        (2, 0, 1, 0, ((33, 41), (41, 57), (64, 69))),
        (2, 0, 2, 0, ((34, 45), (49, 69))),
        (2, 0, 3, 0, ((41, 49),)),
        (2, 1, 0, 0, ((42, 53),)),
        (2, 1, 1, 0, ((49, 57),)),
        (2, 1, 2, 0, ((53, 61),)),
        (2, 1, 3, 0, ((64, 69),)),
    ),
    (
        (2, 0, 1, 3, ((0, 3),)),
        (2, 0, 3, 1, ((0, 9), (12, 19), (20, 37))),
        (2, 1, 4, 0, ((0, 3), (21, 45))),
        (2, 0, 2, 2, ((1, 4), (11, 18))),
        (2, 1, 0, 1, ((3, 12), (12, 19), (40, 45))),
        (2, 1, 1, 1, ((4, 17), (17, 29), (40, 45))),
        (2, 1, 2, 1, ((17, 37), (40, 45))),
        (2, 2, 0, 0, ((29, 45),)),
        (2, 1, 3, 1, ((32, 45),)),
        (2, 2, 1, 0, ((37, 45),)),
    ),
    (
        (2, 1, 2, 3, ((0, 13),)),
        (2, 1, 3, 2, ((0, 21), (33, 41))),
        (2, 1, 4, 2, ((0, 13), (41, 49))),
        (2, 2, 0, 1, ((0, 33), (34, 42), (49, 58))),
        (2, 2, 2, 0, ((0, 5), (8, 34), (41, 49))),
        (2, 2, 1, 1, ((24, 42), (42, 50), (64, 70))),
        (1, 0, 0, 0, ((29, 34), (48, 61))),
        (1, 0, 1, 0, ((33, 41), (50, 69))),
        (1, 0, 2, 0, ((34, 42), (57, 70))),
        (1, 0, 3, 0, ((40, 45),)),
        (1, 1, 0, 0, ((42, 49),)),
        (1, 1, 1, 0, ((48, 53),)),
        (1, 1, 2, 0, ((53, 61),)),
        (1, 1, 3, 0, ((61, 69),)),
    ),
    (
        (2, 2, 2, 3, ((0, 3),)),
        (1, 0, 0, 2, ((0, 3), (4, 9))),
        (1, 0, 1, 2, ((0, 3), (10, 13))),
        (1, 1, 4, 0, ((0, 2), (52, 56), (56, 58), (59, 60))),
        (1, 0, 3, 1, ((1, 9), (12, 18), (21, 46))),
        (1, 0, 2, 2, ((2, 5), (11, 17))),
        (1, 1, 0, 1, ((4, 12), (16, 20), (32, 47))),
        (1, 1, 2, 1, ((4, 12), (48, 50), (55, 57))),
        (1, 2, 0, 0, ((5, 10), (10, 18), (20, 37), (47, 49))),
        (1, 2, 1, 0, ((13, 18), (18, 37), (40, 48), (49, 51))),
        (1, 1, 1, 1, ((16, 21), (21, 46), (51, 54))),
        (1, 2, 2, 0, ((21, 37), (40, 49), (50, 52), (53, 55))),
        (1, 1, 3, 1, ((49, 53), (54, 56), (57, 59))),
    ),
)


class Handle:
    pass


class Parts:
    def __init__(self):
        self.inputs, self.outputs, self.scratch = [], [], []

    def inp(self, array, spec):
        self.inputs.append((Handle(), array, spec))
        return self.inputs[-1][0]

    def out(self, shape, dtype, spec=None):
        self.outputs.append((Handle(), shape_of(shape, dtype), spec or fixed(shape)))
        return self.outputs[-1][0]

    def tmp(self, kind):
        self.scratch.append((Handle(), kind))
        return self.scratch[-1][0]

    def vmem(self, shape, dtype):
        return self.tmp(pltpu.VMEM(shape, dtype))

    def run(self, body, steps, flops, moved, collective):
        handles = [x[0] for x in self.inputs + self.outputs + self.scratch]

        def kernel(*refs):
            body(dict(zip(handles, refs)))

        results = pl.pallas_call(
            kernel,
            grid=(steps,),
            in_specs=[x[2] for x in self.inputs],
            out_specs=[x[2] for x in self.outputs],
            out_shape=[x[1] for x in self.outputs],
            scratch_shapes=[x[1] for x in self.scratch],
            compiler_params=pltpu.CompilerParams(
                dimension_semantics=("arbitrary",),
                vmem_limit_bytes=63 * MIB,
                fuse_transposed_lhs_in_matmul=True,
                collective_id=collective,
                has_side_effects=collective is not None,
            ),
            cost_estimate=pl.CostEstimate(
                flops=int(flops), bytes_accessed=int(moved), transcendentals=0
            ),
        )(*[x[1] for x in self.inputs])
        return dict(zip([x[0] for x in self.outputs], results))


def fixed(shape):
    return pl.BlockSpec(shape, lambda i: (0,) * len(shape), pipeline_mode=pl.Buffered(1))


def bit_of(me, bit):
    return lax.rem(lax.div(me, bit), 2)


def order_of(key):
    return (1, 4, 2, 8) if key in Z_FIRST else (1, 2, 4, 8)


def put_rows(me, held, layer, chunk, block, shards, base, keep, send, height, rows):
    core = bit_of(me, 1)
    places = {}
    count = height // rows
    for k in range(shards // 2):
        differ = {}
        for bit in (2, 4, 8):
            mine = bit_of(me, bit)
            if bit < shards:
                differ[bit] = 1 - mine if (2 * k // bit) % 2 else mine
            else:
                theirs = bit_of(base, bit)
                differ[bit] = mine + theirs - 2 * mine * theirs
        for which, ref in ((core, keep), (1 - core, send)):
            start = (2 * k + which) * height
            for b in range(count):
                bits = order_of((layer, chunk, block + b))[1:]
                place = 4 * differ[bits[0]] + 2 * differ[bits[1]] + differ[bits[2]]
                ref[place, block + b] = held[pl.ds(pl.multiple_of(start + b * rows, 16), rows)]


class Hop:
    def __init__(self, key, hop, keep, send, got, done, sem):
        self.bit, self.hop = order_of(key)[hop], hop
        self.keep, self.send, self.got, self.done, self.sem = keep, send, got, done, sem


class Traffic:
    def __init__(self, parts, number, layer, fresh, state, rows, d, small=None, cross=None):
        legs = HOPS[number]
        self.parts, self.state, self.layer = parts, state, layer
        self.events, self.loads, self.copies = [], [], []
        self.small, self.cross = small, cross
        self.keep, self.send = {}, {}
        self.kept_out, self.done_out = [], []
        bits = set()
        groups = {}
        for leg in legs:
            groups.setdefault(leg[:2], []).append(leg)
        for chunk in fresh:
            groups.setdefault((layer, chunk), [])
        arrays = {}
        count = 0

        def operand(array):
            if id(array) not in arrays:
                arrays[id(array)] = parts.inp(array, pl.BlockSpec(memory_space=pl.ANY))
            return arrays[id(array)]

        for name, members in groups.items():
            made_here = name[0] == layer and name[1] in fresh
            if made_here:
                blocks = list(range(SIZES[name[1]]))
                slots = 8
            else:
                blocks = [leg[2] for leg in members]
                slots = max(8 if leg[3] == 0 else 16 >> leg[3] for leg in members)
            ends = {leg[2]: leg[3] + len(leg[4]) for leg in members}
            finished = [b for b in blocks if ends.get(b, 0) == 4]
            shape = (slots, len(blocks), rows, d)
            if len(finished) == len(blocks):
                keep = parts.vmem(shape, bf16)
            else:
                keep = parts.out(shape, bf16)
            send = None
            if made_here:
                if all(ends.get(b, 0) > 0 for b in blocks):
                    send = parts.vmem(shape, bf16)
                else:
                    send = parts.out(shape, bf16)
                self.keep[name[1]], self.send[name[1]] = keep, send
            if finished:
                done = parts.out((len(finished), rows, d), f32)
                for place, b in enumerate(finished):
                    self.done_out.append((name + (b,), done, place))
            for place, b in enumerate(blocks):
                if b not in finished:
                    sent = send if made_here and ends.get(b, 0) == 0 else None
                    self.kept_out.append((name + (b,), keep, sent, place))
            for hop in range(4):
                users = [leg for leg in members if leg[3] <= hop < leg[3] + len(leg[4])]
                if not users:
                    continue
                got = parts.vmem((8 >> hop, len(users), rows, d), bf16)
                for index, leg in enumerate(users):
                    key, place = leg[:3], blocks.index(leg[2])
                    source = None
                    if hop == 0:
                        if made_here:
                            source = (send, place)
                        else:
                            source = (operand(state[key][1]), state[key][2])
                    final = None
                    if hop == 3:
                        final = (done, finished.index(leg[2]))
                    item = Hop(key, hop, (keep, place), source, (got, index), final, count)
                    count += 1
                    bits.add(item.bit)
                    start, end = leg[4][hop - leg[3]]
                    self.events.append((end, 0, len(self.events), self.finish, item))
                    self.events.append((start, 1, len(self.events), self.begin, item))
            if not made_here:
                for leg in members:
                    kept, _, place = state[leg[:3]]
                    have = 8 if leg[3] == 0 else 16 >> leg[3]
                    self.loads.append((operand(kept), place, have, keep, blocks.index(leg[2])))
        if small is not None:
            self.total = parts.vmem(small[0], f32)
            self.small_got = parts.vmem((4,) + small[0], f32)
            self.small_out = parts.out(small[0], f32)
            bits |= {1, 2, 4, 8}
            for hop, (start, end) in enumerate(small[1]):
                item = (hop, count + hop)
                self.events.append((end, 0, len(self.events), self.small_finish, item))
                self.events.append((start, 1, len(self.events), self.small_begin, item))
            count += 4
        if cross is not None:
            self.cross_out = parts.vmem(cross[0], bf16)
            self.cross_got = parts.vmem(cross[0], bf16)
            self.cross_in = parts.out(cross[0], bf16)
            start, end = cross[1]
            self.events.append((end, 0, len(self.events), self.cross_finish, count))
            self.events.append((start, 1, len(self.events), self.cross_begin, count))
            count += 1
        self.sent = parts.tmp(pltpu.SemaphoreType.DMA((count,)))
        self.arrived = parts.tmp(pltpu.SemaphoreType.DMA((count,)))
        self.loaded = None
        if self.loads:
            self.loaded = parts.tmp(pltpu.SemaphoreType.DMA((len(self.loads),)))
        self.bits = sorted(bits)
        self.events.sort(key=lambda e: e[:3])

    def bind(self, refs, step):
        self.refs, self.step = refs, step
        self.me, self.side = lax.axis_index("wide"), lax.axis_index("narrow")

    def device(self, bit):
        return {"wide": self.me + bit - 2 * bit * bit_of(self.me, bit)}

    def open(self):
        loads = []
        for index, (source, place, slots, keep, at) in enumerate(self.loads):
            copy = pltpu.make_async_copy(
                self.refs[source].at[pl.ds(0, slots), place],
                self.refs[keep].at[pl.ds(0, slots), at],
                self.refs[self.loaded].at[index],
            )
            copy.start()
            loads.append(copy)
        barrier = pltpu.get_barrier_semaphore()
        peers = [self.device(bit) for bit in self.bits]
        if self.cross is not None:
            peers.append({"narrow": 1 - self.side})
        for peer in peers:
            pl.semaphore_signal(barrier, inc=1, device_id=peer, device_id_type=MESH)
        pl.semaphore_wait(barrier, len(peers))
        for copy in loads:
            copy.wait()

    def remote(self, source, target, index, device):
        return pltpu.make_async_remote_copy(
            src_ref=source,
            dst_ref=target,
            send_sem=self.refs[self.sent].at[index],
            recv_sem=self.refs[self.arrived].at[index],
            device_id=device,
            device_id_type=MESH,
        )

    def copy(self, item):
        slots = 8 >> item.hop
        if item.hop == 0:
            source = self.refs[item.send[0]].at[pl.ds(0, 8), item.send[1]]
        else:
            source = self.refs[item.keep[0]].at[pl.ds(slots, slots), item.keep[1]]
        target = self.refs[item.got[0]].at[pl.ds(0, slots), item.got[1]]
        return self.remote(source, target, item.sem, self.device(item.bit))

    def begin(self, item):
        self.copy(item).start()

    def finish(self, item):
        self.copy(item).wait()
        keep, at = self.refs[item.keep[0]], item.keep[1]
        got, place = self.refs[item.got[0]], item.got[1]
        if item.hop == 3:
            done, final = self.refs[item.done[0]], item.done[1]
            done[final] = keep[0, at].astype(f32) + got[0, place].astype(f32)
        else:

            @pl.loop(0, 8 >> item.hop)
            def _(slot):
                total = keep[slot, at].astype(f32) + got[slot, place].astype(f32)
                keep[slot, at] = total.astype(bf16)

    def small_copy(self, item):
        target = self.refs[self.small_got].at[item[0]]
        return self.remote(self.refs[self.total], target, item[1], self.device(1 << item[0]))

    def small_begin(self, item):
        self.small_copy(item).start()

    def small_finish(self, item):
        self.small_copy(item).wait()
        total = self.refs[self.total][...] + self.refs[self.small_got][item[0]]
        self.refs[self.total][...] = total
        if item[0] == 3:
            self.refs[self.small_out][...] = total

    def cross_copy(self, index):
        refs = self.refs
        device = {"narrow": 1 - self.side}
        return self.remote(refs[self.cross_out], refs[self.cross_got], index, device)

    def cross_begin(self, index):
        self.cross_copy(index).start()

    def cross_finish(self, index):
        self.cross_copy(index).wait()
        self.refs[self.cross_in][...] = self.refs[self.cross_got][...]

    def fire(self, low, high=None):
        high = low + 1 if high is None else high

        def spot(time):
            return min(time // 8, self.steps - 1)

        found = [e for e in self.events if low <= e[0] - 8 * spot(e[0]) < high]
        for at in sorted({spot(e[0]) for e in found}):

            @pl.when(self.step == at)
            def _(at=at):
                for event in found:
                    if spot(event[0]) == at:
                        event[3](event[4])

    def close(self, results, finals):
        for key, keep, sent, place in self.kept_out:
            self.state[key] = (results[keep], None if sent is None else results[sent], place)
        for key, done, place in self.done_out:
            self.state.pop(key, None)
            finals[key] = (results[done], place)


def ff_back(number, layer, grads, count, saved, weights, state, finals):
    _, attn_out, ff_up, ff_down, _, gains, _ = weights
    unit1, scale1, rb, act, slope, unit2, scale2, blended = saved
    n, d = unit1.shape
    rows = d // 16
    tiles = act.shape[1] // d
    steps = 2 * tiles + 1
    top = len(grads) == 1
    parts = Parts()
    first = lambda i: jnp.minimum(i, tiles - 1)
    later = lambda i: jnp.clip(i - tiles, 0, tiles - 1)
    h_count = parts.inp(count, scalar_spec())
    h_grads = [parts.inp(grad, fixed((n, d))) for grad in grads]
    h_act = parts.inp(act, pl.BlockSpec((n, d), lambda i: (0, first(i))))
    h_slope = parts.inp(slope, pl.BlockSpec((n, d), lambda i: (0, later(i))))
    h_wd = parts.inp(ff_down, pl.BlockSpec((None, d, d), lambda i: (0, later(i), 0)))
    h_wu = parts.inp(ff_up, pl.BlockSpec((None, d, d), lambda i: (0, 0, later(i))))
    h_wo = parts.inp(attn_out, fixed((None, d, d)))
    h_gains = parts.inp(gains, fixed((None, 2, d)))
    h_unit1, h_scale1 = parts.inp(unit1, fixed((n, d))), parts.inp(scale1, fixed((n, 1)))
    h_unit2, h_scale2 = parts.inp(unit2, fixed((n, d))), parts.inp(scale2, fixed((n, 1)))
    h_rb = parts.inp(rb, fixed((n, d)))
    h_blended = parts.inp(blended, fixed((n, d)))
    h_gr, h_do = parts.out((n, d), f32), parts.out((n, d), bf16)
    h_sums = parts.out((16, d), f32)
    h_acc, h_gb = parts.vmem((n, d), f32), parts.vmem((n, d), bf16)
    h_turned, h_held = parts.vmem((d, n), bf16), parts.vmem((d, d), bf16)
    traffic = Traffic(parts, number, layer, (DOWN, UP), state, rows, d)
    traffic.steps = steps

    def body(refs):
        step = pl.program_id(0)
        traffic.bind(refs, step)
        me = traffic.me
        sums, acc, gb = refs[h_sums], refs[h_acc], refs[h_gb]
        turned, held = refs[h_turned], refs[h_held]

        @pl.when(step == 0)
        def _():
            traffic.open()

        traffic.fire(0)

        @pl.when(step == 0)
        def _():

            def strip(rows, carry):
                g = refs[h_grads[0]][rows].astype(f32)
                if top:
                    row = lax.broadcasted_iota(jnp.int32, (16, 1), 0) + rows.start
                    g = jnp.where(row < refs[h_count][0], g, 0.0)
                else:
                    g = g + refs[h_grads[1]][rows].astype(f32)
                unit = refs[h_unit2][rows]
                back = normalise_back(g, unit, refs[h_scale2][rows], refs[h_gains][1:2])
                acc[rows] = back
                low = back.astype(bf16)
                gb[rows] = low
                found = (low.astype(f32), g, g * unit)
                return tuple(a + fold(b) for a, b in zip(carry, found))

            zero = jnp.zeros((8, d), f32)
            found = each_strip(n, 16, strip, (zero, zero, zero))
            sums[0:8] = zero
            sums[8:16] = zero
            for at, value in zip((4, 5, 7), found):
                sums[at : at + 1] = jnp.sum(value, axis=0, keepdims=True)

        @pl.when(step < tiles)
        def _():
            held[...] = tn(refs[h_act][...], gb[...]).astype(bf16)
            keep, send = refs[traffic.keep[DOWN]], refs[traffic.send[DOWN]]
            shards = 16 // tiles
            put_rows(
                me, held, layer, DOWN, 0, shards, step * shards, keep, send, rows * tiles, rows
            )

        @pl.when(step == tiles)
        def _():
            turned[...] = refs[h_rb][...].T

        middle = (step >= tiles) & (step < 2 * tiles)

        @pl.when(middle)
        def _():
            grad = nt(gb[...], refs[h_wd][...]) * refs[h_slope][...].astype(f32)
            grad = grad.astype(bf16)
            sums[pl.ds(8 + step - tiles, 1)] = jnp.sum(grad.astype(f32), axis=0, keepdims=True)
            held[0:n] = grad

        traffic.fire(1)

        @pl.when(middle)
        def _():
            acc[...] += nt(held[0:n], refs[h_wu][...])

        traffic.fire(2)

        @pl.when(middle)
        def _():
            held[...] = nn(turned[...], held[0:n]).astype(bf16)

        @pl.when(step == 2 * tiles)
        def _():
            turned[...] = refs[h_blended][...].T

            def strip(rows, carry):
                g = acc[rows]
                unit = refs[h_unit1][rows]
                back = normalise_back(g, unit, refs[h_scale1][rows], refs[h_gains][0:1])
                refs[h_gr][rows] = back
                low = back.astype(bf16)
                gb[rows] = low
                found = (low.astype(f32), g, g * unit)
                return tuple(a + fold(b) for a, b in zip(carry, found))

            zero = jnp.zeros((8, d), f32)
            found = each_strip(n, 16, strip, (zero, zero, zero))
            for at, value in zip((2, 3, 6), found):
                sums[at : at + 1] = jnp.sum(value, axis=0, keepdims=True)
            low = gb[...]
            refs[h_do][...] = nt(low, refs[h_wo][...]).astype(bf16)
            held[...] = nn(turned[...], low).astype(bf16)

        for block in range(tiles + 1):

            @pl.when(step == tiles + block)
            def _(block=block):
                keep, send = refs[traffic.keep[UP]], refs[traffic.send[UP]]
                put_rows(me, held, layer, UP, block, 16, 0, keep, send, rows, rows)

        traffic.fire(5, 1000)

    results = parts.run(body, steps, 2 * n * d * d * (4 * tiles), 4 * d * d * tiles, number)
    traffic.close(results, finals)
    return results[h_gr], results[h_do], results[h_sums]


def attn_back(
    number, layer, arrays, offsets, blended, grad_blended, soft, places, weight, left_rows,
    residual, small, state, finals,
):
    n, d = grad_blended.shape
    per_shard = d // 16
    groups = 3
    wide = d // groups
    heads = H // groups
    steps = 2 * groups
    boxed = places is not None
    parts = Parts()
    early = lambda i: jnp.minimum(i, groups - 1)
    later = lambda i: jnp.clip(i - groups, 0, groups - 1)

    def wide_block(offset):
        return pl.BlockSpec((n, wide), lambda i: (0, early(i) + offset // 2))

    h_q, h_k, h_v = (parts.inp(a, wide_block(o)) for a, o in zip(arrays, offsets))
    h_g = parts.inp(grad_blended, wide_block(0))
    h_o = parts.inp(blended, wide_block(0))
    keys = soft.shape[2]
    h_p = parts.inp(soft, pl.BlockSpec((heads, n, keys), lambda i: (early(i), 0, 0)))
    h_kv = [parts.vmem((keys, wide), bf16) for _ in range(2)]
    h_dp = parts.vmem((n, keys), f32)
    h_w = []
    for index in range(3):
        when = early if (not boxed and index > 0) else later
        spec = pl.BlockSpec((None, d, wide), lambda i, w=when, k=index: (0, 0, w(i) + groups * k))
        h_w.append(parts.inp(weight, spec))
    h_left = [parts.inp(rows, fixed((n, d))) for rows in left_rows]
    h_turned = [parts.vmem((d, n), bf16) for rows in left_rows]
    h_gr = parts.inp(residual, fixed((n, d)))
    h_own = parts.out((n, d), f32)
    h_sums = parts.out((8, d), f32, pl.BlockSpec((8, wide), lambda i: (0, early(i))))
    h_d = [parts.vmem((groups, n, wide), bf16) for _ in range(3)]
    h_ds, h_held = parts.vmem((n, keys), bf16), parts.vmem((d, d), bf16)
    if boxed:
        h_col, h_row = parts.inp(places[0], fixed((n, 2))), parts.inp(places[1], fixed((2, n)))
        h_near = [parts.vmem((n, keys), bf16) for _ in range(2)]
        h_small1, h_small2 = (parts.inp(x, fixed((16, d))) for x in small[:2])
        h_sums2 = parts.inp(small[2], fixed((8, d)))
        h_hot_i, h_hot_j = parts.vmem((32, n), bf16), parts.vmem((keys, 128), bf16)
        h_step_x, h_step_y = parts.vmem((n, keys), bf16), parts.vmem((n, keys), bf16)
        h_far, h_tab = parts.vmem((n, 384), f32), parts.vmem((2 * H, 128), f32)
        h_sums1 = parts.vmem((8, d), f32)
        times = ((21, 29), (29, 37), (37, 45), (45, 47))
        traffic = Traffic(
            parts, number, layer, (IN,), state, per_shard, d, small=((32, d), times)
        )
    else:
        h_acc = parts.vmem((n, d), f32)
        traffic = Traffic(
            parts, number, layer, (IN,), state, per_shard, d, cross=((n, d), (21, 45))
        )
    traffic.steps = steps

    def body(refs):
        step = pl.program_id(0)
        traffic.bind(refs, step)
        me = traffic.me
        turned = [refs[h] for h in h_turned]
        dq, dk, dv = (refs[h] for h in h_d)
        wq, wk, wv = (refs[h] for h in h_w)
        own, held, ds_s = refs[h_own], refs[h_held], refs[h_ds]

        @pl.when(step == 0)
        def _():
            traffic.open()

        traffic.fire(0)

        @pl.when(step == 0)
        def _():
            for target, source in zip(turned, h_left):
                target[...] = refs[source][...].T
            for h in h_kv:
                refs[h][n:keys] = jnp.zeros((keys - n, wide), bf16)
            if boxed:
                col, row = refs[h_col], refs[h_row]
                cx, cy = col[:, 0:1], col[:, 1:2]
                rx, ry = row[0:1], row[1:2]
                hots = hot_columns(cx, cy, n, reverse=True)
                lane = lax.broadcasted_iota(jnp.int32, (n, 128), 1)
                refs[h_hot_j][0:n] = jnp.where(lane < 32, hots, 0.0).astype(bf16)
                refs[h_hot_j][n:keys] = jnp.zeros((keys - n, 128), bf16)
                line = lax.broadcasted_iota(jnp.int32, (32, n), 0)
                cell = jnp.where(line < 16, rx >> 6, ry >> 6)
                refs[h_hot_i][...] = jnp.where(cell == (line & 15), 1.0, 0.0).astype(bf16)
                for h, c, r in ((h_step_x, cx, rx), (h_step_y, cy, ry)):
                    refs[h][:, 0:n] = jnp.where((c & 63) < (r & 63), 1.0, 0.0).astype(bf16)
                    refs[h][:, n:keys] = jnp.zeros((n, keys - n), bf16)

        def table_lines(head):
            far = refs[h_far]
            value = far[...]
            upper = value.astype(bf16)
            lower = (value - upper.astype(f32)).astype(bf16)
            hi = refs[h_hot_i][...]
            cells = nn(hi, upper) + nn(hi, lower)
            lane = lax.broadcasted_iota(jnp.int32, (16, 128), 1)
            for direction in range(2):
                rows = slice(16 * direction, 16 * direction + 16)
                level = cells[rows, 0:128]
                above = cells[rows, 128 * (direction + 1) : 128 * (direction + 2)]
                inside = (lane >= 16 * direction) & (lane < 16 * direction + 16)
                level = jnp.where(inside, level - above, 0.0)
                above = jnp.where(inside, above, 0.0)
                turn = (128 + 1 - 16 * direction) % 128
                line = pltpu.roll(level, turn, 1, stride=1, stride_axis=0)
                turn = (turn + 127) % 128
                line = line + pltpu.roll(above, turn, 1, stride=1, stride_axis=0)
                line = jnp.sum(line, axis=0, keepdims=True) * HD**0.5
                refs[h_tab][pl.ds(2 * heads * step + 2 * head + direction, 1)] = line

        def head_back(head):
            pair, h = head // 2, head % 2
            lanes = slice(128 * pair, 128 * pair + 128)
            mask = head_masks()[h]
            q, k, v, g = (refs[x][:, lanes] for x in (h_q, h_kv[0], h_kv[1], h_g))
            dp_s = refs[h_dp]
            dp_s[...] = nt(g * mask, v)
            tiles = [slice(128 * t, 128 * t + 128) for t in range(keys // 128)]
            for r in range(0, n, SUB):
                rows = slice(r, r + SUB)
                found = [refs[h_p][head, rows, t].astype(f32) for t in tiles]
                grads = [dp_s[rows, t] for t in tiles]
                mean = (g[rows] * mask).astype(f32) * refs[h_o][rows, lanes]
                mean = jnp.sum(mean, axis=-1, keepdims=True)
                for x, y, t in zip(found, grads, tiles):
                    ds = (x * (y - mean)).astype(bf16)
                    ds_s[rows, t] = ds
                    if boxed:
                        refs[h_near[0]][rows, t] = ds * refs[h_step_x][rows, t]
                        refs[h_near[1]][rows, t] = ds * refs[h_step_y][rows, t]
            if boxed:
                hj, far = refs[h_hot_j][...], refs[h_far]
                queries = nn(ds_s[...], jnp.concatenate([k, hj], axis=1))
                far[:, 0:128] = queries[:, 128:]
                queries = queries[:, :128]
                far[:, 128:256] = nn(refs[h_near[0]][...], hj)
                far[:, 256:384] = nn(refs[h_near[1]][...], hj)
            else:
                queries = nn(ds_s[...], k)
            values = (queries, tn(ds_s[...], q)[:n], tn(refs[h_p][head], g)[:n])
            if boxed:
                table_lines(head)
            low = low_lanes(n)
            outs = []
            for ref, value in zip((dq, dk, dv), values):
                value = value.astype(bf16)
                if h == 0:
                    ref[step, :, lanes] = value
                else:
                    value = jnp.where(low, ref[step, :, lanes].astype(f32), value.astype(f32))
                    ref[step, :, lanes] = value.astype(bf16)
                    outs.append(jnp.sum(value, axis=0, keepdims=True))
            if h == 1:
                sums = store_rows([outs[0], outs[2]])
                refs[h_sums][:, lanes] = sums
                if boxed:
                    start = pl.multiple_of(step * wide + 128 * pair, 128)
                    refs[h_sums1][:, pl.ds(start, 128)] = sums

        @pl.when(step < groups)
        def _():
            refs[h_kv[0]][0:n] = refs[h_k][...]
            refs[h_kv[1]][0:n] = refs[h_v][...]

        for head in range(heads):

            @pl.when(step < groups)
            def _(head=head):
                head_back(head)

            traffic.fire(1 + head)

        def gradient(group):
            for index, ref in enumerate((dq, dk, dv)):
                left = turned[min(index, len(turned) - 1)]
                held[:, index * wide : (index + 1) * wide] = nn(left[...], ref[group]).astype(bf16)

        def store_gradient(start):
            for block in range(groups):

                @pl.when(step == start + block)
                def _(block=block):
                    keep, send = refs[traffic.keep[IN]], refs[traffic.send[IN]]
                    put_rows(
                        me, held, layer, IN, block, 16, 0, keep, send, per_shard, per_shard
                    )

        if boxed:

            @pl.when(step < groups)
            def _():
                gradient(step)

            store_gradient(0)

            @pl.when(step == groups - 1)
            def _():
                total = refs[traffic.total]
                total[0:16] = refs[h_small1][...]
                total[0:2] = refs[h_sums1][0:2]
                total[16:32] = refs[h_small2][...]
                total[16:18] = refs[h_sums2][0:2]
                each = d // 128
                for index in range(2 * H):
                    at = 128 * (index % each)
                    row = 12 + index // each
                    total[row : row + 1, at : at + 128] = refs[h_tab][index : index + 1]

        else:

            @pl.when(step < groups)
            def _():
                value = nt(dk[step], wk[...]) + nt(dv[step], wv[...])

                @pl.when(step == 0)
                def _():
                    refs[h_acc][...] = value

                @pl.when((step > 0) & (step < groups - 1))
                def _():
                    refs[h_acc][...] += value

                @pl.when(step == groups - 1)
                def _():
                    refs[traffic.cross_out][...] = (refs[h_acc][...] + value).astype(bf16)

        @pl.when(step >= groups)
        def _():
            group = step - groups
            value = nt(dq[group], wq[...])
            if boxed:
                value = value + nt(dk[group], wk[...]) + nt(dv[group], wv[...])
            else:
                gradient(group)

            @pl.when(step == groups)
            def _():
                own[...] = refs[h_gr][...] + value

            @pl.when(step > groups)
            def _():
                own[...] += value

        if not boxed:
            store_gradient(groups)
        traffic.fire(5, 1000)

    results = parts.run(
        body, steps, 16 * n * n * d + 12 * n * d * d, 2 * H * n * n, number
    )
    traffic.close(results, finals)
    extra = results[traffic.small_out] if boxed else results[traffic.cross_in]
    return results[h_own], results[h_sums], extra


def finish_outputs(me, finals, small, rows, d):
    tiles = SIZES[DOWN]
    share = d // 16
    parts = Parts()
    h_me = parts.inp(me, scalar_spec())
    h_small = parts.inp(small, fixed(small.shape))
    arrays = {}
    for array, _ in finals.values():
        if id(array) not in arrays:
            arrays[id(array)] = parts.inp(array, fixed(array.shape))
    layers = []
    for _ in range(2):
        layers.append(
            (
                parts.out((rows, 3 * d), f32),
                parts.out((rows, d), f32),
                parts.out((rows, tiles * d), f32),
                parts.out((rows * tiles, d), f32),
                parts.out((6, share), f32),
                parts.out((2, share), f32),
                parts.out((1, tiles * share), f32),
            )
        )
    h_table = parts.out((1, share), f32)

    def body(refs):
        me = refs[h_me][0]
        back = lax.rem(d - share * me, d)
        for layer, outs in zip((1, 2), layers):

            def block(chunk, index):
                array, place = finals[(layer, chunk, index)]
                return refs[arrays[id(array)]][place]

            wide = d // 3
            for group in range(3):
                value = block(IN, group)
                for part in range(3):
                    at = part * d + group * wide
                    refs[outs[0]][:, at : at + wide] = value[:, part * wide : (part + 1) * wide]
            refs[outs[1]][...] = block(UP, tiles)
            for index in range(tiles):
                refs[outs[2]][:, index * d : (index + 1) * d] = block(UP, index)
                refs[outs[3]][index * rows : (index + 1) * rows] = block(DOWN, index)
            base = 16 * (layer - 1)
            turned = pltpu.roll(refs[h_small][base : base + 8], back, 1)
            refs[outs[4]][...] = turned[0:6, :share]
            refs[outs[5]][...] = turned[6:8, :share]
            each = tiles * share
            line = jnp.zeros((1, d), f32)
            for index in range(tiles):
                row = refs[h_small][base + 8 + index : base + 9 + index]
                line = jnp.where(lax.div(me, 16 // tiles) == index, row, line)
            inner = lax.rem(me, 16 // tiles)
            turned = pltpu.roll(jnp.broadcast_to(line, (8, d)), lax.rem(d - each * inner, d), 1)
            refs[outs[6]][...] = turned[0:1, :each]
        direction = lax.div(me, 8)
        first = 4 * lax.rem(me, 8)
        line = jnp.zeros((1, 128), f32)
        lane = lax.broadcasted_iota(jnp.int32, (1, 128), 1)
        for head in range(H):
            found = []
            for way in range(2):
                index = 2 * head + way
                at = 128 * (index % (d // 128))
                row = 12 + index // (d // 128)
                found.append(refs[h_small][row : row + 1, at : at + 128])
            values = jnp.where(direction == 0, found[0], found[1])
            for bucket in range(4):
                value = jnp.sum(jnp.where(lane == first + bucket, values, 0.0))
                line = jnp.where(lane == H * bucket + head, value, line)
        refs[h_table][...] = line[:, :share]

    results = parts.run(body, 1, 1, 8 * rows * d, None)
    done = [tuple(results[h][None] for h in outs[:6]) + (results[outs[6]],) for outs in layers]
    return done[0], done[1], results[h_table]


def backward_with_hops(me, first, second, saved_one, saved_two, one, two, extra):
    top, own_count, places, own_b, mid_b, partner_b, soft_one, soft_two, full_one, full_two = extra
    d = own_b.shape[1]
    state, finals = {}, {}
    gr, do, small_two = ff_back(0, 2, [top], own_count, saved_two, second, state, finals)
    own, sums_two, returned = attn_back(
        1, 2, *two, full_two, do, soft_two, None, second[0], [mid_b, partner_b], gr, None, state, finals
    )
    gr, do, small_one = ff_back(
        2, 1, [own, returned], own_count, saved_one, first, state, finals
    )
    own, _, small = attn_back(
        3, 1, *one, full_one, do, soft_one, places, first[0], [own_b], gr,
        (small_one, small_two, sums_two), state, finals,
    )
    return own, finish_outputs(me, finals, small, d // 16, d)


def swap(value, axis, bit):
    size = lax.axis_size(axis)
    return lax.ppermute(value, axis, [(i, i ^ bit) for i in range(size)])


def reduce_slots(parts, axis):
    keep, send = parts
    bit = 1
    while True:
        got = swap(send, axis, bit)
        count = keep.shape[0]
        if count == 1:
            return keep[0].astype(f32) + got[0].astype(f32)
        half = count // 2
        send = (keep[half:].astype(f32) + got[half:].astype(f32)).astype(keep.dtype)
        keep = (keep[:half].astype(f32) + got[:half].astype(f32)).astype(keep.dtype)
        bit *= 2


def reduce_small(rows, me, axis):
    size = lax.axis_size(axis)
    count = rows.shape[0]
    cut = jnp.transpose(rows.reshape(count, size, -1), (1, 0, 2))
    cut = jnp.take(cut, jnp.arange(size, dtype=jnp.int32) ^ me, axis=0)
    bit = 1
    while bit < size:
        pairs = cut.reshape(cut.shape[0] // 2, 2, *cut.shape[1:])
        cut = pairs[:, 0] + swap(pairs[:, 1], axis, bit)
        bit *= 2
    return cut[0]


def body(
    stream,
    lengths,
    layout_boxes,
    self_attn_in,
    self_attn_out,
    self_ff_up,
    self_ff_down,
    self_vectors,
    self_gains,
    self_up_bias,
    cross_attn_in,
    cross_attn_out,
    cross_ff_up,
    cross_ff_down,
    cross_vectors,
    cross_gains,
    cross_up_bias,
    box_table,
    cotangent,
):
    side = lax.axis_index("narrow")
    place = lax.axis_index("wide")
    devices = lax.axis_size("wide")
    me = place.astype(jnp.int32).reshape(1)
    n, d = stream.shape[2:]
    ff = self_ff_up.shape[2]
    first = (
        self_attn_in,
        self_attn_out,
        self_ff_up,
        self_ff_down,
        self_vectors,
        self_gains,
        self_up_bias,
    )
    second = (
        cross_attn_in,
        cross_attn_out,
        cross_ff_up,
        cross_ff_down,
        cross_vectors,
        cross_gains,
        cross_up_bias,
    )
    own_b = stream.reshape(n, d)
    top = cotangent.reshape(n, d)
    own_count = jnp.where(side == 0, lengths[0], lengths[1])
    other_count = jnp.where(side == 0, lengths[1], lengths[0])
    slot = jnp.arange(n, dtype=jnp.int32)
    padding = ((0, 0), (0, n - TEXT))
    boxes = layout_boxes[0]
    text = jnp.pad((boxes[:2] + boxes[2:]) >> 1, padding)
    grid_side = jnp.where(own_count > GRID_LO * GRID_LO, GRID_HI, GRID_LO).astype(jnp.int32)
    patch = jnp.stack([slot % grid_side, slot // grid_side])
    patch = (patch * 1000 + 500) // grid_side
    centres = jnp.where(side == 0, text, patch)
    places = (centres.T, centres)
    tables = jnp.pad(
        jnp.transpose(box_table.reshape(2, NB, H), (2, 0, 1)).reshape(2 * H, NB),
        ((0, 0), (0, 128 - NB)),
    )

    qkv_one = project(own_b, self_attn_in, self_vectors, 0, 3)
    one = ([qkv_one] * 3, (0, PAIRS, 2 * PAIRS))
    blend_one, soft_one, full_one = attend_forward(*one, own_count, places, tables)
    if devices == 16:
        saved_one = feed_forward_sending(blend_one, own_b, first, cross_attn_in, cross_vectors)
        *saved_one, partner_b, q_two = saved_one
    else:
        saved_one = feed_forward(blend_one, own_b, first, own_count, False)
        partner_b = swap(saved_one[-1], "narrow", 1)
        q_two = project(saved_one[-1], cross_attn_in, cross_vectors, 0, 1)
    unit_one, scale_one, rb_one, act_one, slope_one, unit_two, scale_two, mid, mid_b = saved_one
    kv_two = project(partner_b, cross_attn_in, cross_vectors, 1, 2)
    two = ([q_two, kv_two, kv_two], (0, 0, PAIRS))
    blend_two, soft_two, full_two = attend_forward(*two, other_count, None, None)
    saved_two = feed_forward(blend_two, mid, second, own_count, True)
    unit_three, scale_three, rb_two, act_two, slope_two, unit_four, scale_four, final = saved_two

    if devices == 16:
        saved = (unit_one, scale_one, rb_one, act_one, slope_one, unit_two, scale_two, blend_one)
        later = (
            unit_three, scale_three, rb_two, act_two, slope_two, unit_four, scale_four, blend_two
        )
        extra = (
            top, own_count, places, own_b, mid_b, partner_b, soft_one, soft_two, full_one, full_two
        )
        grad_stream, (grads_one, grads_two, grad_table) = backward_with_hops(
            me, first, second, saved, later, one, two, extra
        )
        return (final[None, None], grad_stream[None, None]) + grads_one + grads_two + (grad_table,)

    def large(parts):
        if len(parts) == 2:
            return reduce_slots(parts, "wide")
        return lax.psum_scatter(parts[0].astype(f32), "wide", scatter_dimension=0, tiled=True)

    def columns(value, lead):
        if value.ndim == 2:
            return value[:, lead[0] * d : lead[1] * d][None]
        picked = value[lead[0] : lead[1]]
        return jnp.transpose(picked, (1, 0, 2)).reshape(1, picked.shape[1], -1)

    dz, gb, sums_four, down_two = down_gradient(
        me, own_count, [top], unit_four, scale_four, cross_gains, act_two, devices, True
    )
    down_two = large(down_two)
    du, ups_two, ga, gr, do, sums_three = feed_backward(
        dz, gb, slope_two, unit_three, scale_three, second
    )
    steps = ff // d
    jobs = [(0, 0, 0)] * steps + [(1, 1, 0)]
    up_two = large(weight_gradients(me, jobs, [rb_two, blend_two], [du, ga], devices))
    dq, dk, dv, sums_two_attn = attend_backward(*two, do, soft_two, None)
    grad_partner = project_back([dk, dv], cross_attn_in, 1, None, bf16)
    returned = swap(grad_partner, "narrow", 1)
    grad_own = project_back([dq], cross_attn_in, 0, gr, f32)
    in_two = large(
        weight_gradients(
            me, [(0, 0, 0), (1, 1, 0), (1, 2, 0)], [mid_b, partner_b], [dq, dk, dv], devices
        )
    )

    dz, gb, sums_two, down_one = down_gradient(
        me, own_count, [grad_own, returned], unit_two, scale_two, self_gains, act_one, devices, False
    )
    down_one = large(down_one)
    du, ups_one, ga, gr, do, sums_one = feed_backward(
        dz, gb, slope_one, unit_one, scale_one, first
    )
    up_one = large(weight_gradients(me, jobs, [rb_one, blend_one], [du, ga], devices))
    dq, dk, dv, sums_one_attn, grad_tables = attend_backward(*one, do, soft_one, places)
    in_one = large(
        weight_gradients(
            me, [(0, 0, 0), (0, 1, 0), (0, 2, 0)], [own_b], [dq, dk, dv], devices
        )
    )
    grad_stream = project_back([dq, dk, dv], self_attn_in, 0, gr, f32)

    def ups_rows(ups):
        return jnp.transpose(
            ups.reshape(devices, steps, d // devices), (1, 0, 2)
        ).reshape(steps, d)

    table_row = jnp.transpose(
        grad_tables.reshape(H, 2, 128)[:, :, :NB], (1, 2, 0)
    ).reshape(1, 2 * NB * H)
    small = jnp.concatenate(
        [
            sums_one_attn[:2],
            sums_one[2:3],
            sums_one[1:2],
            sums_two[2:3],
            sums_two[1:2],
            sums_one[0:1],
            sums_two[0:1],
            ups_rows(ups_one),
            sums_two_attn[:2],
            sums_three[2:3],
            sums_three[1:2],
            sums_four[2:3],
            sums_four[1:2],
            sums_three[0:1],
            sums_four[0:1],
            ups_rows(ups_two),
            table_row,
        ]
    )
    small = reduce_small(small, me, "wide")
    half = 8 + steps

    def layer(values, base, inside, up, down):
        return (
            columns(inside, (0, 3)),
            columns(up, (steps, steps + 1)),
            columns(up, (0, steps)),
            down[None],
            values[base : base + 6][None],
            values[base + 6 : base + 8][None],
            values[base + 8 : base + half].reshape(1, -1),
        )

    return (
        (final[None, None], grad_stream[None, None])
        + layer(small, 0, in_one, up_one, down_one)
        + layer(small, half, in_two, up_two, down_two)
        + (small[2 * half :],)
    )


def solution(mesh):
    matrix = P("narrow", None, None)
    layer_in = (matrix,) * 6 + (P("narrow", None),)
    rows = P("narrow", "wide", None, None)
    in_specs = (
        (rows, P(None, "wide"), P("wide", None, None))
        + layer_in * 2
        + (P("narrow", None), rows)
    )
    layer_out = (P("narrow", "wide", None),) * 4 + (
        P("narrow", None, "wide"),
        P("narrow", None, "wide"),
        P("narrow", "wide"),
    )
    out_specs = (rows, rows) + layer_out * 2 + (P("narrow", "wide"),)
    return jax.shard_map(body, mesh=mesh, in_specs=in_specs, out_specs=out_specs, check_vma=False)
```

```python
import functools

import jax
import jax.numpy as jnp
import numpy as np
from jax import lax
from jax.experimental import pallas as pl
from jax.experimental.pallas import tpu as pltpu
from jax.sharding import PartitionSpec as P

H = 12
HD = 64
NB = 32
TEXT = 512
GRID_LO = 16
GRID_HI = 24
PAIRS = H // 2
STRIP = 192
SUB = 32
MIB = 1 << 20

norm_eps = 1e-05
spacing = 64
masked_score = -1e30

f32 = jnp.float32
bf16 = jnp.bfloat16
SMEM = pltpu.MemorySpace.SMEM


def nn(left, right):
    return lax.dot_general(left, right, (((1,), (0,)), ((), ())), preferred_element_type=f32)


def nt(left, right):
    return lax.dot_general(left, right, (((1,), (1,)), ((), ())), preferred_element_type=f32)


def tn(left, right):
    return lax.dot_general(left, right, (((0,), (0,)), ((), ())), preferred_element_type=f32)


def whole(shape):
    return pl.BlockSpec(shape, lambda i: (0,) * len(shape))


def scalar_spec():
    return pl.BlockSpec(memory_space=SMEM)


def call(kernel, grid, in_specs, out_specs, out_shape, scratch, flops, moved, vmem=63):
    return pl.pallas_call(
        kernel,
        grid=grid,
        in_specs=in_specs,
        out_specs=out_specs,
        out_shape=out_shape,
        scratch_shapes=scratch,
        compiler_params=pltpu.CompilerParams(
            dimension_semantics=("arbitrary",),
            vmem_limit_bytes=vmem * MIB,
            fuse_transposed_lhs_in_matmul=True,
        ),
        cost_estimate=pl.CostEstimate(
            flops=int(flops), bytes_accessed=int(moved), transcendentals=0
        ),
    )


def shape_of(shape, dtype):
    return jax.ShapeDtypeStruct(shape, dtype)


def normalise(values):
    average = jnp.mean(values, axis=-1, keepdims=True)
    centred = values - average
    variance = jnp.mean(centred * centred, axis=-1, keepdims=True)
    scale = lax.rsqrt(variance + norm_eps)
    return centred * scale, scale


def normalise_back(grad, unit, scale, gains):
    inner = grad * gains
    mean_one = jnp.mean(inner, axis=-1, keepdims=True)
    mean_two = jnp.mean(inner * unit, axis=-1, keepdims=True)
    return scale * (inner - mean_one - unit * mean_two)


def gelu_both(u):
    t = pltpu.reciprocal(1.0 + (0.3275911 * 0.7071067811865476) * jnp.abs(u), approx=True)
    bell = jnp.exp(-0.5 * (u * u))
    poly = t * (
        0.127414796
        + t * (-0.142248368 + t * (0.7107068705 + t * (-0.7265760135 + t * 0.5307027145)))
    )
    tail = poly * bell
    share = jnp.where(u < 0, tail, 1.0 - tail)
    return u * share, share + (u * 0.3989422804014327) * bell


def each_strip(n, size, body, start=None, unroll=4):
    def step(index, carry):
        return body(pl.ds(pl.multiple_of(index * size, size), size), carry)

    return lax.fori_loop(0, n // size, step, start, unroll=unroll)


def fold(values):
    total = values[0:8]
    for r in range(8, values.shape[0], 8):
        total = total + values[r : r + 8]
    return total


def project(rows, weight, vectors, first, count):
    n, d = rows.shape

    def kernel(x_ref, w_ref, v_ref, o_ref):
        part = pl.program_id(0) + first
        shift = jnp.where(part == 0, v_ref[0:1], jnp.where(part == 2, v_ref[1:2], 0.0))
        o_ref[...] = (nn(x_ref[...], w_ref[...]) + shift).astype(bf16)

    return call(
        kernel,
        (count,),
        [
            whole((n, d)),
            pl.BlockSpec((None, d, d), lambda i: (0, 0, i + first)),
            pl.BlockSpec((None, 6, d), lambda i: (0, 0, 0)),
        ],
        pl.BlockSpec((n, d), lambda i: (0, i)),
        shape_of((n, count * d), bf16),
        [],
        2 * n * d * d * count,
        2 * d * d * count,
    )(rows, weight, vectors)


def head_masks():
    lane = lax.broadcasted_iota(jnp.int32, (1, 2 * HD), 1)
    return [
        jnp.where(lane < HD, HD**-0.5, 0.0).astype(bf16),
        jnp.where(lane < HD, 0.0, HD**-0.5).astype(bf16),
    ]


def count_of(lengths, other=False):
    side = lax.axis_index("narrow")
    text, image = lengths[0, 0], lengths[1, 0]
    return jnp.where(side == (1 if other else 0), text, image)


def patch_centres(n, keys):
    slot = np.arange(n)
    rows = []
    for side in (GRID_HI, GRID_LO):
        for index in (slot % side, slot // side):
            rows.append((index * 1000 + 500) // side)
    return jnp.asarray(np.pad(np.stack(rows), ((0, 0), (0, keys - n))), jnp.int32)


def centres_of(lengths, boxes, patches):
    text = jnp.concatenate(
        [(boxes[0:2] + boxes[2:4]) >> 1, jnp.zeros((2, patches.shape[1] - TEXT), jnp.int32)], axis=1
    )
    patch = jnp.where(lengths[1, 0] > GRID_LO * GRID_LO, patches[0:2], patches[2:4])
    row = jnp.where(lax.axis_index("narrow") == 0, text, patch)
    tall = jnp.concatenate([row, jnp.zeros((6, row.shape[1]), jnp.int32)], axis=0)
    return row, tall.astype(f32).T.astype(jnp.int32)


def table_lines(tables):
    each = NB * H
    lane = lax.broadcasted_iota(jnp.int32, (16, each), 1)
    head = lax.broadcasted_iota(jnp.int32, (16, each), 0)
    line = lax.broadcasted_iota(jnp.int32, (each, 128), 0)
    bucket = lax.broadcasted_iota(jnp.int32, (each, 128), 1)
    inside = line - H * bucket
    hot = jnp.where((inside >= 0) & (inside < H), 1.0, 0.0)
    found = []
    for direction in range(2):
        values = tables[:, direction * each : direction * each + each]
        past = lane - head
        mine = past - H * ((past.astype(f32) + 0.5) * (1.0 / H)).astype(jnp.int32) == 0
        values = jnp.where(mine & (past >= 0), jnp.broadcast_to(values, (16, each)), 0.0)
        found.append(
            lax.dot_general(
                values, hot, (((1,), (0,)), ((), ())),
                precision=lax.Precision.HIGHEST, preferred_element_type=f32,
            )
        )
    return found


def low_lanes(rows):
    return lax.broadcasted_iota(jnp.int32, (rows, 2 * HD), 1) < HD


def hot_columns(coord_x, coord_y, rows, reverse=False):
    lane = lax.broadcasted_iota(jnp.int32, (rows, 128), 1)
    cell = jnp.where((lane & 16) == 0, coord_x >> 6, coord_y >> 6)
    place = lane & 15
    if reverse:
        place = 15 - place
    return jnp.where((cell == place) & (lane < 64), 1.0, 0.0)


def slanted(row, first):
    wide = jnp.broadcast_to(row, (16, 128))
    return pltpu.roll(wide, (128 - first) % 128, 1, stride=1, stride_axis=0)


def spread_tables(table_x, table_y):
    lane = lax.broadcasted_iota(jnp.int32, (16, 128), 1)
    keep = lane < 16
    outs = []
    rows = []
    for row in (table_x, table_y):
        base = jnp.where(keep, slanted(row, 16), 0.0)
        before = jnp.where(keep, slanted(row, 15), 0.0)
        rows.append((base, before - base))

    def split(value, offset):
        upper = value.astype(bf16).astype(f32)
        lower = value - upper
        joined = upper + pltpu.roll(lower, 32, 1)
        return pltpu.roll(joined, offset, 1) if offset else joined

    zero = jnp.zeros((16, 128), f32)
    outs.append(jnp.concatenate([split(rows[0][0], 0), split(rows[1][0], 16)], axis=0))
    outs.append(jnp.concatenate([split(rows[0][1], 0), zero], axis=0))
    outs.append(jnp.concatenate([zero, split(rows[1][1], 16)], axis=0))
    return [value.astype(bf16) for value in outs]


def attend_forward(arrays, offsets, lengths, other, boxes, tables):
    n = arrays[0].shape[0]
    keys = -(-n // 128) * 128
    heads = 4
    boxed = boxes is not None

    def kernel(*refs):
        if boxed:
            cnt, q_ref, k_ref, v_ref, b_ref, c_ref, t_ref, o_ref, p_ref, f_ref = refs[:10]
            k_s, v_s, s_s, step_x, step_y, hot_i, hot_j, lines = refs[10:]
        else:
            cnt, q_ref, k_ref, v_ref, o_ref, p_ref, f_ref, k_s, v_s, s_s = refs
            s_s = [[s_s.at[0]], [s_s.at[1]]]
        live_count = count_of(cnt, other)
        group = pl.program_id(0)

        @pl.when(group == 0)
        def _():
            k_s[n:keys] = jnp.zeros((keys - n, 64 * heads), bf16)
            v_s[n:keys] = jnp.zeros((keys - n, 64 * heads), bf16)
            if boxed:
                row, col = centres_of(cnt, b_ref[...], c_ref[...])
                cx, cy = col[0:n, 0:1], col[0:n, 1:2]
                lines[0], lines[1] = table_lines(t_ref[...])
                hots = hot_columns(cx, cy, n)
                lane = lax.broadcasted_iota(jnp.int32, (n, 128), 1)
                hot_i[...] = jnp.where(lane == 64, 1.0, hots).astype(bf16)
                hot_j[0:n] = jnp.where(lane < 32, hots, 0.0).astype(bf16)
                hot_j[n:keys] = jnp.zeros((keys - n, 128), bf16)
                rx, ry = row[0:1], row[1:2]
                step_x[...] = jnp.where((cx & 63) < (rx & 63), 1.0, 0.0)
                step_y[...] = jnp.where((cy & 63) < (ry & 63), 1.0, 0.0)

        if boxed:
            s_s = [[s_s.at[3 * h + k] for k in range(3)] for h in range(2)]
            lane = lax.broadcasted_iota(jnp.int32, (keys, 128), 1)
            place = lax.broadcasted_iota(jnp.int32, (keys, 128), 0)
            dead = jnp.where((lane == 64) & (place >= live_count), masked_score, 0.0)
            dead = dead.astype(bf16)
        k_s[0:n] = k_ref[...]
        v_s[0:n] = v_ref[...]
        masks = head_masks()
        low = low_lanes(n)
        tiles = [slice(128 * t, 128 * t + 128) for t in range(keys // 128)]

        def scores(head):
            lanes = slice(128 * (head // 2), 128 * (head // 2) + 128)
            part = q_ref[:, lanes] * masks[head % 2]
            to = s_s[head % 2]
            if boxed:
                row = pl.ds(heads * group + head, 1)
                base, dx, dy = spread_tables(lines[0, row], lines[1, row])
                hi, hj = hot_i[...], hot_j[:, :32]
                side = nn(hj, base).astype(bf16) + dead
                side = jnp.concatenate([k_s[:, lanes], side], axis=1)
                to[0][...] = nt(jnp.concatenate([part, hi], axis=1), side)
                to[1][...] = nt(hi, nn(hj, dx).astype(bf16))
                to[2][...] = nt(hi, nn(hj, dy).astype(bf16))
            else:
                to[0][...] = nt(part, k_s[:, lanes])

        def soften(head):
            at = s_s[head % 2]
            for r in range(0, n, SUB):
                rows = slice(r, r + SUB)
                parts = []
                for t, lanes in enumerate(tiles):
                    s = at[0][rows, lanes]
                    if boxed:
                        s = s + step_x[rows, lanes] * at[1][rows, lanes]
                        s = s + step_y[rows, lanes] * at[2][rows, lanes]
                    elif 128 * t + 128 > GRID_LO * GRID_LO:
                        lane = lax.broadcasted_iota(jnp.int32, (1, 128), 1) + 128 * t
                        s = jnp.where(lane < live_count, s, masked_score)
                    parts.append(s)
                peak = functools.reduce(jnp.maximum, parts)
                peak = jnp.max(peak, axis=-1, keepdims=True)
                parts = [jnp.exp(s - peak) for s in parts]
                total = functools.reduce(jnp.add, parts)
                total = 1.0 / jnp.sum(total, axis=-1, keepdims=True)
                for s, lanes in zip(parts, tiles):
                    p_ref[head, rows, lanes] = (s * total).astype(bf16)

        scores(0)
        blends = []
        for head in range(heads):
            if head + 1 < heads:
                scores(head + 1)
            soften(head)
            lanes = slice(128 * (head // 2), 128 * (head // 2) + 128)
            blends.append(nn(p_ref[head], v_s[:, lanes]))
            if head % 2 == 1:
                blend = jnp.where(low, blends[head - 1], blends[head])
                f_ref[:, lanes] = blend
                o_ref[:, lanes] = blend.astype(bf16)

    def wide_block(offset):
        return pl.BlockSpec((n, 64 * heads), lambda i: (0, i + offset * 128 // (64 * heads)))

    in_specs = [scalar_spec()] + [wide_block(offset) for offset in offsets]
    args = [lengths, *arrays]
    scratch = [
        pltpu.VMEM((keys, 64 * heads), bf16),
        pltpu.VMEM((keys, 64 * heads), bf16),
        pltpu.VMEM((6 if boxed else 2, n, keys), f32),
    ]
    if boxed:
        in_specs += [
            pl.BlockSpec((None, 4, TEXT), lambda i: (0, 0, 0)),
            whole((4, keys)),
            whole((1, 2 * NB * H)),
        ]
        args += [boxes, patch_centres(n, keys), tables]
        scratch += [pltpu.VMEM((n, keys), f32)] * 2
        scratch += [pltpu.VMEM((n, 128), bf16), pltpu.VMEM((keys, 128), bf16)]
        scratch += [pltpu.VMEM((2, 16, 128), f32)]
    return call(
        kernel,
        (H // heads,),
        in_specs,
        [wide_block(0), pl.BlockSpec((heads, n, keys), lambda i: (i, 0, 0)), wide_block(0)],
        [
            shape_of((n, H * HD), bf16),
            shape_of((H, n, keys), bf16),
            shape_of((n, H * HD), f32),
        ],
        scratch,
        16 * n * n * H * HD,
        2 * H * n * n,
    )(*args)


def feed_forward(blended, states, weights, lengths, last):
    _, attn_out, ff_up, ff_down, vectors, gains, up_bias = weights
    n, d = blended.shape
    steps = ff_up.shape[2] // d

    def kernel(cnt, o_ref, x_ref, wo_ref, wu_ref, wd_ref, v_ref, g_ref, e_ref, *rest):
        if last:
            unit1, scale1, rb, act, der, unit2, scale2, out, r_s, acc = rest
        else:
            unit1, scale1, rb, act, der, unit2, scale2, out, out_b, r_s, acc = rest
        step = pl.program_id(0)

        @pl.when(step == 0)
        def _():
            branch = nn(o_ref[...], wo_ref[...]) + v_ref[2:3]
            unit, scale = normalise(x_ref[...].astype(f32) + branch)
            unit1[...] = unit
            scale1[...] = scale
            r = unit * g_ref[0:1] + v_ref[3:4]
            r_s[...] = r
            rb[...] = r.astype(bf16)
            acc[...] = r + v_ref[4:5]

        hidden = nn(rb[...], wu_ref[...]) + e_ref[...]
        active, slope = gelu_both(hidden)
        active = active.astype(bf16)
        act[...] = active
        der[...] = slope.astype(bf16)
        acc[...] += nn(active, wd_ref[...])

        @pl.when(step == steps - 1)
        def _():
            unit, scale = normalise(acc[...])
            unit2[...] = unit
            scale2[...] = scale
            z = unit * g_ref[1:2] + v_ref[5:6]
            if last:
                row = lax.broadcasted_iota(jnp.int32, (n, 1), 0)
                out[...] = jnp.where(row < count_of(cnt), z, 0.0)
            else:
                out[...] = z
                out_b[...] = z.astype(bf16)

    columns = pl.BlockSpec((n, d), lambda i: (0, i))
    outs = [
        (whole((n, d)), shape_of((n, d), f32)),
        (whole((n, 1)), shape_of((n, 1), f32)),
        (whole((n, d)), shape_of((n, d), bf16)),
        (columns, shape_of((n, steps * d), bf16)),
        (columns, shape_of((n, steps * d), bf16)),
        (whole((n, d)), shape_of((n, d), f32)),
        (whole((n, 1)), shape_of((n, 1), f32)),
        (whole((n, d)), shape_of((n, d), f32)),
    ]
    if not last:
        outs.append((whole((n, d)), shape_of((n, d), bf16)))
    return call(
        kernel,
        (steps,),
        [
            scalar_spec(),
            whole((n, d)),
            whole((n, d)),
            pl.BlockSpec((None, d, d), lambda i: (0, 0, 0)),
            pl.BlockSpec((None, d, d), lambda i: (0, 0, i)),
            pl.BlockSpec((None, d, d), lambda i: (0, i, 0)),
            pl.BlockSpec((None, 6, d), lambda i: (0, 0, 0)),
            pl.BlockSpec((None, 2, d), lambda i: (0, 0, 0)),
            pl.BlockSpec((1, d), lambda i: (0, i)),
        ],
        [spec for spec, _ in outs],
        [shape for _, shape in outs],
        [pltpu.VMEM((n, d), f32), pltpu.VMEM((n, d), f32)],
        2 * n * d * d * (1 + 2 * steps),
        2 * d * d * (1 + 2 * steps),
    )(lengths, blended, states, attn_out, ff_up, ff_down, vectors, gains, up_bias)


def store_rows(rows):
    d = rows[0].shape[1]
    blank = jnp.zeros((8 - len(rows), d), f32)
    return jnp.concatenate(rows + [blank], axis=0)


def slot_place(index, bits):
    place = 0
    for b in range(bits):
        place = place | (((index >> b) & 1) << (bits - 1 - b))
    return place


class Slots:
    def __init__(self, devices, rows):
        self.devices = devices
        self.rows = rows // devices
        self.bits = (devices // 2).bit_length() - 1
        self.split = self.rows % 16 == 0 and devices & (devices - 1) == 0 and devices > 1

    def put(self, me, held, shards, first_shard, write):
        core = me & 1
        for k in range(shards // 2):
            place = slot_place((first_shard // 2 + k) ^ (me >> 1), self.bits)
            for which in range(2):
                start = (2 * k + (core if which == 0 else 1 - core)) * self.rows
                rows = held[pl.ds(pl.multiple_of(start, 16), self.rows)]
                write(which, place, rows)


def down_gradient(me, count, grads, unit, scale, gains, active, devices, top):
    n, d = unit.shape
    ff = active.shape[1]
    steps = ff // d
    slots = Slots(devices, ff)
    shards = devices // steps

    def kernel(me_ref, cnt, *refs):
        ups = refs[: len(grads)]
        unit_ref, scale_ref, g_ref, act_ref = refs[len(grads) : len(grads) + 4]
        dz, gb, sums, *outs, held = refs[len(grads) + 4 :]
        step = pl.program_id(0)

        @pl.when(step == 0)
        def _():
            if top:
                row = lax.broadcasted_iota(jnp.int32, (n, 1), 0)
                g = jnp.where(row < cnt[0], ups[0][...].astype(f32), 0.0)
            else:
                g = ups[0][...] + ups[1][...].astype(f32)
            unit = unit_ref[...]
            back = normalise_back(g, unit, scale_ref[...], g_ref[1:2])
            dz[...] = back
            low = back.astype(bf16)
            gb[...] = low
            sums[...] = store_rows(
                [
                    jnp.sum(g * unit, axis=0, keepdims=True),
                    jnp.sum(g, axis=0, keepdims=True),
                    jnp.sum(low.astype(f32), axis=0, keepdims=True),
                ]
            )

        value = tn(act_ref[...], gb[...]).astype(bf16)
        if slots.split:
            held[...] = value

            def write(which, place, rows):
                outs[which][place] = rows

            slots.put(me_ref[0], held, shards, shards * step, write)
        else:
            outs[0][...] = value

    if slots.split:
        block = (devices // 2, slots.rows, d)
        out_list = [(whole(block), shape_of(block, bf16))] * 2
    else:
        out_list = [(pl.BlockSpec((d, d), lambda i: (i, 0)), shape_of((ff, d), bf16))]
    out_list = [
        (whole((n, d)), shape_of((n, d), f32)),
        (whole((n, d)), shape_of((n, d), bf16)),
        (whole((8, d)), shape_of((8, d), f32)),
    ] + out_list
    results = call(
        kernel,
        (steps,),
        [scalar_spec(), scalar_spec()]
        + [whole((n, d))] * len(grads)
        + [
            whole((n, d)),
            whole((n, 1)),
            pl.BlockSpec((None, 2, d), lambda i: (0, 0, 0)),
            pl.BlockSpec((n, d), lambda i: (0, i)),
        ],
        [spec for spec, _ in out_list],
        [shape for _, shape in out_list],
        [pltpu.VMEM((d, d), bf16)],
        2 * n * d * ff,
        4 * d * ff,
    )(me, count, *grads, unit, scale, gains, active)
    return results[0], results[1], results[2], results[3:]


def feed_backward(grad_sum, grad_branch, slope, unit, scale, weights):
    _, attn_out, ff_up, ff_down, _, gains, _ = weights
    n, d = grad_sum.shape
    steps = ff_up.shape[2] // d

    def kernel(
        dz, gb, der, wd, wu, wo, g_ref, unit_ref, scale_ref, du, ups, ga, gr, do, sums, acc
    ):
        step = pl.program_id(0)

        @pl.when(step == 0)
        def _():
            acc[...] = dz[...]

        grad = (nt(gb[...], wd[...]) * der[...].astype(f32)).astype(bf16)
        du[...] = grad
        ups[...] = jnp.sum(grad.astype(f32), axis=0, keepdims=True)
        acc[...] += nt(grad, wu[...])

        @pl.when(step == steps - 1)
        def _():
            g = acc[...]
            unit = unit_ref[...]
            back = normalise_back(g, unit, scale_ref[...], g_ref[0:1])
            gr[...] = back
            low = back.astype(bf16)
            ga[...] = low
            sums[...] = store_rows(
                [
                    jnp.sum(g * unit, axis=0, keepdims=True),
                    jnp.sum(g, axis=0, keepdims=True),
                    jnp.sum(low.astype(f32), axis=0, keepdims=True),
                ]
            )
            do[...] = nt(low, wo[...]).astype(bf16)

    columns = pl.BlockSpec((n, d), lambda i: (0, i))
    return call(
        kernel,
        (steps,),
        [
            whole((n, d)),
            whole((n, d)),
            columns,
            pl.BlockSpec((None, d, d), lambda i: (0, i, 0)),
            pl.BlockSpec((None, d, d), lambda i: (0, 0, i)),
            pl.BlockSpec((None, d, d), lambda i: (0, 0, 0)),
            pl.BlockSpec((None, 2, d), lambda i: (0, 0, 0)),
            whole((n, d)),
            whole((n, 1)),
        ],
        [
            columns,
            pl.BlockSpec((1, d), lambda i: (0, i)),
            whole((n, d)),
            whole((n, d)),
            whole((n, d)),
            whole((8, d)),
        ],
        [
            shape_of((n, steps * d), bf16),
            shape_of((1, steps * d), f32),
            shape_of((n, d), bf16),
            shape_of((n, d), f32),
            shape_of((n, d), bf16),
            shape_of((8, d), f32),
        ],
        [pltpu.VMEM((n, d), f32)],
        2 * n * d * d * (1 + 2 * steps),
        2 * d * d * (1 + 2 * steps),
    )(grad_sum, grad_branch, slope, ff_down, ff_up, attn_out, gains, unit, scale)


def weight_gradients(me, jobs, lefts, rights, devices):
    n, d = lefts[0].shape
    slots = Slots(devices, d)
    steps = len(jobs)

    def kernel(me_ref, *refs):
        left_refs = refs[: len(lefts)]
        right_refs = refs[len(lefts) : len(lefts) + len(rights)]
        *outs, turned, held = refs[len(lefts) + len(rights) :]
        step = pl.program_id(0)
        for index in range(len(lefts)):
            mine = [j for j, job in enumerate(jobs) if job[0] == index]

            @pl.when(step == mine[0])
            def _(index=index):
                turned[...] = left_refs[index][...].T

        for index in range(len(rights)):
            mine = [j for j, job in enumerate(jobs) if job[1] == index]

            @pl.when((step >= mine[0]) & (step <= mine[-1]))
            def _(index=index):
                value = nn(turned[...], right_refs[index][...]).astype(bf16)
                if slots.split:
                    held[...] = value
                else:
                    outs[0][...] = value

        if slots.split:

            def write(which, place, rows):
                outs[which][place, step] = rows

            slots.put(me_ref[0], held, devices, 0, write)

    def right_spec(index):
        mine = [(j, job[2]) for j, job in enumerate(jobs) if job[1] == index]
        first, block = mine[0]

        def place(i):
            return (0, jnp.clip(i - first, 0, len(mine) - 1) + block)

        return pl.BlockSpec((n, d), place)

    if slots.split:
        block = (devices // 2, steps, slots.rows, d)
        out_list = [(whole(block), shape_of(block, bf16))] * 2
    else:
        out_list = [(pl.BlockSpec((d, d), lambda i: (0, i)), shape_of((d, steps * d), bf16))]
    return call(
        kernel,
        (steps,),
        [scalar_spec()]
        + [whole((n, d))] * len(lefts)
        + [right_spec(index) for index in range(len(rights))],
        [spec for spec, _ in out_list],
        [shape for _, shape in out_list],
        [pltpu.VMEM((d, n), bf16), pltpu.VMEM((d, d), bf16)],
        2 * n * d * d * steps,
        4 * d * d * steps,
    )(me, *lefts, *rights)


def attend_backward(arrays, offsets, grad_blended, soft, places):
    n = grad_blended.shape[0]
    boxed = places is not None
    keys = soft.shape[2]

    def kernel(*refs):
        q_ref, k_ref, v_ref, g_ref, p_ref = refs[:5]
        if boxed:
            col_ref, row_ref = refs[5:7]
            dq_ref, dk_ref, dv_ref, sums, tab = refs[7:12]
            hot_i, hot_j, step_x, step_y, ds_s, far = refs[12:]

            @pl.when(pl.program_id(0) == 0)
            def _():
                cx, cy = col_ref[:, 0:1], col_ref[:, 1:2]
                rx, ry = row_ref[0:1], row_ref[1:2]
                hots = hot_columns(cx, cy, n, reverse=True)
                lane = lax.broadcasted_iota(jnp.int32, (n, 128), 1)
                hot_j[...] = jnp.where(lane < 32, hots, 0.0).astype(bf16)
                row = lax.broadcasted_iota(jnp.int32, (32, n), 0)
                cell = jnp.where(row < 16, rx >> 6, ry >> 6)
                hot_i[...] = jnp.where(cell == (row & 15), 1.0, 0.0).astype(bf16)
                step_x[...] = jnp.where((cx & 63) < (rx & 63), 1.0, 0.0).astype(bf16)
                step_y[...] = jnp.where((cy & 63) < (ry & 63), 1.0, 0.0).astype(bf16)
        else:
            dq_ref, dk_ref, dv_ref, sums, ds_s = refs[5:]
        masks = head_masks()
        q = q_ref[...]
        k = k_ref[...]
        v = v_ref[...]
        g = g_ref[...]
        grads = []
        for h in range(2):
            queries = []
            for r in range(0, n, STRIP):
                gh = g[r : r + STRIP] * masks[h]
                p = p_ref[h, r : r + STRIP, :n].astype(f32)
                dp = nt(gh, v)
                mean = jnp.sum(p * dp, axis=-1, keepdims=True)
                ds = (p * (dp - mean)).astype(bf16)
                ds_s[r : r + STRIP] = ds
                if boxed:
                    hj = hot_j[...]
                    wide = nn(ds, jnp.concatenate([k, hj], axis=1))
                    queries.append(wide[:, :128])
                    far[r : r + STRIP, 0:128] = wide[:, 128:]
                    far[r : r + STRIP, 128:256] = nn(ds * step_x[r : r + STRIP], hj)
                    far[r : r + STRIP, 256:384] = nn(ds * step_y[r : r + STRIP], hj)
                else:
                    queries.append(nn(ds, k))
            grads.append(
                (jnp.concatenate(queries, axis=0), tn(ds_s[...], q), tn(p_ref[h, :, :n], g))
            )
            if boxed:
                value = far[...]
                upper = value.astype(bf16)
                lower = (value - upper.astype(f32)).astype(bf16)
                cells = nn(hot_i[...], upper) + nn(hot_i[...], lower)
                lane = lax.broadcasted_iota(jnp.int32, (16, 128), 1)
                for direction in range(2):
                    rows = slice(16 * direction, 16 * direction + 16)
                    level = cells[rows, 0:128]
                    above = cells[rows, 128 * (direction + 1) : 128 * (direction + 2)]
                    inside = (lane >= 16 * direction) & (lane < 16 * direction + 16)
                    level = jnp.where(inside, level - above, 0.0)
                    above = jnp.where(inside, above, 0.0)
                    turn = (128 + 1 - 16 * direction) % 128
                    line = pltpu.roll(level, turn, 1, stride=1, stride_axis=0)
                    line = line + pltpu.roll(above, (turn + 127) % 128, 1, stride=1, stride_axis=0)
                    line = jnp.sum(line, axis=0, keepdims=True) * HD**0.5
                    tab[2 * h + direction : 2 * h + direction + 1] = line
        low = low_lanes(n)
        outs = []
        for index, ref in enumerate((dq_ref, dk_ref, dv_ref)):
            value = jnp.where(low, grads[0][index], grads[1][index]).astype(bf16)
            ref[...] = value
            outs.append(jnp.sum(value.astype(f32), axis=0, keepdims=True))
        sums[...] = store_rows([outs[0], outs[2]])

    def pair_block(offset):
        return pl.BlockSpec((n, 128), lambda i: (0, i + offset))

    in_specs = [pair_block(offset) for offset in offsets] + [
        pair_block(0),
        pl.BlockSpec((2, n, keys), lambda i: (i, 0, 0)),
    ]
    args = [*arrays, grad_blended, soft]
    outs = [(pair_block(0), shape_of((n, H * HD), bf16))] * 3
    outs.append((pl.BlockSpec((8, 128), lambda i: (0, i)), shape_of((8, H * HD), f32)))
    scratch = [pltpu.VMEM((n, n), bf16)]
    if boxed:
        in_specs += [whole((n, 2)), whole((2, n))]
        args += [*places]
        outs.append(
            (pl.BlockSpec((None, 4, 128), lambda i: (i, 0, 0)), shape_of((PAIRS, 4, 128), f32))
        )
        scratch = [
            pltpu.VMEM((32, n), bf16),
            pltpu.VMEM((n, 128), bf16),
            pltpu.VMEM((n, n), bf16),
            pltpu.VMEM((n, n), bf16),
            pltpu.VMEM((n, n), bf16),
            pltpu.VMEM((n, 384), f32),
        ]
    return call(
        kernel,
        (PAIRS,),
        in_specs,
        [spec for spec, _ in outs],
        [shape for _, shape in outs],
        scratch,
        16 * n * n * H * HD,
        2 * H * n * n,
    )(*args)


def project_back(grads, weight, first, residual, out_type):
    n, d = grads[0].shape
    steps = len(grads)

    def kernel(*refs):
        g_refs = refs[:steps]
        w_ref = refs[steps]
        out, acc = refs[-2:]
        step = pl.program_id(0)
        for index in range(steps):

            @pl.when(step == index)
            def _(index=index):
                value = nt(g_refs[index][...], w_ref[...])
                if index > 0:
                    value = value + acc[...]
                elif residual is not None:
                    value = value + refs[steps + 1][...]
                if index == steps - 1:
                    out[...] = value.astype(out_type)
                else:
                    acc[...] = value

    extra = [] if residual is None else [residual]
    return call(
        kernel,
        (steps,),
        [whole((n, d))] * steps
        + [pl.BlockSpec((None, d, d), lambda i: (0, 0, i + first))]
        + [whole((n, d))] * len(extra),
        whole((n, d)),
        shape_of((n, d), out_type),
        [pltpu.VMEM((n, d), f32)],
        2 * n * d * d * steps,
        2 * d * d * steps,
    )(*grads, weight, *extra)


def feed_forward_sending(blended, states, weights, next_in, next_vectors):
    _, attn_out, ff_up, ff_down, vectors, gains, up_bias = weights
    n, d = blended.shape
    tiles = ff_up.shape[2] // d
    strips = 4
    size = n // strips
    last = strips * tiles
    parts = Parts()
    strip = lambda i: jnp.minimum(i // tiles, strips - 1)
    tile = lambda i: jnp.where(i < last, i % tiles, tiles - 1)
    h_o = parts.inp(blended, fixed((n, d)))
    h_x = parts.inp(states, fixed((n, d)))
    h_wo = parts.inp(attn_out, fixed((None, d, d)))
    h_wu = parts.inp(ff_up, pl.BlockSpec((None, d, d), lambda i: (0, 0, tile(i))))
    h_wd = parts.inp(ff_down, pl.BlockSpec((None, d, d), lambda i: (0, tile(i), 0)))
    h_v, h_g = parts.inp(vectors, fixed((None, 6, d))), parts.inp(gains, fixed((None, 2, d)))
    h_e = parts.inp(up_bias, pl.BlockSpec((1, d), lambda i: (0, tile(i))))
    h_wq = parts.inp(next_in, pl.BlockSpec((None, d, d), lambda i: (0, 0, 0)))
    h_nv = parts.inp(next_vectors, fixed((None, 6, d)))
    h_unit1, h_scale1 = parts.out((n, d), f32), parts.out((n, 1), f32)
    h_rb = parts.out((n, d), bf16)
    block = pl.BlockSpec((size, d), lambda i: (strip(i), tile(i)))
    h_act = parts.out((n, tiles * d), bf16, block)
    h_der = parts.out((n, tiles * d), bf16, block)
    h_unit2, h_scale2 = parts.out((n, d), f32), parts.out((n, 1), f32)
    h_out, h_out_b = parts.out((n, d), f32), parts.out((n, d), bf16)
    h_partner, h_q = parts.out((n, d), bf16), parts.out((n, d), bf16)
    h_acc = parts.vmem((size, d), f32)
    h_got = parts.vmem((n, d), bf16)
    h_sent = parts.tmp(pltpu.SemaphoreType.DMA((strips,)))
    h_arrived = parts.tmp(pltpu.SemaphoreType.DMA((strips,)))

    def body(refs):
        i = pl.program_id(0)
        partner = {"narrow": 1 - lax.axis_index("narrow")}
        v_ref, g_ref, acc = refs[h_v], refs[h_g], refs[h_acc]

        def send(index):
            rows = pl.ds(size * index, size)
            return pltpu.make_async_remote_copy(
                src_ref=refs[h_out_b].at[rows],
                dst_ref=refs[h_got].at[rows],
                send_sem=refs[h_sent].at[index],
                recv_sem=refs[h_arrived].at[index],
                device_id=partner,
                device_id_type=MESH,
            )

        @pl.when(i == 0)
        def _():
            barrier = pltpu.get_barrier_semaphore()
            pl.semaphore_signal(barrier, inc=1, device_id=partner, device_id_type=MESH)
            pl.semaphore_wait(barrier, 1)

        for index in range(strips):
            rows = slice(size * index, size * index + size)

            @pl.when(i == index * tiles)
            def _(rows=rows):
                branch = nn(refs[h_o][rows], refs[h_wo][...]) + v_ref[2:3]
                unit, scale = normalise(refs[h_x][rows].astype(f32) + branch)
                refs[h_unit1][rows] = unit
                refs[h_scale1][rows] = scale
                r = unit * g_ref[0:1] + v_ref[3:4]
                refs[h_rb][rows] = r.astype(bf16)
                acc[...] = r + v_ref[4:5]

        @pl.when(i < last)
        def _():
            rows = pl.ds(pl.multiple_of(lax.div(i, tiles) * size, size), size)
            hidden = nn(refs[h_rb][rows], refs[h_wu][...]) + refs[h_e][...]
            active, slope = gelu_both(hidden)
            active = active.astype(bf16)
            refs[h_act][...] = active
            refs[h_der][...] = slope.astype(bf16)
            acc[...] += nn(active, refs[h_wd][...])

        for index in range(strips):
            rows = slice(size * index, size * index + size)

            @pl.when(i == index * tiles + tiles - 1)
            def _(rows=rows, index=index):
                unit, scale = normalise(acc[...])
                refs[h_unit2][rows] = unit
                refs[h_scale2][rows] = scale
                z = unit * g_ref[1:2] + v_ref[5:6]
                refs[h_out][rows] = z
                refs[h_out_b][rows] = z.astype(bf16)
                send(index).start()

        @pl.when(i == last)
        def _():
            q = nn(refs[h_out_b][...], refs[h_wq][...]) + refs[h_nv][0:1]
            refs[h_q][...] = q.astype(bf16)
            for index in range(strips):
                send(index).wait()
            refs[h_partner][...] = refs[h_got][...]

    results = parts.run(
        body, last + 1, 2 * n * d * d * (2 + 2 * tiles), 2 * d * d * (2 + 2 * tiles * strips), 4
    )
    order = (
        h_unit1, h_scale1, h_rb, h_act, h_der, h_unit2, h_scale2, h_out, h_out_b, h_partner, h_q
    )
    return [results[h] for h in order]


MESH = pl.DeviceIdType.MESH
DOWN, UP, IN = 0, 1, 2
SIZES = (4, 5, 3)

Z_FIRST = (
    (2, 0, 0),
    (2, 1, 0),
    (2, 1, 4),
    (2, 2, 0),
    (1, 0, 0),
    (1, 1, 1),
    (1, 1, 3),
)
HOPS = (
    (
        (2, 0, 2, 0, ((29, 37), (37, 53))),
        (2, 0, 0, 0, ((33, 41), (41, 57), (64, 70))),
        (2, 0, 1, 0, ((34, 45), (49, 69))),
        (2, 1, 0, 0, ((41, 49), (50, 69))),
        (2, 0, 3, 0, ((42, 53),)),
        (2, 1, 1, 0, ((49, 57),)),
        (2, 1, 2, 0, ((53, 61),)),
        (2, 1, 3, 0, ((61, 69),)),
    ),
    (
        (2, 1, 4, 0, ((0, 4), (5, 20), (27, 41), (41, 53))),
        (2, 1, 0, 2, ((0, 5), (18, 27))),
        (2, 0, 2, 2, ((0, 5), (27, 41))),
        (2, 0, 0, 3, ((3, 12),)),
        (2, 1, 2, 1, ((3, 18), (32, 43), (64, 70))),
        (2, 1, 3, 1, ((16, 33), (43, 61))),
        (2, 0, 1, 2, ((19, 33), (53, 69))),
        (2, 1, 1, 1, ((35, 61), (61, 69))),
        (2, 2, 0, 0, ((53, 69),)),
        (2, 0, 3, 1, ((53, 69),)),
        (2, 2, 1, 0, ((61, 69),)),
    ),
    (
        (2, 2, 0, 1, ((0, 21), (34, 42), (42, 53))),
        (2, 2, 2, 0, ((0, 5), (16, 37), (37, 45), (50, 61))),
        (2, 2, 1, 1, ((0, 21), (21, 34), (34, 42))),
        (2, 1, 3, 3, ((16, 33),)),
        (1, 0, 0, 0, ((29, 34), (56, 70))),
        (2, 1, 1, 3, ((32, 41),)),
        (1, 0, 2, 0, ((33, 41), (41, 57))),
        (1, 0, 1, 0, ((34, 42), (50, 69))),
        (1, 1, 0, 0, ((40, 45),)),
        (1, 0, 3, 0, ((42, 50),)),
        (2, 0, 3, 2, ((45, 57),)),
        (1, 1, 1, 0, ((48, 53),)),
        (1, 1, 2, 0, ((53, 61),)),
        (1, 1, 3, 0, ((61, 69),)),
    ),
    (
        (1, 1, 3, 1, ((0, 4), (4, 10), (10, 13))),
        (1, 0, 0, 2, ((0, 3), (8, 11))),
        (1, 1, 4, 0, ((0, 2), (9, 13), (18, 21), (32, 47))),
        (1, 1, 0, 1, ((1, 9), (20, 45), (51, 54))),
        (2, 0, 3, 3, ((3, 9),)),
        (1, 0, 2, 2, ((3, 10), (11, 17))),
        (1, 2, 0, 0, ((5, 10), (52, 56), (56, 58), (59, 60))),
        (1, 0, 1, 2, ((9, 12), (20, 37))),
        (1, 1, 1, 1, ((12, 20), (21, 46), (47, 49))),
        (1, 1, 2, 1, ((12, 20), (48, 50), (55, 57))),
        (1, 2, 1, 0, ((13, 18), (18, 37), (40, 48), (49, 51))),
        (1, 2, 2, 0, ((21, 37), (40, 49), (50, 52), (53, 55))),
        (1, 0, 3, 1, ((49, 53), (54, 56), (57, 59))),
    ),
)


class Handle:
    pass


class Parts:
    def __init__(self):
        self.inputs, self.outputs, self.scratch = [], [], []

    def inp(self, array, spec):
        self.inputs.append((Handle(), array, spec))
        return self.inputs[-1][0]

    def out(self, shape, dtype, spec=None):
        self.outputs.append((Handle(), shape_of(shape, dtype), spec or fixed(shape)))
        return self.outputs[-1][0]

    def tmp(self, kind):
        self.scratch.append((Handle(), kind))
        return self.scratch[-1][0]

    def vmem(self, shape, dtype):
        return self.tmp(pltpu.VMEM(shape, dtype))

    def run(self, body, steps, flops, moved, collective):
        handles = [x[0] for x in self.inputs + self.outputs + self.scratch]

        def kernel(*refs):
            body(dict(zip(handles, refs)))

        results = pl.pallas_call(
            kernel,
            grid=(steps,),
            in_specs=[x[2] for x in self.inputs],
            out_specs=[x[2] for x in self.outputs],
            out_shape=[x[1] for x in self.outputs],
            scratch_shapes=[x[1] for x in self.scratch],
            compiler_params=pltpu.CompilerParams(
                dimension_semantics=("arbitrary",),
                vmem_limit_bytes=63 * MIB,
                fuse_transposed_lhs_in_matmul=True,
                collective_id=collective,
                has_side_effects=collective is not None,
            ),
            cost_estimate=pl.CostEstimate(
                flops=int(flops), bytes_accessed=int(moved), transcendentals=0
            ),
        )(*[x[1] for x in self.inputs])
        return dict(zip([x[0] for x in self.outputs], results))


def fixed(shape):
    return pl.BlockSpec(shape, lambda i: (0,) * len(shape), pipeline_mode=pl.Buffered(1))


def bit_of(me, bit):
    return lax.rem(lax.div(me, bit), 2)


def order_of(key):
    return (1, 4, 2, 8) if key in Z_FIRST else (1, 2, 4, 8)


def put_rows(me, held, layer, chunk, block, shards, base, keep, send, height, rows):
    core = bit_of(me, 1)
    places = {}
    count = height // rows
    for k in range(shards // 2):
        differ = {}
        for bit in (2, 4, 8):
            mine = bit_of(me, bit)
            if bit < shards:
                differ[bit] = 1 - mine if (2 * k // bit) % 2 else mine
            else:
                theirs = bit_of(base, bit)
                differ[bit] = mine + theirs - 2 * mine * theirs
        for which, ref in ((core, keep), (1 - core, send)):
            start = (2 * k + which) * height
            for b in range(count):
                bits = order_of((layer, chunk, block + b))[1:]
                place = 4 * differ[bits[0]] + 2 * differ[bits[1]] + differ[bits[2]]
                ref[place, block + b] = held[pl.ds(pl.multiple_of(start + b * rows, 16), rows)]


class Hop:
    def __init__(self, key, hop, keep, send, got, done, sem):
        self.bit, self.hop = order_of(key)[hop], hop
        self.keep, self.send, self.got, self.done, self.sem = keep, send, got, done, sem


class Traffic:
    def __init__(self, parts, number, layer, fresh, state, rows, d, small=None, cross=None):
        legs = HOPS[number]
        self.parts, self.state, self.layer = parts, state, layer
        self.events, self.loads, self.copies = [], [], []
        self.small, self.cross = small, cross
        self.keep, self.send = {}, {}
        self.kept_out, self.done_out = [], []
        bits = set()
        groups = {}
        for leg in legs:
            groups.setdefault(leg[:2], []).append(leg)
        for chunk in fresh:
            groups.setdefault((layer, chunk), [])
        arrays = {}
        count = 0

        def operand(array):
            if id(array) not in arrays:
                arrays[id(array)] = parts.inp(array, pl.BlockSpec(memory_space=pl.ANY))
            return arrays[id(array)]

        for name, members in groups.items():
            made_here = name[0] == layer and name[1] in fresh
            if made_here:
                blocks = list(range(SIZES[name[1]]))
                slots = 8
            else:
                blocks = [leg[2] for leg in members]
                slots = max(8 if leg[3] == 0 else 16 >> leg[3] for leg in members)
            ends = {leg[2]: leg[3] + len(leg[4]) for leg in members}
            finished = [b for b in blocks if ends.get(b, 0) == 4]
            shape = (slots, len(blocks), rows, d)
            if len(finished) == len(blocks):
                keep = parts.vmem(shape, bf16)
            else:
                keep = parts.out(shape, bf16)
            send = None
            if made_here:
                if all(ends.get(b, 0) > 0 for b in blocks):
                    send = parts.vmem(shape, bf16)
                else:
                    send = parts.out(shape, bf16)
                self.keep[name[1]], self.send[name[1]] = keep, send
            if finished:
                done = parts.out((len(finished), rows, d), f32)
                for place, b in enumerate(finished):
                    self.done_out.append((name + (b,), done, place))
            for place, b in enumerate(blocks):
                if b not in finished:
                    sent = send if made_here and ends.get(b, 0) == 0 else None
                    self.kept_out.append((name + (b,), keep, sent, place))
            for hop in range(4):
                users = [leg for leg in members if leg[3] <= hop < leg[3] + len(leg[4])]
                if not users:
                    continue
                got = parts.vmem((8 >> hop, len(users), rows, d), bf16)
                for index, leg in enumerate(users):
                    key, place = leg[:3], blocks.index(leg[2])
                    source = None
                    if hop == 0:
                        if made_here:
                            source = (send, place)
                        else:
                            source = (operand(state[key][1]), state[key][2])
                    final = None
                    if hop == 3:
                        final = (done, finished.index(leg[2]))
                    item = Hop(key, hop, (keep, place), source, (got, index), final, count)
                    count += 1
                    bits.add(item.bit)
                    start, end = leg[4][hop - leg[3]]
                    self.events.append((end, 0, len(self.events), self.finish, item))
                    self.events.append((start, 1, len(self.events), self.begin, item))
            if not made_here:
                for leg in members:
                    kept, _, place = state[leg[:3]]
                    have = 8 if leg[3] == 0 else 16 >> leg[3]
                    self.loads.append((operand(kept), place, have, keep, blocks.index(leg[2])))
        if small is not None:
            self.total = parts.vmem(small[0], f32)
            self.small_got = parts.vmem((4,) + small[0], f32)
            self.small_out = parts.out(small[0], f32)
            bits |= {1, 2, 4, 8}
            for hop, (start, end) in enumerate(small[1]):
                item = (hop, count + hop)
                self.events.append((end, 0, len(self.events), self.small_finish, item))
                self.events.append((start, 1, len(self.events), self.small_begin, item))
            count += 4
        if cross is not None:
            self.cross_out = parts.vmem(cross[0], bf16)
            self.cross_got = parts.vmem(cross[0], bf16)
            self.cross_in = parts.out(cross[0], bf16)
            for first, size, start, end in cross[1]:
                item = (first, size, count)
                self.events.append((end, 0, len(self.events), self.cross_finish, item))
                self.events.append((start, 1, len(self.events), self.cross_begin, item))
                count += 1
        self.sent = parts.tmp(pltpu.SemaphoreType.DMA((count,)))
        self.arrived = parts.tmp(pltpu.SemaphoreType.DMA((count,)))
        self.loaded = None
        if self.loads:
            self.loaded = parts.tmp(pltpu.SemaphoreType.DMA((len(self.loads),)))
        self.bits = sorted(bits)
        self.events.sort(key=lambda e: e[:3])

    def bind(self, refs, step):
        self.refs, self.step = refs, step
        self.me, self.side = lax.axis_index("wide"), lax.axis_index("narrow")

    def device(self, bit):
        return {"wide": self.me + bit - 2 * bit * bit_of(self.me, bit)}

    def open(self):
        loads = []
        for index, (source, place, slots, keep, at) in enumerate(self.loads):
            copy = pltpu.make_async_copy(
                self.refs[source].at[pl.ds(0, slots), place],
                self.refs[keep].at[pl.ds(0, slots), at],
                self.refs[self.loaded].at[index],
            )
            copy.start()
            loads.append(copy)
        barrier = pltpu.get_barrier_semaphore()
        peers = [self.device(bit) for bit in self.bits]
        if self.cross is not None:
            peers.append({"narrow": 1 - self.side})
        for peer in peers:
            pl.semaphore_signal(barrier, inc=1, device_id=peer, device_id_type=MESH)
        pl.semaphore_wait(barrier, len(peers))
        for copy in loads:
            copy.wait()

    def remote(self, source, target, index, device):
        return pltpu.make_async_remote_copy(
            src_ref=source,
            dst_ref=target,
            send_sem=self.refs[self.sent].at[index],
            recv_sem=self.refs[self.arrived].at[index],
            device_id=device,
            device_id_type=MESH,
        )

    def copy(self, item):
        slots = 8 >> item.hop
        if item.hop == 0:
            source = self.refs[item.send[0]].at[pl.ds(0, 8), item.send[1]]
        else:
            source = self.refs[item.keep[0]].at[pl.ds(slots, slots), item.keep[1]]
        target = self.refs[item.got[0]].at[pl.ds(0, slots), item.got[1]]
        return self.remote(source, target, item.sem, self.device(item.bit))

    def begin(self, item):
        self.copy(item).start()

    def finish(self, item):
        self.copy(item).wait()
        keep, at = self.refs[item.keep[0]], item.keep[1]
        got, place = self.refs[item.got[0]], item.got[1]
        if item.hop == 3:
            done, final = self.refs[item.done[0]], item.done[1]
            done[final] = keep[0, at].astype(f32) + got[0, place].astype(f32)
        else:

            @pl.loop(0, 8 >> item.hop)
            def _(slot):
                total = keep[slot, at].astype(f32) + got[slot, place].astype(f32)
                keep[slot, at] = total.astype(bf16)

    def small_copy(self, item):
        target = self.refs[self.small_got].at[item[0]]
        return self.remote(self.refs[self.total], target, item[1], self.device(1 << item[0]))

    def small_begin(self, item):
        self.small_copy(item).start()

    def small_finish(self, item):
        self.small_copy(item).wait()
        total = self.refs[self.total][...] + self.refs[self.small_got][item[0]]
        self.refs[self.total][...] = total
        if item[0] == 3:
            self.refs[self.small_out][...] = total

    def cross_copy(self, item):
        rows = pl.ds(item[0], item[1])
        device = {"narrow": 1 - self.side}
        source = self.refs[self.cross_out].at[rows]
        return self.remote(source, self.refs[self.cross_got].at[rows], item[2], device)

    def cross_begin(self, item):
        self.cross_copy(item).start()

    def cross_finish(self, item):
        self.cross_copy(item).wait()
        rows = pl.ds(item[0], item[1])
        self.refs[self.cross_in][rows] = self.refs[self.cross_got][rows]

    def fire(self, low, high=None):
        high = low + 1 if high is None else high

        def spot(time):
            return min(time // 8, self.steps - 1)

        found = [e for e in self.events if low <= e[0] - 8 * spot(e[0]) < high]
        for at in sorted({spot(e[0]) for e in found}):

            @pl.when(self.step == at)
            def _(at=at):
                for event in found:
                    if spot(event[0]) == at:
                        event[3](event[4])

    def close(self, results, finals):
        for key, keep, sent, place in self.kept_out:
            self.state[key] = (results[keep], None if sent is None else results[sent], place)
        for key, done, place in self.done_out:
            self.state.pop(key, None)
            finals[key] = (results[done], place)


def ff_back(number, layer, grads, lengths, saved, weights, state, finals):
    _, attn_out, ff_up, ff_down, _, gains, _ = weights
    unit1, scale1, rb, act, slope, unit2, scale2, blended = saved
    n, d = unit1.shape
    rows = d // 16
    tiles = act.shape[1] // d
    steps = 2 * tiles + 1
    top = len(grads) == 1
    parts = Parts()
    first = lambda i: jnp.minimum(i, tiles - 1)
    later = lambda i: jnp.clip(i - tiles, 0, tiles - 1)
    h_count = parts.inp(lengths, scalar_spec())
    h_grads = [parts.inp(grad, fixed((n, d))) for grad in grads]
    h_act = parts.inp(act, pl.BlockSpec((n, d), lambda i: (0, first(i))))
    h_slope = parts.inp(slope, pl.BlockSpec((n, d), lambda i: (0, later(i))))
    h_wd = parts.inp(ff_down, pl.BlockSpec((None, d, d), lambda i: (0, later(i), 0)))
    h_wu = parts.inp(ff_up, pl.BlockSpec((None, d, d), lambda i: (0, 0, later(i))))
    h_wo = parts.inp(attn_out, fixed((None, d, d)))
    h_gains = parts.inp(gains, fixed((None, 2, d)))
    h_unit1, h_scale1 = parts.inp(unit1, fixed((n, d))), parts.inp(scale1, fixed((n, 1)))
    h_unit2, h_scale2 = parts.inp(unit2, fixed((n, d))), parts.inp(scale2, fixed((n, 1)))
    h_rb = parts.inp(rb, fixed((n, d)))
    h_blended = parts.inp(blended, fixed((n, d)))
    h_gr, h_do = parts.out((n, d), f32), parts.out((n, d), bf16)
    h_sums = parts.out((16, d), f32)
    h_acc, h_gb = parts.vmem((n, d), f32), parts.vmem((n, d), bf16)
    h_turned, h_held = parts.vmem((d, n), bf16), parts.vmem((d, d), bf16)
    traffic = Traffic(parts, number, layer, (DOWN, UP), state, rows, d)
    traffic.steps = steps

    def body(refs):
        step = pl.program_id(0)
        traffic.bind(refs, step)
        me = traffic.me
        sums, acc, gb = refs[h_sums], refs[h_acc], refs[h_gb]
        turned, held = refs[h_turned], refs[h_held]

        @pl.when(step == 0)
        def _():
            traffic.open()

        traffic.fire(0)

        @pl.when(step == 0)
        def _():

            def strip(rows, carry):
                g = refs[h_grads[0]][rows].astype(f32)
                if top:
                    row = lax.broadcasted_iota(jnp.int32, (16, 1), 0) + rows.start
                    g = jnp.where(row < count_of(refs[h_count]), g, 0.0)
                else:
                    g = g + refs[h_grads[1]][rows].astype(f32)
                unit = refs[h_unit2][rows]
                back = normalise_back(g, unit, refs[h_scale2][rows], refs[h_gains][1:2])
                acc[rows] = back
                low = back.astype(bf16)
                gb[rows] = low
                found = (low.astype(f32), g, g * unit)
                return tuple(a + fold(b) for a, b in zip(carry, found))

            zero = jnp.zeros((8, d), f32)
            found = each_strip(n, 16, strip, (zero, zero, zero))
            sums[0:8] = zero
            sums[8:16] = zero
            for at, value in zip((4, 5, 7), found):
                sums[at : at + 1] = jnp.sum(value, axis=0, keepdims=True)

        @pl.when(step < tiles)
        def _():
            held[...] = tn(refs[h_act][...], gb[...]).astype(bf16)
            keep, send = refs[traffic.keep[DOWN]], refs[traffic.send[DOWN]]
            shards = 16 // tiles
            put_rows(
                me, held, layer, DOWN, 0, shards, step * shards, keep, send, rows * tiles, rows
            )

        @pl.when(step == tiles)
        def _():
            turned[...] = refs[h_rb][...].T

        middle = (step >= tiles) & (step < 2 * tiles)

        @pl.when(middle)
        def _():
            grad = nt(gb[...], refs[h_wd][...]) * refs[h_slope][...].astype(f32)
            grad = grad.astype(bf16)
            sums[pl.ds(8 + step - tiles, 1)] = jnp.sum(grad.astype(f32), axis=0, keepdims=True)
            held[0:n] = grad

        traffic.fire(1)

        @pl.when(middle)
        def _():
            acc[...] += nt(held[0:n], refs[h_wu][...])

        traffic.fire(2)

        @pl.when(middle)
        def _():
            held[...] = nn(turned[...], held[0:n]).astype(bf16)

        @pl.when(step == 2 * tiles)
        def _():
            turned[...] = refs[h_blended][...].T

            def strip(rows, carry):
                g = acc[rows]
                unit = refs[h_unit1][rows]
                back = normalise_back(g, unit, refs[h_scale1][rows], refs[h_gains][0:1])
                refs[h_gr][rows] = back
                low = back.astype(bf16)
                gb[rows] = low
                found = (low.astype(f32), g, g * unit)
                return tuple(a + fold(b) for a, b in zip(carry, found))

            zero = jnp.zeros((8, d), f32)
            found = each_strip(n, 16, strip, (zero, zero, zero))
            for at, value in zip((2, 3, 6), found):
                sums[at : at + 1] = jnp.sum(value, axis=0, keepdims=True)
            low = gb[...]
            refs[h_do][...] = nt(low, refs[h_wo][...]).astype(bf16)
            held[...] = nn(turned[...], low).astype(bf16)

        for block in range(tiles + 1):

            @pl.when(step == tiles + block)
            def _(block=block):
                keep, send = refs[traffic.keep[UP]], refs[traffic.send[UP]]
                put_rows(me, held, layer, UP, block, 16, 0, keep, send, rows, rows)

        traffic.fire(5, 1000)

    results = parts.run(body, steps, 2 * n * d * d * (4 * tiles), 4 * d * d * tiles, number)
    traffic.close(results, finals)
    return results[h_gr], results[h_do], results[h_sums]


def attn_back(
    number, layer, arrays, offsets, blended, grad_blended, soft, boxes, weight, left_rows,
    residual, small, state, finals,
):
    n, d = grad_blended.shape
    per_shard = d // 16
    groups = 3
    wide = d // groups
    heads = H // groups
    boxed = boxes is not None
    halves = 1 if boxed else 2
    front = halves * groups
    steps = front + groups
    keys = soft.shape[2]
    spans = [(0, keys)] if boxed else [(0, 384), (384, keys)]
    parts = Parts()
    early = lambda i: jnp.where(i < front, lax.rem(i, groups), groups - 1)
    later = lambda i: jnp.clip(i - front, 0, groups - 1)

    def wide_block(offset):
        return pl.BlockSpec((n, wide), lambda i: (0, early(i) + offset // 2))

    h_q, h_k, h_v = (parts.inp(a, wide_block(o)) for a, o in zip(arrays, offsets))
    h_g = parts.inp(grad_blended, wide_block(0))
    h_o = parts.inp(blended, wide_block(0))
    h_p = parts.inp(soft, pl.BlockSpec((heads, n, keys), lambda i: (early(i), 0, 0)))
    h_kv = [parts.vmem((keys, wide), bf16) for _ in range(2)]
    h_dp = parts.vmem((n, keys), f32)
    h_w = []
    for index in range(3):
        when = early if (not boxed and index > 0) else later
        spec = pl.BlockSpec((None, d, wide), lambda i, w=when, k=index: (0, 0, w(i) + groups * k))
        h_w.append(parts.inp(weight, spec))
    h_left = [parts.inp(rows, fixed((n, d))) for rows in left_rows]
    h_turned = [parts.vmem((d, n), bf16) for rows in left_rows]
    h_gr = parts.inp(residual, fixed((n, d)))
    h_own = parts.out((n, d), f32)
    h_sums1 = parts.vmem((8, d), f32) if boxed else parts.out((8, d), f32)
    h_d = [parts.vmem((groups, n, wide), bf16) for _ in range(3)]
    h_ds, h_held = parts.vmem((n, keys), bf16), parts.vmem((d, d), bf16)
    if boxed:
        h_lengths = parts.inp(boxes[0], scalar_spec())
        h_boxes = parts.inp(boxes[1], fixed((None, 4, TEXT)))
        h_patches = parts.inp(patch_centres(n, keys), fixed((4, keys)))
        h_near = [parts.vmem((n, keys), bf16) for _ in range(2)]
        h_small1, h_small2 = (parts.inp(x, fixed((16, d))) for x in small[:2])
        h_sums2 = parts.inp(small[2], fixed((8, d)))
        h_hot_i, h_hot_j = parts.vmem((32, n), bf16), parts.vmem((keys, 128), bf16)
        h_step_x, h_step_y = parts.vmem((n, keys), bf16), parts.vmem((n, keys), bf16)
        h_far, h_tab = parts.vmem((n, 384), f32), parts.vmem((2 * H, 128), f32)
        times = ((21, 29), (29, 37), (37, 45), (45, 47))
        traffic = Traffic(
            parts, number, layer, (IN,), state, per_shard, d, small=((32, d), times)
        )
    else:
        h_acc = parts.vmem((n, d), f32)
        h_half = parts.vmem((groups, n, wide), f32)
        cross = [(0, 384, 21, 69), (384, n - 384, 45, 69)]
        traffic = Traffic(parts, number, layer, (IN,), state, per_shard, d, cross=((n, d), cross))
    traffic.steps = steps

    def body(refs):
        step = pl.program_id(0)
        traffic.bind(refs, step)
        me = traffic.me
        turned = [refs[h] for h in h_turned]
        dq, dk, dv = (refs[h] for h in h_d)
        wq, wk, wv = (refs[h] for h in h_w)
        own, held, ds_s = refs[h_own], refs[h_held], refs[h_ds]

        @pl.when(step == 0)
        def _():
            traffic.open()

        traffic.fire(0)

        @pl.when(step == 0)
        def _():
            for target, source in zip(turned, h_left):
                target[...] = refs[source][...].T
            for h in h_kv:
                refs[h][n:keys] = jnp.zeros((keys - n, wide), bf16)
            if boxed:
                row, col = centres_of(refs[h_lengths], refs[h_boxes][...], refs[h_patches][...])
                cx, cy = col[0:n, 0:1], col[0:n, 1:2]
                rx, ry = row[0:1, 0:n], row[1:2, 0:n]
                hots = hot_columns(cx, cy, n, reverse=True)
                lane = lax.broadcasted_iota(jnp.int32, (n, 128), 1)
                refs[h_hot_j][0:n] = jnp.where(lane < 32, hots, 0.0).astype(bf16)
                refs[h_hot_j][n:keys] = jnp.zeros((keys - n, 128), bf16)
                line = lax.broadcasted_iota(jnp.int32, (32, n), 0)
                cell = jnp.where(line < 16, rx >> 6, ry >> 6)
                refs[h_hot_i][...] = jnp.where(cell == (line & 15), 1.0, 0.0).astype(bf16)
                for h, c, r in ((h_step_x, cx, rx), (h_step_y, cy, ry)):
                    refs[h][:, 0:n] = jnp.where((c & 63) < (r & 63), 1.0, 0.0).astype(bf16)
                    refs[h][:, n:keys] = jnp.zeros((n, keys - n), bf16)

        def table_lines(head):
            far = refs[h_far]
            value = far[...]
            upper = value.astype(bf16)
            lower = (value - upper.astype(f32)).astype(bf16)
            hi = refs[h_hot_i][...]
            cells = nn(hi, upper) + nn(hi, lower)
            lane = lax.broadcasted_iota(jnp.int32, (16, 128), 1)
            for direction in range(2):
                rows = slice(16 * direction, 16 * direction + 16)
                level = cells[rows, 0:128]
                above = cells[rows, 128 * (direction + 1) : 128 * (direction + 2)]
                inside = (lane >= 16 * direction) & (lane < 16 * direction + 16)
                level = jnp.where(inside, level - above, 0.0)
                above = jnp.where(inside, above, 0.0)
                turn = (128 + 1 - 16 * direction) % 128
                line = pltpu.roll(level, turn, 1, stride=1, stride_axis=0)
                turn = (turn + 127) % 128
                line = line + pltpu.roll(above, turn, 1, stride=1, stride_axis=0)
                line = jnp.sum(line, axis=0, keepdims=True) * HD**0.5
                refs[h_tab][pl.ds(2 * heads * step + 2 * head + direction, 1)] = line

        def head_back(head, half):
            pair, h = head // 2, head % 2
            lanes = slice(128 * pair, 128 * pair + 128)
            low_key, high_key = spans[half]
            span, ends = slice(low_key, high_key), slice(low_key, min(high_key, n))
            group = step - half * groups
            mask = head_masks()[h]
            q, k, v, g = (refs[x][:, lanes] for x in (h_q, h_kv[0], h_kv[1], h_g))
            k, v = k[span], v[span]
            dp_s = refs[h_dp]
            dp_s[:, span] = nt(g * mask, v)
            tiles = [slice(t, t + 128) for t in range(low_key, high_key, 128)]
            for r in range(0, n, SUB):
                rows = slice(r, r + SUB)
                mean = (g[rows] * mask).astype(f32) * refs[h_o][rows, lanes]
                mean = jnp.sum(mean, axis=-1, keepdims=True)
                for t in tiles:
                    ds = refs[h_p][head, rows, t].astype(f32) * (dp_s[rows, t] - mean)
                    ds = ds.astype(bf16)
                    ds_s[rows, t] = ds
                    if boxed:
                        refs[h_near[0]][rows, t] = ds * refs[h_step_x][rows, t]
                        refs[h_near[1]][rows, t] = ds * refs[h_step_y][rows, t]
            if boxed:
                hj, far = refs[h_hot_j][...], refs[h_far]
                queries = nn(ds_s[...], jnp.concatenate([k, hj], axis=1))
                far[:, 0:128] = queries[:, 128:]
                queries = queries[:, :128]
                far[:, 128:256] = nn(refs[h_near[0]][...], hj)
                far[:, 256:384] = nn(refs[h_near[1]][...], hj)
            else:
                queries = nn(ds_s[:, span], k)
            count = ends.stop - ends.start
            values = (tn(ds_s[:, span], q)[:count], tn(refs[h_p][head, :, span], g)[:count])
            if boxed:
                table_lines(head)
            outs = []
            low = low_lanes(count)
            for ref, value in zip((dk, dv), values):
                value = value.astype(bf16)
                if h == 0:
                    ref[group, ends, lanes] = value
                else:
                    value = jnp.where(low, ref[group, ends, lanes].astype(f32), value.astype(f32))
                    ref[group, ends, lanes] = value.astype(bf16)
                    outs.append(jnp.sum(value, axis=0, keepdims=True))
            low = low_lanes(n)
            if halves == 2:
                half_s = refs[h_half]
                if half == 0 and h == 0:
                    half_s[group, :, lanes] = queries
                elif half == 0:
                    half_s[group, :, lanes] = jnp.where(low, half_s[group, :, lanes], queries)
                else:
                    queries = half_s[group, :, lanes] + queries
            if half == halves - 1:
                queries = queries.astype(bf16)
                if h == 1:
                    queries = jnp.where(
                        low, dq[group, :, lanes].astype(f32), queries.astype(f32)
                    )
                    outs.append(jnp.sum(queries, axis=0, keepdims=True))
                dq[group, :, lanes] = queries.astype(bf16)
            if h == 1:
                start = pl.multiple_of(group * wide + 128 * pair, 128)
                at = pl.ds(start, 128)
                sums = refs[h_sums1]
                if half == 0:
                    sums[1:2, at] = outs[1]
                else:
                    sums[1:2, at] += outs[1]
                if half == halves - 1:
                    sums[0:1, at] = outs[2]

        if not boxed:

            @pl.when(step == 0)
            def _():
                refs[h_sums1][...] = jnp.zeros((8, d), f32)

        @pl.when(step < front)
        def _():
            refs[h_kv[0]][0:n] = refs[h_k][...]
            refs[h_kv[1]][0:n] = refs[h_v][...]

        for head in range(heads):
            for half in range(halves):

                @pl.when((step >= half * groups) & (step < half * groups + groups))
                def _(head=head, half=half):
                    head_back(head, half)

            traffic.fire(1 + head)

        def gradient(group):
            for index, ref in enumerate((dq, dk, dv)):
                left = turned[min(index, len(turned) - 1)]
                held[:, index * wide : (index + 1) * wide] = nn(left[...], ref[group]).astype(bf16)

        def store_gradient(start):
            for block in range(groups):

                @pl.when(step == start + block)
                def _(block=block):
                    keep, send = refs[traffic.keep[IN]], refs[traffic.send[IN]]
                    put_rows(
                        me, held, layer, IN, block, 16, 0, keep, send, per_shard, per_shard
                    )

        if boxed:

            @pl.when(step < groups)
            def _():
                gradient(step)

            store_gradient(0)

            @pl.when(step == groups - 1)
            def _():
                total = refs[traffic.total]
                total[0:16] = refs[h_small1][...]
                total[0:2] = refs[h_sums1][0:2]
                total[16:32] = refs[h_small2][...]
                total[16:18] = refs[h_sums2][0:2]
                each = d // 128
                for index in range(2 * H):
                    at = 128 * (index % each)
                    row = 12 + index // each
                    total[row : row + 1, at : at + 128] = refs[h_tab][index : index + 1]

        else:

            acc = refs[h_acc]
            for half, (low_key, high_key) in enumerate(spans):
                rows = slice(low_key, min(high_key, n))
                for group in range(groups):

                    @pl.when(step == half * groups + group)
                    def _(rows=rows, group=group):
                        value = nt(dk[group, rows], wk[...]) + nt(dv[group, rows], wv[...])
                        if group > 0:
                            value = value + acc[rows]
                        if group < groups - 1:
                            acc[rows] = value
                        else:
                            refs[traffic.cross_out][rows] = value.astype(bf16)

        @pl.when(step >= front)
        def _():
            group = step - front
            value = nt(dq[group], wq[...])
            if boxed:
                value = value + nt(dk[group], wk[...]) + nt(dv[group], wv[...])
            else:
                gradient(group)

            @pl.when(step == front)
            def _():
                own[...] = refs[h_gr][...] + value

            @pl.when(step > front)
            def _():
                own[...] += value

        if not boxed:
            store_gradient(front)
        traffic.fire(5, 1000)

    results = parts.run(
        body, steps, 16 * n * n * d + 12 * n * d * d, 2 * H * n * n, number
    )
    traffic.close(results, finals)
    extra = results[traffic.small_out] if boxed else results[traffic.cross_in]
    return results[h_own], None if boxed else results[h_sums1], extra


def finish_outputs(me, finals, small, rows, d):
    tiles = SIZES[DOWN]
    share = d // 16
    parts = Parts()
    h_me = parts.inp(me, scalar_spec())
    h_small = parts.inp(small, fixed(small.shape))
    arrays = {}
    for array, _ in finals.values():
        if id(array) not in arrays:
            arrays[id(array)] = parts.inp(array, fixed(array.shape))
    layers = []
    for _ in range(2):
        layers.append(
            (
                parts.out((rows, 3 * d), f32),
                parts.out((rows, d), f32),
                parts.out((rows, tiles * d), f32),
                parts.out((rows * tiles, d), f32),
                parts.out((6, share), f32),
                parts.out((2, share), f32),
                parts.out((1, tiles * share), f32),
            )
        )
    h_table = parts.out((1, share), f32)

    def body(refs):
        me = refs[h_me][0]
        back = lax.rem(d - share * me, d)
        for layer, outs in zip((1, 2), layers):

            def block(chunk, index):
                array, place = finals[(layer, chunk, index)]
                return refs[arrays[id(array)]][place]

            wide = d // 3
            for group in range(3):
                value = block(IN, group)
                for part in range(3):
                    at = part * d + group * wide
                    refs[outs[0]][:, at : at + wide] = value[:, part * wide : (part + 1) * wide]
            refs[outs[1]][...] = block(UP, tiles)
            for index in range(tiles):
                refs[outs[2]][:, index * d : (index + 1) * d] = block(UP, index)
                refs[outs[3]][index * rows : (index + 1) * rows] = block(DOWN, index)
            base = 16 * (layer - 1)
            turned = pltpu.roll(refs[h_small][base : base + 8], back, 1)
            refs[outs[4]][...] = turned[0:6, :share]
            refs[outs[5]][...] = turned[6:8, :share]
            each = tiles * share
            line = jnp.zeros((1, d), f32)
            for index in range(tiles):
                row = refs[h_small][base + 8 + index : base + 9 + index]
                line = jnp.where(lax.div(me, 16 // tiles) == index, row, line)
            inner = lax.rem(me, 16 // tiles)
            turned = pltpu.roll(jnp.broadcast_to(line, (8, d)), lax.rem(d - each * inner, d), 1)
            refs[outs[6]][...] = turned[0:1, :each]
        direction = lax.div(me, 8)
        first = 4 * lax.rem(me, 8)
        line = jnp.zeros((1, 128), f32)
        lane = lax.broadcasted_iota(jnp.int32, (1, 128), 1)
        for head in range(H):
            found = []
            for way in range(2):
                index = 2 * head + way
                at = 128 * (index % (d // 128))
                row = 12 + index // (d // 128)
                found.append(refs[h_small][row : row + 1, at : at + 128])
            values = jnp.where(direction == 0, found[0], found[1])
            for bucket in range(4):
                value = jnp.sum(jnp.where(lane == first + bucket, values, 0.0))
                line = jnp.where(lane == H * bucket + head, value, line)
        refs[h_table][...] = line[:, :share]

    results = parts.run(body, 1, 1, 8 * rows * d, None)
    done = [tuple(results[h][None] for h in outs[:6]) + (results[outs[6]],) for outs in layers]
    return done[0], done[1], results[h_table]


def backward_with_hops(me, first, second, saved_one, saved_two, one, two, extra):
    top, lengths, boxes, own_b, mid_b, partner_b, soft_one, soft_two, full_one, full_two = extra
    d = own_b.shape[1]
    state, finals = {}, {}
    gr, do, small_two = ff_back(0, 2, [top], lengths, saved_two, second, state, finals)
    own, sums_two, returned = attn_back(
        1, 2, *two, full_two, do, soft_two, None, second[0], [mid_b, partner_b], gr, None, state, finals
    )
    gr, do, small_one = ff_back(
        2, 1, [own, returned], lengths, saved_one, first, state, finals
    )
    own, _, small = attn_back(
        3, 1, *one, full_one, do, soft_one, (lengths, boxes), first[0], [own_b], gr,
        (small_one, small_two, sums_two), state, finals,
    )
    return own, finish_outputs(me, finals, small, d // 16, d)


def swap(value, axis, bit):
    size = lax.axis_size(axis)
    return lax.ppermute(value, axis, [(i, i ^ bit) for i in range(size)])


def reduce_slots(parts, axis):
    keep, send = parts
    bit = 1
    while True:
        got = swap(send, axis, bit)
        count = keep.shape[0]
        if count == 1:
            return keep[0].astype(f32) + got[0].astype(f32)
        half = count // 2
        send = (keep[half:].astype(f32) + got[half:].astype(f32)).astype(keep.dtype)
        keep = (keep[:half].astype(f32) + got[:half].astype(f32)).astype(keep.dtype)
        bit *= 2


def reduce_small(rows, me, axis):
    size = lax.axis_size(axis)
    count = rows.shape[0]
    cut = jnp.transpose(rows.reshape(count, size, -1), (1, 0, 2))
    cut = jnp.take(cut, jnp.arange(size, dtype=jnp.int32) ^ me, axis=0)
    bit = 1
    while bit < size:
        pairs = cut.reshape(cut.shape[0] // 2, 2, *cut.shape[1:])
        cut = pairs[:, 0] + swap(pairs[:, 1], axis, bit)
        bit *= 2
    return cut[0]


def body(
    stream,
    lengths,
    layout_boxes,
    self_attn_in,
    self_attn_out,
    self_ff_up,
    self_ff_down,
    self_vectors,
    self_gains,
    self_up_bias,
    cross_attn_in,
    cross_attn_out,
    cross_ff_up,
    cross_ff_down,
    cross_vectors,
    cross_gains,
    cross_up_bias,
    box_table,
    cotangent,
):
    place = lax.axis_index("wide")
    devices = lax.axis_size("wide")
    me = place.astype(jnp.int32).reshape(1)
    n, d = stream.shape[2:]
    ff = self_ff_up.shape[2]
    first = (
        self_attn_in,
        self_attn_out,
        self_ff_up,
        self_ff_down,
        self_vectors,
        self_gains,
        self_up_bias,
    )
    second = (
        cross_attn_in,
        cross_attn_out,
        cross_ff_up,
        cross_ff_down,
        cross_vectors,
        cross_gains,
        cross_up_bias,
    )
    own_b = stream.reshape(n, d)
    top = cotangent.reshape(n, d)
    qkv_one = project(own_b, self_attn_in, self_vectors, 0, 3)
    one = ([qkv_one] * 3, (0, PAIRS, 2 * PAIRS))
    blend_one, soft_one, full_one = attend_forward(*one, lengths, False, layout_boxes, box_table)
    if devices == 16:
        saved_one = feed_forward_sending(blend_one, own_b, first, cross_attn_in, cross_vectors)
        *saved_one, partner_b, q_two = saved_one
    else:
        saved_one = feed_forward(blend_one, own_b, first, lengths, False)
        partner_b = swap(saved_one[-1], "narrow", 1)
        q_two = project(saved_one[-1], cross_attn_in, cross_vectors, 0, 1)
    unit_one, scale_one, rb_one, act_one, slope_one, unit_two, scale_two, mid, mid_b = saved_one
    kv_two = project(partner_b, cross_attn_in, cross_vectors, 1, 2)
    two = ([q_two, kv_two, kv_two], (0, 0, PAIRS))
    blend_two, soft_two, full_two = attend_forward(*two, lengths, True, None, None)
    saved_two = feed_forward(blend_two, mid, second, lengths, True)
    unit_three, scale_three, rb_two, act_two, slope_two, unit_four, scale_four, final = saved_two

    side = lax.axis_index("narrow")
    own_count = jnp.where(side == 0, lengths[0], lengths[1])
    slot = jnp.arange(n, dtype=jnp.int32)
    padding = ((0, 0), (0, n - TEXT))
    boxes = layout_boxes[0]
    text = jnp.pad((boxes[:2] + boxes[2:]) >> 1, padding)
    grid_side = jnp.where(own_count > GRID_LO * GRID_LO, GRID_HI, GRID_LO).astype(jnp.int32)
    patch = jnp.stack([slot % grid_side, slot // grid_side])
    patch = (patch * 1000 + 500) // grid_side
    centres = jnp.where(side == 0, text, patch)
    places = (centres.T, centres)

    if devices == 16:
        saved = (unit_one, scale_one, rb_one, act_one, slope_one, unit_two, scale_two, blend_one)
        later = (
            unit_three, scale_three, rb_two, act_two, slope_two, unit_four, scale_four, blend_two
        )
        extra = (
            top, lengths, layout_boxes, own_b, mid_b, partner_b, soft_one, soft_two, full_one, full_two
        )
        grad_stream, (grads_one, grads_two, grad_table) = backward_with_hops(
            me, first, second, saved, later, one, two, extra
        )
        return (final[None, None], grad_stream[None, None]) + grads_one + grads_two + (grad_table,)

    def large(parts):
        if len(parts) == 2:
            return reduce_slots(parts, "wide")
        return lax.psum_scatter(parts[0].astype(f32), "wide", scatter_dimension=0, tiled=True)

    def columns(value, lead):
        if value.ndim == 2:
            return value[:, lead[0] * d : lead[1] * d][None]
        picked = value[lead[0] : lead[1]]
        return jnp.transpose(picked, (1, 0, 2)).reshape(1, picked.shape[1], -1)

    dz, gb, sums_four, down_two = down_gradient(
        me, own_count, [top], unit_four, scale_four, cross_gains, act_two, devices, True
    )
    down_two = large(down_two)
    du, ups_two, ga, gr, do, sums_three = feed_backward(
        dz, gb, slope_two, unit_three, scale_three, second
    )
    steps = ff // d
    jobs = [(0, 0, 0)] * steps + [(1, 1, 0)]
    up_two = large(weight_gradients(me, jobs, [rb_two, blend_two], [du, ga], devices))
    dq, dk, dv, sums_two_attn = attend_backward(*two, do, soft_two, None)
    grad_partner = project_back([dk, dv], cross_attn_in, 1, None, bf16)
    returned = swap(grad_partner, "narrow", 1)
    grad_own = project_back([dq], cross_attn_in, 0, gr, f32)
    in_two = large(
        weight_gradients(
            me, [(0, 0, 0), (1, 1, 0), (1, 2, 0)], [mid_b, partner_b], [dq, dk, dv], devices
        )
    )

    dz, gb, sums_two, down_one = down_gradient(
        me, own_count, [grad_own, returned], unit_two, scale_two, self_gains, act_one, devices, False
    )
    down_one = large(down_one)
    du, ups_one, ga, gr, do, sums_one = feed_backward(
        dz, gb, slope_one, unit_one, scale_one, first
    )
    up_one = large(weight_gradients(me, jobs, [rb_one, blend_one], [du, ga], devices))
    dq, dk, dv, sums_one_attn, grad_tables = attend_backward(*one, do, soft_one, places)
    in_one = large(
        weight_gradients(
            me, [(0, 0, 0), (0, 1, 0), (0, 2, 0)], [own_b], [dq, dk, dv], devices
        )
    )
    grad_stream = project_back([dq, dk, dv], self_attn_in, 0, gr, f32)

    def ups_rows(ups):
        return jnp.transpose(
            ups.reshape(devices, steps, d // devices), (1, 0, 2)
        ).reshape(steps, d)

    table_row = jnp.transpose(
        grad_tables.reshape(H, 2, 128)[:, :, :NB], (1, 2, 0)
    ).reshape(1, 2 * NB * H)
    small = jnp.concatenate(
        [
            sums_one_attn[:2],
            sums_one[2:3],
            sums_one[1:2],
            sums_two[2:3],
            sums_two[1:2],
            sums_one[0:1],
            sums_two[0:1],
            ups_rows(ups_one),
            sums_two_attn[:2],
            sums_three[2:3],
            sums_three[1:2],
            sums_four[2:3],
            sums_four[1:2],
            sums_three[0:1],
            sums_four[0:1],
            ups_rows(ups_two),
            table_row,
        ]
    )
    small = reduce_small(small, me, "wide")
    half = 8 + steps

    def layer(values, base, inside, up, down):
        return (
            columns(inside, (0, 3)),
            columns(up, (steps, steps + 1)),
            columns(up, (0, steps)),
            down[None],
            values[base : base + 6][None],
            values[base + 6 : base + 8][None],
            values[base + 8 : base + half].reshape(1, -1),
        )

    return (
        (final[None, None], grad_stream[None, None])
        + layer(small, 0, in_one, up_one, down_one)
        + layer(small, half, in_two, up_two, down_two)
        + (small[2 * half :],)
    )


def solution(mesh):
    matrix = P("narrow", None, None)
    layer_in = (matrix,) * 6 + (P("narrow", None),)
    rows = P("narrow", "wide", None, None)
    in_specs = (
        (rows, P(None, "wide"), P("wide", None, None))
        + layer_in * 2
        + (P("narrow", None), rows)
    )
    layer_out = (P("narrow", "wide", None),) * 4 + (
        P("narrow", None, "wide"),
        P("narrow", None, "wide"),
        P("narrow", "wide"),
    )
    out_specs = (rows, rows) + layer_out * 2 + (P("narrow", "wide"),)
    return jax.shard_map(body, mesh=mesh, in_specs=in_specs, out_specs=out_specs, check_vma=False)
```

```python
import functools

import jax
import jax.numpy as jnp
import numpy as np
from jax import lax
from jax.experimental import pallas as pl
from jax.experimental.pallas import tpu as pltpu
from jax.sharding import PartitionSpec as P

H = 12
HD = 64
NB = 32
TEXT = 512
GRID_LO = 16
GRID_HI = 24
PAIRS = H // 2
STRIP = 192
SUB = 32
MIB = 1 << 20

norm_eps = 1e-05
spacing = 64
masked_score = -1e30

f32 = jnp.float32
bf16 = jnp.bfloat16
SMEM = pltpu.MemorySpace.SMEM


def nn(left, right):
    return lax.dot_general(left, right, (((1,), (0,)), ((), ())), preferred_element_type=f32)


def nt(left, right):
    return lax.dot_general(left, right, (((1,), (1,)), ((), ())), preferred_element_type=f32)


def tn(left, right):
    return lax.dot_general(left, right, (((0,), (0,)), ((), ())), preferred_element_type=f32)


def whole(shape):
    return pl.BlockSpec(shape, lambda i: (0,) * len(shape))


def scalar_spec():
    return pl.BlockSpec(memory_space=SMEM)


def call(kernel, grid, in_specs, out_specs, out_shape, scratch, flops, moved, vmem=63):
    return pl.pallas_call(
        kernel,
        grid=grid,
        in_specs=in_specs,
        out_specs=out_specs,
        out_shape=out_shape,
        scratch_shapes=scratch,
        compiler_params=pltpu.CompilerParams(
            dimension_semantics=("arbitrary",),
            vmem_limit_bytes=vmem * MIB,
            fuse_transposed_lhs_in_matmul=True,
        ),
        cost_estimate=pl.CostEstimate(
            flops=int(flops), bytes_accessed=int(moved), transcendentals=0
        ),
    )


def shape_of(shape, dtype):
    return jax.ShapeDtypeStruct(shape, dtype)


def normalise(values):
    average = jnp.mean(values, axis=-1, keepdims=True)
    centred = values - average
    variance = jnp.mean(centred * centred, axis=-1, keepdims=True)
    scale = lax.rsqrt(variance + norm_eps)
    return centred * scale, scale


def normalise_back(grad, unit, scale, gains):
    inner = grad * gains
    mean_one = jnp.mean(inner, axis=-1, keepdims=True)
    mean_two = jnp.mean(inner * unit, axis=-1, keepdims=True)
    return scale * (inner - mean_one - unit * mean_two)


def gelu_both(u):
    t = pltpu.reciprocal(1.0 + (0.3275911 * 0.7071067811865476) * jnp.abs(u), approx=True)
    bell = jnp.exp(-0.5 * (u * u))
    poly = t * (
        0.127414796
        + t * (-0.142248368 + t * (0.7107068705 + t * (-0.7265760135 + t * 0.5307027145)))
    )
    tail = poly * bell
    share = jnp.where(u < 0, tail, 1.0 - tail)
    return u * share, share + (u * 0.3989422804014327) * bell


def each_strip(n, size, body, start=None, unroll=4):
    def step(index, carry):
        return body(pl.ds(pl.multiple_of(index * size, size), size), carry)

    return lax.fori_loop(0, n // size, step, start, unroll=unroll)


def fold(values):
    total = values[0:8]
    for r in range(8, values.shape[0], 8):
        total = total + values[r : r + 8]
    return total


def head_masks():
    lane = lax.broadcasted_iota(jnp.int32, (1, 2 * HD), 1)
    return [
        jnp.where(lane < HD, HD**-0.5, 0.0).astype(bf16),
        jnp.where(lane < HD, 0.0, HD**-0.5).astype(bf16),
    ]


def count_of(lengths, other=False):
    side = lax.axis_index("narrow")
    text, image = lengths[0, 0], lengths[0, 1]
    return jnp.where(side == (1 if other else 0), text, image)


def patch_centres(n, keys):
    slot = np.arange(n)
    rows = []
    for side in (GRID_HI, GRID_LO):
        for index in (slot % side, slot // side):
            rows.append((index * 1000 + 500) // side)
    return jnp.asarray(np.pad(np.stack(rows), ((0, 0), (0, keys - n))), jnp.int32)


def centres_of(lengths, boxes, patches):
    text = jnp.concatenate(
        [(boxes[0:2] + boxes[2:4]) >> 1, jnp.zeros((2, patches.shape[1] - TEXT), jnp.int32)], axis=1
    )
    patch = jnp.where(lengths[0, 1] > GRID_LO * GRID_LO, patches[0:2], patches[2:4])
    row = jnp.where(lax.axis_index("narrow") == 0, text, patch)
    tall = jnp.concatenate([row, jnp.zeros((6, row.shape[1]), jnp.int32)], axis=0)
    return row, tall.astype(f32).T.astype(jnp.int32)


def table_lines(tables):
    each = NB * H
    lane = lax.broadcasted_iota(jnp.int32, (16, each), 1)
    head = lax.broadcasted_iota(jnp.int32, (16, each), 0)
    line = lax.broadcasted_iota(jnp.int32, (each, 128), 0)
    bucket = lax.broadcasted_iota(jnp.int32, (each, 128), 1)
    inside = line - H * bucket
    hot = jnp.where((inside >= 0) & (inside < H), 1.0, 0.0)
    found = []
    for direction in range(2):
        values = tables[:, direction * each : direction * each + each]
        past = lane - head
        mine = past - H * ((past.astype(f32) + 0.5) * (1.0 / H)).astype(jnp.int32) == 0
        values = jnp.where(mine & (past >= 0), jnp.broadcast_to(values, (16, each)), 0.0)
        found.append(
            lax.dot_general(
                values, hot, (((1,), (0,)), ((), ())),
                precision=lax.Precision.HIGHEST, preferred_element_type=f32,
            )
        )
    return found


def low_lanes(rows):
    return lax.broadcasted_iota(jnp.int32, (rows, 2 * HD), 1) < HD


def hot_columns(coord_x, coord_y, rows, reverse=False):
    lane = lax.broadcasted_iota(jnp.int32, (rows, 128), 1)
    cell = jnp.where((lane & 16) == 0, coord_x >> 6, coord_y >> 6)
    place = lane & 15
    if reverse:
        place = 15 - place
    return jnp.where((cell == place) & (lane < 64), 1.0, 0.0)


def slanted(row, first):
    wide = jnp.broadcast_to(row, (16, 128))
    return pltpu.roll(wide, (128 - first) % 128, 1, stride=1, stride_axis=0)


def spread_tables(table_x, table_y):
    lane = lax.broadcasted_iota(jnp.int32, (16, 128), 1)
    keep = lane < 16
    outs = []
    rows = []
    for row in (table_x, table_y):
        base = jnp.where(keep, slanted(row, 16), 0.0)
        before = jnp.where(keep, slanted(row, 15), 0.0)
        rows.append((base, before - base))

    def split(value, offset):
        upper = value.astype(bf16).astype(f32)
        lower = value - upper
        joined = upper + pltpu.roll(lower, 32, 1)
        return pltpu.roll(joined, offset, 1) if offset else joined

    zero = jnp.zeros((16, 128), f32)
    outs.append(jnp.concatenate([split(rows[0][0], 0), split(rows[1][0], 16)], axis=0))
    outs.append(jnp.concatenate([split(rows[0][1], 0), zero], axis=0))
    outs.append(jnp.concatenate([zero, split(rows[1][1], 16)], axis=0))
    return [value.astype(bf16) for value in outs]


def attend_forward(own, source, queries, weight, vectors, lengths, other, boxes, tables):
    n, d = source.shape
    keys = -(-n // 128) * 128
    heads = 4
    wide = HD * heads
    boxed = boxes is not None

    def kernel(*refs):
        if boxed:
            cnt, x_ref, y_ref, wq, wk, wv, vec, b_ref, c_ref, t_ref = refs[:10]
            q_ref, k_ref, v_ref, o_ref, p_ref, f_ref = refs[10:16]
            k_s, v_s, s_s, step_x, step_y, hot_i, hot_j, lines = refs[16:]
        else:
            cnt, x_ref, y_ref, wq, wk, wv, vec = refs[:7]
            q_ref, k_ref, v_ref, o_ref, p_ref, f_ref, k_s, v_s, s_s = refs[7:]
            s_s = [[s_s.at[0]], [s_s.at[1]]]
        live_count = count_of(cnt, other)
        group = pl.program_id(0)

        @pl.when(group == 0)
        def _():
            k_s[n:keys] = jnp.zeros((keys - n, wide), bf16)
            v_s[n:keys] = jnp.zeros((keys - n, wide), bf16)
            if boxed:
                row, col = centres_of(cnt, b_ref[...], c_ref[...])
                cx, cy = col[0:n, 0:1], col[0:n, 1:2]
                lines[0], lines[1] = table_lines(t_ref[...])
                hots = hot_columns(cx, cy, n)
                lane = lax.broadcasted_iota(jnp.int32, (n, 128), 1)
                hot_i[...] = jnp.where(lane == 64, 1.0, hots).astype(bf16)
                hot_j[0:n] = jnp.where(lane < 32, hots, 0.0).astype(bf16)
                hot_j[n:keys] = jnp.zeros((keys - n, 128), bf16)
                rx, ry = row[0:1], row[1:2]
                step_x[...] = jnp.where((cx & 63) < (rx & 63), 1.0, 0.0)
                step_y[...] = jnp.where((cy & 63) < (ry & 63), 1.0, 0.0)

        if boxed:
            s_s = [[s_s.at[3 * h + k] for k in range(3)] for h in range(2)]
            lane = lax.broadcasted_iota(jnp.int32, (keys, 128), 1)
            place = lax.broadcasted_iota(jnp.int32, (keys, 128), 0)
            dead = jnp.where((lane == 64) & (place >= live_count), masked_score, 0.0)
            dead = dead.astype(bf16)
        cut = pl.ds(pl.multiple_of(group * wide, wide), wide)
        if queries:
            q_ref[...] = x_ref[...]
        else:
            q_ref[...] = (nn(x_ref[...], wq[...]) + vec[0, :, cut]).astype(bf16)
        rows = y_ref[...]
        k_s[0:n] = nn(rows, wk[...]).astype(bf16)
        v_s[0:n] = (nn(rows, wv[...]) + vec[1, :, cut]).astype(bf16)
        k_ref[...] = k_s[0:n]
        v_ref[...] = v_s[0:n]
        masks = head_masks()
        low = low_lanes(n)
        tiles = [slice(128 * t, 128 * t + 128) for t in range(keys // 128)]

        def scores(head):
            lanes = slice(128 * (head // 2), 128 * (head // 2) + 128)
            part = q_ref[:, lanes] * masks[head % 2]
            to = s_s[head % 2]
            if boxed:
                row = pl.ds(heads * group + head, 1)
                base, dx, dy = spread_tables(lines[0, row], lines[1, row])
                hi, hj = hot_i[...], hot_j[:, :32]
                side = nn(hj, base).astype(bf16) + dead
                side = jnp.concatenate([k_s[:, lanes], side], axis=1)
                to[0][...] = nt(jnp.concatenate([part, hi], axis=1), side)
                to[1][...] = nt(hi, nn(hj, dx).astype(bf16))
                to[2][...] = nt(hi, nn(hj, dy).astype(bf16))
            else:
                to[0][...] = nt(part, k_s[:, lanes])

        def soften(head):
            at = s_s[head % 2]
            for r in range(0, n, SUB):
                rows = slice(r, r + SUB)
                parts = []
                for t, lanes in enumerate(tiles):
                    s = at[0][rows, lanes]
                    if boxed:
                        s = s + step_x[rows, lanes] * at[1][rows, lanes]
                        s = s + step_y[rows, lanes] * at[2][rows, lanes]
                    elif 128 * t + 128 > GRID_LO * GRID_LO:
                        lane = lax.broadcasted_iota(jnp.int32, (1, 128), 1) + 128 * t
                        s = jnp.where(lane < live_count, s, masked_score)
                    parts.append(s)
                peak = functools.reduce(jnp.maximum, parts)
                peak = jnp.max(peak, axis=-1, keepdims=True)
                parts = [jnp.exp(s - peak) for s in parts]
                total = functools.reduce(jnp.add, parts)
                total = 1.0 / jnp.sum(total, axis=-1, keepdims=True)
                for s, lanes in zip(parts, tiles):
                    p_ref[head, rows, lanes] = (s * total).astype(bf16)

        scores(0)
        blends = []
        for head in range(heads):
            if head + 1 < heads:
                scores(head + 1)
            soften(head)
            lanes = slice(128 * (head // 2), 128 * (head // 2) + 128)
            blends.append(nn(p_ref[head], v_s[:, lanes]))
            if head % 2 == 1:
                blend = jnp.where(low, blends[head - 1], blends[head])
                f_ref[:, lanes] = blend
                o_ref[:, lanes] = blend.astype(bf16)

    block = pl.BlockSpec((n, wide), lambda i: (0, i))
    columns = [
        pl.BlockSpec((None, d, wide), lambda i, k=k: (0, 0, i + k * (H // heads))) for k in range(3)
    ]
    in_specs = [scalar_spec(), block if queries else whole((n, d)), whole((n, d))]
    in_specs += columns + [whole((6, 1, d))]
    args = [lengths, own, source, weight, weight, weight, vectors]
    scratch = [
        pltpu.VMEM((keys, wide), bf16),
        pltpu.VMEM((keys, wide), bf16),
        pltpu.VMEM((6 if boxed else 2, n, keys), f32),
    ]
    if boxed:
        in_specs += [
            pl.BlockSpec((None, 4, TEXT), lambda i: (0, 0, 0)),
            whole((4, keys)),
            whole((1, 2 * NB * H)),
        ]
        args += [boxes, patch_centres(n, keys), tables]
        scratch += [pltpu.VMEM((n, keys), f32)] * 2
        scratch += [pltpu.VMEM((n, 128), bf16), pltpu.VMEM((keys, 128), bf16)]
        scratch += [pltpu.VMEM((2, 16, 128), f32)]
    return call(
        kernel,
        (H // heads,),
        in_specs,
        [block] * 4 + [pl.BlockSpec((heads, n, keys), lambda i: (i, 0, 0)), block],
        [
            shape_of((n, H * HD), bf16),
            shape_of((n, H * HD), bf16),
            shape_of((n, H * HD), bf16),
            shape_of((n, H * HD), bf16),
            shape_of((H, n, keys), bf16),
            shape_of((n, H * HD), f32),
        ],
        scratch,
        16 * n * n * H * HD + 6 * n * d * d,
        2 * H * n * n,
    )(*args)


def feed_forward(blended, states, weights, lengths, last):
    _, attn_out, ff_up, ff_down, vectors, gains, up_bias = weights
    n, d = blended.shape
    steps = ff_up.shape[2] // d

    def kernel(cnt, o_ref, x_ref, wo_ref, wu_ref, wd_ref, v_ref, g_ref, e_ref, *rest):
        if last:
            unit1, scale1, rb, act, der, unit2, scale2, out, r_s, acc = rest
        else:
            unit1, scale1, rb, act, der, unit2, scale2, out, out_b, r_s, acc = rest
        step = pl.program_id(0)

        @pl.when(step == 0)
        def _():
            branch = nn(o_ref[...], wo_ref[...]) + v_ref[2]
            unit, scale = normalise(x_ref[...].astype(f32) + branch)
            unit1[...] = unit
            scale1[...] = scale
            r = unit * g_ref[0:1] + v_ref[3]
            r_s[...] = r
            rb[...] = r.astype(bf16)
            acc[...] = r + v_ref[4]

        hidden = nn(rb[...], wu_ref[...]) + e_ref[...]
        active, slope = gelu_both(hidden)
        active = active.astype(bf16)
        act[...] = active
        der[...] = slope.astype(bf16)
        acc[...] += nn(active, wd_ref[...])

        @pl.when(step == steps - 1)
        def _():
            unit, scale = normalise(acc[...])
            unit2[...] = unit
            scale2[...] = scale
            z = unit * g_ref[1:2] + v_ref[5]
            if last:
                row = lax.broadcasted_iota(jnp.int32, (n, 1), 0)
                out[...] = jnp.where(row < count_of(cnt), z, 0.0)
            else:
                out[...] = z
                out_b[...] = z.astype(bf16)

    columns = pl.BlockSpec((n, d), lambda i: (0, i))
    outs = [
        (whole((n, d)), shape_of((n, d), f32)),
        (whole((n, 1)), shape_of((n, 1), f32)),
        (whole((n, d)), shape_of((n, d), bf16)),
        (columns, shape_of((n, steps * d), bf16)),
        (columns, shape_of((n, steps * d), bf16)),
        (whole((n, d)), shape_of((n, d), f32)),
        (whole((n, 1)), shape_of((n, 1), f32)),
        (whole((n, d)), shape_of((n, d), f32)),
    ]
    if not last:
        outs.append((whole((n, d)), shape_of((n, d), bf16)))
    return call(
        kernel,
        (steps,),
        [
            scalar_spec(),
            whole((n, d)),
            whole((n, d)),
            pl.BlockSpec((None, d, d), lambda i: (0, 0, 0)),
            pl.BlockSpec((None, d, d), lambda i: (0, 0, i)),
            pl.BlockSpec((None, d, d), lambda i: (0, i, 0)),
            whole((6, 1, d)),
            pl.BlockSpec((None, 2, d), lambda i: (0, 0, 0)),
            pl.BlockSpec((1, d), lambda i: (0, i)),
        ],
        [spec for spec, _ in outs],
        [shape for _, shape in outs],
        [pltpu.VMEM((n, d), f32), pltpu.VMEM((n, d), f32)],
        2 * n * d * d * (1 + 2 * steps),
        2 * d * d * (1 + 2 * steps),
    )(lengths, blended, states, attn_out, ff_up, ff_down, vectors, gains, up_bias)


def store_rows(rows):
    d = rows[0].shape[1]
    blank = jnp.zeros((8 - len(rows), d), f32)
    return jnp.concatenate(rows + [blank], axis=0)


def slot_place(index, bits):
    place = 0
    for b in range(bits):
        place = place | (((index >> b) & 1) << (bits - 1 - b))
    return place


class Slots:
    def __init__(self, devices, rows):
        self.devices = devices
        self.rows = rows // devices
        self.bits = (devices // 2).bit_length() - 1
        self.split = self.rows % 16 == 0 and devices & (devices - 1) == 0 and devices > 1

    def put(self, me, held, shards, first_shard, write):
        core = me & 1
        for k in range(shards // 2):
            place = slot_place((first_shard // 2 + k) ^ (me >> 1), self.bits)
            for which in range(2):
                start = (2 * k + (core if which == 0 else 1 - core)) * self.rows
                rows = held[pl.ds(pl.multiple_of(start, 16), self.rows)]
                write(which, place, rows)


def down_gradient(me, count, grads, unit, scale, gains, active, devices, top):
    n, d = unit.shape
    ff = active.shape[1]
    steps = ff // d
    slots = Slots(devices, ff)
    shards = devices // steps

    def kernel(me_ref, cnt, *refs):
        ups = refs[: len(grads)]
        unit_ref, scale_ref, g_ref, act_ref = refs[len(grads) : len(grads) + 4]
        dz, gb, sums, *outs, held = refs[len(grads) + 4 :]
        step = pl.program_id(0)

        @pl.when(step == 0)
        def _():
            if top:
                row = lax.broadcasted_iota(jnp.int32, (n, 1), 0)
                g = jnp.where(row < cnt[0], ups[0][...].astype(f32), 0.0)
            else:
                g = ups[0][...] + ups[1][...].astype(f32)
            unit = unit_ref[...]
            back = normalise_back(g, unit, scale_ref[...], g_ref[1:2])
            dz[...] = back
            low = back.astype(bf16)
            gb[...] = low
            sums[...] = store_rows(
                [
                    jnp.sum(g * unit, axis=0, keepdims=True),
                    jnp.sum(g, axis=0, keepdims=True),
                    jnp.sum(low.astype(f32), axis=0, keepdims=True),
                ]
            )

        value = tn(act_ref[...], gb[...]).astype(bf16)
        if slots.split:
            held[...] = value

            def write(which, place, rows):
                outs[which][place] = rows

            slots.put(me_ref[0], held, shards, shards * step, write)
        else:
            outs[0][...] = value

    if slots.split:
        block = (devices // 2, slots.rows, d)
        out_list = [(whole(block), shape_of(block, bf16))] * 2
    else:
        out_list = [(pl.BlockSpec((d, d), lambda i: (i, 0)), shape_of((ff, d), bf16))]
    out_list = [
        (whole((n, d)), shape_of((n, d), f32)),
        (whole((n, d)), shape_of((n, d), bf16)),
        (whole((8, d)), shape_of((8, d), f32)),
    ] + out_list
    results = call(
        kernel,
        (steps,),
        [scalar_spec(), scalar_spec()]
        + [whole((n, d))] * len(grads)
        + [
            whole((n, d)),
            whole((n, 1)),
            pl.BlockSpec((None, 2, d), lambda i: (0, 0, 0)),
            pl.BlockSpec((n, d), lambda i: (0, i)),
        ],
        [spec for spec, _ in out_list],
        [shape for _, shape in out_list],
        [pltpu.VMEM((d, d), bf16)],
        2 * n * d * ff,
        4 * d * ff,
    )(me, count, *grads, unit, scale, gains, active)
    return results[0], results[1], results[2], results[3:]


def feed_backward(grad_sum, grad_branch, slope, unit, scale, weights):
    _, attn_out, ff_up, ff_down, _, gains, _ = weights
    n, d = grad_sum.shape
    steps = ff_up.shape[2] // d

    def kernel(
        dz, gb, der, wd, wu, wo, g_ref, unit_ref, scale_ref, du, ups, ga, gr, do, sums, acc
    ):
        step = pl.program_id(0)

        @pl.when(step == 0)
        def _():
            acc[...] = dz[...]

        grad = (nt(gb[...], wd[...]) * der[...].astype(f32)).astype(bf16)
        du[...] = grad
        ups[...] = jnp.sum(grad.astype(f32), axis=0, keepdims=True)
        acc[...] += nt(grad, wu[...])

        @pl.when(step == steps - 1)
        def _():
            g = acc[...]
            unit = unit_ref[...]
            back = normalise_back(g, unit, scale_ref[...], g_ref[0:1])
            gr[...] = back
            low = back.astype(bf16)
            ga[...] = low
            sums[...] = store_rows(
                [
                    jnp.sum(g * unit, axis=0, keepdims=True),
                    jnp.sum(g, axis=0, keepdims=True),
                    jnp.sum(low.astype(f32), axis=0, keepdims=True),
                ]
            )
            do[...] = nt(low, wo[...]).astype(bf16)

    columns = pl.BlockSpec((n, d), lambda i: (0, i))
    return call(
        kernel,
        (steps,),
        [
            whole((n, d)),
            whole((n, d)),
            columns,
            pl.BlockSpec((None, d, d), lambda i: (0, i, 0)),
            pl.BlockSpec((None, d, d), lambda i: (0, 0, i)),
            pl.BlockSpec((None, d, d), lambda i: (0, 0, 0)),
            pl.BlockSpec((None, 2, d), lambda i: (0, 0, 0)),
            whole((n, d)),
            whole((n, 1)),
        ],
        [
            columns,
            pl.BlockSpec((1, d), lambda i: (0, i)),
            whole((n, d)),
            whole((n, d)),
            whole((n, d)),
            whole((8, d)),
        ],
        [
            shape_of((n, steps * d), bf16),
            shape_of((1, steps * d), f32),
            shape_of((n, d), bf16),
            shape_of((n, d), f32),
            shape_of((n, d), bf16),
            shape_of((8, d), f32),
        ],
        [pltpu.VMEM((n, d), f32)],
        2 * n * d * d * (1 + 2 * steps),
        2 * d * d * (1 + 2 * steps),
    )(grad_sum, grad_branch, slope, ff_down, ff_up, attn_out, gains, unit, scale)


def weight_gradients(me, jobs, lefts, rights, devices):
    n, d = lefts[0].shape
    slots = Slots(devices, d)
    steps = len(jobs)

    def kernel(me_ref, *refs):
        left_refs = refs[: len(lefts)]
        right_refs = refs[len(lefts) : len(lefts) + len(rights)]
        *outs, turned, held = refs[len(lefts) + len(rights) :]
        step = pl.program_id(0)
        for index in range(len(lefts)):
            mine = [j for j, job in enumerate(jobs) if job[0] == index]

            @pl.when(step == mine[0])
            def _(index=index):
                turned[...] = left_refs[index][...].T

        for index in range(len(rights)):
            mine = [j for j, job in enumerate(jobs) if job[1] == index]

            @pl.when((step >= mine[0]) & (step <= mine[-1]))
            def _(index=index):
                value = nn(turned[...], right_refs[index][...]).astype(bf16)
                if slots.split:
                    held[...] = value
                else:
                    outs[0][...] = value

        if slots.split:

            def write(which, place, rows):
                outs[which][place, step] = rows

            slots.put(me_ref[0], held, devices, 0, write)

    def right_spec(index):
        mine = [(j, job[2]) for j, job in enumerate(jobs) if job[1] == index]
        first, block = mine[0]

        def place(i):
            return (0, jnp.clip(i - first, 0, len(mine) - 1) + block)

        return pl.BlockSpec((n, d), place)

    if slots.split:
        block = (devices // 2, steps, slots.rows, d)
        out_list = [(whole(block), shape_of(block, bf16))] * 2
    else:
        out_list = [(pl.BlockSpec((d, d), lambda i: (0, i)), shape_of((d, steps * d), bf16))]
    return call(
        kernel,
        (steps,),
        [scalar_spec()]
        + [whole((n, d))] * len(lefts)
        + [right_spec(index) for index in range(len(rights))],
        [spec for spec, _ in out_list],
        [shape for _, shape in out_list],
        [pltpu.VMEM((d, n), bf16), pltpu.VMEM((d, d), bf16)],
        2 * n * d * d * steps,
        4 * d * d * steps,
    )(me, *lefts, *rights)


def attend_backward(arrays, offsets, grad_blended, soft, places):
    n = grad_blended.shape[0]
    boxed = places is not None
    keys = soft.shape[2]

    def kernel(*refs):
        q_ref, k_ref, v_ref, g_ref, p_ref = refs[:5]
        if boxed:
            col_ref, row_ref = refs[5:7]
            dq_ref, dk_ref, dv_ref, sums, tab = refs[7:12]
            hot_i, hot_j, step_x, step_y, ds_s, far = refs[12:]

            @pl.when(pl.program_id(0) == 0)
            def _():
                cx, cy = col_ref[:, 0:1], col_ref[:, 1:2]
                rx, ry = row_ref[0:1], row_ref[1:2]
                hots = hot_columns(cx, cy, n, reverse=True)
                lane = lax.broadcasted_iota(jnp.int32, (n, 128), 1)
                hot_j[...] = jnp.where(lane < 32, hots, 0.0).astype(bf16)
                row = lax.broadcasted_iota(jnp.int32, (32, n), 0)
                cell = jnp.where(row < 16, rx >> 6, ry >> 6)
                hot_i[...] = jnp.where(cell == (row & 15), 1.0, 0.0).astype(bf16)
                step_x[...] = jnp.where((cx & 63) < (rx & 63), 1.0, 0.0).astype(bf16)
                step_y[...] = jnp.where((cy & 63) < (ry & 63), 1.0, 0.0).astype(bf16)
        else:
            dq_ref, dk_ref, dv_ref, sums, ds_s = refs[5:]
        masks = head_masks()
        q = q_ref[...]
        k = k_ref[...]
        v = v_ref[...]
        g = g_ref[...]
        grads = []
        for h in range(2):
            queries = []
            for r in range(0, n, STRIP):
                gh = g[r : r + STRIP] * masks[h]
                p = p_ref[h, r : r + STRIP, :n].astype(f32)
                dp = nt(gh, v)
                mean = jnp.sum(p * dp, axis=-1, keepdims=True)
                ds = (p * (dp - mean)).astype(bf16)
                ds_s[r : r + STRIP] = ds
                if boxed:
                    hj = hot_j[...]
                    wide = nn(ds, jnp.concatenate([k, hj], axis=1))
                    queries.append(wide[:, :128])
                    far[r : r + STRIP, 0:128] = wide[:, 128:]
                    far[r : r + STRIP, 128:256] = nn(ds * step_x[r : r + STRIP], hj)
                    far[r : r + STRIP, 256:384] = nn(ds * step_y[r : r + STRIP], hj)
                else:
                    queries.append(nn(ds, k))
            grads.append(
                (jnp.concatenate(queries, axis=0), tn(ds_s[...], q), tn(p_ref[h, :, :n], g))
            )
            if boxed:
                value = far[...]
                upper = value.astype(bf16)
                lower = (value - upper.astype(f32)).astype(bf16)
                cells = nn(hot_i[...], upper) + nn(hot_i[...], lower)
                lane = lax.broadcasted_iota(jnp.int32, (16, 128), 1)
                for direction in range(2):
                    rows = slice(16 * direction, 16 * direction + 16)
                    level = cells[rows, 0:128]
                    above = cells[rows, 128 * (direction + 1) : 128 * (direction + 2)]
                    inside = (lane >= 16 * direction) & (lane < 16 * direction + 16)
                    level = jnp.where(inside, level - above, 0.0)
                    above = jnp.where(inside, above, 0.0)
                    turn = (128 + 1 - 16 * direction) % 128
                    line = pltpu.roll(level, turn, 1, stride=1, stride_axis=0)
                    line = line + pltpu.roll(above, (turn + 127) % 128, 1, stride=1, stride_axis=0)
                    line = jnp.sum(line, axis=0, keepdims=True) * HD**0.5
                    tab[2 * h + direction : 2 * h + direction + 1] = line
        low = low_lanes(n)
        outs = []
        for index, ref in enumerate((dq_ref, dk_ref, dv_ref)):
            value = jnp.where(low, grads[0][index], grads[1][index]).astype(bf16)
            ref[...] = value
            outs.append(jnp.sum(value.astype(f32), axis=0, keepdims=True))
        sums[...] = store_rows([outs[0], outs[2]])

    def pair_block(offset):
        return pl.BlockSpec((n, 128), lambda i: (0, i + offset))

    in_specs = [pair_block(offset) for offset in offsets] + [
        pair_block(0),
        pl.BlockSpec((2, n, keys), lambda i: (i, 0, 0)),
    ]
    args = [*arrays, grad_blended, soft]
    outs = [(pair_block(0), shape_of((n, H * HD), bf16))] * 3
    outs.append((pl.BlockSpec((8, 128), lambda i: (0, i)), shape_of((8, H * HD), f32)))
    scratch = [pltpu.VMEM((n, n), bf16)]
    if boxed:
        in_specs += [whole((n, 2)), whole((2, n))]
        args += [*places]
        outs.append(
            (pl.BlockSpec((None, 4, 128), lambda i: (i, 0, 0)), shape_of((PAIRS, 4, 128), f32))
        )
        scratch = [
            pltpu.VMEM((32, n), bf16),
            pltpu.VMEM((n, 128), bf16),
            pltpu.VMEM((n, n), bf16),
            pltpu.VMEM((n, n), bf16),
            pltpu.VMEM((n, n), bf16),
            pltpu.VMEM((n, 384), f32),
        ]
    return call(
        kernel,
        (PAIRS,),
        in_specs,
        [spec for spec, _ in outs],
        [shape for _, shape in outs],
        scratch,
        16 * n * n * H * HD,
        2 * H * n * n,
    )(*args)


def project_back(grads, weight, first, residual, out_type):
    n, d = grads[0].shape
    steps = len(grads)

    def kernel(*refs):
        g_refs = refs[:steps]
        w_ref = refs[steps]
        out, acc = refs[-2:]
        step = pl.program_id(0)
        for index in range(steps):

            @pl.when(step == index)
            def _(index=index):
                value = nt(g_refs[index][...], w_ref[...])
                if index > 0:
                    value = value + acc[...]
                elif residual is not None:
                    value = value + refs[steps + 1][...]
                if index == steps - 1:
                    out[...] = value.astype(out_type)
                else:
                    acc[...] = value

    extra = [] if residual is None else [residual]
    return call(
        kernel,
        (steps,),
        [whole((n, d))] * steps
        + [pl.BlockSpec((None, d, d), lambda i: (0, 0, i + first))]
        + [whole((n, d))] * len(extra),
        whole((n, d)),
        shape_of((n, d), out_type),
        [pltpu.VMEM((n, d), f32)],
        2 * n * d * d * steps,
        2 * d * d * steps,
    )(*grads, weight, *extra)


def feed_forward_sending(blended, states, weights, next_in, next_vectors):
    _, attn_out, ff_up, ff_down, vectors, gains, up_bias = weights
    n, d = blended.shape
    tiles = ff_up.shape[2] // d
    strips = 3
    size = n // strips
    last = strips * tiles
    parts = Parts()
    strip = lambda i: jnp.minimum(i // tiles, strips - 1)
    tile = lambda i: jnp.where(i < last, i % tiles, tiles - 1)
    h_o = parts.inp(blended, fixed((n, d)))
    h_x = parts.inp(states, fixed((n, d)))
    h_wo = parts.inp(attn_out, fixed((None, d, d)))
    h_wu = parts.inp(ff_up, pl.BlockSpec((None, d, d), lambda i: (0, 0, tile(i))))
    h_wd = parts.inp(ff_down, pl.BlockSpec((None, d, d), lambda i: (0, tile(i), 0)))
    h_v, h_g = parts.inp(vectors, fixed((6, 1, d))), parts.inp(gains, fixed((None, 2, d)))
    h_e = parts.inp(up_bias, pl.BlockSpec((1, d), lambda i: (0, tile(i))))
    h_wq = parts.inp(next_in, pl.BlockSpec((None, d, d), lambda i: (0, 0, 0)))
    h_nv = parts.inp(next_vectors, fixed((6, 1, d)))
    h_unit1, h_scale1 = parts.out((n, d), f32), parts.out((n, 1), f32)
    h_rb = parts.out((n, d), bf16)
    block = pl.BlockSpec((size, d), lambda i: (strip(i), tile(i)))
    h_act = parts.out((n, tiles * d), bf16, block)
    h_der = parts.out((n, tiles * d), bf16, block)
    h_unit2, h_scale2 = parts.out((n, d), f32), parts.out((n, 1), f32)
    h_out, h_out_b = parts.out((n, d), f32), parts.out((n, d), bf16)
    h_partner, h_q = parts.out((n, d), bf16), parts.out((n, d), bf16)
    h_acc = parts.vmem((size, d), f32)
    h_got = parts.vmem((n, d), bf16)
    h_sent = parts.tmp(pltpu.SemaphoreType.DMA((strips,)))
    h_arrived = parts.tmp(pltpu.SemaphoreType.DMA((strips,)))

    def body(refs):
        i = pl.program_id(0)
        partner = {"narrow": 1 - lax.axis_index("narrow")}
        v_ref, g_ref, acc = refs[h_v], refs[h_g], refs[h_acc]

        def send(index):
            rows = pl.ds(size * index, size)
            return pltpu.make_async_remote_copy(
                src_ref=refs[h_out_b].at[rows],
                dst_ref=refs[h_got].at[rows],
                send_sem=refs[h_sent].at[index],
                recv_sem=refs[h_arrived].at[index],
                device_id=partner,
                device_id_type=MESH,
            )

        @pl.when(i == 0)
        def _():
            barrier = pltpu.get_barrier_semaphore()
            pl.semaphore_signal(barrier, inc=1, device_id=partner, device_id_type=MESH)
            pl.semaphore_wait(barrier, 1)

        for index in range(strips):
            rows = slice(size * index, size * index + size)

            @pl.when(i == index * tiles)
            def _(rows=rows):
                branch = nn(refs[h_o][rows], refs[h_wo][...]) + v_ref[2]
                unit, scale = normalise(refs[h_x][rows].astype(f32) + branch)
                refs[h_unit1][rows] = unit
                refs[h_scale1][rows] = scale
                r = unit * g_ref[0:1] + v_ref[3]
                refs[h_rb][rows] = r.astype(bf16)
                acc[...] = r + v_ref[4]

        @pl.when(i < last)
        def _():
            rows = pl.ds(pl.multiple_of(lax.div(i, tiles) * size, size), size)
            hidden = nn(refs[h_rb][rows], refs[h_wu][...]) + refs[h_e][...]
            active, slope = gelu_both(hidden)
            active = active.astype(bf16)
            refs[h_act][...] = active
            refs[h_der][...] = slope.astype(bf16)
            acc[...] += nn(active, refs[h_wd][...])

        for index in range(strips):
            rows = slice(size * index, size * index + size)

            @pl.when(i == index * tiles + tiles - 1)
            def _(rows=rows, index=index):
                unit, scale = normalise(acc[...])
                refs[h_unit2][rows] = unit
                refs[h_scale2][rows] = scale
                z = unit * g_ref[1:2] + v_ref[5]
                refs[h_out][rows] = z
                refs[h_out_b][rows] = z.astype(bf16)
                send(index).start()

        @pl.when(i == last)
        def _():
            q = nn(refs[h_out_b][...], refs[h_wq][...]) + refs[h_nv][0]
            refs[h_q][...] = q.astype(bf16)
            for index in range(strips):
                send(index).wait()
            refs[h_partner][...] = refs[h_got][...]

    results = parts.run(
        body, last + 1, 2 * n * d * d * (2 + 2 * tiles), 2 * d * d * (2 + 2 * tiles * strips), 4
    )
    order = (
        h_unit1, h_scale1, h_rb, h_act, h_der, h_unit2, h_scale2, h_out, h_out_b, h_partner, h_q
    )
    return [results[h] for h in order]


MESH = pl.DeviceIdType.MESH
DOWN, UP, IN = 0, 1, 2
SIZES = (3, 5, 3)


def block_shape(chunk, rows, d):
    return (4 * rows, d // 3) if chunk == DOWN else (rows, d)


Z_FIRST = (
    (2, 0, 0),
    (2, 0, 1),
    (2, 1, 1),
    (2, 2, 0),
    (1, 0, 0),
    (1, 0, 2),
)
HOPS = (
    (
        (2, 0, 0, 0, ((5, 21), (21, 42), (49, 61))),
        (2, 0, 1, 0, ((13, 26), (40, 61))),
        (2, 0, 2, 0, ((24, 33), (33, 53))),
        (2, 1, 0, 0, ((29, 37),)),
        (2, 1, 1, 0, ((37, 45),)),
        (2, 1, 2, 0, ((45, 53),)),
        (2, 1, 3, 0, ((53, 61),)),
    ),
    (
        (2, 1, 4, 0, ((0, 4), (10, 25), (27, 37), (41, 61))),
        (2, 0, 0, 3, ((0, 9),)),
        (2, 1, 0, 1, ((0, 11), (19, 33), (35, 45))),
        (2, 0, 2, 2, ((1, 11), (64, 69))),
        (2, 1, 1, 1, ((10, 25), (64, 69))),
        (2, 0, 1, 2, ((19, 34), (45, 69))),
        (2, 1, 3, 1, ((32, 53), (53, 69))),
        (2, 1, 2, 1, ((43, 69),)),
        (2, 2, 0, 0, ((53, 69),)),
        (2, 2, 1, 0, ((61, 69),)),
    ),
    (
        (2, 1, 3, 3, ((0, 5),)),
        (2, 2, 0, 1, ((0, 21), (25, 34), (56, 62))),
        (2, 2, 1, 1, ((0, 13), (24, 33))),
        (2, 2, 2, 0, ((0, 5), (8, 29), (32, 41))),
        (1, 0, 0, 0, ((5, 21),)),
        (2, 1, 2, 2, ((8, 26), (26, 37))),
        (1, 0, 1, 0, ((13, 26), (32, 50))),
        (1, 0, 2, 0, ((24, 33), (37, 61))),
        (1, 1, 0, 0, ((29, 34), (48, 62))),
        (1, 1, 1, 0, ((37, 45),)),
        (1, 1, 2, 0, ((45, 53),)),
        (1, 1, 3, 0, ((53, 61),)),
    ),
    (
        (1, 0, 2, 2, ((0, 3), (3, 10))),
        (2, 2, 1, 3, ((0, 3),)),
        (1, 0, 1, 2, ((0, 4), (11, 18))),
        (1, 1, 4, 0, ((0, 2), (46, 51), (51, 55), (55, 58))),
        (1, 1, 2, 1, ((1, 9), (16, 19), (20, 37))),
        (2, 2, 2, 3, ((2, 9),)),
        (1, 0, 0, 1, ((4, 13), (17, 21), (32, 46))),
        (1, 2, 0, 0, ((5, 10), (11, 19), (20, 45), (46, 49))),
        (1, 1, 3, 1, ((8, 13), (40, 47), (49, 53))),
        (1, 2, 1, 0, ((13, 18), (48, 54), (54, 57), (57, 59))),
        (2, 1, 1, 3, ((17, 20),)),
        (1, 1, 0, 2, ((18, 21), (46, 50))),
        (1, 1, 1, 1, ((19, 45), (46, 50), (50, 54))),
        (1, 2, 2, 0, ((21, 37), (40, 48), (48, 52), (52, 56))),
    ),
)


class Handle:
    pass


class Parts:
    def __init__(self):
        self.inputs, self.outputs, self.scratch = [], [], []

    def inp(self, array, spec):
        self.inputs.append((Handle(), array, spec))
        return self.inputs[-1][0]

    def out(self, shape, dtype, spec=None):
        self.outputs.append((Handle(), shape_of(shape, dtype), spec or fixed(shape)))
        return self.outputs[-1][0]

    def tmp(self, kind):
        self.scratch.append((Handle(), kind))
        return self.scratch[-1][0]

    def vmem(self, shape, dtype):
        return self.tmp(pltpu.VMEM(shape, dtype))

    def late(self, array, shape=None):
        shape = shape or array.shape
        source = self.inp(array, pl.BlockSpec(memory_space=pl.ANY))
        item = (source, self.vmem(shape, array.dtype), self.tmp(pltpu.SemaphoreType.DMA))
        return item

    def run(self, body, steps, flops, moved, collective):
        handles = [x[0] for x in self.inputs + self.outputs + self.scratch]

        def kernel(*refs):
            body(dict(zip(handles, refs)))

        results = pl.pallas_call(
            kernel,
            grid=(steps,),
            in_specs=[x[2] for x in self.inputs],
            out_specs=[x[2] for x in self.outputs],
            out_shape=[x[1] for x in self.outputs],
            scratch_shapes=[x[1] for x in self.scratch],
            compiler_params=pltpu.CompilerParams(
                dimension_semantics=("arbitrary",),
                vmem_limit_bytes=63 * MIB,
                fuse_transposed_lhs_in_matmul=True,
                collective_id=collective,
                has_side_effects=collective is not None,
            ),
            cost_estimate=pl.CostEstimate(
                flops=int(flops), bytes_accessed=int(moved), transcendentals=0
            ),
        )(*[x[1] for x in self.inputs])
        return dict(zip([x[0] for x in self.outputs], results))


def fetch(refs, item):
    source, target, sem = (refs[h] for h in item)
    if source.shape != target.shape:
        source = source.at[0]
    return pltpu.make_async_copy(source, target, sem)


def fixed(shape):
    return pl.BlockSpec(shape, lambda i: (0,) * len(shape), pipeline_mode=pl.Buffered(1))


def bit_of(me, bit):
    return lax.rem(lax.div(me, bit), 2)


def order_of(key):
    return (1, 4, 2, 8) if key in Z_FIRST else (1, 2, 4, 8)


def put_rows(me, held, layer, chunk, block, shards, base, keep, send, height, rows):
    core = bit_of(me, 1)
    places = {}
    count = height // rows
    for k in range(shards // 2):
        differ = {}
        for bit in (2, 4, 8):
            mine = bit_of(me, bit)
            if bit < shards:
                differ[bit] = 1 - mine if (2 * k // bit) % 2 else mine
            else:
                theirs = bit_of(base, bit)
                differ[bit] = mine + theirs - 2 * mine * theirs
        for which, ref in ((core, keep), (1 - core, send)):
            start = (2 * k + which) * height
            for b in range(count):
                bits = order_of((layer, chunk, block + b))[1:]
                place = 4 * differ[bits[0]] + 2 * differ[bits[1]] + differ[bits[2]]
                ref[place, block + b] = held[pl.ds(pl.multiple_of(start + b * rows, 16), rows)]


class Hop:
    def __init__(self, key, hop, keep, send, got, done, sem, load, flush):
        self.load, self.flush = load, flush
        self.bit, self.hop = order_of(key)[hop], hop
        self.keep, self.send, self.got, self.done, self.sem = keep, send, got, done, sem


class Traffic:
    def __init__(self, parts, number, layer, fresh, state, rows, d, small=None, cross=None):
        legs = HOPS[number]
        self.parts, self.state, self.layer = parts, state, layer
        self.events, self.loads, self.copies = [], [], []
        self.small, self.cross = small, cross
        self.keep, self.send = {}, {}
        self.flushes, self.fresh_flush = [], {}
        self.kept_out, self.done_out = [], []
        bits = set()
        groups = {}
        for leg in legs:
            groups.setdefault(leg[:2], []).append(leg)
        for chunk in fresh:
            groups.setdefault((layer, chunk), [])
        arrays = {}
        count = 0

        def operand(array):
            if id(array) not in arrays:
                arrays[id(array)] = parts.inp(array, pl.BlockSpec(memory_space=pl.ANY))
            return arrays[id(array)]

        for name, members in groups.items():
            made_here = name[0] == layer and name[1] in fresh
            if made_here:
                blocks = list(range(SIZES[name[1]]))
                slots = 8
            else:
                blocks = [leg[2] for leg in members]
                slots = max(8 >> leg[3] for leg in members)
            ends = {leg[2]: leg[3] + len(leg[4]) for leg in members}
            finished = [b for b in blocks if ends.get(b, 0) == 4]
            size = block_shape(name[1], rows, d)
            shape = (slots, len(blocks), *size)
            keep = parts.vmem(shape, bf16)
            keep_out = send_out = None
            if len(finished) < len(blocks):
                keep_out = parts.out(shape, bf16, pl.BlockSpec(memory_space=pl.ANY))
            send = None
            if made_here:
                send = parts.vmem(shape, bf16)
                if not all(ends.get(b, 0) > 0 for b in blocks):
                    send_out = parts.out(shape, bf16, pl.BlockSpec(memory_space=pl.ANY))
                self.keep[name[1]], self.send[name[1]] = keep, send
            flushes = {}
            if finished:
                done = parts.out((len(finished), *size), f32)
                for place, b in enumerate(finished):
                    self.done_out.append((name + (b,), done, place))
            for place, b in enumerate(blocks):
                if b not in finished:
                    sent = send_out if made_here and ends.get(b, 0) == 0 else None
                    self.kept_out.append((name + (b,), keep_out, sent, place))
                    reach = ends.get(b, 0)
                    valid = 8 if reach == 0 else 16 >> reach
                    flushes[b] = [(keep, keep_out, valid, place, len(self.flushes))]
                    self.flushes.append(flushes[b][0])
                    if sent is not None:
                        flushes[b].append((send, send_out, 8, place, len(self.flushes)))
                        self.flushes.append(flushes[b][1])
                    if reach == 0:
                        self.fresh_flush[name[1], b] = flushes[b]
            for hop in range(4):
                users = [leg for leg in members if leg[3] <= hop < leg[3] + len(leg[4])]
                if not users:
                    continue
                got = parts.vmem((8 >> hop, len(users), *size), bf16)
                for index, leg in enumerate(users):
                    key, place = leg[:3], blocks.index(leg[2])
                    load = None
                    half = 8 >> hop
                    if hop == 0 and made_here:
                        source = (send, place, 0)
                    elif hop == 0:
                        source = (operand(state[key][1]), state[key][2], 0)
                    elif hop == leg[3]:
                        source = (operand(state[key][0]), state[key][2], half)
                    else:
                        source = (keep, place, half)
                    if hop == leg[3] and not made_here:
                        load = (operand(state[key][0]), state[key][2], half, keep, place)
                        load = load + (len(self.loads),)
                        self.loads.append(load)
                    flush = flushes.get(leg[2]) if hop + 1 == ends[leg[2]] else None
                    final = None
                    if hop == 3:
                        final = (done, finished.index(leg[2]))
                    item = Hop(
                        key, hop, (keep, place), source, (got, index), final, count, load, flush
                    )
                    count += 1
                    bits.add(item.bit)
                    start, end = leg[4][hop - leg[3]]
                    self.events.append((end, 0, len(self.events), self.finish, item))
                    self.events.append((start, 1, len(self.events), self.begin, item))
        if small is not None:
            self.total = parts.vmem(small[0], f32)
            self.small_got = parts.vmem((4,) + small[0], f32)
            self.small_out = parts.out(small[0], f32)
            bits |= {1, 2, 4, 8}
            for hop, (start, end) in enumerate(small[1]):
                item = (hop, count + hop)
                self.events.append((end, 0, len(self.events), self.small_finish, item))
                self.events.append((start, 1, len(self.events), self.small_begin, item))
            count += 4
        if cross is not None:
            self.cross_out = parts.vmem(cross[0], bf16)
            self.cross_got = parts.vmem(cross[0], bf16)
            self.cross_in = parts.out(cross[0], bf16)
            for first, size, start, end in cross[1]:
                item = (first, size, count)
                self.events.append((end, 0, len(self.events), self.cross_finish, item))
                self.events.append((start, 1, len(self.events), self.cross_begin, item))
                count += 1
        self.sent = parts.tmp(pltpu.SemaphoreType.DMA((count,)))
        self.arrived = parts.tmp(pltpu.SemaphoreType.DMA((count,)))
        self.loaded = None
        if self.loads:
            self.loaded = parts.tmp(pltpu.SemaphoreType.DMA((len(self.loads),)))
        self.flushed = None
        if self.flushes:
            self.flushed = parts.tmp(pltpu.SemaphoreType.DMA((len(self.flushes),)))
        self.bits = sorted(bits)
        self.events.sort(key=lambda e: e[:3])

    def bind(self, refs, step):
        self.refs, self.step = refs, step
        self.me, self.side = lax.axis_index("wide"), lax.axis_index("narrow")

    def device(self, bit):
        return {"wide": self.me + bit - 2 * bit * bit_of(self.me, bit)}

    def load_copy(self, load):
        source, place, slots, keep, at, index = load
        return pltpu.make_async_copy(
            self.refs[source].at[pl.ds(0, slots), place],
            self.refs[keep].at[pl.ds(0, slots), at],
            self.refs[self.loaded].at[index],
        )

    def flush_copy(self, flush):
        source, target, slots, place, index = flush
        return pltpu.make_async_copy(
            self.refs[source].at[pl.ds(0, slots), place],
            self.refs[target].at[pl.ds(0, slots), place],
            self.refs[self.flushed].at[index],
        )

    def open(self):
        barrier = pltpu.get_barrier_semaphore()
        peers = [self.device(bit) for bit in self.bits]
        if self.cross is not None:
            peers.append({"narrow": 1 - self.side})
        for peer in peers:
            pl.semaphore_signal(barrier, inc=1, device_id=peer, device_id_type=MESH)
        for load in self.loads:
            self.load_copy(load).start()
        pl.semaphore_wait(barrier, len(peers))

    def made(self, chunk, block):
        for flush in self.fresh_flush.get((chunk, block), ()):
            self.flush_copy(flush).start()

    def settle(self):
        @pl.when(self.step == self.steps - 1)
        def _():
            for flush in self.flushes:
                self.flush_copy(flush).wait()

    def remote(self, source, target, index, device):
        return pltpu.make_async_remote_copy(
            src_ref=source,
            dst_ref=target,
            send_sem=self.refs[self.sent].at[index],
            recv_sem=self.refs[self.arrived].at[index],
            device_id=device,
            device_id_type=MESH,
        )

    def copy(self, item):
        slots = 8 >> item.hop
        handle, place, low = item.send
        source = self.refs[handle].at[pl.ds(low, slots), place]
        target = self.refs[item.got[0]].at[pl.ds(0, slots), item.got[1]]
        return self.remote(source, target, item.sem, self.device(item.bit))

    def begin(self, item):
        self.copy(item).start()

    def finish(self, item):
        self.copy(item).wait()
        if item.load is not None:
            self.load_copy(item.load).wait()
        keep, at = self.refs[item.keep[0]], item.keep[1]
        got, place = self.refs[item.got[0]], item.got[1]
        if item.hop == 3:
            done, final = self.refs[item.done[0]], item.done[1]
            done[final] = keep[0, at].astype(f32) + got[0, place].astype(f32)
        else:

            @pl.loop(0, 8 >> item.hop)
            def _(slot):
                total = keep[slot, at].astype(f32) + got[slot, place].astype(f32)
                keep[slot, at] = total.astype(bf16)

            for flush in item.flush or ():
                self.flush_copy(flush).start()

    def small_copy(self, item):
        target = self.refs[self.small_got].at[item[0]]
        return self.remote(self.refs[self.total], target, item[1], self.device(1 << item[0]))

    def small_begin(self, item):
        self.small_copy(item).start()

    def small_finish(self, item):
        self.small_copy(item).wait()
        total = self.refs[self.total][...] + self.refs[self.small_got][item[0]]
        self.refs[self.total][...] = total
        if item[0] == 3:
            self.refs[self.small_out][...] = total

    def cross_copy(self, item):
        rows = pl.ds(item[0], item[1])
        device = {"narrow": 1 - self.side}
        source = self.refs[self.cross_out].at[rows]
        return self.remote(source, self.refs[self.cross_got].at[rows], item[2], device)

    def cross_begin(self, item):
        self.cross_copy(item).start()

    def cross_finish(self, item):
        self.cross_copy(item).wait()
        rows = pl.ds(item[0], item[1])
        self.refs[self.cross_in][rows] = self.refs[self.cross_got][rows]

    def fire(self, low, high=None):
        high = low + 1 if high is None else high

        def spot(time):
            return min(time // 8, self.steps - 1)

        found = [e for e in self.events if low <= e[0] - 8 * spot(e[0]) < high]
        for at in sorted({spot(e[0]) for e in found}):

            @pl.when(self.step == at)
            def _(at=at):
                for event in found:
                    if spot(event[0]) == at:
                        event[3](event[4])

    def close(self, results, finals):
        for key, keep, sent, place in self.kept_out:
            self.state[key] = (results[keep], None if sent is None else results[sent], place)
        for key, done, place in self.done_out:
            self.state.pop(key, None)
            finals[key] = (results[done], place)


def ff_back(number, layer, grads, lengths, saved, weights, state, finals):
    _, attn_out, ff_up, ff_down, _, gains, _ = weights
    unit1, scale1, rb, act, slope, unit2, scale2, blended = saved
    n, d = unit1.shape
    rows = d // 16
    tiles = act.shape[1] // d
    front = SIZES[DOWN]
    cut = d // front
    steps = front + tiles + 1
    top = len(grads) == 1
    parts = Parts()
    later = lambda i: jnp.clip(i - front, 0, tiles - 1)
    h_count = parts.inp(lengths, scalar_spec())
    h_grads = [parts.inp(grad, fixed((n, d))) for grad in grads]
    l_act = parts.late(act)
    h_slope = parts.inp(slope, pl.BlockSpec((n, d), lambda i: (0, later(i))))
    h_wd = parts.inp(ff_down, pl.BlockSpec((None, d, d), lambda i: (0, later(i), 0)))
    h_wu = parts.inp(ff_up, pl.BlockSpec((None, d, d), lambda i: (0, 0, later(i))))
    l_wo = parts.late(attn_out, (d, d))
    h_gains = parts.inp(gains, fixed((None, 2, d)))
    l_unit1, h_scale1 = parts.late(unit1), parts.inp(scale1, fixed((n, 1)))
    h_unit2, h_scale2 = parts.inp(unit2, fixed((n, d))), parts.inp(scale2, fixed((n, 1)))
    l_rb, l_blended = parts.late(rb), parts.late(blended)
    lates = (l_act, l_rb, l_unit1, l_wo, l_blended)
    h_act, h_rb, h_unit1, h_wo, h_blended = (item[1] for item in lates)
    h_gr, h_do = parts.out((n, d), f32), parts.out((n, d), bf16)
    h_sums = parts.out((16, d), f32)
    h_acc, h_gb = parts.vmem((n, d), f32), parts.vmem((n, d), bf16)
    h_turned, h_held = parts.vmem((d, n), bf16), parts.vmem((d, d), bf16)
    h_cols = parts.vmem((front, n, cut), bf16)
    h_tall = parts.vmem((tiles * d, cut), bf16)
    traffic = Traffic(parts, number, layer, (DOWN, UP), state, rows, d)
    traffic.steps = steps

    def body(refs):
        step = pl.program_id(0)
        traffic.bind(refs, step)
        me = traffic.me
        sums, acc, gb = refs[h_sums], refs[h_acc], refs[h_gb]
        turned, held = refs[h_turned], refs[h_held]

        @pl.when(step == 0)
        def _():
            traffic.open()

        traffic.fire(0)

        @pl.when(step == 0)
        def _():
            for item in lates:
                fetch(refs, item).start()

            def strip(rows, carry):
                g = refs[h_grads[0]][rows].astype(f32)
                if top:
                    row = lax.broadcasted_iota(jnp.int32, (16, 1), 0) + rows.start
                    g = jnp.where(row < count_of(refs[h_count]), g, 0.0)
                else:
                    g = g + refs[h_grads[1]][rows].astype(f32)
                unit = refs[h_unit2][rows]
                back = normalise_back(g, unit, refs[h_scale2][rows], refs[h_gains][1:2])
                acc[rows] = back
                low = back.astype(bf16)
                gb[rows] = low
                for index in range(front):
                    refs[h_cols][index, rows] = low[:, index * cut : (index + 1) * cut]
                found = (low.astype(f32), g, g * unit)
                return tuple(a + fold(b) for a, b in zip(carry, found))

            zero = jnp.zeros((8, d), f32)
            found = each_strip(n, 16, strip, (zero, zero, zero))
            sums[0:8] = zero
            sums[8:16] = zero
            for at, value in zip((4, 5, 7), found):
                sums[at : at + 1] = jnp.sum(value, axis=0, keepdims=True)
            fetch(refs, l_act).wait()

        @pl.when(step < front)
        def _():
            refs[h_tall][...] = tn(refs[h_act][...], refs[h_cols][step]).astype(bf16)

        for block in range(front):

            @pl.when(step == block)
            def _(block=block):
                keep, send = refs[traffic.keep[DOWN]], refs[traffic.send[DOWN]]
                height = rows * tiles
                put_rows(
                    me, refs[h_tall], layer, DOWN, block, 16, 0, keep, send, height, height
                )
                traffic.made(DOWN, block)

        @pl.when(step == front)
        def _():
            fetch(refs, l_rb).wait()
            turned[...] = refs[h_rb][...].T

        middle = (step >= front) & (step < front + tiles)

        @pl.when(middle)
        def _():
            grad = nt(gb[...], refs[h_wd][...]) * refs[h_slope][...].astype(f32)
            grad = grad.astype(bf16)
            sums[pl.ds(8 + step - front, 1)] = jnp.sum(grad.astype(f32), axis=0, keepdims=True)
            held[0:n] = grad

        traffic.fire(1)

        @pl.when(middle)
        def _():
            acc[...] += nt(held[0:n], refs[h_wu][...])

        traffic.fire(2)

        @pl.when(middle)
        def _():
            held[...] = nn(turned[...], held[0:n]).astype(bf16)

        @pl.when(step == front + tiles)
        def _():
            for item in (l_unit1, l_wo, l_blended):
                fetch(refs, item).wait()
            turned[...] = refs[h_blended][...].T

            def strip(rows, carry):
                g = acc[rows]
                unit = refs[h_unit1][rows]
                back = normalise_back(g, unit, refs[h_scale1][rows], refs[h_gains][0:1])
                refs[h_gr][rows] = back
                low = back.astype(bf16)
                gb[rows] = low
                found = (low.astype(f32), g, g * unit)
                return tuple(a + fold(b) for a, b in zip(carry, found))

            zero = jnp.zeros((8, d), f32)
            found = each_strip(n, 16, strip, (zero, zero, zero))
            for at, value in zip((2, 3, 6), found):
                sums[at : at + 1] = jnp.sum(value, axis=0, keepdims=True)
            low = gb[...]
            refs[h_do][...] = nt(low, refs[h_wo][...]).astype(bf16)
            held[...] = nn(turned[...], low).astype(bf16)

        for block in range(tiles + 1):

            @pl.when(step == front + block)
            def _(block=block):
                keep, send = refs[traffic.keep[UP]], refs[traffic.send[UP]]
                put_rows(me, held, layer, UP, block, 16, 0, keep, send, rows, rows)
                traffic.made(UP, block)

        traffic.fire(5, 1000)
        traffic.settle()

    results = parts.run(body, steps, 2 * n * d * d * (4 * tiles), 4 * d * d * tiles, number)
    traffic.close(results, finals)
    return results[h_gr], results[h_do], results[h_sums]


def attn_back(
    number, layer, arrays, offsets, blended, grad_blended, soft, boxes, weight, left_rows,
    residual, small, state, finals,
):
    n, d = grad_blended.shape
    per_shard = d // 16
    groups = 3
    wide = d // groups
    heads = H // groups
    boxed = boxes is not None
    halves = 1 if boxed else 2
    front = halves * groups
    steps = front + groups
    keys = soft.shape[2]
    spans = [(0, keys)] if boxed else [(0, 384), (384, keys)]
    parts = Parts()
    early = lambda i: jnp.where(i < front, lax.rem(i, groups), groups - 1)
    later = lambda i: jnp.clip(i - front, 0, groups - 1)

    def wide_block(offset):
        return pl.BlockSpec((n, wide), lambda i: (0, early(i) + offset // 2))

    h_q, h_k, h_v = (parts.inp(a, wide_block(o)) for a, o in zip(arrays, offsets))
    h_g = parts.inp(grad_blended, wide_block(0))
    h_o = parts.inp(blended, wide_block(0))
    h_p = parts.inp(soft, pl.BlockSpec((heads, n, keys), lambda i: (early(i), 0, 0)))
    h_kv = [parts.vmem((keys, wide), bf16) for _ in range(2)]
    h_dp = parts.vmem((n, keys), f32)
    h_w = []
    for index in range(3):
        when = early if (not boxed and index > 0) else later
        spec = pl.BlockSpec((None, d, wide), lambda i, w=when, k=index: (0, 0, w(i) + groups * k))
        h_w.append(parts.inp(weight, spec))
    l_left = [parts.late(rows) for rows in left_rows]
    h_turned = [parts.vmem((d, n), bf16) for rows in left_rows]
    l_gr = parts.late(residual)
    h_gr = l_gr[1]
    h_own = parts.out((n, d), f32)
    h_sums1 = parts.vmem((8, d), f32) if boxed else parts.out((8, d), f32)
    h_d = [parts.vmem((groups, n, wide), bf16) for _ in range(3)]
    h_ds, h_held = parts.vmem((n, keys), bf16), parts.vmem((d, d), bf16)
    if boxed:
        h_lengths = parts.inp(boxes[0], scalar_spec())
        h_boxes = parts.inp(boxes[1], fixed((None, 4, TEXT)))
        h_patches = parts.inp(patch_centres(n, keys), fixed((4, keys)))
        h_near = [parts.vmem((n, keys), bf16) for _ in range(2)]
        h_small1, h_small2 = (parts.inp(x, fixed((16, d))) for x in small[:2])
        h_sums2 = parts.inp(small[2], fixed((8, d)))
        h_hot_i, h_hot_j = parts.vmem((32, n), bf16), parts.vmem((keys, 128), bf16)
        h_step_x, h_step_y = parts.vmem((n, keys), bf16), parts.vmem((n, keys), bf16)
        h_far, h_tab = parts.vmem((n, 384), f32), parts.vmem((2 * H, 128), f32)
        times = ((21, 29), (29, 37), (37, 45), (45, 47))
        traffic = Traffic(
            parts, number, layer, (IN,), state, per_shard, d, small=((32, d), times)
        )
    else:
        h_acc = parts.vmem((n, d), f32)
        h_half = parts.vmem((groups, n, wide), f32)
        cross = [(0, 384, 21, 69), (384, n - 384, 45, 69)]
        traffic = Traffic(parts, number, layer, (IN,), state, per_shard, d, cross=((n, d), cross))
    traffic.steps = steps

    def body(refs):
        step = pl.program_id(0)
        traffic.bind(refs, step)
        me = traffic.me
        turned = [refs[h] for h in h_turned]
        dq, dk, dv = (refs[h] for h in h_d)
        wq, wk, wv = (refs[h] for h in h_w)
        own, held, ds_s = refs[h_own], refs[h_held], refs[h_ds]

        @pl.when(step == 0)
        def _():
            traffic.open()

        traffic.fire(0)

        @pl.when(step == 0)
        def _():
            for item in [*l_left, l_gr]:
                fetch(refs, item).start()
            for h in h_kv:
                refs[h][n:keys] = jnp.zeros((keys - n, wide), bf16)
            if boxed:
                row, col = centres_of(refs[h_lengths], refs[h_boxes][...], refs[h_patches][...])
                cx, cy = col[0:n, 0:1], col[0:n, 1:2]
                rx, ry = row[0:1, 0:n], row[1:2, 0:n]
                hots = hot_columns(cx, cy, n, reverse=True)
                lane = lax.broadcasted_iota(jnp.int32, (n, 128), 1)
                refs[h_hot_j][0:n] = jnp.where(lane < 32, hots, 0.0).astype(bf16)
                refs[h_hot_j][n:keys] = jnp.zeros((keys - n, 128), bf16)
                line = lax.broadcasted_iota(jnp.int32, (32, n), 0)
                cell = jnp.where(line < 16, rx >> 6, ry >> 6)
                refs[h_hot_i][...] = jnp.where(cell == (line & 15), 1.0, 0.0).astype(bf16)
                for h, c, r in ((h_step_x, cx, rx), (h_step_y, cy, ry)):
                    refs[h][:, 0:n] = jnp.where((c & 63) < (r & 63), 1.0, 0.0).astype(bf16)
                    refs[h][:, n:keys] = jnp.zeros((n, keys - n), bf16)

        def table_lines(head):
            far = refs[h_far]
            value = far[...]
            upper = value.astype(bf16)
            lower = (value - upper.astype(f32)).astype(bf16)
            hi = refs[h_hot_i][...]
            cells = nn(hi, upper) + nn(hi, lower)
            lane = lax.broadcasted_iota(jnp.int32, (16, 128), 1)
            for direction in range(2):
                rows = slice(16 * direction, 16 * direction + 16)
                level = cells[rows, 0:128]
                above = cells[rows, 128 * (direction + 1) : 128 * (direction + 2)]
                inside = (lane >= 16 * direction) & (lane < 16 * direction + 16)
                level = jnp.where(inside, level - above, 0.0)
                above = jnp.where(inside, above, 0.0)
                turn = (128 + 1 - 16 * direction) % 128
                line = pltpu.roll(level, turn, 1, stride=1, stride_axis=0)
                turn = (turn + 127) % 128
                line = line + pltpu.roll(above, turn, 1, stride=1, stride_axis=0)
                line = jnp.sum(line, axis=0, keepdims=True) * HD**0.5
                refs[h_tab][pl.ds(2 * heads * step + 2 * head + direction, 1)] = line

        def head_back(head, half):
            pair, h = head // 2, head % 2
            lanes = slice(128 * pair, 128 * pair + 128)
            low_key, high_key = spans[half]
            span, ends = slice(low_key, high_key), slice(low_key, min(high_key, n))
            group = step - half * groups
            mask = head_masks()[h]
            q, k, v, g = (refs[x][:, lanes] for x in (h_q, h_kv[0], h_kv[1], h_g))
            k, v = k[span], v[span]
            dp_s = refs[h_dp]
            dp_s[:, span] = nt(g * mask, v)
            tiles = [slice(t, t + 128) for t in range(low_key, high_key, 128)]
            for r in range(0, n, SUB):
                rows = slice(r, r + SUB)
                mean = (g[rows] * mask).astype(f32) * refs[h_o][rows, lanes]
                mean = jnp.sum(mean, axis=-1, keepdims=True)
                for t in tiles:
                    ds = refs[h_p][head, rows, t].astype(f32) * (dp_s[rows, t] - mean)
                    ds = ds.astype(bf16)
                    ds_s[rows, t] = ds
                    if boxed:
                        refs[h_near[0]][rows, t] = ds * refs[h_step_x][rows, t]
                        refs[h_near[1]][rows, t] = ds * refs[h_step_y][rows, t]
            if boxed:
                hj, far = refs[h_hot_j][...], refs[h_far]
                queries = nn(ds_s[...], jnp.concatenate([k, hj], axis=1))
                far[:, 0:128] = queries[:, 128:]
                queries = queries[:, :128]
                far[:, 128:256] = nn(refs[h_near[0]][...], hj)
                far[:, 256:384] = nn(refs[h_near[1]][...], hj)
            else:
                queries = nn(ds_s[:, span], k)
            count = ends.stop - ends.start
            values = (tn(ds_s[:, span], q)[:count], tn(refs[h_p][head, :, span], g)[:count])
            if boxed:
                table_lines(head)
            outs = []
            low = low_lanes(count)
            for ref, value in zip((dk, dv), values):
                value = value.astype(bf16)
                if h == 0:
                    ref[group, ends, lanes] = value
                else:
                    value = jnp.where(low, ref[group, ends, lanes].astype(f32), value.astype(f32))
                    ref[group, ends, lanes] = value.astype(bf16)
                    outs.append(jnp.sum(value, axis=0, keepdims=True))
            low = low_lanes(n)
            if halves == 2:
                half_s = refs[h_half]
                if half == 0 and h == 0:
                    half_s[group, :, lanes] = queries
                elif half == 0:
                    half_s[group, :, lanes] = jnp.where(low, half_s[group, :, lanes], queries)
                else:
                    queries = half_s[group, :, lanes] + queries
            if half == halves - 1:
                queries = queries.astype(bf16)
                if h == 1:
                    queries = jnp.where(
                        low, dq[group, :, lanes].astype(f32), queries.astype(f32)
                    )
                    outs.append(jnp.sum(queries, axis=0, keepdims=True))
                dq[group, :, lanes] = queries.astype(bf16)
            if h == 1:
                start = pl.multiple_of(group * wide + 128 * pair, 128)
                at = pl.ds(start, 128)
                sums = refs[h_sums1]
                if half == 0:
                    sums[1:2, at] = outs[1]
                else:
                    sums[1:2, at] += outs[1]
                if half == halves - 1:
                    sums[0:1, at] = outs[2]

        if not boxed:

            @pl.when(step == 0)
            def _():
                refs[h_sums1][...] = jnp.zeros((8, d), f32)

        @pl.when(step < front)
        def _():
            refs[h_kv[0]][0:n] = refs[h_k][...]
            refs[h_kv[1]][0:n] = refs[h_v][...]

        for head in range(heads):
            for half in range(halves):

                @pl.when((step >= half * groups) & (step < half * groups + groups))
                def _(head=head, half=half):
                    head_back(head, half)

            traffic.fire(1 + head)

        @pl.when(step == (0 if boxed else front - 1))
        def _():
            for target, item in zip(turned, l_left):
                fetch(refs, item).wait()
                target[...] = refs[item[1]][...].T
            fetch(refs, l_gr).wait()

        def gradient(group):
            for index, ref in enumerate((dq, dk, dv)):
                left = turned[min(index, len(turned) - 1)]
                held[:, index * wide : (index + 1) * wide] = nn(left[...], ref[group]).astype(bf16)

        def store_gradient(start):
            for block in range(groups):

                @pl.when(step == start + block)
                def _(block=block):
                    keep, send = refs[traffic.keep[IN]], refs[traffic.send[IN]]
                    put_rows(
                        me, held, layer, IN, block, 16, 0, keep, send, per_shard, per_shard
                    )
                    traffic.made(IN, block)

        if boxed:

            @pl.when(step < groups)
            def _():
                gradient(step)

            store_gradient(0)

            @pl.when(step == groups - 1)
            def _():
                total = refs[traffic.total]
                total[0:16] = refs[h_small1][...]
                total[0:2] = refs[h_sums1][0:2]
                total[16:32] = refs[h_small2][...]
                total[16:18] = refs[h_sums2][0:2]
                each = d // 128
                for index in range(2 * H):
                    at = 128 * (index % each)
                    row = 12 + index // each
                    total[row : row + 1, at : at + 128] = refs[h_tab][index : index + 1]

        else:

            acc = refs[h_acc]
            for half, (low_key, high_key) in enumerate(spans):
                rows = slice(low_key, min(high_key, n))
                for group in range(groups):

                    @pl.when(step == half * groups + group)
                    def _(rows=rows, group=group):
                        value = nt(dk[group, rows], wk[...]) + nt(dv[group, rows], wv[...])
                        if group > 0:
                            value = value + acc[rows]
                        if group < groups - 1:
                            acc[rows] = value
                        else:
                            refs[traffic.cross_out][rows] = value.astype(bf16)

        @pl.when(step >= front)
        def _():
            group = step - front
            value = nt(dq[group], wq[...])
            if boxed:
                value = value + nt(dk[group], wk[...]) + nt(dv[group], wv[...])
            else:
                gradient(group)

            @pl.when(step == front)
            def _():
                own[...] = refs[h_gr][...] + value

            @pl.when(step > front)
            def _():
                own[...] += value

        if not boxed:
            store_gradient(front)
        traffic.fire(5, 1000)
        traffic.settle()

    results = parts.run(
        body, steps, 16 * n * n * d + 12 * n * d * d, 2 * H * n * n, number
    )
    traffic.close(results, finals)
    extra = results[traffic.small_out] if boxed else results[traffic.cross_in]
    return results[h_own], None if boxed else results[h_sums1], extra


def finish_outputs(me, finals, small, own, rows, d):
    tiles = 4
    share = d // 16
    cut = d // SIZES[DOWN]
    parts = Parts()
    h_me = parts.inp(me, scalar_spec())
    h_small = parts.inp(small, fixed(small.shape))
    arrays = {}
    for array, _ in finals.values():
        if id(array) not in arrays:
            arrays[id(array)] = parts.inp(array, fixed(array.shape))
    layers = []
    for _ in range(2):
        layers.append(
            (
                parts.out((rows, 3 * d), f32),
                parts.out((rows, d), f32),
                parts.out((rows, tiles * d), f32),
                parts.out((rows * tiles, d), f32),
                parts.out((6, 1, share), f32),
                parts.out((2, share), f32),
                parts.out((1, tiles * share), f32),
            )
        )
    h_table = parts.out((1, share), f32)
    h_own, h_stream = parts.inp(own, fixed(own.shape)), parts.out(own.shape, f32)

    def body(refs):
        me = refs[h_me][0]
        refs[h_stream][...] = refs[h_own][...]
        back = lax.rem(d - share * me, d)
        for layer, outs in zip((1, 2), layers):

            def block(chunk, index):
                array, place = finals[(layer, chunk, index)]
                return refs[arrays[id(array)]][place]

            wide = d // 3
            for group in range(3):
                value = block(IN, group)
                for part in range(3):
                    at = part * d + group * wide
                    refs[outs[0]][:, at : at + wide] = value[:, part * wide : (part + 1) * wide]
            refs[outs[1]][...] = block(UP, tiles)
            for index in range(tiles):
                refs[outs[2]][:, index * d : (index + 1) * d] = block(UP, index)
            for index in range(SIZES[DOWN]):
                refs[outs[3]][:, index * cut : (index + 1) * cut] = block(DOWN, index)
            base = 16 * (layer - 1)
            turned = pltpu.roll(refs[h_small][base : base + 8], back, 1)
            for index in range(6):
                refs[outs[4]][index] = turned[index : index + 1, :share]
            refs[outs[5]][...] = turned[6:8, :share]
            each = tiles * share
            line = jnp.zeros((1, d), f32)
            for index in range(tiles):
                row = refs[h_small][base + 8 + index : base + 9 + index]
                line = jnp.where(lax.div(me, 16 // tiles) == index, row, line)
            inner = lax.rem(me, 16 // tiles)
            turned = pltpu.roll(jnp.broadcast_to(line, (8, d)), lax.rem(d - each * inner, d), 1)
            refs[outs[6]][...] = turned[0:1, :each]
        direction = lax.div(me, 8)
        first = 4 * lax.rem(me, 8)
        line = jnp.zeros((1, 128), f32)
        lane = lax.broadcasted_iota(jnp.int32, (1, 128), 1)
        for head in range(H):
            found = []
            for way in range(2):
                index = 2 * head + way
                at = 128 * (index % (d // 128))
                row = 12 + index // (d // 128)
                found.append(refs[h_small][row : row + 1, at : at + 128])
            values = jnp.where(direction == 0, found[0], found[1])
            for bucket in range(4):
                value = jnp.sum(jnp.where(lane == first + bucket, values, 0.0))
                line = jnp.where(lane == H * bucket + head, value, line)
        refs[h_table][...] = line[:, :share]

    results = parts.run(body, 1, 1, 8 * rows * d, None)
    done = []
    for outs in layers:
        values = [results[h] for h in outs]
        vectors = jnp.transpose(values[4], (1, 0, 2))
        done.append(tuple(v[None] for v in values[:4]) + (vectors, values[5][None], values[6]))
    return results[h_stream], done[0], done[1], results[h_table]


def backward_with_hops(me, first, second, saved_one, saved_two, one, two, extra):
    top, lengths, boxes, own_b, mid_b, partner_b, soft_one, soft_two, full_one, full_two = extra
    d = own_b.shape[1]
    state, finals = {}, {}
    gr, do, small_two = ff_back(0, 2, [top], lengths, saved_two, second, state, finals)
    own, sums_two, returned = attn_back(
        1, 2, *two, full_two, do, soft_two, None, second[0], [mid_b, partner_b], gr, None, state, finals
    )
    gr, do, small_one = ff_back(
        2, 1, [own, returned], lengths, saved_one, first, state, finals
    )
    own, _, small = attn_back(
        3, 1, *one, full_one, do, soft_one, (lengths, boxes), first[0], [own_b], gr,
        (small_one, small_two, sums_two), state, finals,
    )
    return finish_outputs(me, finals, small, own, d // 16, d)


def swap(value, axis, bit):
    size = lax.axis_size(axis)
    return lax.ppermute(value, axis, [(i, i ^ bit) for i in range(size)])


def reduce_slots(parts, axis):
    keep, send = parts
    bit = 1
    while True:
        got = swap(send, axis, bit)
        count = keep.shape[0]
        if count == 1:
            return keep[0].astype(f32) + got[0].astype(f32)
        half = count // 2
        send = (keep[half:].astype(f32) + got[half:].astype(f32)).astype(keep.dtype)
        keep = (keep[:half].astype(f32) + got[:half].astype(f32)).astype(keep.dtype)
        bit *= 2


def reduce_small(rows, me, axis):
    size = lax.axis_size(axis)
    count = rows.shape[0]
    cut = jnp.transpose(rows.reshape(count, size, -1), (1, 0, 2))
    cut = jnp.take(cut, jnp.arange(size, dtype=jnp.int32) ^ me, axis=0)
    bit = 1
    while bit < size:
        pairs = cut.reshape(cut.shape[0] // 2, 2, *cut.shape[1:])
        cut = pairs[:, 0] + swap(pairs[:, 1], axis, bit)
        bit *= 2
    return cut[0]


def body(
    stream,
    lengths,
    layout_boxes,
    self_attn_in,
    self_attn_out,
    self_ff_up,
    self_ff_down,
    self_vectors,
    self_gains,
    self_up_bias,
    cross_attn_in,
    cross_attn_out,
    cross_ff_up,
    cross_ff_down,
    cross_vectors,
    cross_gains,
    cross_up_bias,
    box_table,
    cotangent,
):
    pair = lengths.T
    place = lax.axis_index("wide")
    devices = lax.axis_size("wide")
    me = place.astype(jnp.int32).reshape(1)
    n, d = stream.shape[2:]
    ff = self_ff_up.shape[2]
    first = (
        self_attn_in,
        self_attn_out,
        self_ff_up,
        self_ff_down,
        jnp.transpose(self_vectors, (1, 0, 2)),
        self_gains,
        self_up_bias,
    )
    second = (
        cross_attn_in,
        cross_attn_out,
        cross_ff_up,
        cross_ff_down,
        jnp.transpose(cross_vectors, (1, 0, 2)),
        cross_gains,
        cross_up_bias,
    )
    own_b = stream.reshape(n, d)
    top = cotangent.reshape(n, d)
    found = attend_forward(
        own_b, own_b, False, self_attn_in, first[4], pair, False, layout_boxes, box_table
    )
    *rows_one, blend_one, soft_one, full_one = found
    one = (rows_one, (0, 0, 0))
    if devices == 16:
        saved_one = feed_forward_sending(blend_one, own_b, first, cross_attn_in, second[4])
        *saved_one, partner_b, q_two = saved_one
    else:
        saved_one = feed_forward(blend_one, own_b, first, pair, False)
        partner_b = swap(saved_one[-1], "narrow", 1)
        q_two = saved_one[-1]
    unit_one, scale_one, rb_one, act_one, slope_one, unit_two, scale_two, mid, mid_b = saved_one
    found = attend_forward(
        q_two, partner_b, devices == 16, cross_attn_in, second[4], pair, True, None, None
    )
    *rows_two, blend_two, soft_two, full_two = found
    two = (rows_two, (0, 0, 0))
    saved_two = feed_forward(blend_two, mid, second, pair, True)
    unit_three, scale_three, rb_two, act_two, slope_two, unit_four, scale_four, final = saved_two

    side = lax.axis_index("narrow")
    own_count = jnp.where(side == 0, lengths[0], lengths[1])
    slot = jnp.arange(n, dtype=jnp.int32)
    padding = ((0, 0), (0, n - TEXT))
    boxes = layout_boxes[0]
    text = jnp.pad((boxes[:2] + boxes[2:]) >> 1, padding)
    grid_side = jnp.where(own_count > GRID_LO * GRID_LO, GRID_HI, GRID_LO).astype(jnp.int32)
    patch = jnp.stack([slot % grid_side, slot // grid_side])
    patch = (patch * 1000 + 500) // grid_side
    centres = jnp.where(side == 0, text, patch)
    places = (centres.T, centres)

    if devices == 16:
        saved = (unit_one, scale_one, rb_one, act_one, slope_one, unit_two, scale_two, blend_one)
        later = (
            unit_three, scale_three, rb_two, act_two, slope_two, unit_four, scale_four, blend_two
        )
        extra = (
            top, pair, layout_boxes, own_b, mid_b, partner_b, soft_one, soft_two, full_one, full_two
        )
        grad_stream, grads_one, grads_two, grad_table = backward_with_hops(
            me, first, second, saved, later, one, two, extra
        )
        return (final[None, None], grad_stream[None, None]) + grads_one + grads_two + (grad_table,)

    def large(parts):
        if len(parts) == 2:
            return reduce_slots(parts, "wide")
        return lax.psum_scatter(parts[0].astype(f32), "wide", scatter_dimension=0, tiled=True)

    def columns(value, lead):
        if value.ndim == 2:
            return value[:, lead[0] * d : lead[1] * d][None]
        picked = value[lead[0] : lead[1]]
        return jnp.transpose(picked, (1, 0, 2)).reshape(1, picked.shape[1], -1)

    dz, gb, sums_four, down_two = down_gradient(
        me, own_count, [top], unit_four, scale_four, cross_gains, act_two, devices, True
    )
    down_two = large(down_two)
    du, ups_two, ga, gr, do, sums_three = feed_backward(
        dz, gb, slope_two, unit_three, scale_three, second
    )
    steps = ff // d
    jobs = [(0, 0, 0)] * steps + [(1, 1, 0)]
    up_two = large(weight_gradients(me, jobs, [rb_two, blend_two], [du, ga], devices))
    dq, dk, dv, sums_two_attn = attend_backward(*two, do, soft_two, None)
    grad_partner = project_back([dk, dv], cross_attn_in, 1, None, bf16)
    returned = swap(grad_partner, "narrow", 1)
    grad_own = project_back([dq], cross_attn_in, 0, gr, f32)
    in_two = large(
        weight_gradients(
            me, [(0, 0, 0), (1, 1, 0), (1, 2, 0)], [mid_b, partner_b], [dq, dk, dv], devices
        )
    )

    dz, gb, sums_two, down_one = down_gradient(
        me, own_count, [grad_own, returned], unit_two, scale_two, self_gains, act_one, devices, False
    )
    down_one = large(down_one)
    du, ups_one, ga, gr, do, sums_one = feed_backward(
        dz, gb, slope_one, unit_one, scale_one, first
    )
    up_one = large(weight_gradients(me, jobs, [rb_one, blend_one], [du, ga], devices))
    dq, dk, dv, sums_one_attn, grad_tables = attend_backward(*one, do, soft_one, places)
    in_one = large(
        weight_gradients(
            me, [(0, 0, 0), (0, 1, 0), (0, 2, 0)], [own_b], [dq, dk, dv], devices
        )
    )
    grad_stream = project_back([dq, dk, dv], self_attn_in, 0, gr, f32)

    def ups_rows(ups):
        return jnp.transpose(
            ups.reshape(devices, steps, d // devices), (1, 0, 2)
        ).reshape(steps, d)

    table_row = jnp.transpose(
        grad_tables.reshape(H, 2, 128)[:, :, :NB], (1, 2, 0)
    ).reshape(1, 2 * NB * H)
    small = jnp.concatenate(
        [
            sums_one_attn[:2],
            sums_one[2:3],
            sums_one[1:2],
            sums_two[2:3],
            sums_two[1:2],
            sums_one[0:1],
            sums_two[0:1],
            ups_rows(ups_one),
            sums_two_attn[:2],
            sums_three[2:3],
            sums_three[1:2],
            sums_four[2:3],
            sums_four[1:2],
            sums_three[0:1],
            sums_four[0:1],
            ups_rows(ups_two),
            table_row,
        ]
    )
    small = reduce_small(small, me, "wide")
    half = 8 + steps

    def layer(values, base, inside, up, down):
        return (
            columns(inside, (0, 3)),
            columns(up, (steps, steps + 1)),
            columns(up, (0, steps)),
            down[None],
            values[base : base + 6][None],
            values[base + 6 : base + 8][None],
            values[base + 8 : base + half].reshape(1, -1),
        )

    return (
        (final[None, None], grad_stream[None, None])
        + layer(small, 0, in_one, up_one, down_one)
        + layer(small, half, in_two, up_two, down_two)
        + (small[2 * half :],)
    )


def solution(mesh):
    matrix = P("narrow", None, None)
    layer_in = (matrix,) * 6 + (P("narrow", None),)
    rows = P("narrow", "wide", None, None)
    in_specs = (
        (rows, P(None, "wide"), P("wide", None, None))
        + layer_in * 2
        + (P("narrow", None), rows)
    )
    layer_out = (P("narrow", "wide", None),) * 4 + (
        P("narrow", None, "wide"),
        P("narrow", None, "wide"),
        P("narrow", "wide"),
    )
    out_specs = (rows, rows) + layer_out * 2 + (P("narrow", "wide"),)
    return jax.shard_map(body, mesh=mesh, in_specs=in_specs, out_specs=out_specs, check_vma=False)
```

```python
import functools

import jax
import jax.numpy as jnp
import numpy as np
from jax import lax
from jax.experimental import pallas as pl
from jax.experimental.pallas import tpu as pltpu
from jax.sharding import PartitionSpec as P

H = 12
HD = 64
NB = 32
TEXT = 512
GRID_LO = 16
GRID_HI = 24
PAIRS = H // 2
STRIP = 192
SUB = 32
MIB = 1 << 20

norm_eps = 1e-05
spacing = 64
masked_score = -1e30

f32 = jnp.float32
bf16 = jnp.bfloat16
SMEM = pltpu.MemorySpace.SMEM


def nn(left, right):
    return lax.dot_general(left, right, (((1,), (0,)), ((), ())), preferred_element_type=f32)


def nt(left, right):
    return lax.dot_general(left, right, (((1,), (1,)), ((), ())), preferred_element_type=f32)


def tn(left, right):
    return lax.dot_general(left, right, (((0,), (0,)), ((), ())), preferred_element_type=f32)


def whole(shape):
    return pl.BlockSpec(shape, lambda i: (0,) * len(shape))


def scalar_spec():
    return pl.BlockSpec(memory_space=SMEM)


def call(kernel, grid, in_specs, out_specs, out_shape, scratch, flops, moved, vmem=63):
    return pl.pallas_call(
        kernel,
        grid=grid,
        in_specs=in_specs,
        out_specs=out_specs,
        out_shape=out_shape,
        scratch_shapes=scratch,
        compiler_params=pltpu.CompilerParams(
            dimension_semantics=("arbitrary",),
            vmem_limit_bytes=vmem * MIB,
            fuse_transposed_lhs_in_matmul=True,
        ),
        cost_estimate=pl.CostEstimate(
            flops=int(flops), bytes_accessed=int(moved), transcendentals=0
        ),
    )


def shape_of(shape, dtype):
    return jax.ShapeDtypeStruct(shape, dtype)


def normalise(values):
    average = jnp.mean(values, axis=-1, keepdims=True)
    centred = values - average
    variance = jnp.mean(centred * centred, axis=-1, keepdims=True)
    scale = lax.rsqrt(variance + norm_eps)
    return centred * scale, scale


def normalise_back(grad, unit, scale, gains):
    inner = grad * gains
    mean_one = jnp.mean(inner, axis=-1, keepdims=True)
    mean_two = jnp.mean(inner * unit, axis=-1, keepdims=True)
    return scale * (inner - mean_one - unit * mean_two)


def gelu_both(u):
    t = pltpu.reciprocal(1.0 + (0.3275911 * 0.7071067811865476) * jnp.abs(u), approx=True)
    bell = jnp.exp(-0.5 * (u * u))
    poly = t * (
        0.127414796
        + t * (-0.142248368 + t * (0.7107068705 + t * (-0.7265760135 + t * 0.5307027145)))
    )
    tail = poly * bell
    share = jnp.where(u < 0, tail, 1.0 - tail)
    return u * share, share + (u * 0.3989422804014327) * bell


def each_strip(n, size, body, start=None, unroll=9):
    def step(index, carry):
        return body(pl.ds(pl.multiple_of(index * size, size), size), carry)

    return lax.fori_loop(0, n // size, step, start, unroll=unroll)


def fold(values):
    total = values[0:8]
    for r in range(8, values.shape[0], 8):
        total = total + values[r : r + 8]
    return total


def head_masks():
    lane = lax.broadcasted_iota(jnp.int32, (1, 2 * HD), 1)
    return [
        jnp.where(lane < HD, HD**-0.5, 0.0).astype(bf16),
        jnp.where(lane < HD, 0.0, HD**-0.5).astype(bf16),
    ]


def count_of(lengths, other=False):
    side = lax.axis_index("narrow")
    text, image = lengths[0, 0], lengths[0, 1]
    return jnp.where(side == (1 if other else 0), text, image)


def patch_centres(n, keys):
    slot = np.arange(n)
    rows = []
    for side in (GRID_HI, GRID_LO):
        for index in (slot % side, slot // side):
            rows.append((index * 1000 + 500) // side)
    return jnp.asarray(np.pad(np.stack(rows), ((0, 0), (0, keys - n))), jnp.int32)


def centres_of(lengths, boxes, patches):
    text = jnp.concatenate(
        [(boxes[0:2] + boxes[2:4]) >> 1, jnp.zeros((2, patches.shape[1] - TEXT), jnp.int32)], axis=1
    )
    patch = jnp.where(lengths[0, 1] > GRID_LO * GRID_LO, patches[0:2], patches[2:4])
    row = jnp.where(lax.axis_index("narrow") == 0, text, patch)
    tall = jnp.concatenate([row, jnp.zeros((6, row.shape[1]), jnp.int32)], axis=0)
    return row, tall.astype(f32).T.astype(jnp.int32)


def table_lines(tables):
    each = NB * H
    lane = lax.broadcasted_iota(jnp.int32, (16, each), 1)
    head = lax.broadcasted_iota(jnp.int32, (16, each), 0)
    line = lax.broadcasted_iota(jnp.int32, (each, 128), 0)
    bucket = lax.broadcasted_iota(jnp.int32, (each, 128), 1)
    inside = line - H * bucket
    hot = jnp.where((inside >= 0) & (inside < H), 1.0, 0.0)
    found = []
    for direction in range(2):
        values = tables[:, direction * each : direction * each + each]
        past = lane - head
        mine = past - H * ((past.astype(f32) + 0.5) * (1.0 / H)).astype(jnp.int32) == 0
        values = jnp.where(mine & (past >= 0), jnp.broadcast_to(values, (16, each)), 0.0)
        found.append(
            lax.dot_general(
                values, hot, (((1,), (0,)), ((), ())),
                precision=lax.Precision.HIGHEST, preferred_element_type=f32,
            )
        )
    return found


def low_lanes(rows):
    return lax.broadcasted_iota(jnp.int32, (rows, 2 * HD), 1) < HD


def hot_columns(coord_x, coord_y, rows, reverse=False):
    lane = lax.broadcasted_iota(jnp.int32, (rows, 128), 1)
    cell = jnp.where((lane & 16) == 0, coord_x >> 6, coord_y >> 6)
    place = lane & 15
    if reverse:
        place = 15 - place
    return jnp.where((cell == place) & (lane < 64), 1.0, 0.0)


def slanted(row, first):
    wide = jnp.broadcast_to(row, (16, 128))
    return pltpu.roll(wide, (128 - first) % 128, 1, stride=1, stride_axis=0)


def spread_tables(table_x, table_y):
    lane = lax.broadcasted_iota(jnp.int32, (16, 128), 1)
    keep = lane < 16
    outs = []
    rows = []
    for row in (table_x, table_y):
        base = jnp.where(keep, slanted(row, 16), 0.0)
        before = jnp.where(keep, slanted(row, 15), 0.0)
        rows.append((base, before - base))

    def split(value, offset):
        upper = value.astype(bf16).astype(f32)
        lower = value - upper
        joined = upper + pltpu.roll(lower, 32, 1)
        return pltpu.roll(joined, offset, 1) if offset else joined

    zero = jnp.zeros((16, 128), f32)
    outs.append(jnp.concatenate([split(rows[0][0], 0), split(rows[1][0], 16)], axis=0))
    outs.append(jnp.concatenate([split(rows[0][1], 0), zero], axis=0))
    outs.append(jnp.concatenate([zero, split(rows[1][1], 16)], axis=0))
    return [value.astype(bf16) for value in outs]


def attend_forward(own, source, queries, weight, vectors, lengths, other, boxes, tables):
    n, d = source.shape
    keys = -(-n // 128) * 128
    heads = 4
    wide = HD * heads
    boxed = boxes is not None

    def kernel(*refs):
        if boxed:
            cnt, x_ref, y_ref, wq, wk, wv, vec, b_ref, c_ref, t_ref = refs[:10]
            q_ref, k_ref, v_ref, o_ref, p_ref, f_ref = refs[10:16]
            k_s, v_s, s_s, step_x, step_y, hot_i, hot_j, lines = refs[16:]
        else:
            cnt, x_ref, y_ref, wq, wk, wv, vec = refs[:7]
            q_ref, k_ref, v_ref, o_ref, p_ref, f_ref, k_s, v_s, s_s = refs[7:]
            s_s = [[s_s.at[0]], [s_s.at[1]]]
        live_count = count_of(cnt, other)
        group = pl.program_id(0)

        @pl.when(group == 0)
        def _():
            k_s[n:keys] = jnp.zeros((keys - n, wide), bf16)
            v_s[n:keys] = jnp.zeros((keys - n, wide), bf16)
            if boxed:
                row, col = centres_of(cnt, b_ref[...], c_ref[...])
                cx, cy = col[0:n, 0:1], col[0:n, 1:2]
                lines[0], lines[1] = table_lines(t_ref[...])
                hots = hot_columns(cx, cy, n)
                lane = lax.broadcasted_iota(jnp.int32, (n, 128), 1)
                hot_i[...] = jnp.where(lane == 64, 1.0, hots).astype(bf16)
                hot_j[0:n] = jnp.where(lane < 32, hots, 0.0).astype(bf16)
                hot_j[n:keys] = jnp.zeros((keys - n, 128), bf16)
                rx, ry = row[0:1], row[1:2]
                step_x[...] = jnp.where((cx & 63) < (rx & 63), 1.0, 0.0)
                step_y[...] = jnp.where((cy & 63) < (ry & 63), 1.0, 0.0)

        if boxed:
            s_s = [[s_s.at[3 * h + k] for k in range(3)] for h in range(2)]
            lane = lax.broadcasted_iota(jnp.int32, (keys, 128), 1)
            place = lax.broadcasted_iota(jnp.int32, (keys, 128), 0)
            dead = jnp.where((lane == 64) & (place >= live_count), masked_score, 0.0)
            dead = dead.astype(bf16)
        cut = pl.ds(pl.multiple_of(group * wide, wide), wide)
        if queries:
            q_ref[...] = x_ref[...]
        else:
            q_ref[...] = (nn(x_ref[...], wq[...]) + vec[0, :, cut]).astype(bf16)
        rows = y_ref[...]
        k_s[0:n] = nn(rows, wk[...]).astype(bf16)
        v_s[0:n] = (nn(rows, wv[...]) + vec[1, :, cut]).astype(bf16)
        k_ref[...] = k_s[0:n]
        v_ref[...] = v_s[0:n]
        masks = head_masks()
        low = low_lanes(n)
        tiles = [slice(128 * t, 128 * t + 128) for t in range(keys // 128)]

        def scores(head):
            lanes = slice(128 * (head // 2), 128 * (head // 2) + 128)
            part = q_ref[:, lanes] * masks[head % 2]
            to = s_s[head % 2]
            if boxed:
                row = pl.ds(heads * group + head, 1)
                base, dx, dy = spread_tables(lines[0, row], lines[1, row])
                hi, hj = hot_i[...], hot_j[:, :32]
                side = nn(hj, base).astype(bf16) + dead
                side = jnp.concatenate([k_s[:, lanes], side], axis=1)
                to[0][...] = nt(jnp.concatenate([part, hi], axis=1), side)
                to[1][...] = nt(hi, nn(hj, dx).astype(bf16))
                to[2][...] = nt(hi, nn(hj, dy).astype(bf16))
            else:
                to[0][...] = nt(part, k_s[:, lanes])

        def soften(head):
            at = s_s[head % 2]
            for r in range(0, n, SUB):
                rows = slice(r, r + SUB)
                parts = []
                for t, lanes in enumerate(tiles):
                    s = at[0][rows, lanes]
                    if boxed:
                        s = s + step_x[rows, lanes] * at[1][rows, lanes]
                        s = s + step_y[rows, lanes] * at[2][rows, lanes]
                    elif 128 * t + 128 > GRID_LO * GRID_LO:
                        lane = lax.broadcasted_iota(jnp.int32, (1, 128), 1) + 128 * t
                        s = jnp.where(lane < live_count, s, masked_score)
                    parts.append(s)
                peak = functools.reduce(jnp.maximum, parts)
                peak = jnp.max(peak, axis=-1, keepdims=True)
                parts = [jnp.exp(s - peak) for s in parts]
                total = functools.reduce(jnp.add, parts)
                total = 1.0 / jnp.sum(total, axis=-1, keepdims=True)
                for s, lanes in zip(parts, tiles):
                    p_ref[head, rows, lanes] = (s * total).astype(bf16)

        scores(0)
        blends = []
        for head in range(heads):
            if head + 1 < heads:
                scores(head + 1)
            soften(head)
            lanes = slice(128 * (head // 2), 128 * (head // 2) + 128)
            blends.append(nn(p_ref[head], v_s[:, lanes]))
            if head % 2 == 1:
                blend = jnp.where(low, blends[head - 1], blends[head])
                f_ref[:, lanes] = blend
                o_ref[:, lanes] = blend.astype(bf16)

    block = pl.BlockSpec((n, wide), lambda i: (0, i))
    columns = [
        pl.BlockSpec((None, d, wide), lambda i, k=k: (0, 0, i + k * (H // heads))) for k in range(3)
    ]
    in_specs = [scalar_spec(), block if queries else whole((n, d)), whole((n, d))]
    in_specs += columns + [whole((6, 1, d))]
    args = [lengths, own, source, weight, weight, weight, vectors]
    scratch = [
        pltpu.VMEM((keys, wide), bf16),
        pltpu.VMEM((keys, wide), bf16),
        pltpu.VMEM((6 if boxed else 2, n, keys), f32),
    ]
    if boxed:
        in_specs += [
            pl.BlockSpec((None, 4, TEXT), lambda i: (0, 0, 0)),
            whole((4, keys)),
            whole((1, 2 * NB * H)),
        ]
        args += [boxes, patch_centres(n, keys), tables]
        scratch += [pltpu.VMEM((n, keys), f32)] * 2
        scratch += [pltpu.VMEM((n, 128), bf16), pltpu.VMEM((keys, 128), bf16)]
        scratch += [pltpu.VMEM((2, 16, 128), f32)]
    return call(
        kernel,
        (H // heads,),
        in_specs,
        [block] * 4 + [pl.BlockSpec((heads, n, keys), lambda i: (i, 0, 0)), block],
        [
            shape_of((n, H * HD), bf16),
            shape_of((n, H * HD), bf16),
            shape_of((n, H * HD), bf16),
            shape_of((n, H * HD), bf16),
            shape_of((H, n, keys), bf16),
            shape_of((n, H * HD), f32),
        ],
        scratch,
        16 * n * n * H * HD + 6 * n * d * d,
        2 * H * n * n,
    )(*args)


def feed_forward(blended, states, weights, lengths, last):
    _, attn_out, ff_up, ff_down, vectors, gains, up_bias = weights
    n, d = blended.shape
    steps = ff_up.shape[2] // d

    def kernel(cnt, o_ref, x_ref, wo_ref, wu_ref, wd_ref, v_ref, g_ref, e_ref, *rest):
        if last:
            unit1, scale1, rb, act, der, unit2, scale2, out, r_s, acc = rest
        else:
            unit1, scale1, rb, act, der, unit2, scale2, out, out_b, r_s, acc = rest
        step = pl.program_id(0)

        @pl.when(step == 0)
        def _():
            branch = nn(o_ref[...], wo_ref[...]) + v_ref[2]
            unit, scale = normalise(x_ref[...].astype(f32) + branch)
            unit1[...] = unit
            scale1[...] = scale
            r = unit * g_ref[0:1] + v_ref[3]
            r_s[...] = r
            rb[...] = r.astype(bf16)
            acc[...] = r + v_ref[4]

        hidden = nn(rb[...], wu_ref[...]) + e_ref[...]
        active, slope = gelu_both(hidden)
        active = active.astype(bf16)
        act[...] = active
        der[...] = slope.astype(bf16)
        acc[...] += nn(active, wd_ref[...])

        @pl.when(step == steps - 1)
        def _():
            unit, scale = normalise(acc[...])
            unit2[...] = unit
            scale2[...] = scale
            z = unit * g_ref[1:2] + v_ref[5]
            if last:
                row = lax.broadcasted_iota(jnp.int32, (n, 1), 0)
                out[...] = jnp.where(row < count_of(cnt), z, 0.0)
            else:
                out[...] = z
                out_b[...] = z.astype(bf16)

    columns = pl.BlockSpec((n, d), lambda i: (0, i))
    outs = [
        (whole((n, d)), shape_of((n, d), f32)),
        (whole((n, 1)), shape_of((n, 1), f32)),
        (whole((n, d)), shape_of((n, d), bf16)),
        (columns, shape_of((n, steps * d), bf16)),
        (columns, shape_of((n, steps * d), bf16)),
        (whole((n, d)), shape_of((n, d), f32)),
        (whole((n, 1)), shape_of((n, 1), f32)),
        (whole((n, d)), shape_of((n, d), f32)),
    ]
    if not last:
        outs.append((whole((n, d)), shape_of((n, d), bf16)))
    return call(
        kernel,
        (steps,),
        [
            scalar_spec(),
            whole((n, d)),
            whole((n, d)),
            pl.BlockSpec((None, d, d), lambda i: (0, 0, 0)),
            pl.BlockSpec((None, d, d), lambda i: (0, 0, i)),
            pl.BlockSpec((None, d, d), lambda i: (0, i, 0)),
            whole((6, 1, d)),
            pl.BlockSpec((None, 2, d), lambda i: (0, 0, 0)),
            pl.BlockSpec((1, d), lambda i: (0, i)),
        ],
        [spec for spec, _ in outs],
        [shape for _, shape in outs],
        [pltpu.VMEM((n, d), f32), pltpu.VMEM((n, d), f32)],
        2 * n * d * d * (1 + 2 * steps),
        2 * d * d * (1 + 2 * steps),
    )(lengths, blended, states, attn_out, ff_up, ff_down, vectors, gains, up_bias)


def store_rows(rows):
    d = rows[0].shape[1]
    blank = jnp.zeros((8 - len(rows), d), f32)
    return jnp.concatenate(rows + [blank], axis=0)


def slot_place(index, bits):
    place = 0
    for b in range(bits):
        place = place | (((index >> b) & 1) << (bits - 1 - b))
    return place


class Slots:
    def __init__(self, devices, rows):
        self.devices = devices
        self.rows = rows // devices
        self.bits = (devices // 2).bit_length() - 1
        self.split = self.rows % 16 == 0 and devices & (devices - 1) == 0 and devices > 1

    def put(self, me, held, shards, first_shard, write):
        core = me & 1
        for k in range(shards // 2):
            place = slot_place((first_shard // 2 + k) ^ (me >> 1), self.bits)
            for which in range(2):
                start = (2 * k + (core if which == 0 else 1 - core)) * self.rows
                rows = held[pl.ds(pl.multiple_of(start, 16), self.rows)]
                write(which, place, rows)


def down_gradient(me, count, grads, unit, scale, gains, active, devices, top):
    n, d = unit.shape
    ff = active.shape[1]
    steps = ff // d
    slots = Slots(devices, ff)
    shards = devices // steps

    def kernel(me_ref, cnt, *refs):
        ups = refs[: len(grads)]
        unit_ref, scale_ref, g_ref, act_ref = refs[len(grads) : len(grads) + 4]
        dz, gb, sums, *outs, held = refs[len(grads) + 4 :]
        step = pl.program_id(0)

        @pl.when(step == 0)
        def _():
            if top:
                row = lax.broadcasted_iota(jnp.int32, (n, 1), 0)
                g = jnp.where(row < cnt[0], ups[0][...].astype(f32), 0.0)
            else:
                g = ups[0][...] + ups[1][...].astype(f32)
            unit = unit_ref[...]
            back = normalise_back(g, unit, scale_ref[...], g_ref[1:2])
            dz[...] = back
            low = back.astype(bf16)
            gb[...] = low
            sums[...] = store_rows(
                [
                    jnp.sum(g * unit, axis=0, keepdims=True),
                    jnp.sum(g, axis=0, keepdims=True),
                    jnp.sum(low.astype(f32), axis=0, keepdims=True),
                ]
            )

        value = tn(act_ref[...], gb[...]).astype(bf16)
        if slots.split:
            held[...] = value

            def write(which, place, rows):
                outs[which][place] = rows

            slots.put(me_ref[0], held, shards, shards * step, write)
        else:
            outs[0][...] = value

    if slots.split:
        block = (devices // 2, slots.rows, d)
        out_list = [(whole(block), shape_of(block, bf16))] * 2
    else:
        out_list = [(pl.BlockSpec((d, d), lambda i: (i, 0)), shape_of((ff, d), bf16))]
    out_list = [
        (whole((n, d)), shape_of((n, d), f32)),
        (whole((n, d)), shape_of((n, d), bf16)),
        (whole((8, d)), shape_of((8, d), f32)),
    ] + out_list
    results = call(
        kernel,
        (steps,),
        [scalar_spec(), scalar_spec()]
        + [whole((n, d))] * len(grads)
        + [
            whole((n, d)),
            whole((n, 1)),
            pl.BlockSpec((None, 2, d), lambda i: (0, 0, 0)),
            pl.BlockSpec((n, d), lambda i: (0, i)),
        ],
        [spec for spec, _ in out_list],
        [shape for _, shape in out_list],
        [pltpu.VMEM((d, d), bf16)],
        2 * n * d * ff,
        4 * d * ff,
    )(me, count, *grads, unit, scale, gains, active)
    return results[0], results[1], results[2], results[3:]


def feed_backward(grad_sum, grad_branch, slope, unit, scale, weights):
    _, attn_out, ff_up, ff_down, _, gains, _ = weights
    n, d = grad_sum.shape
    steps = ff_up.shape[2] // d

    def kernel(
        dz, gb, der, wd, wu, wo, g_ref, unit_ref, scale_ref, du, ups, ga, gr, do, sums, acc
    ):
        step = pl.program_id(0)

        @pl.when(step == 0)
        def _():
            acc[...] = dz[...]

        grad = (nt(gb[...], wd[...]) * der[...].astype(f32)).astype(bf16)
        du[...] = grad
        ups[...] = jnp.sum(grad.astype(f32), axis=0, keepdims=True)
        acc[...] += nt(grad, wu[...])

        @pl.when(step == steps - 1)
        def _():
            g = acc[...]
            unit = unit_ref[...]
            back = normalise_back(g, unit, scale_ref[...], g_ref[0:1])
            gr[...] = back
            low = back.astype(bf16)
            ga[...] = low
            sums[...] = store_rows(
                [
                    jnp.sum(g * unit, axis=0, keepdims=True),
                    jnp.sum(g, axis=0, keepdims=True),
                    jnp.sum(low.astype(f32), axis=0, keepdims=True),
                ]
            )
            do[...] = nt(low, wo[...]).astype(bf16)

    columns = pl.BlockSpec((n, d), lambda i: (0, i))
    return call(
        kernel,
        (steps,),
        [
            whole((n, d)),
            whole((n, d)),
            columns,
            pl.BlockSpec((None, d, d), lambda i: (0, i, 0)),
            pl.BlockSpec((None, d, d), lambda i: (0, 0, i)),
            pl.BlockSpec((None, d, d), lambda i: (0, 0, 0)),
            pl.BlockSpec((None, 2, d), lambda i: (0, 0, 0)),
            whole((n, d)),
            whole((n, 1)),
        ],
        [
            columns,
            pl.BlockSpec((1, d), lambda i: (0, i)),
            whole((n, d)),
            whole((n, d)),
            whole((n, d)),
            whole((8, d)),
        ],
        [
            shape_of((n, steps * d), bf16),
            shape_of((1, steps * d), f32),
            shape_of((n, d), bf16),
            shape_of((n, d), f32),
            shape_of((n, d), bf16),
            shape_of((8, d), f32),
        ],
        [pltpu.VMEM((n, d), f32)],
        2 * n * d * d * (1 + 2 * steps),
        2 * d * d * (1 + 2 * steps),
    )(grad_sum, grad_branch, slope, ff_down, ff_up, attn_out, gains, unit, scale)


def weight_gradients(me, jobs, lefts, rights, devices):
    n, d = lefts[0].shape
    slots = Slots(devices, d)
    steps = len(jobs)

    def kernel(me_ref, *refs):
        left_refs = refs[: len(lefts)]
        right_refs = refs[len(lefts) : len(lefts) + len(rights)]
        *outs, turned, held = refs[len(lefts) + len(rights) :]
        step = pl.program_id(0)
        for index in range(len(lefts)):
            mine = [j for j, job in enumerate(jobs) if job[0] == index]

            @pl.when(step == mine[0])
            def _(index=index):
                turned[...] = left_refs[index][...].T

        for index in range(len(rights)):
            mine = [j for j, job in enumerate(jobs) if job[1] == index]

            @pl.when((step >= mine[0]) & (step <= mine[-1]))
            def _(index=index):
                value = nn(turned[...], right_refs[index][...]).astype(bf16)
                if slots.split:
                    held[...] = value
                else:
                    outs[0][...] = value

        if slots.split:

            def write(which, place, rows):
                outs[which][place, step] = rows

            slots.put(me_ref[0], held, devices, 0, write)

    def right_spec(index):
        mine = [(j, job[2]) for j, job in enumerate(jobs) if job[1] == index]
        first, block = mine[0]

        def place(i):
            return (0, jnp.clip(i - first, 0, len(mine) - 1) + block)

        return pl.BlockSpec((n, d), place)

    if slots.split:
        block = (devices // 2, steps, slots.rows, d)
        out_list = [(whole(block), shape_of(block, bf16))] * 2
    else:
        out_list = [(pl.BlockSpec((d, d), lambda i: (0, i)), shape_of((d, steps * d), bf16))]
    return call(
        kernel,
        (steps,),
        [scalar_spec()]
        + [whole((n, d))] * len(lefts)
        + [right_spec(index) for index in range(len(rights))],
        [spec for spec, _ in out_list],
        [shape for _, shape in out_list],
        [pltpu.VMEM((d, n), bf16), pltpu.VMEM((d, d), bf16)],
        2 * n * d * d * steps,
        4 * d * d * steps,
    )(me, *lefts, *rights)


def attend_backward(arrays, offsets, grad_blended, soft, places):
    n = grad_blended.shape[0]
    boxed = places is not None
    keys = soft.shape[2]

    def kernel(*refs):
        q_ref, k_ref, v_ref, g_ref, p_ref = refs[:5]
        if boxed:
            col_ref, row_ref = refs[5:7]
            dq_ref, dk_ref, dv_ref, sums, tab = refs[7:12]
            hot_i, hot_j, step_x, step_y, ds_s, far = refs[12:]

            @pl.when(pl.program_id(0) == 0)
            def _():
                cx, cy = col_ref[:, 0:1], col_ref[:, 1:2]
                rx, ry = row_ref[0:1], row_ref[1:2]
                hots = hot_columns(cx, cy, n, reverse=True)
                lane = lax.broadcasted_iota(jnp.int32, (n, 128), 1)
                hot_j[...] = jnp.where(lane < 32, hots, 0.0).astype(bf16)
                row = lax.broadcasted_iota(jnp.int32, (32, n), 0)
                cell = jnp.where(row < 16, rx >> 6, ry >> 6)
                hot_i[...] = jnp.where(cell == (row & 15), 1.0, 0.0).astype(bf16)
                step_x[...] = jnp.where((cx & 63) < (rx & 63), 1.0, 0.0).astype(bf16)
                step_y[...] = jnp.where((cy & 63) < (ry & 63), 1.0, 0.0).astype(bf16)
        else:
            dq_ref, dk_ref, dv_ref, sums, ds_s = refs[5:]
        masks = head_masks()
        q = q_ref[...]
        k = k_ref[...]
        v = v_ref[...]
        g = g_ref[...]
        grads = []
        for h in range(2):
            queries = []
            for r in range(0, n, STRIP):
                gh = g[r : r + STRIP] * masks[h]
                p = p_ref[h, r : r + STRIP, :n].astype(f32)
                dp = nt(gh, v)
                mean = jnp.sum(p * dp, axis=-1, keepdims=True)
                ds = (p * (dp - mean)).astype(bf16)
                ds_s[r : r + STRIP] = ds
                if boxed:
                    hj = hot_j[...]
                    wide = nn(ds, jnp.concatenate([k, hj], axis=1))
                    queries.append(wide[:, :128])
                    far[r : r + STRIP, 0:128] = wide[:, 128:]
                    far[r : r + STRIP, 128:256] = nn(ds * step_x[r : r + STRIP], hj)
                    far[r : r + STRIP, 256:384] = nn(ds * step_y[r : r + STRIP], hj)
                else:
                    queries.append(nn(ds, k))
            grads.append(
                (jnp.concatenate(queries, axis=0), tn(ds_s[...], q), tn(p_ref[h, :, :n], g))
            )
            if boxed:
                value = far[...]
                upper = value.astype(bf16)
                lower = (value - upper.astype(f32)).astype(bf16)
                cells = nn(hot_i[...], upper) + nn(hot_i[...], lower)
                lane = lax.broadcasted_iota(jnp.int32, (16, 128), 1)
                for direction in range(2):
                    rows = slice(16 * direction, 16 * direction + 16)
                    level = cells[rows, 0:128]
                    above = cells[rows, 128 * (direction + 1) : 128 * (direction + 2)]
                    inside = (lane >= 16 * direction) & (lane < 16 * direction + 16)
                    level = jnp.where(inside, level - above, 0.0)
                    above = jnp.where(inside, above, 0.0)
                    turn = (128 + 1 - 16 * direction) % 128
                    line = pltpu.roll(level, turn, 1, stride=1, stride_axis=0)
                    line = line + pltpu.roll(above, (turn + 127) % 128, 1, stride=1, stride_axis=0)
                    line = jnp.sum(line, axis=0, keepdims=True) * HD**0.5
                    tab[2 * h + direction : 2 * h + direction + 1] = line
        low = low_lanes(n)
        outs = []
        for index, ref in enumerate((dq_ref, dk_ref, dv_ref)):
            value = jnp.where(low, grads[0][index], grads[1][index]).astype(bf16)
            ref[...] = value
            outs.append(jnp.sum(value.astype(f32), axis=0, keepdims=True))
        sums[...] = store_rows([outs[0], outs[2]])

    def pair_block(offset):
        return pl.BlockSpec((n, 128), lambda i: (0, i + offset))

    in_specs = [pair_block(offset) for offset in offsets] + [
        pair_block(0),
        pl.BlockSpec((2, n, keys), lambda i: (i, 0, 0)),
    ]
    args = [*arrays, grad_blended, soft]
    outs = [(pair_block(0), shape_of((n, H * HD), bf16))] * 3
    outs.append((pl.BlockSpec((8, 128), lambda i: (0, i)), shape_of((8, H * HD), f32)))
    scratch = [pltpu.VMEM((n, n), bf16)]
    if boxed:
        in_specs += [whole((n, 2)), whole((2, n))]
        args += [*places]
        outs.append(
            (pl.BlockSpec((None, 4, 128), lambda i: (i, 0, 0)), shape_of((PAIRS, 4, 128), f32))
        )
        scratch = [
            pltpu.VMEM((32, n), bf16),
            pltpu.VMEM((n, 128), bf16),
            pltpu.VMEM((n, n), bf16),
            pltpu.VMEM((n, n), bf16),
            pltpu.VMEM((n, n), bf16),
            pltpu.VMEM((n, 384), f32),
        ]
    return call(
        kernel,
        (PAIRS,),
        in_specs,
        [spec for spec, _ in outs],
        [shape for _, shape in outs],
        scratch,
        16 * n * n * H * HD,
        2 * H * n * n,
    )(*args)


def project_back(grads, weight, first, residual, out_type):
    n, d = grads[0].shape
    steps = len(grads)

    def kernel(*refs):
        g_refs = refs[:steps]
        w_ref = refs[steps]
        out, acc = refs[-2:]
        step = pl.program_id(0)
        for index in range(steps):

            @pl.when(step == index)
            def _(index=index):
                value = nt(g_refs[index][...], w_ref[...])
                if index > 0:
                    value = value + acc[...]
                elif residual is not None:
                    value = value + refs[steps + 1][...]
                if index == steps - 1:
                    out[...] = value.astype(out_type)
                else:
                    acc[...] = value

    extra = [] if residual is None else [residual]
    return call(
        kernel,
        (steps,),
        [whole((n, d))] * steps
        + [pl.BlockSpec((None, d, d), lambda i: (0, 0, i + first))]
        + [whole((n, d))] * len(extra),
        whole((n, d)),
        shape_of((n, d), out_type),
        [pltpu.VMEM((n, d), f32)],
        2 * n * d * d * steps,
        2 * d * d * steps,
    )(*grads, weight, *extra)


def feed_forward_sending(blended, states, weights, next_in, next_vectors):
    _, attn_out, ff_up, ff_down, vectors, gains, up_bias = weights
    n, d = blended.shape
    tiles = ff_up.shape[2] // d
    strips = 3
    size = n // strips
    last = strips * tiles
    parts = Parts()
    strip = lambda i: jnp.minimum(i // tiles, strips - 1)
    tile = lambda i: jnp.where(i < last, i % tiles, tiles - 1)
    h_o = parts.inp(blended, fixed((n, d)))
    h_x = parts.inp(states, fixed((n, d)))
    h_wo = parts.inp(attn_out, fixed((None, d, d)))
    h_wu = parts.inp(ff_up, pl.BlockSpec((None, d, d), lambda i: (0, 0, tile(i))))
    h_wd = parts.inp(ff_down, pl.BlockSpec((None, d, d), lambda i: (0, tile(i), 0)))
    h_v, h_g = parts.inp(vectors, fixed((6, 1, d))), parts.inp(gains, fixed((None, 2, d)))
    h_e = parts.inp(up_bias, pl.BlockSpec((1, d), lambda i: (0, tile(i))))
    h_wq = parts.inp(next_in, pl.BlockSpec((None, d, d), lambda i: (0, 0, 0)))
    h_nv = parts.inp(next_vectors, fixed((6, 1, d)))
    h_unit1, h_scale1 = parts.out((n, d), f32), parts.out((n, 1), f32)
    h_rb = parts.out((n, d), bf16)
    block = pl.BlockSpec((size, d), lambda i: (strip(i), tile(i)))
    h_act = parts.out((n, tiles * d), bf16, block)
    h_der = parts.out((n, tiles * d), bf16, block)
    h_unit2, h_scale2 = parts.out((n, d), f32), parts.out((n, 1), f32)
    h_out, h_out_b = parts.out((n, d), f32), parts.out((n, d), bf16)
    h_partner, h_q = parts.out((n, d), bf16), parts.out((n, d), bf16)
    h_acc = parts.vmem((size, d), f32)
    h_got = parts.vmem((n, d), bf16)
    h_sent = parts.tmp(pltpu.SemaphoreType.DMA((strips,)))
    h_arrived = parts.tmp(pltpu.SemaphoreType.DMA((strips,)))

    def body(refs):
        i = pl.program_id(0)
        partner = {"narrow": 1 - lax.axis_index("narrow")}
        v_ref, g_ref, acc = refs[h_v], refs[h_g], refs[h_acc]

        def send(index):
            rows = pl.ds(size * index, size)
            return pltpu.make_async_remote_copy(
                src_ref=refs[h_out_b].at[rows],
                dst_ref=refs[h_got].at[rows],
                send_sem=refs[h_sent].at[index],
                recv_sem=refs[h_arrived].at[index],
                device_id=partner,
                device_id_type=MESH,
            )

        @pl.when(i == 0)
        def _():
            barrier = pltpu.get_barrier_semaphore()
            pl.semaphore_signal(barrier, inc=1, device_id=partner, device_id_type=MESH)
            pl.semaphore_wait(barrier, 1)

        for index in range(strips):
            rows = slice(size * index, size * index + size)

            @pl.when(i == index * tiles)
            def _(rows=rows):
                branch = nn(refs[h_o][rows], refs[h_wo][...]) + v_ref[2]
                unit, scale = normalise(refs[h_x][rows].astype(f32) + branch)
                refs[h_unit1][rows] = unit
                refs[h_scale1][rows] = scale
                r = unit * g_ref[0:1] + v_ref[3]
                refs[h_rb][rows] = r.astype(bf16)
                acc[...] = r + v_ref[4]

        @pl.when(i < last)
        def _():
            rows = pl.ds(pl.multiple_of(lax.div(i, tiles) * size, size), size)
            hidden = nn(refs[h_rb][rows], refs[h_wu][...]) + refs[h_e][...]
            active, slope = gelu_both(hidden)
            active = active.astype(bf16)
            refs[h_act][...] = active
            refs[h_der][...] = slope.astype(bf16)
            acc[...] += nn(active, refs[h_wd][...])

        for index in range(strips):
            rows = slice(size * index, size * index + size)

            @pl.when(i == index * tiles + tiles - 1)
            def _(rows=rows, index=index):
                unit, scale = normalise(acc[...])
                refs[h_unit2][rows] = unit
                refs[h_scale2][rows] = scale
                z = unit * g_ref[1:2] + v_ref[5]
                refs[h_out][rows] = z
                refs[h_out_b][rows] = z.astype(bf16)
                send(index).start()

        @pl.when(i == last)
        def _():
            q = nn(refs[h_out_b][...], refs[h_wq][...]) + refs[h_nv][0]
            refs[h_q][...] = q.astype(bf16)
            for index in range(strips):
                send(index).wait()
            refs[h_partner][...] = refs[h_got][...]

    results = parts.run(
        body, last + 1, 2 * n * d * d * (2 + 2 * tiles), 2 * d * d * (2 + 2 * tiles * strips), 4
    )
    order = (
        h_unit1, h_scale1, h_rb, h_act, h_der, h_unit2, h_scale2, h_out, h_out_b, h_partner, h_q
    )
    return [results[h] for h in order]


MESH = pl.DeviceIdType.MESH
DOWN, UP, IN = 0, 1, 2
SIZES = (3, 5, 3)


def block_shape(chunk, rows, d):
    return (4 * rows, d // 3) if chunk == DOWN else (rows, d)


Z_FIRST = (
    (2, 0, 0),
    (2, 0, 1),
    (2, 1, 1),
    (2, 2, 0),
    (1, 0, 0),
    (1, 0, 2),
)
HOPS = (
    (
        (2, 0, 0, 0, ((5, 21), (21, 42), (49, 61))),
        (2, 0, 1, 0, ((13, 26), (40, 61))),
        (2, 0, 2, 0, ((24, 33), (33, 53))),
        (2, 1, 0, 0, ((29, 37),)),
        (2, 1, 1, 0, ((37, 45),)),
        (2, 1, 2, 0, ((45, 53),)),
        (2, 1, 3, 0, ((53, 61),)),
    ),
    (
        (2, 1, 4, 0, ((0, 4), (10, 25), (27, 37), (41, 61))),
        (2, 0, 0, 3, ((0, 9),)),
        (2, 1, 0, 1, ((0, 11), (19, 33), (35, 45))),
        (2, 0, 2, 2, ((1, 11), (64, 69))),
        (2, 1, 1, 1, ((10, 25), (64, 69))),
        (2, 0, 1, 2, ((19, 34), (45, 69))),
        (2, 1, 3, 1, ((32, 53), (53, 69))),
        (2, 1, 2, 1, ((43, 69),)),
        (2, 2, 0, 0, ((53, 69),)),
        (2, 2, 1, 0, ((61, 69),)),
    ),
    (
        (2, 1, 3, 3, ((0, 5),)),
        (2, 2, 0, 1, ((0, 21), (25, 34), (56, 62))),
        (2, 2, 1, 1, ((0, 13), (24, 33))),
        (2, 2, 2, 0, ((0, 5), (8, 29), (32, 41))),
        (1, 0, 0, 0, ((5, 21),)),
        (2, 1, 2, 2, ((8, 26), (26, 37))),
        (1, 0, 1, 0, ((13, 26), (32, 50))),
        (1, 0, 2, 0, ((24, 33), (37, 61))),
        (1, 1, 0, 0, ((29, 34), (48, 62))),
        (1, 1, 1, 0, ((37, 45),)),
        (1, 1, 2, 0, ((45, 53),)),
        (1, 1, 3, 0, ((53, 61),)),
    ),
    (
        (1, 0, 2, 2, ((0, 3), (3, 10))),
        (2, 2, 1, 3, ((0, 3),)),
        (1, 0, 1, 2, ((0, 4), (11, 18))),
        (1, 1, 4, 0, ((0, 2), (46, 51), (51, 55), (55, 58))),
        (1, 1, 2, 1, ((1, 9), (16, 19), (20, 37))),
        (2, 2, 2, 3, ((2, 9),)),
        (1, 0, 0, 1, ((4, 13), (17, 21), (32, 46))),
        (1, 2, 0, 0, ((5, 10), (11, 19), (20, 45), (46, 49))),
        (1, 1, 3, 1, ((8, 13), (40, 47), (49, 53))),
        (1, 2, 1, 0, ((13, 18), (48, 54), (54, 57), (57, 59))),
        (2, 1, 1, 3, ((17, 20),)),
        (1, 1, 0, 2, ((18, 21), (46, 50))),
        (1, 1, 1, 1, ((19, 45), (46, 50), (50, 54))),
        (1, 2, 2, 0, ((21, 37), (40, 48), (48, 52), (52, 56))),
    ),
)


class Handle:
    pass


class Parts:
    def __init__(self):
        self.inputs, self.outputs, self.scratch = [], [], []

    def inp(self, array, spec):
        self.inputs.append((Handle(), array, spec))
        return self.inputs[-1][0]

    def out(self, shape, dtype, spec=None):
        self.outputs.append((Handle(), shape_of(shape, dtype), spec or fixed(shape)))
        return self.outputs[-1][0]

    def tmp(self, kind):
        self.scratch.append((Handle(), kind))
        return self.scratch[-1][0]

    def vmem(self, shape, dtype):
        return self.tmp(pltpu.VMEM(shape, dtype))

    def late(self, array, shape=None):
        shape = shape or array.shape
        source = self.inp(array, pl.BlockSpec(memory_space=pl.ANY))
        item = (source, self.vmem(shape, array.dtype), self.tmp(pltpu.SemaphoreType.DMA))
        return item

    def run(self, body, steps, flops, moved, collective):
        handles = [x[0] for x in self.inputs + self.outputs + self.scratch]

        def kernel(*refs):
            body(dict(zip(handles, refs)))

        results = pl.pallas_call(
            kernel,
            grid=(steps,),
            in_specs=[x[2] for x in self.inputs],
            out_specs=[x[2] for x in self.outputs],
            out_shape=[x[1] for x in self.outputs],
            scratch_shapes=[x[1] for x in self.scratch],
            compiler_params=pltpu.CompilerParams(
                dimension_semantics=("arbitrary",),
                vmem_limit_bytes=63 * MIB,
                fuse_transposed_lhs_in_matmul=True,
                collective_id=collective,
                has_side_effects=collective is not None,
            ),
            cost_estimate=pl.CostEstimate(
                flops=int(flops), bytes_accessed=int(moved), transcendentals=0
            ),
        )(*[x[1] for x in self.inputs])
        return dict(zip([x[0] for x in self.outputs], results))


def fetch(refs, item):
    source, target, sem = (refs[h] for h in item)
    if source.shape != target.shape:
        source = source.at[0]
    return pltpu.make_async_copy(source, target, sem)


def fixed(shape):
    return pl.BlockSpec(shape, lambda i: (0,) * len(shape), pipeline_mode=pl.Buffered(1))


def bit_of(me, bit):
    return lax.rem(lax.div(me, bit), 2)


def order_of(key):
    return (1, 4, 2, 8) if key in Z_FIRST else (1, 2, 4, 8)


def put_rows(me, held, layer, chunk, block, shards, base, keep, send, height, rows):
    core = bit_of(me, 1)
    places = {}
    count = height // rows
    for k in range(shards // 2):
        differ = {}
        for bit in (2, 4, 8):
            mine = bit_of(me, bit)
            if bit < shards:
                differ[bit] = 1 - mine if (2 * k // bit) % 2 else mine
            else:
                theirs = bit_of(base, bit)
                differ[bit] = mine + theirs - 2 * mine * theirs
        for which, ref in ((core, keep), (1 - core, send)):
            start = (2 * k + which) * height
            for b in range(count):
                bits = order_of((layer, chunk, block + b))[1:]
                place = 4 * differ[bits[0]] + 2 * differ[bits[1]] + differ[bits[2]]
                ref[place, block + b] = held[pl.ds(pl.multiple_of(start + b * rows, 16), rows)]


class Hop:
    def __init__(self, key, hop, keep, send, got, done, sem, load, flush):
        self.load, self.flush = load, flush
        self.bit, self.hop = order_of(key)[hop], hop
        self.keep, self.send, self.got, self.done, self.sem = keep, send, got, done, sem


class Traffic:
    def __init__(self, parts, number, layer, fresh, state, rows, d, small=None, cross=None):
        legs = HOPS[number]
        self.parts, self.state, self.layer = parts, state, layer
        self.events, self.loads, self.copies = [], [], []
        self.small, self.cross = small, cross
        self.keep, self.send = {}, {}
        self.flushes, self.fresh_flush = [], {}
        self.kept_out, self.done_out = [], []
        bits = set()
        groups = {}
        for leg in legs:
            groups.setdefault(leg[:2], []).append(leg)
        for chunk in fresh:
            groups.setdefault((layer, chunk), [])
        arrays = {}
        count = 0

        def operand(array):
            if id(array) not in arrays:
                arrays[id(array)] = parts.inp(array, pl.BlockSpec(memory_space=pl.ANY))
            return arrays[id(array)]

        for name, members in groups.items():
            made_here = name[0] == layer and name[1] in fresh
            if made_here:
                blocks = list(range(SIZES[name[1]]))
                slots = 8
            else:
                blocks = [leg[2] for leg in members]
                slots = max(8 >> leg[3] for leg in members)
            ends = {leg[2]: leg[3] + len(leg[4]) for leg in members}
            finished = [b for b in blocks if ends.get(b, 0) == 4]
            size = block_shape(name[1], rows, d)
            shape = (slots, len(blocks), *size)
            keep = parts.vmem(shape, bf16)
            keep_out = send_out = None
            if len(finished) < len(blocks):
                keep_out = parts.out(shape, bf16, pl.BlockSpec(memory_space=pl.ANY))
            send = None
            if made_here:
                send = parts.vmem(shape, bf16)
                if not all(ends.get(b, 0) > 0 for b in blocks):
                    send_out = parts.out(shape, bf16, pl.BlockSpec(memory_space=pl.ANY))
                self.keep[name[1]], self.send[name[1]] = keep, send
            flushes = {}
            if finished:
                done = parts.out((len(finished), *size), f32)
                for place, b in enumerate(finished):
                    self.done_out.append((name + (b,), done, place))
            for place, b in enumerate(blocks):
                if b not in finished:
                    sent = send_out if made_here and ends.get(b, 0) == 0 else None
                    self.kept_out.append((name + (b,), keep_out, sent, place))
                    reach = ends.get(b, 0)
                    valid = 8 if reach == 0 else 16 >> reach
                    flushes[b] = [(keep, keep_out, valid, place, len(self.flushes))]
                    self.flushes.append(flushes[b][0])
                    if sent is not None:
                        flushes[b].append((send, send_out, 8, place, len(self.flushes)))
                        self.flushes.append(flushes[b][1])
                    if reach == 0:
                        self.fresh_flush[name[1], b] = flushes[b]
            for hop in range(4):
                users = [leg for leg in members if leg[3] <= hop < leg[3] + len(leg[4])]
                if not users:
                    continue
                got = parts.vmem((8 >> hop, len(users), *size), bf16)
                for index, leg in enumerate(users):
                    key, place = leg[:3], blocks.index(leg[2])
                    load = None
                    half = 8 >> hop
                    if hop == 0 and made_here:
                        source = (send, place, 0)
                    elif hop == 0:
                        source = (operand(state[key][1]), state[key][2], 0)
                    elif hop == leg[3]:
                        source = (operand(state[key][0]), state[key][2], half)
                    else:
                        source = (keep, place, half)
                    if hop == leg[3] and not made_here:
                        load = (operand(state[key][0]), state[key][2], half, keep, place)
                        load = load + (len(self.loads),)
                        self.loads.append(load)
                    flush = flushes.get(leg[2]) if hop + 1 == ends[leg[2]] else None
                    final = None
                    if hop == 3:
                        final = (done, finished.index(leg[2]))
                    item = Hop(
                        key, hop, (keep, place), source, (got, index), final, count, load, flush
                    )
                    count += 1
                    bits.add(item.bit)
                    start, end = leg[4][hop - leg[3]]
                    self.events.append((end, 0, len(self.events), self.finish, item))
                    self.events.append((start, 1, len(self.events), self.begin, item))
        if small is not None:
            self.total = parts.vmem(small[0], f32)
            self.small_got = parts.vmem((4,) + small[0], f32)
            self.small_out = parts.out(small[0], f32)
            bits |= {1, 2, 4, 8}
            for hop, (start, end) in enumerate(small[1]):
                item = (hop, count + hop)
                self.events.append((end, 0, len(self.events), self.small_finish, item))
                self.events.append((start, 1, len(self.events), self.small_begin, item))
            count += 4
        if cross is not None:
            self.cross_out = parts.vmem(cross[0], bf16)
            self.cross_got = parts.vmem(cross[0], bf16)
            self.cross_in = parts.out(cross[0], bf16)
            for first, size, start, end in cross[1]:
                item = (first, size, count)
                self.events.append((end, 0, len(self.events), self.cross_finish, item))
                self.events.append((start, 1, len(self.events), self.cross_begin, item))
                count += 1
        self.sent = parts.tmp(pltpu.SemaphoreType.DMA((count,)))
        self.arrived = parts.tmp(pltpu.SemaphoreType.DMA((count,)))
        self.loaded = None
        if self.loads:
            self.loaded = parts.tmp(pltpu.SemaphoreType.DMA((len(self.loads),)))
        self.flushed = None
        if self.flushes:
            self.flushed = parts.tmp(pltpu.SemaphoreType.DMA((len(self.flushes),)))
        self.bits = sorted(bits)
        self.events.sort(key=lambda e: e[:3])

    def bind(self, refs, step):
        self.refs, self.step = refs, step
        self.me, self.side = lax.axis_index("wide"), lax.axis_index("narrow")

    def device(self, bit):
        return {"wide": self.me + bit - 2 * bit * bit_of(self.me, bit)}

    def load_copy(self, load):
        source, place, slots, keep, at, index = load
        return pltpu.make_async_copy(
            self.refs[source].at[pl.ds(0, slots), place],
            self.refs[keep].at[pl.ds(0, slots), at],
            self.refs[self.loaded].at[index],
        )

    def flush_copy(self, flush):
        source, target, slots, place, index = flush
        return pltpu.make_async_copy(
            self.refs[source].at[pl.ds(0, slots), place],
            self.refs[target].at[pl.ds(0, slots), place],
            self.refs[self.flushed].at[index],
        )

    def open(self):
        barrier = pltpu.get_barrier_semaphore()
        peers = [self.device(bit) for bit in self.bits]
        if self.cross is not None:
            peers.append({"narrow": 1 - self.side})
        for peer in peers:
            pl.semaphore_signal(barrier, inc=1, device_id=peer, device_id_type=MESH)
        for load in self.loads:
            self.load_copy(load).start()
        pl.semaphore_wait(barrier, len(peers))

    def made(self, chunk, block):
        for flush in self.fresh_flush.get((chunk, block), ()):
            self.flush_copy(flush).start()

    def settle(self):
        @pl.when(self.step == self.steps - 1)
        def _():
            for flush in self.flushes:
                self.flush_copy(flush).wait()

    def remote(self, source, target, index, device):
        return pltpu.make_async_remote_copy(
            src_ref=source,
            dst_ref=target,
            send_sem=self.refs[self.sent].at[index],
            recv_sem=self.refs[self.arrived].at[index],
            device_id=device,
            device_id_type=MESH,
        )

    def copy(self, item):
        slots = 8 >> item.hop
        handle, place, low = item.send
        source = self.refs[handle].at[pl.ds(low, slots), place]
        target = self.refs[item.got[0]].at[pl.ds(0, slots), item.got[1]]
        return self.remote(source, target, item.sem, self.device(item.bit))

    def begin(self, item):
        self.copy(item).start()

    def finish(self, item):
        self.copy(item).wait()
        if item.load is not None:
            self.load_copy(item.load).wait()
        keep, at = self.refs[item.keep[0]], item.keep[1]
        got, place = self.refs[item.got[0]], item.got[1]
        if item.hop == 3:
            done, final = self.refs[item.done[0]], item.done[1]
            done[final] = keep[0, at].astype(f32) + got[0, place].astype(f32)
        else:

            @pl.loop(0, 8 >> item.hop)
            def _(slot):
                keep[slot, at] = keep[slot, at] + got[slot, place]

            for flush in item.flush or ():
                self.flush_copy(flush).start()

    def small_copy(self, item):
        target = self.refs[self.small_got].at[item[0]]
        return self.remote(self.refs[self.total], target, item[1], self.device(1 << item[0]))

    def small_begin(self, item):
        self.small_copy(item).start()

    def small_finish(self, item):
        self.small_copy(item).wait()
        total = self.refs[self.total][...] + self.refs[self.small_got][item[0]]
        self.refs[self.total][...] = total
        if item[0] == 3:
            self.refs[self.small_out][...] = total

    def cross_copy(self, item):
        rows = pl.ds(item[0], item[1])
        device = {"narrow": 1 - self.side}
        source = self.refs[self.cross_out].at[rows]
        return self.remote(source, self.refs[self.cross_got].at[rows], item[2], device)

    def cross_begin(self, item):
        self.cross_copy(item).start()

    def cross_finish(self, item):
        self.cross_copy(item).wait()
        rows = pl.ds(item[0], item[1])
        self.refs[self.cross_in][rows] = self.refs[self.cross_got][rows]

    def fire(self, low, high=None):
        high = low + 1 if high is None else high

        def spot(time):
            return min(time // 8, self.steps - 1)

        found = [e for e in self.events if low <= e[0] - 8 * spot(e[0]) < high]
        for at in sorted({spot(e[0]) for e in found}):

            @pl.when(self.step == at)
            def _(at=at):
                for event in found:
                    if spot(event[0]) == at:
                        event[3](event[4])

    def close(self, results, finals):
        for key, keep, sent, place in self.kept_out:
            self.state[key] = (results[keep], None if sent is None else results[sent], place)
        for key, done, place in self.done_out:
            self.state.pop(key, None)
            finals[key] = (results[done], place)


def ff_back(number, layer, grads, lengths, saved, weights, state, finals):
    _, attn_out, ff_up, ff_down, _, gains, _ = weights
    unit1, scale1, rb, act, slope, unit2, scale2, blended = saved
    n, d = unit1.shape
    rows = d // 16
    tiles = act.shape[1] // d
    front = SIZES[DOWN]
    cut = d // front
    steps = front + tiles + 1
    top = len(grads) == 1
    parts = Parts()
    later = lambda i: jnp.clip(i - front, 0, tiles - 1)
    h_count = parts.inp(lengths, scalar_spec())
    h_grads = [parts.inp(grad, fixed((n, d))) for grad in grads]
    l_act = parts.late(act)
    h_slope = parts.inp(slope, pl.BlockSpec((n, d), lambda i: (0, later(i))))
    h_wd = parts.inp(ff_down, pl.BlockSpec((None, d, d), lambda i: (0, later(i), 0)))
    h_wu = parts.inp(ff_up, pl.BlockSpec((None, d, d), lambda i: (0, 0, later(i))))
    l_wo = parts.late(attn_out, (d, d))
    h_gains = parts.inp(gains, fixed((None, 2, d)))
    l_unit1, h_scale1 = parts.late(unit1), parts.inp(scale1, fixed((n, 1)))
    h_unit2, h_scale2 = parts.inp(unit2, fixed((n, d))), parts.inp(scale2, fixed((n, 1)))
    l_rb, l_blended = parts.late(rb), parts.late(blended)
    lates = (l_act, l_rb, l_unit1, l_wo, l_blended)
    h_act, h_rb, h_unit1, h_wo, h_blended = (item[1] for item in lates)
    h_gr, h_do = parts.out((n, d), f32), parts.out((n, d), bf16)
    h_sums = parts.out((16, d), f32)
    h_acc, h_gb = parts.vmem((n, d), f32), parts.vmem((n, d), bf16)
    h_turned, h_held = parts.vmem((d, n), bf16), parts.vmem((d, d), bf16)
    h_cols = parts.vmem((front, n, cut), bf16)
    h_tall = parts.vmem((tiles * d, cut), bf16)
    traffic = Traffic(parts, number, layer, (DOWN, UP), state, rows, d)
    traffic.steps = steps

    def body(refs):
        step = pl.program_id(0)
        traffic.bind(refs, step)
        me = traffic.me
        sums, acc, gb = refs[h_sums], refs[h_acc], refs[h_gb]
        turned, held = refs[h_turned], refs[h_held]

        @pl.when(step == 0)
        def _():
            traffic.open()

        traffic.fire(0)

        @pl.when(step == 0)
        def _():
            for item in lates:
                fetch(refs, item).start()

            def strip(rows, carry):
                g = refs[h_grads[0]][rows].astype(f32)
                if top:
                    row = lax.broadcasted_iota(jnp.int32, (16, 1), 0) + rows.start
                    g = jnp.where(row < count_of(refs[h_count]), g, 0.0)
                else:
                    g = g + refs[h_grads[1]][rows].astype(f32)
                unit = refs[h_unit2][rows]
                back = normalise_back(g, unit, refs[h_scale2][rows], refs[h_gains][1:2])
                acc[rows] = back
                low = back.astype(bf16)
                gb[rows] = low
                for index in range(front):
                    refs[h_cols][index, rows] = low[:, index * cut : (index + 1) * cut]
                found = (low.astype(f32), g, g * unit)
                return tuple(a + fold(b) for a, b in zip(carry, found))

            zero = jnp.zeros((8, d), f32)
            found = each_strip(n, 16, strip, (zero, zero, zero))
            sums[0:8] = zero
            sums[8:16] = zero
            for at, value in zip((4, 5, 7), found):
                sums[at : at + 1] = jnp.sum(value, axis=0, keepdims=True)
            fetch(refs, l_act).wait()

        @pl.when(step < front)
        def _():
            refs[h_tall][...] = tn(refs[h_act][...], refs[h_cols][step]).astype(bf16)

        for block in range(front):

            @pl.when(step == block)
            def _(block=block):
                keep, send = refs[traffic.keep[DOWN]], refs[traffic.send[DOWN]]
                height = rows * tiles
                put_rows(
                    me, refs[h_tall], layer, DOWN, block, 16, 0, keep, send, height, height
                )
                traffic.made(DOWN, block)

        @pl.when(step == front)
        def _():
            fetch(refs, l_rb).wait()
            turned[...] = refs[h_rb][...].T

        middle = (step >= front) & (step < front + tiles)

        @pl.when(middle)
        def _():
            grad = nt(gb[...], refs[h_wd][...]) * refs[h_slope][...].astype(f32)
            grad = grad.astype(bf16)
            sums[pl.ds(8 + step - front, 1)] = jnp.sum(grad.astype(f32), axis=0, keepdims=True)
            held[0:n] = grad

        traffic.fire(1)

        @pl.when(middle)
        def _():
            acc[...] += nt(held[0:n], refs[h_wu][...])

        traffic.fire(2)

        @pl.when(middle)
        def _():
            held[...] = nn(turned[...], held[0:n]).astype(bf16)

        @pl.when(step == front + tiles)
        def _():
            for item in (l_unit1, l_wo, l_blended):
                fetch(refs, item).wait()
            turned[...] = refs[h_blended][...].T

            def strip(rows, carry):
                g = acc[rows]
                unit = refs[h_unit1][rows]
                back = normalise_back(g, unit, refs[h_scale1][rows], refs[h_gains][0:1])
                refs[h_gr][rows] = back
                low = back.astype(bf16)
                gb[rows] = low
                found = (low.astype(f32), g, g * unit)
                return tuple(a + fold(b) for a, b in zip(carry, found))

            zero = jnp.zeros((8, d), f32)
            found = each_strip(n, 16, strip, (zero, zero, zero))
            for at, value in zip((2, 3, 6), found):
                sums[at : at + 1] = jnp.sum(value, axis=0, keepdims=True)
            low = gb[...]
            refs[h_do][...] = nt(low, refs[h_wo][...]).astype(bf16)
            held[...] = nn(turned[...], low).astype(bf16)

        for block in range(tiles + 1):

            @pl.when(step == front + block)
            def _(block=block):
                keep, send = refs[traffic.keep[UP]], refs[traffic.send[UP]]
                put_rows(me, held, layer, UP, block, 16, 0, keep, send, rows, rows)
                traffic.made(UP, block)

        traffic.fire(5, 1000)
        traffic.settle()

    results = parts.run(body, steps, 2 * n * d * d * (4 * tiles), 4 * d * d * tiles, number)
    traffic.close(results, finals)
    return results[h_gr], results[h_do], results[h_sums]


def attn_back(
    number, layer, arrays, offsets, blended, grad_blended, soft, boxes, weight, left_rows,
    residual, small, state, finals,
):
    n, d = grad_blended.shape
    per_shard = d // 16
    groups = 3
    wide = d // groups
    heads = H // groups
    boxed = boxes is not None
    halves = 1 if boxed else 2
    front = halves * groups
    steps = front + groups
    keys = soft.shape[2]
    spans = [(0, keys)] if boxed else [(0, 384), (384, keys)]
    parts = Parts()
    early = lambda i: jnp.where(i < front, lax.rem(i, groups), groups - 1)
    later = lambda i: jnp.clip(i - front, 0, groups - 1)

    def wide_block(offset):
        return pl.BlockSpec((n, wide), lambda i: (0, early(i) + offset // 2))

    h_q, h_k, h_v = (parts.inp(a, wide_block(o)) for a, o in zip(arrays, offsets))
    h_g = parts.inp(grad_blended, wide_block(0))
    h_o = parts.inp(blended, wide_block(0))
    h_p = parts.inp(soft, pl.BlockSpec((heads, n, keys), lambda i: (early(i), 0, 0)))
    h_kv = [parts.vmem((keys, wide), bf16) for _ in range(2)]
    h_dp = parts.vmem((n, keys), f32)
    h_w = []
    for index in range(3):
        when = early if (not boxed and index > 0) else later
        spec = pl.BlockSpec((None, d, wide), lambda i, w=when, k=index: (0, 0, w(i) + groups * k))
        h_w.append(parts.inp(weight, spec))
    l_left = [parts.late(rows) for rows in left_rows]
    h_turned = [parts.vmem((d, n), bf16) for rows in left_rows]
    l_gr = parts.late(residual)
    h_gr = l_gr[1]
    h_own = parts.out((n, d), f32)
    h_sums1 = parts.vmem((8, d), f32) if boxed else parts.out((8, d), f32)
    h_d = [parts.vmem((groups, n, wide), bf16) for _ in range(3)]
    h_ds, h_held = parts.vmem((n, keys), bf16), parts.vmem((d, d), bf16)
    if boxed:
        h_lengths = parts.inp(boxes[0], scalar_spec())
        h_boxes = parts.inp(boxes[1], fixed((None, 4, TEXT)))
        h_patches = parts.inp(patch_centres(n, keys), fixed((4, keys)))
        h_near = [parts.vmem((n, keys), bf16) for _ in range(2)]
        h_small1, h_small2 = (parts.inp(x, fixed((16, d))) for x in small[:2])
        h_sums2 = parts.inp(small[2], fixed((8, d)))
        h_hot_i, h_hot_j = parts.vmem((32, n), bf16), parts.vmem((keys, 128), bf16)
        h_step_x, h_step_y = parts.vmem((n, keys), bf16), parts.vmem((n, keys), bf16)
        h_far, h_tab = parts.vmem((n, 384), f32), parts.vmem((2 * H, 128), f32)
        times = ((21, 29), (29, 37), (37, 45), (45, 47))
        traffic = Traffic(
            parts, number, layer, (IN,), state, per_shard, d, small=((32, d), times)
        )
    else:
        h_acc = parts.vmem((n, d), f32)
        h_half = parts.vmem((groups, n, wide), f32)
        cross = [(0, 384, 21, 69), (384, n - 384, 45, 69)]
        traffic = Traffic(parts, number, layer, (IN,), state, per_shard, d, cross=((n, d), cross))
    traffic.steps = steps

    def body(refs):
        step = pl.program_id(0)
        traffic.bind(refs, step)
        me = traffic.me
        turned = [refs[h] for h in h_turned]
        dq, dk, dv = (refs[h] for h in h_d)
        wq, wk, wv = (refs[h] for h in h_w)
        own, held, ds_s = refs[h_own], refs[h_held], refs[h_ds]

        @pl.when(step == 0)
        def _():
            traffic.open()

        traffic.fire(0)

        @pl.when(step == 0)
        def _():
            for item in [*l_left, l_gr]:
                fetch(refs, item).start()
            for h in h_kv:
                refs[h][n:keys] = jnp.zeros((keys - n, wide), bf16)
            if boxed:
                row, col = centres_of(refs[h_lengths], refs[h_boxes][...], refs[h_patches][...])
                cx, cy = col[0:n, 0:1], col[0:n, 1:2]
                rx, ry = row[0:1, 0:n], row[1:2, 0:n]
                hots = hot_columns(cx, cy, n, reverse=True)
                lane = lax.broadcasted_iota(jnp.int32, (n, 128), 1)
                refs[h_hot_j][0:n] = jnp.where(lane < 32, hots, 0.0).astype(bf16)
                refs[h_hot_j][n:keys] = jnp.zeros((keys - n, 128), bf16)
                line = lax.broadcasted_iota(jnp.int32, (32, n), 0)
                cell = jnp.where(line < 16, rx >> 6, ry >> 6)
                refs[h_hot_i][...] = jnp.where(cell == (line & 15), 1.0, 0.0).astype(bf16)
                for h, c, r in ((h_step_x, cx, rx), (h_step_y, cy, ry)):
                    refs[h][:, 0:n] = jnp.where((c & 63) < (r & 63), 1.0, 0.0).astype(bf16)
                    refs[h][:, n:keys] = jnp.zeros((n, keys - n), bf16)

        def table_lines(head):
            far = refs[h_far]
            value = far[...]
            upper = value.astype(bf16)
            lower = (value - upper.astype(f32)).astype(bf16)
            hi = refs[h_hot_i][...]
            cells = nn(hi, upper) + nn(hi, lower)
            lane = lax.broadcasted_iota(jnp.int32, (16, 128), 1)
            for direction in range(2):
                rows = slice(16 * direction, 16 * direction + 16)
                level = cells[rows, 0:128]
                above = cells[rows, 128 * (direction + 1) : 128 * (direction + 2)]
                inside = (lane >= 16 * direction) & (lane < 16 * direction + 16)
                level = jnp.where(inside, level - above, 0.0)
                above = jnp.where(inside, above, 0.0)
                turn = (128 + 1 - 16 * direction) % 128
                line = pltpu.roll(level, turn, 1, stride=1, stride_axis=0)
                turn = (turn + 127) % 128
                line = line + pltpu.roll(above, turn, 1, stride=1, stride_axis=0)
                line = jnp.sum(line, axis=0, keepdims=True) * HD**0.5
                refs[h_tab][pl.ds(2 * heads * step + 2 * head + direction, 1)] = line

        def head_back(head, half):
            pair, h = head // 2, head % 2
            lanes = slice(128 * pair, 128 * pair + 128)
            low_key, high_key = spans[half]
            span, ends = slice(low_key, high_key), slice(low_key, min(high_key, n))
            group = step - half * groups
            mask = head_masks()[h]
            q, k, v, g = (refs[x][:, lanes] for x in (h_q, h_kv[0], h_kv[1], h_g))
            k, v = k[span], v[span]
            dp_s = refs[h_dp]
            dp_s[:, span] = nt(g * mask, v)
            tiles = [slice(t, t + 128) for t in range(low_key, high_key, 128)]
            for r in range(0, n, SUB):
                rows = slice(r, r + SUB)
                mean = (g[rows] * mask).astype(f32) * refs[h_o][rows, lanes]
                mean = jnp.sum(mean, axis=-1, keepdims=True)
                for t in tiles:
                    ds = refs[h_p][head, rows, t].astype(f32) * (dp_s[rows, t] - mean)
                    ds = ds.astype(bf16)
                    ds_s[rows, t] = ds
                    if boxed:
                        refs[h_near[0]][rows, t] = ds * refs[h_step_x][rows, t]
                        refs[h_near[1]][rows, t] = ds * refs[h_step_y][rows, t]
            if boxed:
                hj, far = refs[h_hot_j][...], refs[h_far]
                queries = nn(ds_s[...], jnp.concatenate([k, hj], axis=1))
                far[:, 0:128] = queries[:, 128:]
                queries = queries[:, :128]
                far[:, 128:256] = nn(refs[h_near[0]][...], hj)
                far[:, 256:384] = nn(refs[h_near[1]][...], hj)
            else:
                queries = nn(ds_s[:, span], k)
            count = ends.stop - ends.start
            values = (tn(ds_s[:, span], q)[:count], tn(refs[h_p][head, :, span], g)[:count])
            if boxed:
                table_lines(head)
            outs = []
            low = low_lanes(count)
            for ref, value in zip((dk, dv), values):
                value = value.astype(bf16)
                if h == 0:
                    ref[group, ends, lanes] = value
                else:
                    value = jnp.where(low, ref[group, ends, lanes].astype(f32), value.astype(f32))
                    ref[group, ends, lanes] = value.astype(bf16)
                    outs.append(jnp.sum(value, axis=0, keepdims=True))
            low = low_lanes(n)
            if halves == 2:
                half_s = refs[h_half]
                if half == 0 and h == 0:
                    half_s[group, :, lanes] = queries
                elif half == 0:
                    half_s[group, :, lanes] = jnp.where(low, half_s[group, :, lanes], queries)
                else:
                    queries = half_s[group, :, lanes] + queries
            if half == halves - 1:
                queries = queries.astype(bf16)
                if h == 1:
                    queries = jnp.where(
                        low, dq[group, :, lanes].astype(f32), queries.astype(f32)
                    )
                    outs.append(jnp.sum(queries, axis=0, keepdims=True))
                dq[group, :, lanes] = queries.astype(bf16)
            if h == 1:
                start = pl.multiple_of(group * wide + 128 * pair, 128)
                at = pl.ds(start, 128)
                sums = refs[h_sums1]
                if half == 0:
                    sums[1:2, at] = outs[1]
                else:
                    sums[1:2, at] += outs[1]
                if half == halves - 1:
                    sums[0:1, at] = outs[2]

        if not boxed:

            @pl.when(step == 0)
            def _():
                refs[h_sums1][...] = jnp.zeros((8, d), f32)

        @pl.when(step < front)
        def _():
            refs[h_kv[0]][0:n] = refs[h_k][...]
            refs[h_kv[1]][0:n] = refs[h_v][...]

        for head in range(heads):
            for half in range(halves):

                @pl.when((step >= half * groups) & (step < half * groups + groups))
                def _(head=head, half=half):
                    head_back(head, half)

            traffic.fire(1 + head)

        @pl.when(step == (0 if boxed else front - 1))
        def _():
            for target, item in zip(turned, l_left):
                fetch(refs, item).wait()
                target[...] = refs[item[1]][...].T
            fetch(refs, l_gr).wait()

        def gradient(group):
            for index, ref in enumerate((dq, dk, dv)):
                left = turned[min(index, len(turned) - 1)]
                held[:, index * wide : (index + 1) * wide] = nn(left[...], ref[group]).astype(bf16)

        def store_gradient(start):
            for block in range(groups):

                @pl.when(step == start + block)
                def _(block=block):
                    keep, send = refs[traffic.keep[IN]], refs[traffic.send[IN]]
                    put_rows(
                        me, held, layer, IN, block, 16, 0, keep, send, per_shard, per_shard
                    )
                    traffic.made(IN, block)

        if boxed:

            @pl.when(step < groups)
            def _():
                gradient(step)

            store_gradient(0)

            @pl.when(step == groups - 1)
            def _():
                total = refs[traffic.total]
                total[0:16] = refs[h_small1][...]
                total[0:2] = refs[h_sums1][0:2]
                total[16:32] = refs[h_small2][...]
                total[16:18] = refs[h_sums2][0:2]
                each = d // 128
                for index in range(2 * H):
                    at = 128 * (index % each)
                    row = 12 + index // each
                    total[row : row + 1, at : at + 128] = refs[h_tab][index : index + 1]

        else:

            acc = refs[h_acc]
            for half, (low_key, high_key) in enumerate(spans):
                rows = slice(low_key, min(high_key, n))
                for group in range(groups):

                    @pl.when(step == half * groups + group)
                    def _(rows=rows, group=group):
                        value = nt(dk[group, rows], wk[...]) + nt(dv[group, rows], wv[...])
                        if group > 0:
                            value = value + acc[rows]
                        if group < groups - 1:
                            acc[rows] = value
                        else:
                            refs[traffic.cross_out][rows] = value.astype(bf16)

        @pl.when(step >= front)
        def _():
            group = step - front
            value = nt(dq[group], wq[...])
            if boxed:
                value = value + nt(dk[group], wk[...]) + nt(dv[group], wv[...])
            else:
                gradient(group)

            @pl.when(step == front)
            def _():
                own[...] = refs[h_gr][...] + value

            @pl.when(step > front)
            def _():
                own[...] += value

        if not boxed:
            store_gradient(front)
        traffic.fire(5, 1000)
        traffic.settle()

    results = parts.run(
        body, steps, 16 * n * n * d + 12 * n * d * d, 2 * H * n * n, number
    )
    traffic.close(results, finals)
    extra = results[traffic.small_out] if boxed else results[traffic.cross_in]
    return results[h_own], None if boxed else results[h_sums1], extra


def finish_outputs(me, finals, small, own, rows, d):
    tiles = 4
    share = d // 16
    cut = d // SIZES[DOWN]
    parts = Parts()
    h_me = parts.inp(me, scalar_spec())
    h_small = parts.inp(small, fixed(small.shape))
    arrays = {}
    for array, _ in finals.values():
        if id(array) not in arrays:
            arrays[id(array)] = parts.inp(array, fixed(array.shape))
    layers = []
    for _ in range(2):
        layers.append(
            (
                parts.out((rows, 3 * d), f32),
                parts.out((rows, d), f32),
                parts.out((rows, tiles * d), f32),
                parts.out((rows * tiles, d), f32),
                parts.out((6, 1, share), f32),
                parts.out((2, share), f32),
                parts.out((1, tiles * share), f32),
            )
        )
    h_table = parts.out((1, share), f32)
    h_own, h_stream = parts.inp(own, fixed(own.shape)), parts.out(own.shape, f32)

    def body(refs):
        me = refs[h_me][0]
        refs[h_stream][...] = refs[h_own][...]
        back = lax.rem(d - share * me, d)
        for layer, outs in zip((1, 2), layers):

            def block(chunk, index):
                array, place = finals[(layer, chunk, index)]
                return refs[arrays[id(array)]][place]

            wide = d // 3
            for group in range(3):
                value = block(IN, group)
                for part in range(3):
                    at = part * d + group * wide
                    refs[outs[0]][:, at : at + wide] = value[:, part * wide : (part + 1) * wide]
            refs[outs[1]][...] = block(UP, tiles)
            for index in range(tiles):
                refs[outs[2]][:, index * d : (index + 1) * d] = block(UP, index)
            for index in range(SIZES[DOWN]):
                refs[outs[3]][:, index * cut : (index + 1) * cut] = block(DOWN, index)
            base = 16 * (layer - 1)
            turned = pltpu.roll(refs[h_small][base : base + 8], back, 1)
            for index in range(6):
                refs[outs[4]][index] = turned[index : index + 1, :share]
            refs[outs[5]][...] = turned[6:8, :share]
            each = tiles * share
            line = jnp.zeros((1, d), f32)
            for index in range(tiles):
                row = refs[h_small][base + 8 + index : base + 9 + index]
                line = jnp.where(lax.div(me, 16 // tiles) == index, row, line)
            inner = lax.rem(me, 16 // tiles)
            turned = pltpu.roll(jnp.broadcast_to(line, (8, d)), lax.rem(d - each * inner, d), 1)
            refs[outs[6]][...] = turned[0:1, :each]
        direction = lax.div(me, 8)
        first = 4 * lax.rem(me, 8)
        line = jnp.zeros((1, 128), f32)
        lane = lax.broadcasted_iota(jnp.int32, (1, 128), 1)
        for head in range(H):
            found = []
            for way in range(2):
                index = 2 * head + way
                at = 128 * (index % (d // 128))
                row = 12 + index // (d // 128)
                found.append(refs[h_small][row : row + 1, at : at + 128])
            values = jnp.where(direction == 0, found[0], found[1])
            for bucket in range(4):
                value = jnp.sum(jnp.where(lane == first + bucket, values, 0.0))
                line = jnp.where(lane == H * bucket + head, value, line)
        refs[h_table][...] = line[:, :share]

    results = parts.run(body, 1, 1, 8 * rows * d, None)
    done = []
    for outs in layers:
        values = [results[h] for h in outs]
        vectors = jnp.transpose(values[4], (1, 0, 2))
        done.append(tuple(v[None] for v in values[:4]) + (vectors, values[5][None], values[6]))
    return results[h_stream], done[0], done[1], results[h_table]


def backward_with_hops(me, first, second, saved_one, saved_two, one, two, extra):
    top, lengths, boxes, own_b, mid_b, partner_b, soft_one, soft_two, full_one, full_two = extra
    d = own_b.shape[1]
    state, finals = {}, {}
    gr, do, small_two = ff_back(0, 2, [top], lengths, saved_two, second, state, finals)
    own, sums_two, returned = attn_back(
        1, 2, *two, full_two, do, soft_two, None, second[0], [mid_b, partner_b], gr, None, state, finals
    )
    gr, do, small_one = ff_back(
        2, 1, [own, returned], lengths, saved_one, first, state, finals
    )
    own, _, small = attn_back(
        3, 1, *one, full_one, do, soft_one, (lengths, boxes), first[0], [own_b], gr,
        (small_one, small_two, sums_two), state, finals,
    )
    return finish_outputs(me, finals, small, own, d // 16, d)


def swap(value, axis, bit):
    size = lax.axis_size(axis)
    return lax.ppermute(value, axis, [(i, i ^ bit) for i in range(size)])


def reduce_slots(parts, axis):
    keep, send = parts
    bit = 1
    while True:
        got = swap(send, axis, bit)
        count = keep.shape[0]
        if count == 1:
            return keep[0].astype(f32) + got[0].astype(f32)
        half = count // 2
        send = (keep[half:].astype(f32) + got[half:].astype(f32)).astype(keep.dtype)
        keep = (keep[:half].astype(f32) + got[:half].astype(f32)).astype(keep.dtype)
        bit *= 2


def reduce_small(rows, me, axis):
    size = lax.axis_size(axis)
    count = rows.shape[0]
    cut = jnp.transpose(rows.reshape(count, size, -1), (1, 0, 2))
    cut = jnp.take(cut, jnp.arange(size, dtype=jnp.int32) ^ me, axis=0)
    bit = 1
    while bit < size:
        pairs = cut.reshape(cut.shape[0] // 2, 2, *cut.shape[1:])
        cut = pairs[:, 0] + swap(pairs[:, 1], axis, bit)
        bit *= 2
    return cut[0]


def body(
    stream,
    lengths,
    layout_boxes,
    self_attn_in,
    self_attn_out,
    self_ff_up,
    self_ff_down,
    self_vectors,
    self_gains,
    self_up_bias,
    cross_attn_in,
    cross_attn_out,
    cross_ff_up,
    cross_ff_down,
    cross_vectors,
    cross_gains,
    cross_up_bias,
    box_table,
    cotangent,
):
    pair = lengths.T
    place = lax.axis_index("wide")
    devices = lax.axis_size("wide")
    me = place.astype(jnp.int32).reshape(1)
    n, d = stream.shape[2:]
    ff = self_ff_up.shape[2]
    first = (
        self_attn_in,
        self_attn_out,
        self_ff_up,
        self_ff_down,
        jnp.transpose(self_vectors, (1, 0, 2)),
        self_gains,
        self_up_bias,
    )
    second = (
        cross_attn_in,
        cross_attn_out,
        cross_ff_up,
        cross_ff_down,
        jnp.transpose(cross_vectors, (1, 0, 2)),
        cross_gains,
        cross_up_bias,
    )
    own_b = stream.reshape(n, d)
    top = cotangent.reshape(n, d)
    found = attend_forward(
        own_b, own_b, False, self_attn_in, first[4], pair, False, layout_boxes, box_table
    )
    *rows_one, blend_one, soft_one, full_one = found
    one = (rows_one, (0, 0, 0))
    if devices == 16:
        saved_one = feed_forward_sending(blend_one, own_b, first, cross_attn_in, second[4])
        *saved_one, partner_b, q_two = saved_one
    else:
        saved_one = feed_forward(blend_one, own_b, first, pair, False)
        partner_b = swap(saved_one[-1], "narrow", 1)
        q_two = saved_one[-1]
    unit_one, scale_one, rb_one, act_one, slope_one, unit_two, scale_two, mid, mid_b = saved_one
    found = attend_forward(
        q_two, partner_b, devices == 16, cross_attn_in, second[4], pair, True, None, None
    )
    *rows_two, blend_two, soft_two, full_two = found
    two = (rows_two, (0, 0, 0))
    saved_two = feed_forward(blend_two, mid, second, pair, True)
    unit_three, scale_three, rb_two, act_two, slope_two, unit_four, scale_four, final = saved_two

    side = lax.axis_index("narrow")
    own_count = jnp.where(side == 0, lengths[0], lengths[1])
    slot = jnp.arange(n, dtype=jnp.int32)
    padding = ((0, 0), (0, n - TEXT))
    boxes = layout_boxes[0]
    text = jnp.pad((boxes[:2] + boxes[2:]) >> 1, padding)
    grid_side = jnp.where(own_count > GRID_LO * GRID_LO, GRID_HI, GRID_LO).astype(jnp.int32)
    patch = jnp.stack([slot % grid_side, slot // grid_side])
    patch = (patch * 1000 + 500) // grid_side
    centres = jnp.where(side == 0, text, patch)
    places = (centres.T, centres)

    if devices == 16:
        saved = (unit_one, scale_one, rb_one, act_one, slope_one, unit_two, scale_two, blend_one)
        later = (
            unit_three, scale_three, rb_two, act_two, slope_two, unit_four, scale_four, blend_two
        )
        extra = (
            top, pair, layout_boxes, own_b, mid_b, partner_b, soft_one, soft_two, full_one, full_two
        )
        grad_stream, grads_one, grads_two, grad_table = backward_with_hops(
            me, first, second, saved, later, one, two, extra
        )
        return (final[None, None], grad_stream[None, None]) + grads_one + grads_two + (grad_table,)

    def large(parts):
        if len(parts) == 2:
            return reduce_slots(parts, "wide")
        return lax.psum_scatter(parts[0].astype(f32), "wide", scatter_dimension=0, tiled=True)

    def columns(value, lead):
        if value.ndim == 2:
            return value[:, lead[0] * d : lead[1] * d][None]
        picked = value[lead[0] : lead[1]]
        return jnp.transpose(picked, (1, 0, 2)).reshape(1, picked.shape[1], -1)

    dz, gb, sums_four, down_two = down_gradient(
        me, own_count, [top], unit_four, scale_four, cross_gains, act_two, devices, True
    )
    down_two = large(down_two)
    du, ups_two, ga, gr, do, sums_three = feed_backward(
        dz, gb, slope_two, unit_three, scale_three, second
    )
    steps = ff // d
    jobs = [(0, 0, 0)] * steps + [(1, 1, 0)]
    up_two = large(weight_gradients(me, jobs, [rb_two, blend_two], [du, ga], devices))
    dq, dk, dv, sums_two_attn = attend_backward(*two, do, soft_two, None)
    grad_partner = project_back([dk, dv], cross_attn_in, 1, None, bf16)
    returned = swap(grad_partner, "narrow", 1)
    grad_own = project_back([dq], cross_attn_in, 0, gr, f32)
    in_two = large(
        weight_gradients(
            me, [(0, 0, 0), (1, 1, 0), (1, 2, 0)], [mid_b, partner_b], [dq, dk, dv], devices
        )
    )

    dz, gb, sums_two, down_one = down_gradient(
        me, own_count, [grad_own, returned], unit_two, scale_two, self_gains, act_one, devices, False
    )
    down_one = large(down_one)
    du, ups_one, ga, gr, do, sums_one = feed_backward(
        dz, gb, slope_one, unit_one, scale_one, first
    )
    up_one = large(weight_gradients(me, jobs, [rb_one, blend_one], [du, ga], devices))
    dq, dk, dv, sums_one_attn, grad_tables = attend_backward(*one, do, soft_one, places)
    in_one = large(
        weight_gradients(
            me, [(0, 0, 0), (0, 1, 0), (0, 2, 0)], [own_b], [dq, dk, dv], devices
        )
    )
    grad_stream = project_back([dq, dk, dv], self_attn_in, 0, gr, f32)

    def ups_rows(ups):
        return jnp.transpose(
            ups.reshape(devices, steps, d // devices), (1, 0, 2)
        ).reshape(steps, d)

    table_row = jnp.transpose(
        grad_tables.reshape(H, 2, 128)[:, :, :NB], (1, 2, 0)
    ).reshape(1, 2 * NB * H)
    small = jnp.concatenate(
        [
            sums_one_attn[:2],
            sums_one[2:3],
            sums_one[1:2],
            sums_two[2:3],
            sums_two[1:2],
            sums_one[0:1],
            sums_two[0:1],
            ups_rows(ups_one),
            sums_two_attn[:2],
            sums_three[2:3],
            sums_three[1:2],
            sums_four[2:3],
            sums_four[1:2],
            sums_three[0:1],
            sums_four[0:1],
            ups_rows(ups_two),
            table_row,
        ]
    )
    small = reduce_small(small, me, "wide")
    half = 8 + steps

    def layer(values, base, inside, up, down):
        return (
            columns(inside, (0, 3)),
            columns(up, (steps, steps + 1)),
            columns(up, (0, steps)),
            down[None],
            values[base : base + 6][None],
            values[base + 6 : base + 8][None],
            values[base + 8 : base + half].reshape(1, -1),
        )

    return (
        (final[None, None], grad_stream[None, None])
        + layer(small, 0, in_one, up_one, down_one)
        + layer(small, half, in_two, up_two, down_two)
        + (small[2 * half :],)
    )


def solution(mesh):
    matrix = P("narrow", None, None)
    layer_in = (matrix,) * 6 + (P("narrow", None),)
    rows = P("narrow", "wide", None, None)
    in_specs = (
        (rows, P(None, "wide"), P("wide", None, None))
        + layer_in * 2
        + (P("narrow", None), rows)
    )
    layer_out = (P("narrow", "wide", None),) * 4 + (
        P("narrow", None, "wide"),
        P("narrow", None, "wide"),
        P("narrow", "wide"),
    )
    out_specs = (rows, rows) + layer_out * 2 + (P("narrow", "wide"),)
    return jax.shard_map(body, mesh=mesh, in_specs=in_specs, out_specs=out_specs, check_vma=False)
```
